32 devices in a mesh: row: 8 (over z, y), col: 4 (over x, core).
Axes of the slice: x: 2, y: 2, z: 4, core: 2. Of those that a mesh axis runs over, the one named last changes fastest.
Arguments:
- image_tokens: bfloat16 [51200, 768], P(('row', 'col')), may hold values from -9 to 9
- image_norm_gain: float32 [2, 768], replicated, may hold values from 0.5 to 1.5
- image_norm_bias: float32 [2, 768], replicated, may hold values from -1.75 to 1.75
- image_qkv: bfloat16 [768, 2304], P('col'), may hold values from -0.21875 to 0.21875
- image_out: bfloat16 [768, 768], P('col'), may hold values from -0.625 to 0.625
- image_up: bfloat16 [768, 3072], P('col'), may hold values from -0.21875 to 0.21875
- image_down: bfloat16 [3072, 768], P('col'), may hold values from -0.15625 to 0.15625
- text_tokens: bfloat16 [16384, 768], P(('row', 'col')), may hold values from -6 to 6
- text_lengths: int32 [1024], P(('row', 'col')), may hold values from 4 to 16, as said below
- norm1_gain: float32 [768], replicated, may hold values from 0.5 to 1.5
- norm1_bias: float32 [768], replicated, may hold values from -1.75 to 1.75
- norm2_gain: float32 [768], replicated, may hold values from 0.5 to 1.5
- norm2_bias: float32 [768], replicated, may hold values from -1.75 to 1.75
- text_qkv: bfloat16 [768, 2304], replicated, may hold values from -0.21875 to 0.21875
- text_out: bfloat16 [768, 768], replicated, may hold values from -0.625 to 0.625
- text_up: bfloat16 [768, 3072], replicated, may hold values from -0.21875 to 0.21875
- text_down: bfloat16 [3072, 768], replicated, may hold values from -0.15625 to 0.15625
- text_proj: bfloat16 [768, 768], replicated, may hold values from -0.21875 to 0.21875
Outputs:
- mean_loss: float32 [], replicated
- text_hidden: bfloat16 [16384, 768], P(('row', 'col'))
- text_input_grad: bfloat16 [16384, 768], P(('row', 'col'))
- grad_norm1_gain: float32 [768], replicated
- grad_norm1_bias: float32 [768], replicated
- grad_norm2_gain: float32 [768], replicated
- grad_norm2_bias: float32 [768], replicated
- grad_qkv: float32 [768, 2304], P('row', 'col')
- grad_out: float32 [768, 768], P('row', 'col')
- grad_up: float32 [768, 3072], P('row', 'col')
- grad_down: float32 [3072, 768], P('row', 'col')
- grad_proj: float32 [768, 768], P('row', 'col')
The draws below stay inside these ranges and needn't reach their ends.
Inputs may be any that keep to these rules, and one draw needn't show every extreme that they name: Caption n's true tokens are its first text_lengths[n] slots; some caption has 16 and some has 4.
All inputs are finite; a program needn't handle non-finite values.
Results may differ from the reference program's by a relative error of at most 0.015.
Values may be sent and summed in bfloat16 or wider, within the bound.
A program may use at most 256 MiB of HBM per device.

```python
import math
import jax
import jax.numpy as jnp
from jax import lax

D = 768
HEADS = 12
FF = 3072
IMG_TOK = 50
TXT_TOK = 16
LEN_MIN = 4
PAIRS = 1024


def draw_text_lengths(key, part):
    key = jax.random.fold_in(key, 7)
    pick_key, long_key, short_key = jax.random.split(key, 3)
    lengths = jax.random.randint(pick_key, (PAIRS,), LEN_MIN, TXT_TOK + 1)
    longest = jax.random.randint(long_key, (), 0, PAIRS)
    shortest = (longest + 1 + jax.random.randint(short_key, (), 0, PAIRS - 1)) % PAIRS
    lengths = lengths.at[longest].set(TXT_TOK)
    lengths = lengths.at[shortest].set(LEN_MIN)
    return lengths.astype(jnp.int32)


def draw_image_tokens(key, part):
    key = jax.random.fold_in(key, 11)
    token_key, image_key = jax.random.split(key, 2)
    token_part = jax.random.normal(token_key, (PAIRS * IMG_TOK, D), jnp.float32)
    image_part = 2.0 * jax.random.normal(image_key, (PAIRS, D), jnp.float32)
    shaped = token_part.reshape(PAIRS, IMG_TOK, D) + image_part[:, None, :]
    return jnp.clip(shaped.reshape(PAIRS * IMG_TOK, D), -9.0, 9.0).astype(jnp.bfloat16)


def block_scale(stream_key, extent, cuts, smallest, high):
    level, own = 1.0, jax.random.fold_in(stream_key, 6)
    for axis_at, parts in cuts:
        heights = jnp.exp(jax.random.uniform(jax.random.fold_in(own, axis_at), (parts,), jnp.float32, smallest / len(cuts), high / len(cuts)))
        level = level * jnp.repeat(heights, extent[axis_at] // parts).reshape([-1 if axis == axis_at else 1 for axis in range(len(extent))])
    return level


def gaussian(stream_key, extent, scale, most, cuts=(), kind=jnp.bfloat16):
    level = block_scale(stream_key, extent, cuts, -0.22, 0.18) if cuts else 1.0
    result = jax.random.normal(stream_key, extent, jnp.float32) * scale * level
    return jnp.minimum(jnp.maximum(result, -most), most).astype(kind)


def setup_inputs(seed: int = 0) -> dict:
    seeds = jax.random.split(jax.random.key(seed), 19)
    image_tokens = draw_image_tokens(jax.random.fold_in(seeds[18], 71), 0)
    image_norm_gain = jnp.clip(1.0 + 0.1 * jax.random.normal(seeds[1], (2, D), jnp.float32), 0.5, 1.5)
    image_norm_bias = gaussian(seeds[2], (2, D), 0.3, 1.75, (), jnp.float32)
    image_qkv = gaussian(seeds[3], (D, 3 * D), D ** -0.5, 0.21875, ((0, 4),))
    image_out = gaussian(seeds[4], (D, D), (D // 8) ** -0.5, 0.625, ((0, 4),))
    image_up = gaussian(seeds[5], (D, FF), D ** -0.5, 0.21875, ((0, 4),))
    image_down = gaussian(seeds[6], (FF, D), (FF // 2) ** -0.5, 0.15625, ((0, 4),))
    text_tokens = gaussian(seeds[7], (PAIRS * TXT_TOK, D), 1.0, 6.0, ((0, 32),))
    text_lengths = draw_text_lengths(jax.random.fold_in(seeds[18], 71), 0)
    norm1_gain = jnp.clip(1.0 + 0.1 * jax.random.normal(seeds[9], (D,), jnp.float32), 0.5, 1.5)
    norm1_bias = gaussian(seeds[10], (D,), 0.3, 1.75, (), jnp.float32)
    norm2_gain = jnp.clip(1.0 + 0.1 * jax.random.normal(seeds[11], (D,), jnp.float32), 0.5, 1.5)
    norm2_bias = gaussian(seeds[12], (D,), 0.3, 1.75, (), jnp.float32)
    text_qkv = gaussian(seeds[13], (D, 3 * D), D ** -0.5, 0.21875)
    text_out = gaussian(seeds[14], (D, D), (D // 8) ** -0.5, 0.625)
    text_up = gaussian(seeds[15], (D, FF), D ** -0.5, 0.21875)
    text_down = gaussian(seeds[16], (FF, D), (FF // 2) ** -0.5, 0.15625)
    text_proj = gaussian(seeds[17], (D, D), D ** -0.5, 0.21875)
    return {"image_tokens": image_tokens, "image_norm_gain": image_norm_gain, "image_norm_bias": image_norm_bias, "image_qkv": image_qkv, "image_out": image_out, "image_up": image_up, "image_down": image_down, "text_tokens": text_tokens, "text_lengths": text_lengths, "norm1_gain": norm1_gain, "norm1_bias": norm1_bias, "norm2_gain": norm2_gain, "norm2_bias": norm2_bias, "text_qkv": text_qkv, "text_out": text_out, "text_up": text_up, "text_down": text_down, "text_proj": text_proj}


norm_eps = 1e-06
logit_scale = 50.0
masked_score = -1e+30
highest = lax.Precision.HIGHEST

@jax.custom_vjp
def low(v):
    return lax.optimization_barrier(v.astype(jnp.bfloat16)).astype(jnp.float32)

@jax.custom_vjp
def low_back(v):
    return v

def low_keep(v):
    return (low(v), None)

def low_pass(kept, grad):
    return (grad,)

def back_keep(v):
    return (v, None)

def back_low(kept, grad):
    return (low(grad),)
low.defvjp(low_keep, low_pass)
low_back.defvjp(back_keep, back_low)

def both_round(value):
    return low(low_back(value))

def layer_norm(row_data, gain_vec, bias_vec):
    row_mean = lax.optimization_barrier(jnp.mean(row_data, axis=-1, keepdims=True))
    centered = row_data - row_mean
    variance = lax.optimization_barrier(jnp.mean(centered * centered, axis=-1, keepdims=True))
    return centered * lax.rsqrt(variance + norm_eps) * gain_vec + bias_vec

def unit_rows(row_data):
    return row_data * lax.rsqrt(lax.optimization_barrier(jnp.sum(row_data * row_data, axis=-1, keepdims=True)) + norm_eps)

def exact_gelu(pre_act):
    return jax.nn.gelu(pre_act, approximate=False)

def matmul(left_side, right_side):
    return jnp.einsum('...d,de->...e', left_side, right_side, precision=highest)

def block_forward(hidden_in, valid_keys, gains, biases, w_qkv, w_out, w_up, w_down):
    groups, length, model_width = hidden_in.shape
    normed1 = low(layer_norm(hidden_in, gains[0], biases[0]))
    united_qkv = matmul(normed1, w_qkv)
    query_heads = both_round(united_qkv[..., :model_width]).reshape(groups, length, HEADS, -1)
    key_heads = both_round(united_qkv[..., model_width:2 * model_width]).reshape(groups, length, HEADS, -1)
    value_heads = both_round(united_qkv[..., 2 * model_width:]).reshape(groups, length, HEADS, -1)
    factor = query_heads.shape[-1] ** (-0.5)
    scores = jnp.einsum('gqhe,gkhe->ghqk', query_heads, key_heads, precision=highest) * factor
    scores = low_back(jnp.where(valid_keys[:, None, None, :], scores, masked_score))
    totals = jax.nn.logsumexp(scores, axis=-1, keepdims=True)
    prob_low = low(jnp.exp(scores - totals))
    mixed_heads = both_round(jnp.einsum('ghqk,gkhe->gqhe', prob_low, value_heads, precision=highest))
    hidden_mid = hidden_in + low_back(matmul(mixed_heads.reshape(groups, length, model_width), w_out))
    normed2 = low(layer_norm(hidden_mid, gains[1], biases[1]))
    pre_act = low_back(matmul(normed2, w_up))
    inner_act = low(exact_gelu(pre_act))
    return hidden_mid + low_back(matmul(inner_act, w_down))

def reference(image_tokens, image_norm_gain, image_norm_bias, image_qkv, image_out, image_up, image_down, text_tokens, text_lengths, norm1_gain, norm1_bias, norm2_gain, norm2_bias, text_qkv, text_out, text_up, text_down, text_proj):
    model_width = image_tokens.shape[1]
    pair_total = text_lengths.shape[0]
    image_group = math.gcd(pair_total, 64)
    image_seq = image_tokens.astype(jnp.float32).reshape(pair_total // image_group, image_group, IMG_TOK, model_width)
    image_gains = (image_norm_gain[0], image_norm_gain[1])
    image_biases = (image_norm_bias[0], image_norm_bias[1])
    iw_qkv = image_qkv.astype(jnp.float32)
    iw_out = image_out.astype(jnp.float32)
    iw_up = image_up.astype(jnp.float32)
    iw_down = image_down.astype(jnp.float32)

    def image_step(group_tokens):
        valid_keys = jnp.ones(group_tokens.shape[:2], dtype=bool)
        hidden_out = block_forward(group_tokens, valid_keys, image_gains, image_biases, iw_qkv, iw_out, iw_up, iw_down)
        return low(unit_rows(lax.optimization_barrier(jnp.mean(hidden_out, axis=1))))
    image_embed = lax.map(image_step, image_seq).reshape(pair_total, model_width)
    text_group = math.gcd(pair_total, 256)
    group_count = pair_total // text_group
    positions = lax.broadcasted_iota(jnp.int32, (pair_total, TXT_TOK), 1)
    valid_all = positions < text_lengths[:, None]
    weight_all = valid_all.astype(jnp.float32) / text_lengths[:, None].astype(jnp.float32)
    valid_groups = valid_all.reshape(group_count, text_group, TXT_TOK)
    weight_groups = weight_all.reshape(group_count, text_group, TXT_TOK)
    row_size = math.gcd(pair_total, 512)

    def forward(tokens_in, gain1, bias1, gain2, bias2, w_qkv, w_out, w_up, w_down, w_proj):

        def text_step(group_in):
            group_tokens, group_valid, group_weight = group_in
            state_out = block_forward(group_tokens, group_valid, (gain1, gain2), (bias1, bias2), w_qkv, w_out, w_up, w_down)
            pooled = low(lax.optimization_barrier(jnp.sum(state_out * group_weight[:, :, None], axis=1)))
            projected = low_back(matmul(pooled, w_proj))
            return (state_out, low(unit_rows(projected)))
        token_groups = tokens_in.reshape(group_count, text_group, TXT_TOK, model_width)
        states, text_embed = lax.map(jax.checkpoint(text_step), (token_groups, valid_groups, weight_groups))
        text_embed = text_embed.reshape(pair_total, model_width)

        def sim_step(image_block):
            sims = low_back(logit_scale * jnp.einsum('id,jd->ij', image_block, text_embed, precision=highest))
            return (jax.nn.logsumexp(sims, axis=1), jax.nn.logsumexp(sims, axis=0))
        row_blocks = image_embed.reshape(pair_total // row_size, row_size, model_width)
        row_lse, col_parts = lax.map(jax.checkpoint(sim_step), row_blocks)
        col_lse = jax.nn.logsumexp(col_parts, axis=0)
        positives = logit_scale * lax.optimization_barrier(jnp.sum(image_embed * text_embed, axis=1))
        objective = 0.5 * jnp.sum(row_lse.reshape(-1) + col_lse - 2.0 * positives)
        return (objective, states)
    objective, back_fn, states = jax.vjp(forward, text_tokens.astype(jnp.float32), norm1_gain, norm1_bias, norm2_gain, norm2_bias, text_qkv.astype(jnp.float32), text_out.astype(jnp.float32), text_up.astype(jnp.float32), text_down.astype(jnp.float32), text_proj.astype(jnp.float32), has_aux=True)
    grads = back_fn(jnp.ones((), jnp.float32))
    mean_loss = objective / pair_total
    text_hidden = states.reshape(pair_total * TXT_TOK, model_width).astype(jnp.bfloat16)
    text_input_grad = grads[0].astype(jnp.bfloat16)
    return (mean_loss, text_hidden, text_input_grad, grads[1], grads[2], grads[3], grads[4], grads[5], grads[6], grads[7], grads[8], grads[9])
```

```python
import functools
import math

import jax
import jax.numpy as jnp
from jax import lax
from jax.experimental import pallas as pl
from jax.experimental.pallas import tpu as pltpu
from jax.sharding import PartitionSpec as P

HEADS = 12
IMG_TOK = 50
norm_eps = 1e-06
logit_scale = 50.0
masked_score = -1e30
log2e = math.log2(math.e)
f32 = jnp.float32
bf16 = jnp.bfloat16
VMEM_LIMIT = 60 * 2**20


def dot_nn(a, b):
    return lax.dot_general(a, b, (((1,), (0,)), ((), ())), preferred_element_type=f32)


def dot_nt(a, b):
    return lax.dot_general(a, b, (((1,), (1,)), ((), ())), preferred_element_type=f32)


def dot_tn(a, b):
    return lax.dot_general(a, b, (((0,), (0,)), ((), ())), preferred_element_type=f32)


def split_low(x):
    high = x.astype(bf16)
    return high, (x - high.astype(f32)).astype(bf16)


def normed(x):
    centered = x - jnp.mean(x, axis=-1, keepdims=True)
    spread = lax.rsqrt(jnp.mean(centered * centered, axis=-1, keepdims=True) + norm_eps)
    return centered * spread, spread


def layer_norm(x, gain, bias):
    return normed(x)[0] * gain + bias


def normal_tail(x):
    size = jnp.abs(x)
    t = 1.0 / (1.0 + (0.3275911 * math.sqrt(0.5)) * size)
    bell = jnp.exp2((-0.5 * log2e) * (x * x))
    series = 0.5 * 1.061405429
    for factor in (-1.453152027, 1.421413741, -0.284496736, 0.254829592):
        series = series * t + 0.5 * factor
    return size, bell, series * t * bell


def gelu(x):
    size, _, tail = normal_tail(x)
    return jnp.maximum(x, 0.0) - size * tail


def gelu_and_slope(x):
    size, bell, tail = normal_tail(x)
    value = jnp.maximum(x, 0.0) - size * tail
    below = jnp.where(x >= 0.0, 1.0 - tail, tail)
    return value, below + x * (bell * (1.0 / math.sqrt(2.0 * math.pi)))


def lane_halves(width):
    lane = lax.broadcasted_iota(jnp.int32, (1, width), 1)
    first = (lane < width // 2).astype(f32)
    return first.astype(bf16), (1.0 - first).astype(bf16)


def stack_heads(x, first, second):
    return jnp.concatenate([x * first, x * second], axis=0)


def join_heads(stacked):
    rows, width = stacked.shape[0] // 2, stacked.shape[1]
    lane = lax.broadcasted_iota(jnp.int32, (rows, width), 1)
    return jnp.where(lane < width // 2, stacked[:rows], stacked[rows:])


def soft_weights(query, key, bias, factor):
    scores = dot_nt(query, key) * (factor * log2e) + bias
    weights = jnp.exp2(scores - jnp.max(scores, axis=-1, keepdims=True))
    return weights, 1.0 / jnp.sum(weights, axis=-1, keepdims=True)


def text_bias(key_bias_ref, block, rows, length):
    near = lax.broadcasted_iota(jnp.int32, (rows, rows), 0) // length
    far = lax.broadcasted_iota(jnp.int32, (rows, rows), 1) // length
    columns = pl.ds(pl.multiple_of(block * rows, rows), rows)
    bias = jnp.where(near == far, key_bias_ref[:, columns], masked_score)
    return jnp.concatenate([bias, bias], axis=0)


def member(len_ref, captions, tokens):
    length = tokens // captions
    token = lax.broadcasted_iota(jnp.int32, (captions, tokens), 1)
    caption = lax.broadcasted_iota(jnp.int32, (captions, tokens), 0)
    return ((token // length == caption) & (token % length < len_ref[...])).astype(f32)


def spread_rows(x, length):
    rows, width = x.shape
    return jnp.broadcast_to(x[:, None, :], (rows, length, width)).reshape(rows * length, width)


def text_forward_kernel(
    tok_ref, len_ref, key_bias_ref, gain1, bias1, gain2, bias2, qkv_hbm, out_hbm, up_hbm, down_hbm, proj_hbm,
    hidden_ref, embed_ref, projected_ref, pooled_ref, inner_sum_ref, heads_ref, mixed_ref, mid_ref, slope_ref,
    w_qkv, w_out, w_up, w_down, w_proj, norm_ref, inner_ref, sems,
):
    tokens, width = tok_ref.shape
    captions = len_ref.shape[0]
    length = tokens // captions
    wide = w_up.shape[1]
    pairs = ((qkv_hbm, w_qkv), (out_hbm, w_out), (up_hbm, w_up), (down_hbm, w_down), (proj_hbm, w_proj))
    loads = [pltpu.make_async_copy(s, d, sems.at[i]) for i, (s, d) in enumerate(pairs)]
    for load in loads:
        load.start()

    band = 128

    @pl.loop(0, tokens // band)
    def _(i):
        rows = pl.ds(pl.multiple_of(i * band, band), band)
        norm_ref[rows, :] = layer_norm(tok_ref[rows, :].astype(f32), gain1[...], bias1[...]).astype(bf16)

    loads[0].wait()

    @pl.loop(0, 3 * width // 256)
    def _(j):
        columns = pl.ds(pl.multiple_of(j * 256, 256), 256)
        heads_ref[:, columns] = dot_nn(norm_ref[...], w_qkv[:, columns]).astype(bf16)

    first, second = lane_halves(128)
    factor = (width // HEADS) ** -0.5

    @pl.loop(0, tokens // band)
    def _(block):
        rows = pl.ds(pl.multiple_of(block * band, band), band)
        bias = text_bias(key_bias_ref, block, band, length)
        for pair in range(width // 128):
            at = pair * 128
            query = stack_heads(heads_ref[rows, at : at + 128], first, second)
            weights, scale = soft_weights(query, heads_ref[rows, width + at : width + at + 128], bias, factor)
            value = heads_ref[rows, 2 * width + at : 2 * width + at + 128]
            mixed = dot_nn(weights.astype(bf16), value) * scale
            mixed_ref[rows, at : at + 128] = join_heads(mixed).astype(bf16)

    loads[1].wait()

    @pl.loop(0, tokens // band)
    def _(i):
        rows = pl.ds(pl.multiple_of(i * band, band), band)
        mid = tok_ref[rows, :].astype(f32) + dot_nn(mixed_ref[rows, :], w_out[...])
        mid_ref[rows, :] = mid
        norm_ref[rows, :] = layer_norm(mid, gain2[...], bias2[...]).astype(bf16)

    loads[2].wait()
    chosen = member(len_ref, captions, tokens)
    chosen_low = chosen.astype(bf16)
    place = lax.broadcasted_iota(jnp.int32, (captions, length, 1), 1)
    valid = (place < len_ref[...].reshape(captions, 1, 1)).astype(f32).reshape(tokens, 1)

    @pl.loop(0, wide // 256)
    def _(j):
        columns = pl.ds(pl.multiple_of(j * 256, 256), 256)
        value, slope = gelu_and_slope(dot_nn(norm_ref[...], w_up[:, columns]))
        value = value.astype(bf16)
        inner_ref[:, columns] = value
        slope_ref[:, columns] = (slope * valid).astype(bf16)
        inner_sum_ref[:, columns] = dot_nn(chosen_low, value).astype(bf16)

    loads[3].wait()
    inverse = 1.0 / len_ref[...].astype(f32)

    @pl.loop(0, width // 256)
    def _(j):
        columns = pl.ds(pl.multiple_of(j * 256, 256), 256)
        state = mid_ref[:, columns] + dot_nn(inner_ref[...], w_down[:, columns])
        hidden_ref[:, columns] = state.astype(bf16)
        high, low = split_low(state)
        pooled_ref[:, columns] = ((dot_nn(chosen_low, high) + dot_nn(chosen_low, low)) * inverse).astype(bf16)

    loads[4].wait()
    projected = dot_nn(pooled_ref[...], w_proj[...])
    projected_ref[...] = projected
    embed_ref[...] = (
        projected * lax.rsqrt(jnp.sum(projected * projected, axis=-1, keepdims=True) + norm_eps)
    ).astype(bf16)


def text_backward_kernel(
    tok_ref, len_ref, key_bias_ref, gain1, bias1, gain2, bias2, embed_grad_ref, projected_ref,
    heads_ref, mixed_ref, mid_ref, slope_ref, qkv_hbm, out_hbm, up_hbm, down_hbm, proj_hbm,
    proj_grad_ref, branch_ref, up_grad_ref, out_grad_ref, qkv_grad_ref, input_grad_ref, norm_grad_ref,
    w_qkv, w_out, w_up, w_down, w_proj, norm_ref, pre_grad_ref, wide_ref, mid_grad_ref, low_grad_ref,
    mixed_grad_ref, heads_grad_ref, sems,
):
    tokens, width = tok_ref.shape
    captions = len_ref.shape[0]
    length = tokens // captions
    wide = w_up.shape[1]
    col_parts = up_grad_ref.shape[0]
    pairs = ((proj_hbm, w_proj), (down_hbm, w_down), (up_hbm, w_up), (out_hbm, w_out), (qkv_hbm, w_qkv))
    loads = [pltpu.make_async_copy(s, d, sems.at[i]) for i, (s, d) in enumerate(pairs)]
    for load in loads:
        load.start()
    band = 128

    @pl.loop(0, tokens // band)
    def _(i):
        rows = pl.ds(pl.multiple_of(i * band, band), band)
        norm_ref[rows, :] = layer_norm(mid_ref[rows, :], gain2[...], bias2[...]).astype(bf16)

    projected = projected_ref[...]
    embed_grad = embed_grad_ref[...]
    r = lax.rsqrt(jnp.sum(projected * projected, axis=-1, keepdims=True) + norm_eps)
    along = jnp.sum(projected * embed_grad, axis=-1, keepdims=True)
    proj_grad = (r * embed_grad - (r * r * r) * projected * along).astype(bf16)
    proj_grad_ref[...] = proj_grad
    loads[0].wait()
    state_grad = dot_nt(proj_grad, w_proj[...]) * (1.0 / len_ref[...].astype(f32))
    branch = state_grad.astype(bf16)
    branch_ref[...] = branch
    loads[1].wait()
    loads[2].wait()

    for part in range(col_parts):
        step = wide // col_parts

        @pl.loop(0, step // 256)
        def _(j):
            columns = pl.ds(pl.multiple_of(part * step + j * 256, 256), 256)
            inner_grad = dot_nt(branch, w_down[columns, :])
            pre_grad = (spread_rows(inner_grad, length) * slope_ref[:, columns].astype(f32)).astype(bf16)
            pre_grad_ref[:, columns] = pre_grad
            local = pl.ds(pl.multiple_of(j * 256, 256), 256)
            up_grad_ref[part, :, local] = dot_tn(norm_ref[...], pre_grad).astype(bf16)

    place = lax.broadcasted_iota(jnp.int32, (captions, length, 1), 1)
    valid = (place < len_ref[...].reshape(captions, 1, 1)).astype(f32).reshape(tokens, 1)

    @pl.loop(0, width // 256)
    def _(j):
        columns = pl.ds(pl.multiple_of(j * 256, 256), 256)
        wide_ref[:, columns] = dot_nt(pre_grad_ref[...], w_up[columns, :])

    mid_grad_ref[...] = spread_rows(state_grad, length) * valid
    norm_grad_ref[...] = jnp.zeros_like(norm_grad_ref)

    @pl.loop(0, tokens // band)
    def _(i):
        rows = pl.ds(pl.multiple_of(i * band, band), band)
        unit, spread = normed(mid_ref[rows, :])
        outer = wide_ref[rows, :]
        norm_grad_ref[2:3, :] += jnp.sum(outer * unit, axis=0, keepdims=True)
        norm_grad_ref[3:4, :] += jnp.sum(outer, axis=0, keepdims=True)
        outer = outer * gain2[...]
        inner = outer - jnp.mean(outer, axis=-1, keepdims=True)
        inner = inner - unit * jnp.mean(outer * unit, axis=-1, keepdims=True)
        mid_grad = mid_grad_ref[rows, :] + spread * inner
        mid_grad_ref[rows, :] = mid_grad
        low_grad_ref[rows, :] = mid_grad.astype(bf16)

    loads[3].wait()
    step = width // col_parts
    for part in range(col_parts):
        out_grad_ref[part] = dot_tn(
            mixed_ref[...], low_grad_ref[:, part * step : (part + 1) * step]
        ).astype(bf16)

    @pl.loop(0, tokens // band)
    def _(i):
        rows = pl.ds(pl.multiple_of(i * band, band), band)
        mixed_grad_ref[rows, :] = dot_nt(low_grad_ref[rows, :], w_out[...]).astype(bf16)
        norm_ref[rows, :] = layer_norm(tok_ref[rows, :].astype(f32), gain1[...], bias1[...]).astype(bf16)

    first, second = lane_halves(128)
    factor = (width // HEADS) ** -0.5

    @pl.loop(0, tokens // band)
    def _(block):
        rows = pl.ds(pl.multiple_of(block * band, band), band)
        bias = text_bias(key_bias_ref, block, band, length)
        for pair in range(width // 128):
            at = pair * 128
            query = stack_heads(heads_ref[rows, at : at + 128], first, second)
            key = heads_ref[rows, width + at : width + at + 128]
            value = heads_ref[rows, 2 * width + at : 2 * width + at + 128]
            grad = stack_heads(mixed_grad_ref[rows, at : at + 128], first, second)
            weights, scale = soft_weights(query, key, bias, factor)
            probs = weights * scale
            prob_grad = dot_nt(grad, value)
            total = jnp.sum(prob_grad * probs, axis=-1, keepdims=True)
            score_grad = (probs * (prob_grad - total)).astype(bf16)
            query_grad = join_heads(dot_nn(score_grad, key)) * factor
            heads_grad_ref[rows, at : at + 128] = query_grad.astype(bf16)
            key_grad = dot_tn(score_grad, query) * factor
            heads_grad_ref[rows, width + at : width + at + 128] = key_grad.astype(bf16)
            value_grad = dot_tn(probs.astype(bf16), grad)
            heads_grad_ref[rows, 2 * width + at : 2 * width + at + 128] = value_grad.astype(bf16)

    step = 3 * width // col_parts
    for part in range(col_parts):
        qkv_grad_ref[part] = dot_tn(
            norm_ref[...], heads_grad_ref[:, part * step : (part + 1) * step]
        ).astype(bf16)
    loads[4].wait()

    @pl.loop(0, width // 256)
    def _(j):
        columns = pl.ds(pl.multiple_of(j * 256, 256), 256)
        wide_ref[:, columns] = dot_nt(heads_grad_ref[...], w_qkv[columns, :])

    @pl.loop(0, tokens // band)
    def _(i):
        rows = pl.ds(pl.multiple_of(i * band, band), band)
        unit, spread = normed(tok_ref[rows, :].astype(f32))
        outer = wide_ref[rows, :]
        norm_grad_ref[0:1, :] += jnp.sum(outer * unit, axis=0, keepdims=True)
        norm_grad_ref[1:2, :] += jnp.sum(outer, axis=0, keepdims=True)
        outer = outer * gain1[...]
        inner = outer - jnp.mean(outer, axis=-1, keepdims=True)
        inner = inner - unit * jnp.mean(outer * unit, axis=-1, keepdims=True)
        input_grad_ref[rows, :] = (mid_grad_ref[rows, :] + spread * inner).astype(bf16)


def group_mean(images, rows):
    token = lax.broadcasted_iota(jnp.int32, (images, rows), 1)
    image = lax.broadcasted_iota(jnp.int32, (images, rows), 0)
    inside = (token >= image * IMG_TOK) & (token < (image + 1) * IMG_TOK)
    return inside.astype(f32).astype(bf16)


def load_parts(parts, target, sems, col, col_count):
    depth = target.shape[0] // col_count
    copies = []
    for k, part in enumerate(parts):
        place = pl.multiple_of((col ^ k) * depth, depth)
        copies.append(pltpu.make_async_copy(part, target.at[pl.ds(place, depth)], sems.at[k]))
    return copies


def image_mix_kernel(
    col_count, tok_ref, gain_ref, bias_ref, *refs,
):
    qkv_parts, out_parts = refs[:col_count], refs[col_count : 2 * col_count]
    normed_ref, mean_ref, w_qkv, w_out, norm_ref, heads_ref, mixed_ref, sems = refs[2 * col_count :]
    rows, width = tok_ref.shape
    images = rows // IMG_TOK
    step = pl.program_id(0)
    col = lax.axis_index("col")

    @pl.when(step == 0)
    def _():
        copies = load_parts(qkv_parts, w_qkv, sems.at[0], col, col_count)
        copies += load_parts(out_parts, w_out, sems.at[1], col, col_count)
        for copy in copies:
            copy.start()
        for copy in copies:
            copy.wait()

    norm_ref[...] = layer_norm(tok_ref[...].astype(f32), gain_ref[0:1, :], bias_ref[0:1, :]).astype(bf16)

    @pl.loop(0, 3 * width // 256)
    def _(j):
        columns = pl.ds(pl.multiple_of(j * 256, 256), 256)
        heads_ref[:, columns] = dot_nn(norm_ref[...], w_qkv[:, columns]).astype(bf16)

    first, second = lane_halves(128)
    factor = (width // HEADS) ** -0.5
    window = 112
    for pair in range(images // 2):
        start, low = pair * 2 * IMG_TOK, (pair * 2 * IMG_TOK) // 16 * 16
        near = lax.broadcasted_iota(jnp.int32, (window, window), 0) + low
        far = lax.broadcasted_iota(jnp.int32, (window, window), 1) + low
        same = (near >= start) & (near < start + 2 * IMG_TOK) & (far >= start) & (far < start + 2 * IMG_TOK)
        same = same & ((near >= start + IMG_TOK) == (far >= start + IMG_TOK))
        bias = jnp.where(same, 0.0, masked_score)
        bias = jnp.concatenate([bias, bias], axis=0)
        keep = lax.broadcasted_iota(jnp.int32, (16, 128), 0) + low < start
        span = slice(low, low + window)

        @pl.loop(0, width // 128)
        def _(two):
            at = pl.multiple_of(two * 128, 128)
            query = stack_heads(heads_ref[span, pl.ds(at, 128)], first, second)
            weights, scale = soft_weights(query, heads_ref[span, pl.ds(width + at, 128)], bias, factor)
            value = heads_ref[span, pl.ds(2 * width + at, 128)]
            mixed = join_heads(dot_nn(weights.astype(bf16), value) * scale)
            if low == start:
                mixed_ref[span, pl.ds(at, 128)] = mixed.astype(bf16)
            else:
                former = mixed_ref[low : low + 16, pl.ds(at, 128)].astype(f32)
                mixed_ref[low : low + 16, pl.ds(at, 128)] = jnp.where(keep, former, mixed[:16]).astype(bf16)
                mixed_ref[low + 16 : low + window, pl.ds(at, 128)] = mixed[16:].astype(bf16)

    mid = tok_ref[...].astype(f32) + dot_nn(mixed_ref[...], w_out[...])
    normed_ref[...] = layer_norm(mid, gain_ref[1:2, :], bias_ref[1:2, :]).astype(bf16)
    high, low = split_low(mid)
    select = group_mean(images, rows)
    mean_ref[...] = (dot_nn(select, high) + dot_nn(select, low)) * (1.0 / IMG_TOK)


def image_embed_kernel(col_count, normed_ref, mean_ref, *refs):
    up_parts, down_parts = refs[:col_count], refs[col_count : 2 * col_count]
    embed_ref, w_up, w_down, sum_ref, sems = refs[2 * col_count :]
    rows, width = normed_ref.shape
    images = rows // IMG_TOK
    wide = w_up.shape[1]
    step = pl.program_id(0)
    col = lax.axis_index("col")
    downs = load_parts(down_parts, w_down, sems.at[1], col, col_count)

    @pl.when(step == 0)
    def _():
        ups = load_parts(up_parts, w_up, sems.at[0], col, col_count)
        for copy in ups + downs:
            copy.start()
        for copy in ups:
            copy.wait()

    select = group_mean(images, rows)

    @pl.loop(0, wide // 256)
    def _(j):
        columns = pl.ds(pl.multiple_of(j * 256, 256), 256)
        inner = gelu(dot_nn(normed_ref[...], w_up[:, columns])).astype(bf16)
        sum_ref[pl.ds(pl.multiple_of(step * images, images), images), columns] = dot_nn(select, inner)

    @pl.when(step == pl.num_programs(0) - 1)
    def _():
        for copy in downs:
            copy.wait()
        high, low = split_low(sum_ref[...] * (1.0 / IMG_TOK))
        pooled = mean_ref[...] + dot_nn(high, w_down[...]) + dot_nn(low, w_down[...])
        embed_ref[...] = (
            pooled * lax.rsqrt(jnp.sum(pooled * pooled, axis=-1, keepdims=True) + norm_eps)
        ).astype(bf16)


def whole(shape):
    return pl.BlockSpec(shape, lambda *_: (0,) * len(shape))


in_vmem = pl.BlockSpec(memory_space=pltpu.VMEM)
anywhere = pl.BlockSpec(memory_space=pl.ANY)


def plain(kernel, outs, ins, scratch, name, **settings):
    return pl.pallas_call(
        kernel,
        out_shape=outs,
        in_specs=ins,
        out_specs=[in_vmem] * len(outs),
        scratch_shapes=scratch,
        compiler_params=pltpu.CompilerParams(vmem_limit_bytes=VMEM_LIMIT, **settings),
        name=name,
    )


def array(shape, dtype):
    return jax.ShapeDtypeStruct(shape, dtype)


def partners(x, col_count):
    order = [(i, i ^ 2) for i in range(col_count)]
    near = [(i, i ^ 1) for i in range(col_count)]
    far = lax.ppermute(x, "col", order)
    return [x, lax.ppermute(x, "col", near), far, lax.ppermute(far, "col", near)]


def body(
    image_tokens, image_norm_gain, image_norm_bias, image_qkv, image_out, image_up, image_down,
    text_tokens, text_lengths, norm1_gain, norm1_bias, norm2_gain, norm2_bias,
    text_qkv, text_out, text_up, text_down, text_proj,
):
    tokens, width = text_tokens.shape
    captions = text_lengths.shape[0]
    length = tokens // captions
    wide = text_up.shape[1]
    row_count, col_count = lax.axis_size("row"), lax.axis_size("col")
    row, col = lax.axis_index("row"), lax.axis_index("col")
    pair_total = captions * row_count * col_count
    image_rows, images = image_tokens.shape[0], image_tokens.shape[0] // IMG_TOK

    qkv_parts = partners(image_qkv, col_count)
    out_parts = partners(image_out, col_count)
    up_parts = partners(image_up, col_count)
    down_parts = partners(image_down, col_count)

    lengths = text_lengths.reshape(captions, 1)
    place = lax.broadcasted_iota(jnp.int32, (captions, length), 1)
    key_bias = jnp.where(place < lengths, 0.0, masked_score).reshape(1, tokens)
    vectors = [v.reshape(1, width) for v in (norm1_gain, norm1_bias, norm2_gain, norm2_bias)]
    weights = (text_qkv, text_out, text_up, text_down, text_proj)
    weight_scratch = [pltpu.VMEM(w.shape, bf16) for w in weights]

    (hidden, text_embed, projected, pooled, inner_sum, heads, mixed, mid, slope) = plain(
        text_forward_kernel,
        (
            array((tokens, width), bf16),
            array((captions, width), bf16),
            array((captions, width), f32),
            array((captions, width), bf16),
            array((captions, wide), bf16),
            array((tokens, 3 * width), bf16),
            array((tokens, width), bf16),
            array((tokens, width), f32),
            array((tokens, wide), bf16),
        ),
        [in_vmem] * 7 + [anywhere] * 5,
        weight_scratch
        + [pltpu.VMEM((tokens, width), bf16), pltpu.VMEM((tokens, wide), bf16), pltpu.SemaphoreType.DMA((5,))],
        "text_forward",
    )(text_tokens, lengths, key_bias, *vectors, *weights)

    groups = 4
    group_rows, group_images = image_rows // groups, images // groups
    parts = [anywhere] * (2 * col_count)
    image_tokens, text_embed = lax.optimization_barrier((image_tokens, text_embed))
    image_normed, image_mean = pl.pallas_call(
        functools.partial(image_mix_kernel, col_count),
        grid=(groups,),
        out_shape=(array((image_rows, width), bf16), array((images, width), f32)),
        in_specs=[
            pl.BlockSpec((group_rows, width), lambda i: (i, 0)),
            whole(image_norm_gain.shape),
            whole(image_norm_bias.shape),
        ]
        + parts,
        out_specs=(
            pl.BlockSpec((group_rows, width), lambda i: (i, 0)),
            pl.BlockSpec((group_images, width), lambda i: (i, 0)),
        ),
        scratch_shapes=[
            pltpu.VMEM((width, 3 * width), bf16),
            pltpu.VMEM((width, width), bf16),
            pltpu.VMEM((group_rows, width), bf16),
            pltpu.VMEM((group_rows, 3 * width), bf16),
            pltpu.VMEM((group_rows, width), bf16),
            pltpu.SemaphoreType.DMA((2, col_count)),
        ],
        compiler_params=pltpu.CompilerParams(vmem_limit_bytes=VMEM_LIMIT),
        name="image_mix",
    )(image_tokens, image_norm_gain, image_norm_bias, *qkv_parts, *out_parts)
    image_embed = pl.pallas_call(
        functools.partial(image_embed_kernel, col_count),
        grid=(groups,),
        out_shape=array((images, width), bf16),
        in_specs=[pl.BlockSpec((group_rows, width), lambda i: (i, 0)), whole((images, width))] + parts,
        out_specs=whole((images, width)),
        scratch_shapes=[
            pltpu.VMEM((width, wide), bf16),
            pltpu.VMEM((wide, width), bf16),
            pltpu.VMEM((images, wide), f32),
            pltpu.SemaphoreType.DMA((2, col_count)),
        ],
        compiler_params=pltpu.CompilerParams(vmem_limit_bytes=VMEM_LIMIT),
        name="image_embed",
    )(image_normed, image_mean, *up_parts, *down_parts)

    both = ("row", "col")
    image_all = lax.all_gather(image_embed, both, axis=0, tiled=True)
    sims = logit_scale * dot_nt(image_all, text_embed)
    lifted = jnp.exp(sims)
    row_sums = lax.psum(jnp.sum(lifted, axis=1), both)
    col_sums = jnp.sum(lifted, axis=0)
    sim_grad = (0.5 * (lifted / row_sums[:, None] + lifted / col_sums[None, :])).astype(bf16)
    image_own = image_embed.astype(f32)
    embed_grad = logit_scale * (dot_tn(sim_grad, image_all) - image_own)
    positives = logit_scale * jnp.sum(image_own * text_embed.astype(f32), axis=1)
    loss_part = 0.5 * jnp.sum(jnp.log(col_sums) - 2.0 * positives)

    (proj_grad, branch, up_grad, out_grad, qkv_grad, input_grad, norm_grads) = plain(
        text_backward_kernel,
        (
            array((captions, width), bf16),
            array((captions, width), bf16),
            array((col_count, width, wide // col_count), bf16),
            array((col_count, width, width // col_count), bf16),
            array((col_count, width, 3 * width // col_count), bf16),
            array((tokens, width), bf16),
            array((8, width), f32),
        ),
        [in_vmem] * 13 + [anywhere] * 5,
        weight_scratch
        + [
            pltpu.VMEM((tokens, width), bf16),
            pltpu.VMEM((tokens, wide), bf16),
            pltpu.VMEM((tokens, width), f32),
            pltpu.VMEM((tokens, width), f32),
            pltpu.VMEM((tokens, width), bf16),
            pltpu.VMEM((tokens, width), bf16),
            pltpu.VMEM((tokens, 3 * width), bf16),
            pltpu.SemaphoreType.DMA((5,)),
        ],
        "text_backward",
    )(
        text_tokens, lengths, key_bias, *vectors, embed_grad, projected, heads, mixed, mid, slope, *weights,
    )

    def scattered(matrix):
        blocks = matrix.reshape(col_count * row_count, width // row_count, matrix.shape[2])
        return lax.psum_scatter(blocks, ("col", "row"), scatter_dimension=0, tiled=True)[0].astype(f32)

    def by_row(x):
        x = lax.all_to_all(x, "row", split_axis=1, concat_axis=0, tiled=True)
        return lax.all_gather(x, "col", axis=0, tiled=True)

    def by_col(x):
        x = lax.all_gather(x, "row", axis=0, tiled=True)
        return lax.all_to_all(x, "col", split_axis=1, concat_axis=0, tiled=True)

    grad_down = dot_tn(by_row(inner_sum), by_col(branch))
    grad_proj = dot_tn(by_row(pooled), by_col(proj_grad))
    loss_total, norm_total = lax.psum((loss_part, norm_grads), both)
    mean_loss = (loss_total + 0.5 * jnp.sum(jnp.log(row_sums))) / pair_total
    return (
        mean_loss, hidden, input_grad, norm_total[0], norm_total[1], norm_total[2], norm_total[3],
        scattered(qkv_grad), scattered(out_grad), scattered(up_grad), grad_down, grad_proj,
    )


def solution(mesh):
    split = P(("row", "col"), None)
    grid = P("row", "col")
    in_specs = (
        split, P(), P(), P("col", None), P("col", None), P("col", None), P("col", None), split, P(("row", "col")),
    ) + (P(),) * 9
    out_specs = (P(), split, split, P(), P(), P(), P(), grid, grid, grid, grid, grid)
    return jax.shard_map(body, mesh=mesh, in_specs=in_specs, out_specs=out_specs, check_vma=False)
```

```python
import functools
import math

import jax
import jax.numpy as jnp
from jax import lax
from jax.experimental import pallas as pl
from jax.experimental.pallas import tpu as pltpu
from jax.sharding import PartitionSpec as P

HEADS = 12
IMG_TOK = 50
norm_eps = 1e-06
logit_scale = 50.0
masked_score = -1e30
log2e = math.log2(math.e)
f32 = jnp.float32
bf16 = jnp.bfloat16
VMEM_LIMIT = 60 * 2**20
MESH = pl.DeviceIdType.MESH


def dot_nn(a, b):
    return lax.dot_general(a, b, (((1,), (0,)), ((), ())), preferred_element_type=f32)


def dot_nt(a, b):
    return lax.dot_general(a, b, (((1,), (1,)), ((), ())), preferred_element_type=f32)


def dot_tn(a, b):
    return lax.dot_general(a, b, (((0,), (0,)), ((), ())), preferred_element_type=f32)


def split_low(x):
    high = x.astype(bf16)
    return high, (x - high.astype(f32)).astype(bf16)


def normed(x):
    centered = x - jnp.mean(x, axis=-1, keepdims=True)
    spread = lax.rsqrt(jnp.mean(centered * centered, axis=-1, keepdims=True) + norm_eps)
    return centered * spread, spread


def layer_norm(x, gain, bias):
    return normed(x)[0] * gain + bias


def normal_tail(x):
    size = jnp.abs(x)
    t = 1.0 / (1.0 + (0.3275911 * math.sqrt(0.5)) * size)
    bell = jnp.exp2((-0.5 * log2e) * (x * x))
    series = 0.5 * 1.061405429
    for factor in (-1.453152027, 1.421413741, -0.284496736, 0.254829592):
        series = series * t + 0.5 * factor
    return size, bell, series * t * bell


def gelu(x):
    size, _, tail = normal_tail(x)
    return jnp.maximum(x, 0.0) - size * tail


def gelu_and_slope(x):
    size, bell, tail = normal_tail(x)
    value = jnp.maximum(x, 0.0) - size * tail
    below = jnp.where(x >= 0.0, 1.0 - tail, tail)
    return value, below + x * (bell * (1.0 / math.sqrt(2.0 * math.pi)))


def lane_halves(width):
    lane = lax.broadcasted_iota(jnp.int32, (1, width), 1)
    first = (lane < width // 2).astype(f32)
    return first.astype(bf16), (1.0 - first).astype(bf16)


def stack_heads(x, first, second):
    return jnp.concatenate([x * first, x * second], axis=0)


def join_heads(stacked):
    rows, width = stacked.shape[0] // 2, stacked.shape[1]
    lane = lax.broadcasted_iota(jnp.int32, (rows, width), 1)
    return jnp.where(lane < width // 2, stacked[:rows], stacked[rows:])


def soft_weights(query, key, bias, factor):
    scores = dot_nt(query, key) * (factor * log2e) + bias
    weights = jnp.exp2(scores - jnp.max(scores, axis=-1, keepdims=True))
    return weights, 1.0 / jnp.sum(weights, axis=-1, keepdims=True)


def text_bias(key_bias_ref, block, rows, length):
    near = lax.broadcasted_iota(jnp.int32, (rows, rows), 0) // length
    far = lax.broadcasted_iota(jnp.int32, (rows, rows), 1) // length
    columns = pl.ds(pl.multiple_of(block * rows, rows), rows)
    bias = jnp.where(near == far, key_bias_ref[:, columns], masked_score)
    return jnp.concatenate([bias, bias], axis=0)


def member(len_ref, captions, tokens):
    length = tokens // captions
    token = lax.broadcasted_iota(jnp.int32, (captions, tokens), 1)
    caption = lax.broadcasted_iota(jnp.int32, (captions, tokens), 0)
    return ((token // length == caption) & (token % length < len_ref[...])).astype(f32)


def spread_rows(x, length):
    rows, width = x.shape
    return jnp.broadcast_to(x[:, None, :], (rows, length, width)).reshape(rows * length, width)


def text_forward_kernel(
    tok_ref, len_ref, key_bias_ref, gain1, bias1, gain2, bias2, qkv_hbm, out_hbm, up_hbm, down_hbm, proj_hbm,
    hidden_ref, embed_ref, projected_ref, pooled_ref, inner_sum_ref, heads_ref, mixed_ref, mid_ref, slope_ref,
    w_qkv, w_out, w_up, w_down, w_proj, norm_ref, inner_ref, sems,
):
    tokens, width = tok_ref.shape
    captions = len_ref.shape[0]
    length = tokens // captions
    wide = w_up.shape[1]
    pairs = ((qkv_hbm, w_qkv), (out_hbm, w_out), (up_hbm, w_up), (down_hbm, w_down), (proj_hbm, w_proj))
    loads = [pltpu.make_async_copy(s, d, sems.at[i]) for i, (s, d) in enumerate(pairs)]
    for load in loads:
        load.start()

    band = 128

    @pl.loop(0, tokens // band)
    def _(i):
        rows = pl.ds(pl.multiple_of(i * band, band), band)
        norm_ref[rows, :] = layer_norm(tok_ref[rows, :].astype(f32), gain1[...], bias1[...]).astype(bf16)

    loads[0].wait()

    @pl.loop(0, 3 * width // 256)
    def _(j):
        columns = pl.ds(pl.multiple_of(j * 256, 256), 256)
        heads_ref[:, columns] = dot_nn(norm_ref[...], w_qkv[:, columns]).astype(bf16)

    first, second = lane_halves(128)
    factor = (width // HEADS) ** -0.5

    @pl.loop(0, tokens // band)
    def _(block):
        rows = pl.ds(pl.multiple_of(block * band, band), band)
        bias = text_bias(key_bias_ref, block, band, length)
        for pair in range(width // 128):
            at = pair * 128
            query = stack_heads(heads_ref[rows, at : at + 128], first, second)
            weights, scale = soft_weights(query, heads_ref[rows, width + at : width + at + 128], bias, factor)
            value = heads_ref[rows, 2 * width + at : 2 * width + at + 128]
            mixed = dot_nn(weights.astype(bf16), value) * scale
            mixed_ref[rows, at : at + 128] = join_heads(mixed).astype(bf16)

    loads[1].wait()

    @pl.loop(0, tokens // band)
    def _(i):
        rows = pl.ds(pl.multiple_of(i * band, band), band)
        mid = tok_ref[rows, :].astype(f32) + dot_nn(mixed_ref[rows, :], w_out[...])
        mid_ref[rows, :] = mid
        norm_ref[rows, :] = layer_norm(mid, gain2[...], bias2[...]).astype(bf16)

    loads[2].wait()
    chosen = member(len_ref, captions, tokens)
    chosen_low = chosen.astype(bf16)
    place = lax.broadcasted_iota(jnp.int32, (captions, length, 1), 1)
    valid = (place < len_ref[...].reshape(captions, 1, 1)).astype(f32).reshape(tokens, 1)

    @pl.loop(0, wide // 256)
    def _(j):
        columns = pl.ds(pl.multiple_of(j * 256, 256), 256)
        value, slope = gelu_and_slope(dot_nn(norm_ref[...], w_up[:, columns]))
        value = value.astype(bf16)
        inner_ref[:, columns] = value
        slope_ref[:, columns] = (slope * valid).astype(bf16)
        inner_sum_ref[:, columns] = dot_nn(chosen_low, value).astype(bf16)

    loads[3].wait()
    inverse = 1.0 / len_ref[...].astype(f32)

    @pl.loop(0, width // 256)
    def _(j):
        columns = pl.ds(pl.multiple_of(j * 256, 256), 256)
        state = mid_ref[:, columns] + dot_nn(inner_ref[...], w_down[:, columns])
        hidden_ref[:, columns] = state.astype(bf16)
        high, low = split_low(state)
        pooled_ref[:, columns] = ((dot_nn(chosen_low, high) + dot_nn(chosen_low, low)) * inverse).astype(bf16)

    loads[4].wait()
    projected = dot_nn(pooled_ref[...], w_proj[...])
    projected_ref[...] = projected
    embed_ref[...] = (
        projected * lax.rsqrt(jnp.sum(projected * projected, axis=-1, keepdims=True) + norm_eps)
    ).astype(bf16)


def load_weights(pairs, sems):
    loads = [pltpu.make_async_copy(s, d, sems.at[i]) for i, (s, d) in enumerate(pairs)]
    for load in loads:
        load.start()
    return loads


def spans(count, size):
    return lambda i: pl.ds(pl.multiple_of(i * size, size), size)


def norm_backward(outer, unit, spread, gain):
    outer = outer * gain
    inner = outer - jnp.mean(outer, axis=-1, keepdims=True)
    return spread * (inner - unit * jnp.mean(outer * unit, axis=-1, keepdims=True))


class TextBackward:
    band = 128

    def __init__(self, names, refs):
        for name, ref in zip(names, refs, strict=True):
            setattr(self, name, ref)
        self.tokens, self.width = self.tok.shape
        self.captions = self.lens.shape[0]
        self.length = self.tokens // self.captions
        self.wide = self.w_up.shape[1]
        pairs = (
            (self.proj_hbm, self.w_proj), (self.down_hbm, self.w_down), (self.up_hbm, self.w_up),
            (self.out_hbm, self.w_out), (self.qkv_hbm, self.w_qkv),
        )
        self.loads = load_weights(pairs, self.sems)

    def rows(self, i):
        return pl.ds(pl.multiple_of(i * self.band, self.band), self.band)

    def bands(self, step):
        pl.loop(0, self.tokens // self.band)(lambda i: step(self.rows(i)))

    def project(self):
        def renorm(rows):
            self.norm[rows, :] = layer_norm(self.mid[rows, :], self.gain2[...], self.bias2[...]).astype(bf16)

        self.bands(renorm)
        projected = self.projected[...]
        embed_grad = self.embed_grad[...]
        r = lax.rsqrt(jnp.sum(projected * projected, axis=-1, keepdims=True) + norm_eps)
        along = jnp.sum(projected * embed_grad, axis=-1, keepdims=True)
        proj_grad = (r * embed_grad - (r * r * r) * projected * along).astype(bf16)
        self.loads[0].wait()
        state_grad = dot_nt(proj_grad, self.w_proj[...]) * (1.0 / self.lens[...].astype(f32))
        self.branch[...] = state_grad.astype(bf16)
        place = lax.broadcasted_iota(jnp.int32, (self.captions, self.length, 1), 1)
        valid = (place < self.lens[...].reshape(self.captions, 1, 1)).astype(f32).reshape(self.tokens, 1)
        self.mid_grad[...] = spread_rows(state_grad, self.length) * valid
        return proj_grad, self.branch[...]

    def inner(self, col_parts, store_up):
        self.loads[1].wait()
        branch = self.branch[...]
        step = self.wide // col_parts
        for part in range(col_parts):

            @pl.loop(0, step // 256)
            def _(j):
                columns = pl.ds(pl.multiple_of(part * step + j * 256, 256), 256)
                inner_grad = dot_nt(branch, self.w_down[columns, :])
                pre_grad = spread_rows(inner_grad, self.length) * self.slope[:, columns].astype(f32)
                pre_grad = pre_grad.astype(bf16)
                self.pre_grad[:, columns] = pre_grad
                local = pl.ds(pl.multiple_of(j * 256, 256), 256)
                store_up(part, local, dot_tn(self.norm[...], pre_grad).astype(bf16))

    def middle(self):
        self.loads[2].wait()

        @pl.loop(0, self.width // 256)
        def _(j):
            columns = pl.ds(pl.multiple_of(j * 256, 256), 256)
            self.outer[:, columns] = dot_nt(self.pre_grad[...], self.w_up[columns, :])

        self.norm_grad[...] = jnp.zeros_like(self.norm_grad)

        def through_norm(rows):
            unit, spread = normed(self.mid[rows, :])
            outer = self.outer[rows, :]
            self.norm_grad[2:3, :] += jnp.sum(outer * unit, axis=0, keepdims=True)
            self.norm_grad[3:4, :] += jnp.sum(outer, axis=0, keepdims=True)
            mid_grad = self.mid_grad[rows, :] + norm_backward(outer, unit, spread, self.gain2[...])
            self.mid_grad[rows, :] = mid_grad
            self.low_grad[rows, :] = mid_grad.astype(bf16)

        self.bands(through_norm)

    def output(self, col_parts, store_out):
        step = self.width // col_parts
        for part in range(col_parts):
            store_out(part, dot_tn(self.mixed[...], self.low_grad[:, part * step : (part + 1) * step]).astype(bf16))
        self.loads[3].wait()

        def through_out(rows):
            self.mixed_grad[rows, :] = dot_nt(self.low_grad[rows, :], self.w_out[...]).astype(bf16)
            norm = layer_norm(self.tok[rows, :].astype(f32), self.gain1[...], self.bias1[...])
            self.norm[rows, :] = norm.astype(bf16)

        self.bands(through_out)

    def attention(self):
        first, second = lane_halves(128)
        width = self.width
        factor = (width // HEADS) ** -0.5

        @pl.loop(0, self.tokens // self.band)
        def _(block):
            rows = self.rows(block)
            bias = text_bias(self.key_bias, block, self.band, self.length)
            for pair in range(width // 128):
                at = pair * 128
                query = stack_heads(self.heads[rows, at : at + 128], first, second)
                key = self.heads[rows, width + at : width + at + 128]
                value = self.heads[rows, 2 * width + at : 2 * width + at + 128]
                grad = stack_heads(self.mixed_grad[rows, at : at + 128], first, second)
                weights, scale = soft_weights(query, key, bias, factor)
                probs = weights * scale
                prob_grad = dot_nt(grad, value)
                total = jnp.sum(prob_grad * probs, axis=-1, keepdims=True)
                score_grad = (probs * (prob_grad - total)).astype(bf16)
                query_grad = join_heads(dot_nn(score_grad, key)) * factor
                self.heads_grad[rows, at : at + 128] = query_grad.astype(bf16)
                key_grad = dot_tn(score_grad, query) * factor
                self.heads_grad[rows, width + at : width + at + 128] = key_grad.astype(bf16)
                value_grad = dot_tn(probs.astype(bf16), grad)
                self.heads_grad[rows, 2 * width + at : 2 * width + at + 128] = value_grad.astype(bf16)

    def heads_weights(self, col_parts, store_qkv):
        step = 3 * self.width // col_parts
        for part in range(col_parts):
            store_qkv(
                part, dot_tn(self.norm[...], self.heads_grad[:, part * step : (part + 1) * step]).astype(bf16)
            )

    def input(self):
        self.loads[4].wait()

        @pl.loop(0, self.width // 256)
        def _(j):
            columns = pl.ds(pl.multiple_of(j * 256, 256), 256)
            self.outer[:, columns] = dot_nt(self.heads_grad[...], self.w_qkv[columns, :])

        def through_norm(rows):
            unit, spread = normed(self.tok[rows, :].astype(f32))
            outer = self.outer[rows, :]
            self.norm_grad[0:1, :] += jnp.sum(outer * unit, axis=0, keepdims=True)
            self.norm_grad[1:2, :] += jnp.sum(outer, axis=0, keepdims=True)
            inner = norm_backward(outer, unit, spread, self.gain1[...])
            self.input_grad[rows, :] = (self.mid_grad[rows, :] + inner).astype(bf16)

        self.bands(through_norm)


backward_ins = (
    "tok", "lens", "key_bias", "gain1", "bias1", "gain2", "bias2", "embed_grad", "projected", "heads",
    "mixed", "mid", "slope", "qkv_hbm", "out_hbm", "up_hbm", "down_hbm", "proj_hbm",
)
backward_scratch = (
    "w_qkv", "w_out", "w_up", "w_down", "w_proj", "norm", "pre_grad", "outer", "mid_grad", "low_grad",
    "mixed_grad", "heads_grad", "sems",
)
scatter_names = (
    "held", "near", "x1", "y1", "x2", "y2", "far", "sends", "recvs",
)
exchange_names = (
    "own", "all", "sends", "recvs",
)


def text_backward_kernel(*refs):
    outs = ("proj_grad", "branch", "up_grad", "out_grad", "qkv_grad", "input_grad", "norm_grad")
    t = TextBackward(backward_ins + outs + backward_scratch, refs)
    parts = t.up_grad.shape[0]

    def store_up(part, columns, value):
        t.up_grad[part, :, columns] = value

    def store_out(part, value):
        t.out_grad[part] = value

    def store_qkv(part, value):
        t.qkv_grad[part] = value

    t.proj_grad[...] = t.project()[0]
    t.inner(parts, store_up)
    t.middle()
    t.output(parts, store_out)
    t.attention()
    t.heads_weights(parts, store_qkv)
    t.input()


class Place:
    def __init__(self, z_count=4, y_count=2, x_count=2, k_count=2):
        self.row, self.col = lax.axis_index("row"), lax.axis_index("col")
        self.z, self.y = self.row // y_count, self.row % y_count
        self.x, self.k = self.col // k_count, self.col % k_count
        self.rows, self.cols = z_count * y_count, x_count * k_count
        self.count = self.rows * self.cols
        self.me = self.row * self.cols + self.col

    def at(self, **moved):
        z, y, x, k = (moved.get(name, getattr(self, name)) for name in "zyxk")
        return z * 2 + y, x * 2 + k

    def peer(self, distance):
        other = (self.me + distance) % self.count
        return other // self.cols, other % self.cols

    def greet(self):
        barrier = pltpu.get_barrier_semaphore()

        @pl.loop(1, self.count)
        def _(distance):
            pl.semaphore_signal(barrier, inc=1, device_id=self.peer(distance), device_id_type=MESH)

        pl.semaphore_wait(barrier, self.count - 1)


def remote(src, dst, send, recv, to):
    return pltpu.make_async_remote_copy(
        src_ref=src, dst_ref=dst, send_sem=send, recv_sem=recv, device_id=to, device_id_type=MESH
    )


class Exchange:
    def __init__(self, place, source, slots, sends, recvs):
        self.place, self.source, self.slots, self.sends, self.recvs = place, source, slots, sends, recvs

    def copy(self, distance):
        to = self.place.peer(distance)
        sems = self.sends.at[distance - 1], self.recvs.at[distance - 1]
        return remote(self.source(to), self.slots.at[self.place.me], *sems, to)

    def start(self):
        pl.loop(1, self.place.count)(lambda distance: self.copy(distance).start())

    def finish(self):
        pl.loop(1, self.place.count)(lambda distance: self.copy(distance).wait())


class GradientScatter:
    def __init__(self, place, held, near, x1, y1, x2, y2, far, sends, recvs):
        self.place, self.held, self.near, self.far = place, held, near, far
        self.x1, self.y1, self.x2, self.y2 = x1, y1, x2, y2
        self.sends, self.recvs = sends, recvs
        half = held.shape[5] // 2
        self.one, self.two = pl.ds(0, half), pl.ds(half, half)

    def copy(self, n, src, dst, **moved):
        return remote(src, dst, self.sends.at[n], self.recvs.at[n], self.place.at(**moved))

    def copies(self, stage):
        p, held = self.place, self.held
        x, y, z, k = p.x, p.y, p.z, p.k
        every = slice(None)
        if stage == 0:
            return [self.copy(0, held.at[:, 1 - k], self.near, k=1 - k)]
        if stage == 1:
            return [
                self.copy(1, held.at[1 - x, k, :, :, :, self.one], self.x1, x=1 - x),
                self.copy(2, held.at[:, k, :, 1 - y, :, self.two], self.y1, y=1 - y),
            ]
        if stage == 2:
            return [
                self.copy(3, held.at[x, k, :, 1 - y, :, self.one], self.y2, y=1 - y),
                self.copy(4, held.at[1 - x, k, :, y, :, self.two], self.x2, x=1 - x),
            ]
        copies = []
        for distance in range(1, held.shape[2]):
            other = (z + distance) % held.shape[2]
            copies.append(self.copy(4 + distance, held.at[x, k, other, y], self.far.at[distance - 1], z=other))
        return copies

    def start(self, stage):
        for copy in self.copies(stage):
            copy.start()

    def finish(self, stage):
        for copy in self.copies(stage):
            copy.wait()
        p, held = self.place, self.held
        x, y, k = p.x, p.y, p.k
        z_count = held.shape[2]

        def add(target, source):
            target[...] = (target[...].astype(f32) + source[...].astype(f32)).astype(bf16)

        if stage == 0:
            for i in range(2):
                for j in range(2):
                    pl.loop(0, z_count)(lambda z: add(held.at[i, k, z, j], self.near.at[i, z, j]))
        if stage == 1:
            for i in range(2):
                pl.loop(0, z_count)(lambda z: add(held.at[x, k, z, i, :, self.one], self.x1.at[z, i]))
                pl.loop(0, z_count)(lambda z: add(held.at[i, k, z, y, :, self.two], self.y1.at[i, z]))
        if stage == 2:
            pl.loop(0, z_count)(lambda z: add(held.at[x, k, z, y, :, self.one], self.y2.at[z]))
            pl.loop(0, z_count)(lambda z: add(held.at[x, k, z, y, :, self.two], self.x2.at[z]))
        if stage == 3:
            total = held[x, k, p.z, y].astype(f32)
            for i in range(z_count - 1):
                total = total + self.far[i].astype(f32)
            return total


def scatter_scratch(rows, columns):
    shapes = [
        (2, 2, 4, 2, rows, columns), (2, 4, 2, rows, columns), (4, 2, rows, columns // 2), (2, 4, rows, columns // 2),
        (4, rows, columns // 2), (4, rows, columns // 2), (3, rows, columns),
    ]
    return [pltpu.VMEM(shape, bf16) for shape in shapes] + [pltpu.SemaphoreType.DMA((8,))] * 2


def text_backward_joined_kernel(*refs):
    ins = backward_ins + ("factors", "loss")
    outs = ("up_out", "out_out", "qkv_out", "down_out", "proj_out", "input_grad", "norm_out")
    sets = tuple(name + tag for tag in ("_a", "_b") for name in scatter_names)
    swaps = tuple(name + tag for tag in ("_factors", "_late", "_last") for name in exchange_names)
    names = ins + outs + backward_scratch + sets + ("branch", "norm_grad") + swaps
    t = TextBackward(names, refs)
    place = Place()
    width = t.width
    scatter_a, scatter_b = (
        GradientScatter(place, *(getattr(t, name + tag) for name in scatter_names)) for tag in ("_a", "_b")
    )
    factors = Exchange(
        place, lambda to: t.own_factors.at[to[1]], t.all_factors, t.sends_factors, t.recvs_factors
    )
    late = Exchange(place, lambda to: t.own_late, t.all_late, t.sends_late, t.recvs_late)
    last = Exchange(place, lambda to: t.own_last, t.all_last, t.sends_last, t.recvs_last)
    cols = place.cols

    def blocked(value):
        return value.reshape(4, 2, value.shape[0] // 8, value.shape[1])

    def store_up(part, columns, value):
        t.held_a[part // 2, part % 2, :, :, :, columns] = blocked(value)

    qkv_step, out_step = 3 * width // cols, width // cols

    def store_out(part, value):
        t.held_b[part // 2, part % 2, :, :, :, qkv_step:] = blocked(value)

    def store_qkv(part, value):
        t.held_b[part // 2, part % 2, :, :, :, :qkv_step] = blocked(value)

    proj_grad, branch = t.project()
    for part in range(cols):
        columns = slice(part * out_step, (part + 1) * out_step)
        t.own_factors[part] = jnp.concatenate([branch[:, columns], proj_grad[:, columns]], axis=1)
    t.all_factors[place.me] = t.own_factors[place.col]
    place.greet()
    factors.start()
    t.inner(cols, store_up)
    scatter_a.start(0)
    t.middle()
    scatter_a.finish(0)
    scatter_a.start(1)
    t.own_late[...] = jnp.concatenate([t.norm_grad[2:3, :], t.norm_grad[3:4, :], t.loss[...]], axis=1)
    t.all_late[place.me] = t.own_late[...]
    late.start()
    t.output(cols, store_out)
    scatter_a.finish(1)
    scatter_a.start(2)
    t.attention()
    t.heads_weights(cols, store_qkv)
    scatter_b.start(0)
    scatter_a.finish(2)
    scatter_a.start(3)
    scatter_b.finish(0)
    scatter_b.start(1)
    t.input()
    t.own_last[...] = jnp.concatenate([t.norm_grad[0:1, :], t.norm_grad[1:2, :]], axis=1)
    t.all_last[place.me] = t.own_last[...]
    scatter_b.finish(1)
    scatter_b.start(2)
    last.start()
    t.up_out[...] = scatter_a.finish(3)
    factors.finish()
    grown = dot_tn(
        t.factors[...].reshape(-1, t.factors.shape[2]), t.all_factors[...].reshape(-1, t.all_factors.shape[2])
    )
    inner_step = t.wide // place.rows
    t.down_out[...] = grown[:inner_step, :out_step]
    t.proj_out[...] = grown[inner_step : inner_step + width // place.rows, out_step:]
    late.finish()
    scatter_b.finish(2)
    scatter_b.start(3)
    last.finish()
    t.norm_out[:, : 2 * width] = jnp.sum(t.all_last[...], axis=0)
    t.norm_out[:, 2 * width :] = jnp.sum(t.all_late[...], axis=0)
    total = scatter_b.finish(3)
    t.qkv_out[...] = total[:, :qkv_step]
    t.out_out[...] = total[:, qkv_step:]


def group_mean(images, rows):
    token = lax.broadcasted_iota(jnp.int32, (images, rows), 1)
    image = lax.broadcasted_iota(jnp.int32, (images, rows), 0)
    inside = (token >= image * IMG_TOK) & (token < (image + 1) * IMG_TOK)
    return inside.astype(f32).astype(bf16)


def load_parts(parts, target, sems, col, col_count):
    depth = target.shape[0] // col_count
    copies = []
    for k, part in enumerate(parts):
        place = pl.multiple_of((col ^ k) * depth, depth)
        copies.append(pltpu.make_async_copy(part, target.at[pl.ds(place, depth)], sems.at[k]))
    return copies


def image_mix_kernel(
    col_count, tok_ref, gain_ref, bias_ref, *refs,
):
    qkv_parts, out_parts = refs[:col_count], refs[col_count : 2 * col_count]
    normed_ref, mean_ref, w_qkv, w_out, norm_ref, heads_ref, mixed_ref, sems = refs[2 * col_count :]
    rows, width = tok_ref.shape
    images = rows // IMG_TOK
    step = pl.program_id(0)
    col = lax.axis_index("col")

    @pl.when(step == 0)
    def _():
        copies = load_parts(qkv_parts, w_qkv, sems.at[0], col, col_count)
        copies += load_parts(out_parts, w_out, sems.at[1], col, col_count)
        for copy in copies:
            copy.start()
        for copy in copies:
            copy.wait()

    norm_ref[...] = layer_norm(tok_ref[...].astype(f32), gain_ref[0:1, :], bias_ref[0:1, :]).astype(bf16)

    @pl.loop(0, 3 * width // 256)
    def _(j):
        columns = pl.ds(pl.multiple_of(j * 256, 256), 256)
        heads_ref[:, columns] = dot_nn(norm_ref[...], w_qkv[:, columns]).astype(bf16)

    first, second = lane_halves(128)
    factor = (width // HEADS) ** -0.5
    window = 112
    for pair in range(images // 2):
        start, low = pair * 2 * IMG_TOK, (pair * 2 * IMG_TOK) // 16 * 16
        near = lax.broadcasted_iota(jnp.int32, (window, window), 0) + low
        far = lax.broadcasted_iota(jnp.int32, (window, window), 1) + low
        same = (near >= start) & (near < start + 2 * IMG_TOK) & (far >= start) & (far < start + 2 * IMG_TOK)
        same = same & ((near >= start + IMG_TOK) == (far >= start + IMG_TOK))
        bias = jnp.where(same, 0.0, masked_score)
        bias = jnp.concatenate([bias, bias], axis=0)
        keep = lax.broadcasted_iota(jnp.int32, (16, 128), 0) + low < start
        span = slice(low, low + window)

        @pl.loop(0, width // 128)
        def _(two):
            at = pl.multiple_of(two * 128, 128)
            query = stack_heads(heads_ref[span, pl.ds(at, 128)], first, second)
            weights, scale = soft_weights(query, heads_ref[span, pl.ds(width + at, 128)], bias, factor)
            value = heads_ref[span, pl.ds(2 * width + at, 128)]
            mixed = join_heads(dot_nn(weights.astype(bf16), value) * scale)
            if low == start:
                mixed_ref[span, pl.ds(at, 128)] = mixed.astype(bf16)
            else:
                former = mixed_ref[low : low + 16, pl.ds(at, 128)].astype(f32)
                mixed_ref[low : low + 16, pl.ds(at, 128)] = jnp.where(keep, former, mixed[:16]).astype(bf16)
                mixed_ref[low + 16 : low + window, pl.ds(at, 128)] = mixed[16:].astype(bf16)

    mid = tok_ref[...].astype(f32) + dot_nn(mixed_ref[...], w_out[...])
    normed_ref[...] = layer_norm(mid, gain_ref[1:2, :], bias_ref[1:2, :]).astype(bf16)
    high, low = split_low(mid)
    select = group_mean(images, rows)
    mean_ref[...] = (dot_nn(select, high) + dot_nn(select, low)) * (1.0 / IMG_TOK)


def image_embed_kernel(col_count, normed_ref, mean_ref, *refs):
    up_parts, down_parts = refs[:col_count], refs[col_count : 2 * col_count]
    embed_ref, w_up, w_down, sum_ref, sems = refs[2 * col_count :]
    rows, width = normed_ref.shape
    images = rows // IMG_TOK
    wide = w_up.shape[1]
    step = pl.program_id(0)
    col = lax.axis_index("col")
    downs = load_parts(down_parts, w_down, sems.at[1], col, col_count)

    @pl.when(step == 0)
    def _():
        ups = load_parts(up_parts, w_up, sems.at[0], col, col_count)
        for copy in ups + downs:
            copy.start()
        for copy in ups:
            copy.wait()

    select = group_mean(images, rows)

    @pl.loop(0, wide // 256)
    def _(j):
        columns = pl.ds(pl.multiple_of(j * 256, 256), 256)
        inner = gelu(dot_nn(normed_ref[...], w_up[:, columns])).astype(bf16)
        sum_ref[pl.ds(pl.multiple_of(step * images, images), images), columns] = dot_nn(select, inner)

    @pl.when(step == pl.num_programs(0) - 1)
    def _():
        for copy in downs:
            copy.wait()
        high, low = split_low(sum_ref[...] * (1.0 / IMG_TOK))
        pooled = mean_ref[...] + dot_nn(high, w_down[...]) + dot_nn(low, w_down[...])
        embed_ref[...] = (
            pooled * lax.rsqrt(jnp.sum(pooled * pooled, axis=-1, keepdims=True) + norm_eps)
        ).astype(bf16)


def whole(shape):
    return pl.BlockSpec(shape, lambda *_: (0,) * len(shape))


in_vmem = pl.BlockSpec(memory_space=pltpu.VMEM)
anywhere = pl.BlockSpec(memory_space=pl.ANY)


def plain(kernel, outs, ins, scratch, name, **settings):
    return pl.pallas_call(
        kernel,
        out_shape=outs,
        in_specs=ins,
        out_specs=[in_vmem] * len(outs),
        scratch_shapes=scratch,
        compiler_params=pltpu.CompilerParams(vmem_limit_bytes=VMEM_LIMIT, **settings),
        name=name,
    )


def array(shape, dtype):
    return jax.ShapeDtypeStruct(shape, dtype)


def partners(x, col_count):
    order = [(i, i ^ 2) for i in range(col_count)]
    near = [(i, i ^ 1) for i in range(col_count)]
    far = lax.ppermute(x, "col", order)
    return [x, lax.ppermute(x, "col", near), far, lax.ppermute(far, "col", near)]


def body(
    image_tokens, image_norm_gain, image_norm_bias, image_qkv, image_out, image_up, image_down,
    text_tokens, text_lengths, norm1_gain, norm1_bias, norm2_gain, norm2_bias,
    text_qkv, text_out, text_up, text_down, text_proj,
):
    tokens, width = text_tokens.shape
    captions = text_lengths.shape[0]
    length = tokens // captions
    wide = text_up.shape[1]
    row_count, col_count = lax.axis_size("row"), lax.axis_size("col")
    row, col = lax.axis_index("row"), lax.axis_index("col")
    pair_total = captions * row_count * col_count
    image_rows, images = image_tokens.shape[0], image_tokens.shape[0] // IMG_TOK

    qkv_parts = partners(image_qkv, col_count)
    out_parts = partners(image_out, col_count)
    up_parts = partners(image_up, col_count)
    down_parts = partners(image_down, col_count)

    lengths = text_lengths.reshape(captions, 1)
    place = lax.broadcasted_iota(jnp.int32, (captions, length), 1)
    key_bias = jnp.where(place < lengths, 0.0, masked_score).reshape(1, tokens)
    vectors = [v.reshape(1, width) for v in (norm1_gain, norm1_bias, norm2_gain, norm2_bias)]
    weights = (text_qkv, text_out, text_up, text_down, text_proj)
    weight_scratch = [pltpu.VMEM(w.shape, bf16) for w in weights]

    (hidden, text_embed, projected, pooled, inner_sum, heads, mixed, mid, slope) = plain(
        text_forward_kernel,
        (
            array((tokens, width), bf16),
            array((captions, width), bf16),
            array((captions, width), f32),
            array((captions, width), bf16),
            array((captions, wide), bf16),
            array((tokens, 3 * width), bf16),
            array((tokens, width), bf16),
            array((tokens, width), f32),
            array((tokens, wide), bf16),
        ),
        [in_vmem] * 7 + [anywhere] * 5,
        weight_scratch
        + [pltpu.VMEM((tokens, width), bf16), pltpu.VMEM((tokens, wide), bf16), pltpu.SemaphoreType.DMA((5,))],
        "text_forward",
    )(text_tokens, lengths, key_bias, *vectors, *weights)

    groups = 4
    group_rows, group_images = image_rows // groups, images // groups
    parts = [anywhere] * (2 * col_count)
    image_tokens, text_embed = lax.optimization_barrier((image_tokens, text_embed))
    image_normed, image_mean = pl.pallas_call(
        functools.partial(image_mix_kernel, col_count),
        grid=(groups,),
        out_shape=(array((image_rows, width), bf16), array((images, width), f32)),
        in_specs=[
            pl.BlockSpec((group_rows, width), lambda i: (i, 0)),
            whole(image_norm_gain.shape),
            whole(image_norm_bias.shape),
        ]
        + parts,
        out_specs=(
            pl.BlockSpec((group_rows, width), lambda i: (i, 0)),
            pl.BlockSpec((group_images, width), lambda i: (i, 0)),
        ),
        scratch_shapes=[
            pltpu.VMEM((width, 3 * width), bf16),
            pltpu.VMEM((width, width), bf16),
            pltpu.VMEM((group_rows, width), bf16),
            pltpu.VMEM((group_rows, 3 * width), bf16),
            pltpu.VMEM((group_rows, width), bf16),
            pltpu.SemaphoreType.DMA((2, col_count)),
        ],
        compiler_params=pltpu.CompilerParams(vmem_limit_bytes=VMEM_LIMIT),
        name="image_mix",
    )(image_tokens, image_norm_gain, image_norm_bias, *qkv_parts, *out_parts)
    image_embed = pl.pallas_call(
        functools.partial(image_embed_kernel, col_count),
        grid=(groups,),
        out_shape=array((images, width), bf16),
        in_specs=[pl.BlockSpec((group_rows, width), lambda i: (i, 0)), whole((images, width))] + parts,
        out_specs=whole((images, width)),
        scratch_shapes=[
            pltpu.VMEM((width, wide), bf16),
            pltpu.VMEM((wide, width), bf16),
            pltpu.VMEM((images, wide), f32),
            pltpu.SemaphoreType.DMA((2, col_count)),
        ],
        compiler_params=pltpu.CompilerParams(vmem_limit_bytes=VMEM_LIMIT),
        name="image_embed",
    )(image_normed, image_mean, *up_parts, *down_parts)

    both = ("row", "col")
    image_all = lax.all_gather(image_embed, both, axis=0, tiled=True)
    sims = logit_scale * dot_nt(image_all, text_embed)
    lifted = jnp.exp(sims)
    row_sums = lax.psum(jnp.sum(lifted, axis=1), both)
    col_sums = jnp.sum(lifted, axis=0)
    sim_grad = (0.5 * (lifted / row_sums[:, None] + lifted / col_sums[None, :])).astype(bf16)
    image_own = image_embed.astype(f32)
    embed_grad = logit_scale * (dot_tn(sim_grad, image_all) - image_own)
    positives = logit_scale * jnp.sum(image_own * text_embed.astype(f32), axis=1)
    loss_part = 0.5 * jnp.sum(jnp.log(col_sums) - 2.0 * positives)

    backward_in = (
        text_tokens, lengths, key_bias, *vectors, embed_grad, projected, heads, mixed, mid, slope, *weights,
    )
    backward_specs = [in_vmem] * 13 + [anywhere] * 5
    backward_buffers = weight_scratch + [
        pltpu.VMEM((tokens, width), bf16),
        pltpu.VMEM((tokens, wide), bf16),
        pltpu.VMEM((tokens, width), f32),
        pltpu.VMEM((tokens, width), f32),
        pltpu.VMEM((tokens, width), bf16),
        pltpu.VMEM((tokens, width), bf16),
        pltpu.VMEM((tokens, 3 * width), bf16),
        pltpu.SemaphoreType.DMA((5,)),
    ]

    def by_row(x):
        x = lax.all_to_all(x, "row", split_axis=1, concat_axis=0, tiled=True)
        return lax.all_gather(x, "col", axis=0, tiled=True)

    def by_col(x):
        x = lax.all_gather(x, "row", axis=0, tiled=True)
        return lax.all_to_all(x, "col", split_axis=1, concat_axis=0, tiled=True)

    count = row_count * col_count
    if (row_count, col_count) == (8, 4):
        row_blocks = [inner_sum.reshape(captions, row_count, -1), pooled.reshape(captions, row_count, -1)]
        packed = jnp.concatenate(row_blocks, axis=2)
        packed = jnp.pad(packed, ((0, 0), (0, 0), (0, -packed.shape[2] % 128))).transpose(1, 0, 2)
        packed = lax.all_to_all(packed, "row", split_axis=0, concat_axis=0)
        factors = lax.all_gather(packed, "col", axis=1).reshape(count, captions, -1)
        out_step, inner_step = width // col_count, wide // row_count
        rows = width // row_count
        up_grad, out_grad, qkv_grad, grad_down, grad_proj, input_grad, norm_total = plain(
            text_backward_joined_kernel,
            (
                array((rows, wide // col_count), f32),
                array((rows, out_step), f32),
                array((rows, 3 * out_step), f32),
                array((inner_step, out_step), f32),
                array((rows, out_step), f32),
                array((tokens, width), bf16),
                array((1, 4 * width + 128), f32),
            ),
            backward_specs + [in_vmem] * 2,
            backward_buffers
            + scatter_scratch(rows, wide // col_count)
            + scatter_scratch(rows, 4 * out_step)
            + [
                pltpu.VMEM((captions, width), bf16),
                pltpu.VMEM((8, width), f32),
                pltpu.VMEM((col_count, captions, 2 * out_step), bf16),
                pltpu.VMEM((count, captions, 2 * out_step), bf16),
                pltpu.SemaphoreType.DMA((count - 1,)),
                pltpu.SemaphoreType.DMA((count - 1,)),
                pltpu.VMEM((1, 2 * width + 128), f32),
                pltpu.VMEM((count, 1, 2 * width + 128), f32),
                pltpu.SemaphoreType.DMA((count - 1,)),
                pltpu.SemaphoreType.DMA((count - 1,)),
                pltpu.VMEM((1, 2 * width), f32),
                pltpu.VMEM((count, 1, 2 * width), f32),
                pltpu.SemaphoreType.DMA((count - 1,)),
                pltpu.SemaphoreType.DMA((count - 1,)),
            ],
            "text_backward_joined",
            collective_id=3,
            has_side_effects=True,
        )(*backward_in, factors, jnp.full((1, 128), loss_part))
        norm_total = norm_total[0]
        norms = [norm_total[i * width : (i + 1) * width] for i in range(4)]
        loss_total = norm_total[4 * width]
    else:
        (proj_grad, branch, up_grad, out_grad, qkv_grad, input_grad, norm_grads) = plain(
            text_backward_kernel,
            (
                array((captions, width), bf16),
                array((captions, width), bf16),
                array((col_count, width, wide // col_count), bf16),
                array((col_count, width, width // col_count), bf16),
                array((col_count, width, 3 * width // col_count), bf16),
                array((tokens, width), bf16),
                array((8, width), f32),
            ),
            backward_specs,
            backward_buffers,
            "text_backward",
        )(*backward_in)

        def scattered(matrix):
            blocks = matrix.reshape(count, width // row_count, matrix.shape[2])
            return lax.psum_scatter(blocks, ("col", "row"), scatter_dimension=0, tiled=True)[0].astype(f32)

        up_grad, out_grad, qkv_grad = scattered(up_grad), scattered(out_grad), scattered(qkv_grad)
        grad_down = dot_tn(by_row(inner_sum), by_col(branch))
        grad_proj = dot_tn(by_row(pooled), by_col(proj_grad))
        loss_total, norm_total = lax.psum((loss_part, norm_grads), both)
        norms = [norm_total[i] for i in range(4)]
    mean_loss = (loss_total + 0.5 * jnp.sum(jnp.log(row_sums))) / pair_total
    return (
        mean_loss, hidden, input_grad, *norms, qkv_grad, out_grad, up_grad, grad_down, grad_proj,
    )


def solution(mesh):
    split = P(("row", "col"), None)
    grid = P("row", "col")
    in_specs = (
        split, P(), P(), P("col", None), P("col", None), P("col", None), P("col", None), split, P(("row", "col")),
    ) + (P(),) * 9
    out_specs = (P(), split, split, P(), P(), P(), P(), grid, grid, grid, grid, grid)
    return jax.shard_map(body, mesh=mesh, in_specs=in_specs, out_specs=out_specs, check_vma=False)
```

```python
import functools
import math
from types import SimpleNamespace

import jax
import jax.numpy as jnp
from jax import lax
from jax.experimental import pallas as pl
from jax.experimental.pallas import tpu as pltpu
from jax.sharding import PartitionSpec as P

HEADS = 12
IMG_TOK = 50
norm_eps = 1e-06
logit_scale = 50.0
masked_score = -1e30
log2e = math.log2(math.e)
f32 = jnp.float32
bf16 = jnp.bfloat16
VMEM_LIMIT = 60 * 2**20
MESH = pl.DeviceIdType.MESH


def dot_nn(a, b):
    return lax.dot_general(a, b, (((1,), (0,)), ((), ())), preferred_element_type=f32)


def dot_nt(a, b):
    return lax.dot_general(a, b, (((1,), (1,)), ((), ())), preferred_element_type=f32)


def dot_tn(a, b):
    return lax.dot_general(a, b, (((0,), (0,)), ((), ())), preferred_element_type=f32)


def split_low(x):
    high = x.astype(bf16)
    return high, (x - high.astype(f32)).astype(bf16)


def normed(x):
    centered = x - jnp.mean(x, axis=-1, keepdims=True)
    spread = lax.rsqrt(jnp.mean(centered * centered, axis=-1, keepdims=True) + norm_eps)
    return centered * spread, spread


def layer_norm(x, gain, bias):
    return normed(x)[0] * gain + bias


def normal_tail(x):
    size = jnp.abs(x)
    t = 1.0 / (1.0 + (0.3275911 * math.sqrt(0.5)) * size)
    bell = jnp.exp2((-0.5 * log2e) * (x * x))
    series = 0.5 * 1.061405429
    for factor in (-1.453152027, 1.421413741, -0.284496736, 0.254829592):
        series = series * t + 0.5 * factor
    return size, bell, series * t * bell


def gelu(x):
    size, _, tail = normal_tail(x)
    return jnp.maximum(x, 0.0) - size * tail


def gelu_and_slope(x):
    size, bell, tail = normal_tail(x)
    value = jnp.maximum(x, 0.0) - size * tail
    below = jnp.where(x >= 0.0, 1.0 - tail, tail)
    return value, below + x * (bell * (1.0 / math.sqrt(2.0 * math.pi)))


def lane_halves(width):
    lane = lax.broadcasted_iota(jnp.int32, (1, width), 1)
    first = (lane < width // 2).astype(f32)
    return first.astype(bf16), (1.0 - first).astype(bf16)


def stack_heads(x, first, second):
    return jnp.concatenate([x * first, x * second], axis=0)


def join_heads(stacked):
    rows, width = stacked.shape[0] // 2, stacked.shape[1]
    lane = lax.broadcasted_iota(jnp.int32, (rows, width), 1)
    return jnp.where(lane < width // 2, stacked[:rows], stacked[rows:])


def soft_weights(query, key, bias, factor):
    scores = dot_nt(query, key) * (factor * log2e) + bias
    weights = jnp.exp2(scores - jnp.max(scores, axis=-1, keepdims=True))
    return weights, 1.0 / jnp.sum(weights, axis=-1, keepdims=True)


def set_lengths(lengths_ref, lens_ref, key_bias_ref):
    captions, tokens = lens_ref.shape[0], key_bias_ref.shape[1]
    length = tokens // captions
    caption = lax.broadcasted_iota(jnp.int32, (captions, 1), 0)
    token = lax.broadcasted_iota(jnp.int32, (1, tokens), 1)
    column, row = jnp.zeros((captions, 1), jnp.int32), jnp.zeros((1, tokens), jnp.int32)
    for n in range(captions):
        column = jnp.where(caption == n, lengths_ref[n], column)
        row = jnp.where(token // length == n, lengths_ref[n], row)
    lens_ref[...] = column
    key_bias_ref[...] = jnp.where(token % length < row, 0.0, masked_score)


def as_row(ref):
    return ref[...].reshape(1, ref.shape[0])


def text_bias(key_bias_ref, block, rows, length):
    near = lax.broadcasted_iota(jnp.int32, (rows, rows), 0) // length
    far = lax.broadcasted_iota(jnp.int32, (rows, rows), 1) // length
    columns = pl.ds(pl.multiple_of(block * rows, rows), rows)
    bias = jnp.where(near == far, key_bias_ref[:, columns], masked_score)
    return jnp.concatenate([bias, bias], axis=0)


def member(len_ref, captions, tokens):
    length = tokens // captions
    token = lax.broadcasted_iota(jnp.int32, (captions, tokens), 1)
    caption = lax.broadcasted_iota(jnp.int32, (captions, tokens), 0)
    return ((token // length == caption) & (token % length < len_ref[...])).astype(f32)


def spread_rows(x, length):
    rows, width = x.shape
    return jnp.broadcast_to(x[:, None, :], (rows, length, width)).reshape(rows * length, width)


def text_forward(
    after_up, tok_ref, lengths_ref, gain1, bias1, gain2, bias2, qkv_hbm, out_hbm, up_hbm, down_hbm, proj_hbm,
    hidden_ref, embed_ref, projected_ref, pooled_ref, inner_sum_ref, heads_ref, mixed_ref, mid_ref, slope_ref,
    w_qkv, w_out, w_up, w_down, w_proj, norm_ref, inner_ref, len_ref, key_bias_ref, sems,
):
    tokens, width = tok_ref.shape
    set_lengths(lengths_ref, len_ref, key_bias_ref)
    captions = len_ref.shape[0]
    length = tokens // captions
    wide = w_up.shape[1]
    pairs = ((qkv_hbm, w_qkv), (out_hbm, w_out), (up_hbm, w_up), (down_hbm, w_down), (proj_hbm, w_proj))
    loads = [pltpu.make_async_copy(s, d, sems.at[i]) for i, (s, d) in enumerate(pairs)]
    for load in loads:
        load.start()

    band = 128

    @pl.loop(0, tokens // band)
    def _(i):
        rows = pl.ds(pl.multiple_of(i * band, band), band)
        norm_ref[rows, :] = layer_norm(tok_ref[rows, :].astype(f32), as_row(gain1), as_row(bias1)).astype(bf16)

    loads[0].wait()

    @pl.loop(0, 3 * width // 256)
    def _(j):
        columns = pl.ds(pl.multiple_of(j * 256, 256), 256)
        heads_ref[:, columns] = dot_nn(norm_ref[...], w_qkv[:, columns]).astype(bf16)

    first, second = lane_halves(128)
    factor = (width // HEADS) ** -0.5

    @pl.loop(0, tokens // band)
    def _(block):
        rows = pl.ds(pl.multiple_of(block * band, band), band)
        bias = text_bias(key_bias_ref, block, band, length)
        for pair in range(width // 128):
            at = pair * 128
            query = stack_heads(heads_ref[rows, at : at + 128], first, second)
            weights, scale = soft_weights(query, heads_ref[rows, width + at : width + at + 128], bias, factor)
            value = heads_ref[rows, 2 * width + at : 2 * width + at + 128]
            mixed = dot_nn(weights.astype(bf16), value) * scale
            mixed_ref[rows, at : at + 128] = join_heads(mixed).astype(bf16)

    loads[1].wait()

    @pl.loop(0, tokens // band)
    def _(i):
        rows = pl.ds(pl.multiple_of(i * band, band), band)
        mid = tok_ref[rows, :].astype(f32) + dot_nn(mixed_ref[rows, :], w_out[...])
        mid_ref[rows, :] = mid
        norm_ref[rows, :] = layer_norm(mid, as_row(gain2), as_row(bias2)).astype(bf16)

    loads[2].wait()
    chosen = member(len_ref, captions, tokens)
    chosen_low = chosen.astype(bf16)
    place = lax.broadcasted_iota(jnp.int32, (captions, length, 1), 1)
    valid = (place < len_ref[...].reshape(captions, 1, 1)).astype(f32).reshape(tokens, 1)

    @pl.loop(0, wide // 256)
    def _(j):
        columns = pl.ds(pl.multiple_of(j * 256, 256), 256)
        value, slope = gelu_and_slope(dot_nn(norm_ref[...], w_up[:, columns]))
        value = value.astype(bf16)
        inner_ref[:, columns] = value
        slope_ref[:, columns] = (slope * valid).astype(bf16)
        inner_sum_ref[:, columns] = dot_nn(chosen_low, value).astype(bf16)

    after_up()
    loads[3].wait()
    inverse = 1.0 / len_ref[...].astype(f32)

    @pl.loop(0, width // 256)
    def _(j):
        columns = pl.ds(pl.multiple_of(j * 256, 256), 256)
        state = mid_ref[:, columns] + dot_nn(inner_ref[...], w_down[:, columns])
        hidden_ref[:, columns] = state.astype(bf16)
        high, low = split_low(state)
        pooled_ref[:, columns] = ((dot_nn(chosen_low, high) + dot_nn(chosen_low, low)) * inverse).astype(bf16)

    loads[4].wait()
    projected = dot_nn(pooled_ref[...], w_proj[...])
    projected_ref[...] = projected
    embed_ref[...] = (
        projected * lax.rsqrt(jnp.sum(projected * projected, axis=-1, keepdims=True) + norm_eps)
    ).astype(bf16)


def text_forward_kernel(*refs):
    text_forward(lambda: None, *refs)


def text_forward_joined_kernel(*refs):
    ins, shards, outs, wholes = refs[:11], refs[11:13], refs[13:22], refs[22:24]
    scratch, sems = refs[24:-3], refs[-3:]
    place = Place()
    place.greet_near()
    gathers = [Gather(place, *pair, *(sem.at[i] for sem in sems)) for i, pair in enumerate(zip(shards, wholes))]
    for gather in gathers:
        gather.start()
    text_forward(gathers[0].relay, *ins, *outs, *scratch)
    gathers[1].relay()
    for gather in gathers:
        gather.finish()


def load_weights(pairs, sems):
    loads = [pltpu.make_async_copy(s, d, sems.at[i]) for i, (s, d) in enumerate(pairs)]
    for load in loads:
        load.start()
    return loads


def spans(count, size):
    return lambda i: pl.ds(pl.multiple_of(i * size, size), size)


def norm_backward(outer, unit, spread, gain):
    outer = outer * gain
    inner = outer - jnp.mean(outer, axis=-1, keepdims=True)
    return spread * (inner - unit * jnp.mean(outer * unit, axis=-1, keepdims=True))


class TextBackward:
    band = 128

    def __init__(self, names, refs):
        for name, ref in zip(names, refs, strict=True):
            setattr(self, name, ref)
        self.tokens, self.width = self.tok.shape
        self.captions = self.lens.shape[0]
        set_lengths(self.lengths, self.lens, self.key_bias)
        self.length = self.tokens // self.captions
        self.wide = self.w_up.shape[1]
        pairs = (
            (self.proj_hbm, self.w_proj), (self.down_hbm, self.w_down), (self.up_hbm, self.w_up),
            (self.out_hbm, self.w_out), (self.qkv_hbm, self.w_qkv),
        )
        self.loads = load_weights(pairs, self.sems)

    def rows(self, i):
        return pl.ds(pl.multiple_of(i * self.band, self.band), self.band)

    def bands(self, step):
        pl.loop(0, self.tokens // self.band)(lambda i: step(self.rows(i)))

    def project(self):
        def renorm(rows):
            self.norm[rows, :] = layer_norm(self.mid[rows, :], as_row(self.gain2), as_row(self.bias2)).astype(bf16)

        self.bands(renorm)
        projected = self.projected[...]
        embed_grad = self.embed_grad[...]
        r = lax.rsqrt(jnp.sum(projected * projected, axis=-1, keepdims=True) + norm_eps)
        along = jnp.sum(projected * embed_grad, axis=-1, keepdims=True)
        proj_grad = (r * embed_grad - (r * r * r) * projected * along).astype(bf16)
        self.loads[0].wait()
        state_grad = dot_nt(proj_grad, self.w_proj[...]) * (1.0 / self.lens[...].astype(f32))
        self.branch[...] = state_grad.astype(bf16)
        place = lax.broadcasted_iota(jnp.int32, (self.captions, self.length, 1), 1)
        valid = (place < self.lens[...].reshape(self.captions, 1, 1)).astype(f32).reshape(self.tokens, 1)
        self.mid_grad[...] = spread_rows(state_grad, self.length) * valid
        return proj_grad, self.branch[...]

    def inner(self, col_parts, store_up):
        self.loads[1].wait()
        branch = self.branch[...]
        step = self.wide // col_parts
        for part in range(col_parts):

            @pl.loop(0, step // 256)
            def _(j):
                columns = pl.ds(pl.multiple_of(part * step + j * 256, 256), 256)
                inner_grad = dot_nt(branch, self.w_down[columns, :])
                pre_grad = spread_rows(inner_grad, self.length) * self.slope[:, columns].astype(f32)
                pre_grad = pre_grad.astype(bf16)
                self.pre_grad[:, columns] = pre_grad
                local = pl.ds(pl.multiple_of(j * 256, 256), 256)
                store_up(part, local, dot_tn(self.norm[...], pre_grad).astype(bf16))

    def middle(self):
        self.loads[2].wait()

        @pl.loop(0, self.width // 256)
        def _(j):
            columns = pl.ds(pl.multiple_of(j * 256, 256), 256)
            self.outer[:, columns] = dot_nt(self.pre_grad[...], self.w_up[columns, :])

        self.norm_grad[...] = jnp.zeros_like(self.norm_grad)

        def through_norm(rows):
            unit, spread = normed(self.mid[rows, :])
            outer = self.outer[rows, :]
            self.norm_grad[2:3, :] += jnp.sum(outer * unit, axis=0, keepdims=True)
            self.norm_grad[3:4, :] += jnp.sum(outer, axis=0, keepdims=True)
            mid_grad = self.mid_grad[rows, :] + norm_backward(outer, unit, spread, as_row(self.gain2))
            self.mid_grad[rows, :] = mid_grad
            self.low_grad[rows, :] = mid_grad.astype(bf16)

        self.bands(through_norm)

    def output(self, col_parts, store_out):
        step = self.width // col_parts
        for part in range(col_parts):
            store_out(part, dot_tn(self.mixed[...], self.low_grad[:, part * step : (part + 1) * step]).astype(bf16))
        self.loads[3].wait()

        def through_out(rows):
            self.mixed_grad[rows, :] = dot_nt(self.low_grad[rows, :], self.w_out[...]).astype(bf16)
            norm = layer_norm(self.tok[rows, :].astype(f32), as_row(self.gain1), as_row(self.bias1))
            self.norm[rows, :] = norm.astype(bf16)

        self.bands(through_out)

    def attention(self):
        first, second = lane_halves(128)
        width = self.width
        factor = (width // HEADS) ** -0.5

        @pl.loop(0, self.tokens // self.band)
        def _(block):
            rows = self.rows(block)
            bias = text_bias(self.key_bias, block, self.band, self.length)
            for pair in range(width // 128):
                at = pair * 128
                query = stack_heads(self.heads[rows, at : at + 128], first, second)
                key = self.heads[rows, width + at : width + at + 128]
                value = self.heads[rows, 2 * width + at : 2 * width + at + 128]
                grad = stack_heads(self.mixed_grad[rows, at : at + 128], first, second)
                weights, scale = soft_weights(query, key, bias, factor)
                probs = weights * scale
                prob_grad = dot_nt(grad, value)
                total = jnp.sum(prob_grad * probs, axis=-1, keepdims=True)
                score_grad = (probs * (prob_grad - total)).astype(bf16)
                query_grad = join_heads(dot_nn(score_grad, key)) * factor
                self.heads_grad[rows, at : at + 128] = query_grad.astype(bf16)
                key_grad = dot_tn(score_grad, query) * factor
                self.heads_grad[rows, width + at : width + at + 128] = key_grad.astype(bf16)
                value_grad = dot_tn(probs.astype(bf16), grad)
                self.heads_grad[rows, 2 * width + at : 2 * width + at + 128] = value_grad.astype(bf16)

    def heads_weights(self, col_parts, store_qkv):
        step = 3 * self.width // col_parts
        for part in range(col_parts):
            store_qkv(
                part, dot_tn(self.norm[...], self.heads_grad[:, part * step : (part + 1) * step]).astype(bf16)
            )

    def input(self):
        self.loads[4].wait()

        @pl.loop(0, self.width // 256)
        def _(j):
            columns = pl.ds(pl.multiple_of(j * 256, 256), 256)
            self.outer[:, columns] = dot_nt(self.heads_grad[...], self.w_qkv[columns, :])

        def through_norm(rows):
            unit, spread = normed(self.tok[rows, :].astype(f32))
            outer = self.outer[rows, :]
            self.norm_grad[0:1, :] += jnp.sum(outer * unit, axis=0, keepdims=True)
            self.norm_grad[1:2, :] += jnp.sum(outer, axis=0, keepdims=True)
            inner = norm_backward(outer, unit, spread, as_row(self.gain1))
            self.input_grad[rows, :] = (self.mid_grad[rows, :] + inner).astype(bf16)

        self.bands(through_norm)


backward_ins = (
    "tok", "lengths", "gain1", "bias1", "gain2", "bias2", "embed_grad", "projected", "heads",
    "mixed", "mid", "slope", "qkv_hbm", "out_hbm", "up_hbm", "down_hbm", "proj_hbm",
)
backward_scratch = (
    "w_qkv", "w_out", "w_up", "w_down", "w_proj", "norm", "pre_grad", "outer", "mid_grad", "low_grad",
    "mixed_grad", "heads_grad",
    "lens", "key_bias", "sems",
)
scatter_names = (
    "held", "near", "x1", "y1", "x2", "y2", "far", "sends", "recvs",
)
exchange_names = (
    "own", "all", "sends", "recvs",
)


def text_backward_kernel(*refs):
    outs = ("proj_grad", "branch", "up_grad", "out_grad", "qkv_grad", "input_grad", "norm_grad")
    t = TextBackward(backward_ins + outs + backward_scratch, refs)
    parts = t.up_grad.shape[0]

    def store_up(part, columns, value):
        t.up_grad[part, :, columns] = value

    def store_out(part, value):
        t.out_grad[part] = value

    def store_qkv(part, value):
        t.qkv_grad[part] = value

    t.proj_grad[...] = t.project()[0]
    t.inner(parts, store_up)
    t.middle()
    t.output(parts, store_out)
    t.attention()
    t.heads_weights(parts, store_qkv)
    t.input()


class Place:
    def __init__(self, z_count=4, y_count=2, x_count=2, k_count=2):
        self.row, self.col = lax.axis_index("row"), lax.axis_index("col")
        self.z, self.y = self.row // y_count, self.row % y_count
        self.x, self.k = self.col // k_count, self.col % k_count
        self.rows, self.cols = z_count * y_count, x_count * k_count
        self.count = self.rows * self.cols
        self.me = self.row * self.cols + self.col

    def at(self, **moved):
        z, y, x, k = (moved.get(name, getattr(self, name)) for name in "zyxk")
        return z * 2 + y, x * 2 + k

    def peer(self, distance):
        other = (self.me + distance) % self.count
        return other // self.cols, other % self.cols

    def greet(self):
        barrier = pltpu.get_barrier_semaphore()

        @pl.loop(1, self.count)
        def _(distance):
            pl.semaphore_signal(barrier, inc=1, device_id=self.peer(distance), device_id_type=MESH)

        pl.semaphore_wait(barrier, self.count - 1)

    def greet_near(self):
        barrier = pltpu.get_barrier_semaphore()
        for other in (self.at(k=1 - self.k), self.at(x=1 - self.x)):
            pl.semaphore_signal(barrier, inc=1, device_id=other, device_id_type=MESH)
        pl.semaphore_wait(barrier, 2)


def remote(src, dst, send, recv, to):
    return pltpu.make_async_remote_copy(
        src_ref=src, dst_ref=dst, send_sem=send, recv_sem=recv, device_id=to, device_id_type=MESH
    )


class Gather:
    def __init__(self, place, shard, whole, local, sends, recvs):
        depth = shard.shape[0]

        def block(col):
            return whole.at[pl.ds(pl.multiple_of(col * depth, depth), depth)]

        own, across = block(place.col), block(place.at(x=1 - place.x)[1])
        mate, next_chip = place.at(k=1 - place.k), place.at(x=1 - place.x)
        self.local = pltpu.make_async_copy(shard, own, local)
        self.near = remote(shard, own, sends.at[0], recvs.at[0], mate)
        self.far = remote(shard, own, sends.at[1], recvs.at[1], next_chip)
        self.passed = remote(across, across, sends.at[2], recvs.at[2], mate)

    def start(self):
        self.far.start()
        self.near.start()
        self.local.start()

    def relay(self):
        self.far.wait()
        self.passed.start()

    def finish(self):
        self.local.wait()
        self.near.wait()
        self.passed.wait()


class Exchange:
    def __init__(self, place, source, slots, sends, recvs):
        self.place, self.source, self.slots, self.sends, self.recvs = place, source, slots, sends, recvs

    def copy(self, distance):
        to = self.place.peer(distance)
        sems = self.sends.at[distance - 1], self.recvs.at[distance - 1]
        return remote(self.source(to), self.slots.at[self.place.me], *sems, to)

    def start(self):
        pl.loop(1, self.place.count)(lambda distance: self.copy(distance).start())

    def finish(self):
        pl.loop(1, self.place.count)(lambda distance: self.copy(distance).wait())


class GradientScatter:
    def __init__(self, place, held, near, x1, y1, x2, y2, far, sends, recvs):
        self.place, self.held, self.near, self.far = place, held, near, far
        self.x1, self.y1, self.x2, self.y2 = x1, y1, x2, y2
        self.sends, self.recvs = sends, recvs
        half = held.shape[5] // 2
        self.one, self.two = pl.ds(0, half), pl.ds(half, half)

    def copy(self, n, src, dst, **moved):
        return remote(src, dst, self.sends.at[n], self.recvs.at[n], self.place.at(**moved))

    def copies(self, stage):
        p, held = self.place, self.held
        x, y, z, k = p.x, p.y, p.z, p.k
        every = slice(None)
        if stage == 0:
            return [self.copy(0, held.at[:, 1 - k], self.near, k=1 - k)]
        if stage == 1:
            return [
                self.copy(1, held.at[1 - x, k, :, :, :, self.one], self.x1, x=1 - x),
                self.copy(2, held.at[:, k, :, 1 - y, :, self.two], self.y1, y=1 - y),
            ]
        if stage == 2:
            return [
                self.copy(3, held.at[x, k, :, 1 - y, :, self.one], self.y2, y=1 - y),
                self.copy(4, held.at[1 - x, k, :, y, :, self.two], self.x2, x=1 - x),
            ]
        copies = []
        for distance in range(1, held.shape[2]):
            other = (z + distance) % held.shape[2]
            copies.append(self.copy(4 + distance, held.at[x, k, other, y], self.far.at[distance - 1], z=other))
        return copies

    def start(self, stage):
        for copy in self.copies(stage):
            copy.start()

    def finish(self, stage):
        for copy in self.copies(stage):
            copy.wait()
        p, held = self.place, self.held
        x, y, k = p.x, p.y, p.k
        z_count = held.shape[2]

        def add(target, source):
            target[...] = (target[...].astype(f32) + source[...].astype(f32)).astype(bf16)

        if stage == 0:
            for i in range(2):
                for j in range(2):
                    pl.loop(0, z_count)(lambda z: add(held.at[i, k, z, j], self.near.at[i, z, j]))
        if stage == 1:
            for i in range(2):
                pl.loop(0, z_count)(lambda z: add(held.at[x, k, z, i, :, self.one], self.x1.at[z, i]))
                pl.loop(0, z_count)(lambda z: add(held.at[i, k, z, y, :, self.two], self.y1.at[i, z]))
        if stage == 2:
            pl.loop(0, z_count)(lambda z: add(held.at[x, k, z, y, :, self.one], self.y2.at[z]))
            pl.loop(0, z_count)(lambda z: add(held.at[x, k, z, y, :, self.two], self.x2.at[z]))
        if stage == 3:
            total = held[x, k, p.z, y].astype(f32)
            for i in range(z_count - 1):
                total = total + self.far[i].astype(f32)
            return total


def scatter_scratch(rows, columns):
    shapes = [
        (2, 2, 4, 2, rows, columns), (2, 4, 2, rows, columns), (4, 2, rows, columns // 2), (2, 4, rows, columns // 2),
        (4, rows, columns // 2), (4, rows, columns // 2), (3, rows, columns),
    ]
    return [pltpu.VMEM(shape, bf16) for shape in shapes] + [pltpu.SemaphoreType.DMA((8,))] * 2


def text_backward_joined_kernel(*refs):
    ins = backward_ins + ("factors", "loss")
    outs = ("up_out", "out_out", "qkv_out", "down_out", "proj_out", "input_grad", "norm_out")
    sets = tuple(name + tag for tag in ("_a", "_b") for name in scatter_names)
    swaps = tuple(name + tag for tag in ("_factors", "_late", "_last") for name in exchange_names)
    names = ins + outs + backward_scratch + sets + ("branch", "norm_grad") + swaps
    t = TextBackward(names, refs)
    place = Place()
    width = t.width
    scatter_a, scatter_b = (
        GradientScatter(place, *(getattr(t, name + tag) for name in scatter_names)) for tag in ("_a", "_b")
    )
    factors = Exchange(
        place, lambda to: t.own_factors.at[to[1]], t.all_factors, t.sends_factors, t.recvs_factors
    )
    late = Exchange(place, lambda to: t.own_late, t.all_late, t.sends_late, t.recvs_late)
    last = Exchange(place, lambda to: t.own_last, t.all_last, t.sends_last, t.recvs_last)
    cols = place.cols

    def blocked(value):
        return value.reshape(4, 2, value.shape[0] // 8, value.shape[1])

    def store_up(part, columns, value):
        t.held_a[part // 2, part % 2, :, :, :, columns] = blocked(value)

    qkv_step, out_step = 3 * width // cols, width // cols

    def store_out(part, value):
        t.held_b[part // 2, part % 2, :, :, :, qkv_step:] = blocked(value)

    def store_qkv(part, value):
        t.held_b[part // 2, part % 2, :, :, :, :qkv_step] = blocked(value)

    proj_grad, branch = t.project()
    for part in range(cols):
        columns = slice(part * out_step, (part + 1) * out_step)
        t.own_factors[part] = jnp.concatenate([branch[:, columns], proj_grad[:, columns]], axis=1)
    t.all_factors[place.me] = t.own_factors[place.col]
    place.greet()
    factors.start()
    t.inner(cols, store_up)
    scatter_a.start(0)
    t.middle()
    scatter_a.finish(0)
    scatter_a.start(1)
    t.own_late[...] = jnp.concatenate([t.norm_grad[2:3, :], t.norm_grad[3:4, :], t.loss[...]], axis=1)
    t.all_late[place.me] = t.own_late[...]
    late.start()
    t.output(cols, store_out)
    scatter_a.finish(1)
    scatter_a.start(2)
    t.attention()
    t.heads_weights(cols, store_qkv)
    scatter_b.start(0)
    scatter_a.finish(2)
    scatter_a.start(3)
    scatter_b.finish(0)
    scatter_b.start(1)
    t.input()
    t.own_last[...] = jnp.concatenate([t.norm_grad[0:1, :], t.norm_grad[1:2, :]], axis=1)
    t.all_last[place.me] = t.own_last[...]
    scatter_b.finish(1)
    scatter_b.start(2)
    last.start()
    t.up_out[...] = scatter_a.finish(3)
    factors.finish()
    grown = dot_tn(
        t.factors[...].reshape(-1, t.factors.shape[2]), t.all_factors[...].reshape(-1, t.all_factors.shape[2])
    )
    inner_step = t.wide // place.rows
    t.down_out[...] = grown[:inner_step, :out_step]
    t.proj_out[...] = grown[inner_step : inner_step + width // place.rows, out_step:]
    late.finish()
    scatter_b.finish(2)
    scatter_b.start(3)
    last.finish()
    t.norm_out[:, : 2 * width] = jnp.sum(t.all_last[...], axis=0)
    t.norm_out[:, 2 * width :] = jnp.sum(t.all_late[...], axis=0)
    total = scatter_b.finish(3)
    t.qkv_out[...] = total[:, :qkv_step]
    t.out_out[...] = total[:, qkv_step:]


def group_mean(images, rows):
    token = lax.broadcasted_iota(jnp.int32, (images, rows), 1)
    image = lax.broadcasted_iota(jnp.int32, (images, rows), 0)
    inside = (token >= image * IMG_TOK) & (token < (image + 1) * IMG_TOK)
    return inside.astype(f32).astype(bf16)


def load_parts(parts, target, sems, col, col_count):
    depth = target.shape[0] // col_count
    copies = []
    for k, part in enumerate(parts):
        place = pl.multiple_of((col ^ k) * depth, depth)
        copies.append(pltpu.make_async_copy(part, target.at[pl.ds(place, depth)], sems.at[k]))
    return copies


def image_mix(tokens, gain_ref, bias_ref, w_qkv, w_out, norm_ref, heads_ref, mixed_ref):
    rows, width = tokens.shape
    images = rows // IMG_TOK
    norm_ref[...] = layer_norm(tokens.astype(f32), gain_ref[0:1, :], bias_ref[0:1, :]).astype(bf16)

    @pl.loop(0, 3 * width // 256)
    def _(j):
        columns = pl.ds(pl.multiple_of(j * 256, 256), 256)
        heads_ref[:, columns] = dot_nn(norm_ref[...], w_qkv[:, columns]).astype(bf16)

    first, second = lane_halves(128)
    factor = (width // HEADS) ** -0.5
    window = 112
    for pair in range(images // 2):
        start, low = pair * 2 * IMG_TOK, (pair * 2 * IMG_TOK) // 16 * 16
        near = lax.broadcasted_iota(jnp.int32, (window, window), 0) + low
        far = lax.broadcasted_iota(jnp.int32, (window, window), 1) + low
        same = (near >= start) & (near < start + 2 * IMG_TOK) & (far >= start) & (far < start + 2 * IMG_TOK)
        same = same & ((near >= start + IMG_TOK) == (far >= start + IMG_TOK))
        bias = jnp.where(same, 0.0, masked_score)
        bias = jnp.concatenate([bias, bias], axis=0)
        keep = lax.broadcasted_iota(jnp.int32, (16, 128), 0) + low < start
        span = slice(low, low + window)

        @pl.loop(0, width // 128)
        def _(two):
            at = pl.multiple_of(two * 128, 128)
            query = stack_heads(heads_ref[span, pl.ds(at, 128)], first, second)
            weights, scale = soft_weights(query, heads_ref[span, pl.ds(width + at, 128)], bias, factor)
            value = heads_ref[span, pl.ds(2 * width + at, 128)]
            mixed = join_heads(dot_nn(weights.astype(bf16), value) * scale)
            if low == start:
                mixed_ref[span, pl.ds(at, 128)] = mixed.astype(bf16)
            else:
                former = mixed_ref[low : low + 16, pl.ds(at, 128)].astype(f32)
                mixed_ref[low : low + 16, pl.ds(at, 128)] = jnp.where(keep, former, mixed[:16]).astype(bf16)
                mixed_ref[low + 16 : low + window, pl.ds(at, 128)] = mixed[16:].astype(bf16)

    mid = tokens.astype(f32) + dot_nn(mixed_ref[...], w_out[...])
    high, low = split_low(mid)
    select = group_mean(images, rows)
    mean = (dot_nn(select, high) + dot_nn(select, low)) * (1.0 / IMG_TOK)
    return layer_norm(mid, gain_ref[1:2, :], bias_ref[1:2, :]).astype(bf16), mean


def image_mix_kernel(col_count, tok_ref, gain_ref, bias_ref, *refs):
    qkv_parts, out_parts = refs[:col_count], refs[col_count : 2 * col_count]
    normed_ref, mean_ref, w_qkv, w_out, *buffers, sems = refs[2 * col_count :]
    col = lax.axis_index("col")

    @pl.when(pl.program_id(0) == 0)
    def _():
        copies = load_parts(qkv_parts, w_qkv, sems.at[0], col, col_count)
        copies += load_parts(out_parts, w_out, sems.at[1], col, col_count)
        for copy in copies:
            copy.start()
        for copy in copies:
            copy.wait()

    normed_ref[...], mean_ref[...] = image_mix(tok_ref[...], gain_ref, bias_ref, w_qkv, w_out, *buffers)


def image_embed_kernel(col_count, normed_ref, mean_ref, *refs):
    up_parts, down_parts = refs[:col_count], refs[col_count : 2 * col_count]
    embed_ref, w_up, w_down, sum_ref, sems = refs[2 * col_count :]
    rows, width = normed_ref.shape
    images = rows // IMG_TOK
    wide = w_up.shape[1]
    step = pl.program_id(0)
    col = lax.axis_index("col")
    downs = load_parts(down_parts, w_down, sems.at[1], col, col_count)

    @pl.when(step == 0)
    def _():
        ups = load_parts(up_parts, w_up, sems.at[0], col, col_count)
        for copy in ups + downs:
            copy.start()
        for copy in ups:
            copy.wait()

    select = group_mean(images, rows)

    @pl.loop(0, wide // 256)
    def _(j):
        columns = pl.ds(pl.multiple_of(j * 256, 256), 256)
        inner = gelu(dot_nn(normed_ref[...], w_up[:, columns])).astype(bf16)
        sum_ref[pl.ds(pl.multiple_of(step * images, images), images), columns] = dot_nn(select, inner)

    @pl.when(step == pl.num_programs(0) - 1)
    def _():
        for copy in downs:
            copy.wait()
        high, low = split_low(sum_ref[...] * (1.0 / IMG_TOK))
        pooled = mean_ref[...] + dot_nn(high, w_down[...]) + dot_nn(low, w_down[...])
        embed_ref[...] = (
            pooled * lax.rsqrt(jnp.sum(pooled * pooled, axis=-1, keepdims=True) + norm_eps)
        ).astype(bf16)


image_names = (
    "tok", "gain", "bias", "qkv_hbm", "out_hbm", "up_hbm", "down_hbm", "text_embed", "own_factors",
    "embed_grad", "all_factors", "loss",
    "w_qkv", "w_out", "w_up", "w_down", "norm", "heads", "mixed", "normed", "mean", "sums", "own", "images",
    "own_sums", "all_sums", "loads", "local", "sends", "recvs", "factor_sends", "factor_recvs", "factor_local",
    "image_sends", "image_recvs", "pass_sends", "pass_recvs", "sum_sends", "sum_recvs",
)


def image_joined_kernel(*refs):
    t = SimpleNamespace(**dict(zip(image_names, refs, strict=True)))
    place = Place()
    loads = load_weights(((t.qkv_hbm, t.w_qkv), (t.out_hbm, t.w_out)), t.loads)
    place.greet()
    up, down = (
        Gather(place, shard, target, t.local.at[i], t.sends.at[i], t.recvs.at[i])
        for i, (shard, target) in enumerate(((t.up_hbm, t.w_up), (t.down_hbm, t.w_down)))
    )
    up.start()
    rows, width = t.tok.shape
    group_rows = t.norm.shape[0]
    groups = rows // group_rows
    group_images = group_rows // IMG_TOK
    for load in loads:
        load.wait()

    @pl.loop(0, groups)
    def _(group):
        span = pl.ds(pl.multiple_of(group * group_rows, 16), group_rows)
        normed2, mean = image_mix(
            t.tok[span, :], t.gain, t.bias, t.w_qkv, t.w_out, t.norm, t.heads, t.mixed
        )
        t.normed[span, :] = normed2
        t.mean[pl.ds(pl.multiple_of(group * group_images, 8), group_images), :] = mean

        @pl.when(group == groups // 2)
        def _():
            up.relay()
            down.start()

    factors = Exchange(
        place, lambda to: t.own_factors.at[to[0]], t.all_factors, t.factor_sends, t.factor_recvs
    )
    own_factor = pltpu.make_async_copy(
        t.own_factors.at[place.row], t.all_factors.at[place.me], t.factor_local.at[0]
    )
    own_factor.start()
    factors.start()
    up.finish()

    halves, _, chips, half_images, _ = t.images.shape
    half_rows = half_images * IMG_TOK
    wide = t.w_up.shape[1]
    select = group_mean(half_images, half_rows)
    chip = place.row * 2 + place.x

    def image_copy(half, distance):
        other = (chip + distance) % chips
        mine = t.images.at[half, place.k, chip]
        sems = t.image_sends.at[half, distance - 1], t.image_recvs.at[half, distance - 1]
        return remote(mine, mine, *sems, (other // 2, other % 2 * 2 + place.k))

    def pass_copy(half):
        held = t.images.at[half, place.k]
        return remote(held, held, t.pass_sends.at[half], t.pass_recvs.at[half], place.at(k=1 - place.k))

    for half in range(halves):
        span = slice(half * half_rows, (half + 1) * half_rows)

        @pl.loop(0, wide // 256)
        def _(j):
            columns = pl.ds(pl.multiple_of(j * 256, 256), 256)
            inner = gelu(dot_nn(t.normed[span, :], t.w_up[:, columns])).astype(bf16)
            t.sums[:, columns] = dot_nn(select, inner)

        if half == 0:
            down.relay()
            down.finish()
        else:
            pl.loop(1, chips)(lambda distance: image_copy(half - 1, distance).wait())
            pass_copy(half - 1).start()
        high, low = split_low(t.sums[...] * (1.0 / IMG_TOK))
        pooled = dot_nn(jnp.concatenate([high, low], axis=0), t.w_down[...])
        part = slice(half * half_images, (half + 1) * half_images)
        pooled = t.mean[part, :] + pooled[:half_images] + pooled[half_images:]
        embed = pooled * lax.rsqrt(jnp.sum(pooled * pooled, axis=-1, keepdims=True) + norm_eps)
        t.own[part, :] = embed.astype(bf16)
        t.images[half, place.k, chip] = embed.astype(bf16)
        pl.loop(1, chips)(lambda distance: image_copy(half, distance).start())

    pl.loop(1, chips)(lambda distance: image_copy(halves - 1, distance).wait())
    pass_copy(halves - 1).start()
    for half in range(halves):
        pass_copy(half).wait()

    images = t.images[...].reshape(-1, width)
    own = t.own[...].astype(f32)
    lifted = jnp.exp2(dot_nt(t.text_embed[...], images) * (logit_scale * log2e))
    col_sums = jnp.sum(lifted, axis=1, keepdims=True)
    t.own_sums[...] = jnp.sum(lifted, axis=0, keepdims=True)
    t.all_sums[place.me] = t.own_sums[...]
    sums = Exchange(place, lambda to: t.own_sums, t.all_sums, t.sum_sends, t.sum_recvs)
    sums.start()
    positives = logit_scale * jnp.sum(own * t.text_embed[...].astype(f32), axis=(0, 1), keepdims=True)
    sums.finish()
    row_sums = jnp.sum(t.all_sums[...], axis=0)
    sim_grad = (0.5 * (lifted * (1.0 / row_sums) + lifted * (1.0 / col_sums))).astype(bf16)
    t.embed_grad[...] = logit_scale * (dot_nn(sim_grad, images) - own)
    logs = jnp.sum(jnp.log(col_sums), axis=(0, 1), keepdims=True)
    logs = logs + jnp.sum(jnp.log(row_sums), axis=(0, 1), keepdims=True) * (1.0 / place.count)
    t.loss[...] = jnp.broadcast_to(0.5 * logs - positives, t.loss.shape)
    own_factor.wait()
    factors.finish()


def whole(shape):
    return pl.BlockSpec(shape, lambda *_: (0,) * len(shape))


in_vmem = pl.BlockSpec(memory_space=pltpu.VMEM)
in_smem = pl.BlockSpec(memory_space=pltpu.SMEM)
anywhere = pl.BlockSpec(memory_space=pl.ANY)


def plain(kernel, outs, ins, scratch, name, out_specs=None, **settings):
    return pl.pallas_call(
        kernel,
        out_shape=outs,
        in_specs=ins,
        out_specs=out_specs or [in_vmem] * len(outs),
        scratch_shapes=scratch,
        compiler_params=pltpu.CompilerParams(vmem_limit_bytes=VMEM_LIMIT, **settings),
        name=name,
    )


def array(shape, dtype):
    return jax.ShapeDtypeStruct(shape, dtype)


def partners(x, col_count):
    order = [(i, i ^ 2) for i in range(col_count)]
    near = [(i, i ^ 1) for i in range(col_count)]
    far = lax.ppermute(x, "col", order)
    return [x, lax.ppermute(x, "col", near), far, lax.ppermute(far, "col", near)]


def body(
    image_tokens, image_norm_gain, image_norm_bias, image_qkv, image_out, image_up, image_down,
    text_tokens, text_lengths, norm1_gain, norm1_bias, norm2_gain, norm2_bias,
    text_qkv, text_out, text_up, text_down, text_proj,
):
    tokens, width = text_tokens.shape
    captions = text_lengths.shape[0]
    length = tokens // captions
    wide = text_up.shape[1]
    row_count, col_count = lax.axis_size("row"), lax.axis_size("col")
    row, col = lax.axis_index("row"), lax.axis_index("col")
    pair_total = captions * row_count * col_count
    image_rows, images = image_tokens.shape[0], image_tokens.shape[0] // IMG_TOK

    count = row_count * col_count
    joined = (row_count, col_count) == (8, 4)
    vectors = (norm1_gain, norm1_bias, norm2_gain, norm2_bias)
    weights = (text_qkv, text_out, text_up, text_down, text_proj)
    weight_scratch = [pltpu.VMEM(w.shape, bf16) for w in weights]

    text_outs = (
        array((tokens, width), bf16),
        array((captions, width), bf16),
        array((captions, width), f32),
        array((captions, width), bf16),
        array((captions, wide), bf16),
        array((tokens, 3 * width), bf16),
        array((tokens, width), bf16),
        array((tokens, width), f32),
        array((tokens, wide), bf16),
    )
    text_specs = [in_vmem, in_smem] + [in_vmem] * 4 + [anywhere] * 5
    text_buffers = weight_scratch + [
        pltpu.VMEM((tokens, width), bf16),
        pltpu.VMEM((tokens, wide), bf16),
        pltpu.VMEM((captions, 1), jnp.int32),
        pltpu.VMEM((1, tokens), f32),
        pltpu.SemaphoreType.DMA((5,)),
    ]
    text_in = (text_tokens, text_lengths, *vectors, *weights)
    groups = 4
    group_rows, group_images = image_rows // groups, images // groups
    mix_buffers = [
        pltpu.VMEM((group_rows, width), bf16),
        pltpu.VMEM((group_rows, 3 * width), bf16),
        pltpu.VMEM((group_rows, width), bf16),
    ]
    mix_weights = [pltpu.VMEM((width, 3 * width), bf16), pltpu.VMEM((width, width), bf16)]
    embed_weights = [pltpu.VMEM((width, wide), bf16), pltpu.VMEM((wide, width), bf16)]
    both = ("row", "col")

    if joined:
        *text_results, whole_qkv, whole_out = plain(
            text_forward_joined_kernel,
            text_outs + (array((width, 3 * width), bf16), array((width, width), bf16)),
            text_specs + [anywhere] * 2,
            text_buffers + [pltpu.SemaphoreType.DMA((2,))] + [pltpu.SemaphoreType.DMA((2, 3))] * 2,
            "text_forward_joined",
            out_specs=[in_vmem] * len(text_outs) + [anywhere] * 2,
            collective_id=1,
            has_side_effects=True,
        )(*text_in, image_qkv, image_out)
        (hidden, text_embed, projected, pooled, inner_sum, heads, mixed, mid, slope) = text_results
        row_blocks = [inner_sum.reshape(captions, row_count, -1), pooled.reshape(captions, row_count, -1)]
        packed = jnp.concatenate(row_blocks, axis=2)
        packed = jnp.pad(packed, ((0, 0), (0, 0), (0, -packed.shape[2] % 128))).transpose(1, 0, 2)
        chips, halves = count // 2, 2
        embed_grad, factors, loss_part = plain(
            image_joined_kernel,
            (array((captions, width), f32), array((count, *packed.shape[1:]), bf16), array((1, 128), f32)),
            [in_vmem] * 3 + [anywhere] * 4 + [in_vmem] * 2,
            mix_weights
            + embed_weights
            + mix_buffers
            + [
                pltpu.VMEM((image_rows, width), bf16),
                pltpu.VMEM((images, width), f32),
                pltpu.VMEM((images // halves, wide), f32),
                pltpu.VMEM((images, width), bf16),
                pltpu.VMEM((halves, 2, chips, images // halves, width), bf16),
                pltpu.VMEM((1, pair_total), f32),
                pltpu.VMEM((count, 1, pair_total), f32),
                pltpu.SemaphoreType.DMA((2,)),
                pltpu.SemaphoreType.DMA((2,)),
                pltpu.SemaphoreType.DMA((2, 3)),
                pltpu.SemaphoreType.DMA((2, 3)),
                pltpu.SemaphoreType.DMA((count - 1,)),
                pltpu.SemaphoreType.DMA((count - 1,)),
                pltpu.SemaphoreType.DMA((1,)),
                pltpu.SemaphoreType.DMA((halves, chips - 1)),
                pltpu.SemaphoreType.DMA((halves, chips - 1)),
                pltpu.SemaphoreType.DMA((halves,)),
                pltpu.SemaphoreType.DMA((halves,)),
                pltpu.SemaphoreType.DMA((count - 1,)),
                pltpu.SemaphoreType.DMA((count - 1,)),
            ],
            "image_joined",
            out_specs=[in_vmem, anywhere, in_vmem],
            collective_id=2,
            has_side_effects=True,
        )(
            image_tokens, image_norm_gain, image_norm_bias, whole_qkv, whole_out, image_up, image_down,
            text_embed, packed,
        )
    else:
        (hidden, text_embed, projected, pooled, inner_sum, heads, mixed, mid, slope) = plain(
            text_forward_kernel, text_outs, text_specs, text_buffers, "text_forward"
        )(*text_in)
        qkv_parts = partners(image_qkv, col_count)
        out_parts = partners(image_out, col_count)
        up_parts = partners(image_up, col_count)
        down_parts = partners(image_down, col_count)
        parts = [anywhere] * (2 * col_count)
        image_normed, image_mean = pl.pallas_call(
            functools.partial(image_mix_kernel, col_count),
            grid=(groups,),
            out_shape=(array((image_rows, width), bf16), array((images, width), f32)),
            in_specs=[
                pl.BlockSpec((group_rows, width), lambda i: (i, 0)),
                whole(image_norm_gain.shape),
                whole(image_norm_bias.shape),
            ]
            + parts,
            out_specs=(
                pl.BlockSpec((group_rows, width), lambda i: (i, 0)),
                pl.BlockSpec((group_images, width), lambda i: (i, 0)),
            ),
            scratch_shapes=mix_weights + mix_buffers + [pltpu.SemaphoreType.DMA((2, col_count))],
            compiler_params=pltpu.CompilerParams(vmem_limit_bytes=VMEM_LIMIT),
            name="image_mix",
        )(image_tokens, image_norm_gain, image_norm_bias, *qkv_parts, *out_parts)
        image_embed = pl.pallas_call(
            functools.partial(image_embed_kernel, col_count),
            grid=(groups,),
            out_shape=array((images, width), bf16),
            in_specs=[pl.BlockSpec((group_rows, width), lambda i: (i, 0)), whole((images, width))] + parts,
            out_specs=whole((images, width)),
            scratch_shapes=embed_weights
            + [pltpu.VMEM((images, wide), f32), pltpu.SemaphoreType.DMA((2, col_count))],
            compiler_params=pltpu.CompilerParams(vmem_limit_bytes=VMEM_LIMIT),
            name="image_embed",
        )(image_normed, image_mean, *up_parts, *down_parts)

        image_all = lax.all_gather(image_embed, both, axis=0, tiled=True)
        lifted = jnp.exp(logit_scale * dot_nt(image_all, text_embed))
        row_sums = lax.psum(jnp.sum(lifted, axis=1), both)
        col_sums = jnp.sum(lifted, axis=0)
        sim_grad = (0.5 * (lifted / row_sums[:, None] + lifted / col_sums[None, :])).astype(bf16)
        image_own = image_embed.astype(f32)
        embed_grad = logit_scale * (dot_tn(sim_grad, image_all) - image_own)
        positives = logit_scale * jnp.sum(image_own * text_embed.astype(f32), axis=1)
        loss_part = 0.5 * jnp.sum(jnp.log(col_sums) - 2.0 * positives)
        loss_part = loss_part + 0.5 * jnp.sum(jnp.log(row_sums)) / count

    backward_in = (
        text_tokens, text_lengths, *vectors, embed_grad, projected, heads, mixed, mid, slope, *weights,
    )
    backward_specs = [in_vmem, in_smem] + [in_vmem] * 10 + [anywhere] * 5
    backward_buffers = weight_scratch + [
        pltpu.VMEM((tokens, width), bf16),
        pltpu.VMEM((tokens, wide), bf16),
        pltpu.VMEM((tokens, width), f32),
        pltpu.VMEM((tokens, width), f32),
        pltpu.VMEM((tokens, width), bf16),
        pltpu.VMEM((tokens, width), bf16),
        pltpu.VMEM((tokens, 3 * width), bf16),
        pltpu.VMEM((captions, 1), jnp.int32),
        pltpu.VMEM((1, tokens), f32),
        pltpu.SemaphoreType.DMA((5,)),
    ]

    def by_row(x):
        x = lax.all_to_all(x, "row", split_axis=1, concat_axis=0, tiled=True)
        return lax.all_gather(x, "col", axis=0, tiled=True)

    def by_col(x):
        x = lax.all_gather(x, "row", axis=0, tiled=True)
        return lax.all_to_all(x, "col", split_axis=1, concat_axis=0, tiled=True)

    if joined:
        out_step, inner_step = width // col_count, wide // row_count
        rows = width // row_count
        up_grad, out_grad, qkv_grad, grad_down, grad_proj, input_grad, norm_total = plain(
            text_backward_joined_kernel,
            (
                array((rows, wide // col_count), f32),
                array((rows, out_step), f32),
                array((rows, 3 * out_step), f32),
                array((inner_step, out_step), f32),
                array((rows, out_step), f32),
                array((tokens, width), bf16),
                array((1, 4 * width + 128), f32),
            ),
            backward_specs + [in_vmem] * 2,
            backward_buffers
            + scatter_scratch(rows, wide // col_count)
            + scatter_scratch(rows, 4 * out_step)
            + [
                pltpu.VMEM((captions, width), bf16),
                pltpu.VMEM((8, width), f32),
                pltpu.VMEM((col_count, captions, 2 * out_step), bf16),
                pltpu.VMEM((count, captions, 2 * out_step), bf16),
                pltpu.SemaphoreType.DMA((count - 1,)),
                pltpu.SemaphoreType.DMA((count - 1,)),
                pltpu.VMEM((1, 2 * width + 128), f32),
                pltpu.VMEM((count, 1, 2 * width + 128), f32),
                pltpu.SemaphoreType.DMA((count - 1,)),
                pltpu.SemaphoreType.DMA((count - 1,)),
                pltpu.VMEM((1, 2 * width), f32),
                pltpu.VMEM((count, 1, 2 * width), f32),
                pltpu.SemaphoreType.DMA((count - 1,)),
                pltpu.SemaphoreType.DMA((count - 1,)),
            ],
            "text_backward_joined",
            collective_id=3,
            has_side_effects=True,
        )(*backward_in, factors, loss_part)
        norm_total = norm_total[0]
        norms = [norm_total[i * width : (i + 1) * width] for i in range(4)]
        loss_total = norm_total[4 * width]
    else:
        (proj_grad, branch, up_grad, out_grad, qkv_grad, input_grad, norm_grads) = plain(
            text_backward_kernel,
            (
                array((captions, width), bf16),
                array((captions, width), bf16),
                array((col_count, width, wide // col_count), bf16),
                array((col_count, width, width // col_count), bf16),
                array((col_count, width, 3 * width // col_count), bf16),
                array((tokens, width), bf16),
                array((8, width), f32),
            ),
            backward_specs,
            backward_buffers,
            "text_backward",
        )(*backward_in)

        def scattered(matrix):
            blocks = matrix.reshape(count, width // row_count, matrix.shape[2])
            return lax.psum_scatter(blocks, ("col", "row"), scatter_dimension=0, tiled=True)[0].astype(f32)

        up_grad, out_grad, qkv_grad = scattered(up_grad), scattered(out_grad), scattered(qkv_grad)
        grad_down = dot_tn(by_row(inner_sum), by_col(branch))
        grad_proj = dot_tn(by_row(pooled), by_col(proj_grad))
        loss_total, norm_total = lax.psum((loss_part, norm_grads), both)
        norms = [norm_total[i] for i in range(4)]
    mean_loss = loss_total / pair_total
    return (
        mean_loss, hidden, input_grad, *norms, qkv_grad, out_grad, up_grad, grad_down, grad_proj,
    )


def solution(mesh):
    split = P(("row", "col"), None)
    grid = P("row", "col")
    in_specs = (
        split, P(), P(), P("col", None), P("col", None), P("col", None), P("col", None), split, P(("row", "col")),
    ) + (P(),) * 9
    out_specs = (P(), split, split, P(), P(), P(), P(), grid, grid, grid, grid, grid)
    return jax.shard_map(body, mesh=mesh, in_specs=in_specs, out_specs=out_specs, check_vma=False)
```

```python
import functools
import math
from types import SimpleNamespace

import jax
import jax.numpy as jnp
from jax import lax
from jax.experimental import pallas as pl
from jax.experimental.pallas import tpu as pltpu
from jax.sharding import PartitionSpec as P

HEADS = 12
IMG_TOK = 50
norm_eps = 1e-06
logit_scale = 50.0
masked_score = -1e30
log2e = math.log2(math.e)
f32 = jnp.float32
bf16 = jnp.bfloat16
VMEM_LIMIT = 60 * 2**20
MESH = pl.DeviceIdType.MESH


def dot_nn(a, b):
    return lax.dot_general(a, b, (((1,), (0,)), ((), ())), preferred_element_type=f32)


def dot_nt(a, b):
    return lax.dot_general(a, b, (((1,), (1,)), ((), ())), preferred_element_type=f32)


def dot_tn(a, b):
    return lax.dot_general(a, b, (((0,), (0,)), ((), ())), preferred_element_type=f32)


def split_low(x):
    high = x.astype(bf16)
    return high, (x - high.astype(f32)).astype(bf16)


def normed(x):
    centered = x - jnp.mean(x, axis=-1, keepdims=True)
    spread = lax.rsqrt(jnp.mean(centered * centered, axis=-1, keepdims=True) + norm_eps)
    return centered * spread, spread


def layer_norm(x, gain, bias):
    return normed(x)[0] * gain + bias


def gelu(x):
    return x * (0.5 + 0.5 * lax.erf(x * math.sqrt(0.5)))


def gelu_and_slope(x):
    below = 0.5 + 0.5 * lax.erf(x * math.sqrt(0.5))
    bell = jnp.exp2((-0.5 * log2e) * (x * x))
    return x * below, below + x * (bell * (1.0 / math.sqrt(2.0 * math.pi)))


def lane_halves(width):
    lane = lax.broadcasted_iota(jnp.int32, (1, width), 1)
    first = (lane < width // 2).astype(f32)
    return first.astype(bf16), (1.0 - first).astype(bf16)


def stack_heads(x, first, second):
    return jnp.concatenate([x * first, x * second], axis=0)


def join_heads(stacked):
    rows, width = stacked.shape[0] // 2, stacked.shape[1]
    lane = lax.broadcasted_iota(jnp.int32, (rows, width), 1)
    return jnp.where(lane < width // 2, stacked[:rows], stacked[rows:])


def soft_weights(query, key, bias, factor):
    scores = dot_nt(query, key) * (factor * log2e) + bias
    weights = jnp.exp2(scores - jnp.max(scores, axis=-1, keepdims=True))
    return weights, 1.0 / jnp.sum(weights, axis=-1, keepdims=True)


def set_lengths(lengths_ref, lens_ref, key_bias_ref):
    captions, tokens = lens_ref.shape[0], key_bias_ref.shape[1]
    length = tokens // captions
    caption = lax.broadcasted_iota(jnp.int32, (captions, 1), 0)
    token = lax.broadcasted_iota(jnp.int32, (1, tokens), 1)
    column, row = jnp.zeros((captions, 1), jnp.int32), jnp.zeros((1, tokens), jnp.int32)
    for n in range(captions):
        column = jnp.where(caption == n, lengths_ref[n], column)
        row = jnp.where(token // length == n, lengths_ref[n], row)
    lens_ref[...] = column
    key_bias_ref[...] = jnp.where(token % length < row, 0.0, masked_score)


def as_row(ref):
    return ref[...].reshape(1, ref.shape[0])


def text_bias(key_bias_ref, block, rows, length):
    near = lax.broadcasted_iota(jnp.int32, (rows, rows), 0) // length
    far = lax.broadcasted_iota(jnp.int32, (rows, rows), 1) // length
    columns = pl.ds(pl.multiple_of(block * rows, rows), rows)
    bias = jnp.where(near == far, key_bias_ref[:, columns], masked_score)
    return jnp.concatenate([bias, bias], axis=0)


def member(len_ref, captions, tokens):
    length = tokens // captions
    token = lax.broadcasted_iota(jnp.int32, (captions, tokens), 1)
    caption = lax.broadcasted_iota(jnp.int32, (captions, tokens), 0)
    return ((token // length == caption) & (token % length < len_ref[...])).astype(f32)


def spread_rows(x, length):
    rows, width = x.shape
    return jnp.broadcast_to(x[:, None, :], (rows, length, width)).reshape(rows * length, width)


def wide_steps(total, most=768):
    step = math.gcd(total, most)

    def loop(body):
        @pl.loop(0, total // step)
        def _(j):
            body(pl.ds(pl.multiple_of(j * step, 128), step))

    return loop


class TextForward:
    band = 128

    def __init__(self, names, refs):
        for name, ref in zip(names, refs, strict=True):
            setattr(self, name, ref)
        self.tokens, self.width = self.tok.shape
        self.captions = self.lens.shape[0]
        self.length = self.tokens // self.captions
        self.wide = self.w_up.shape[1]
        pairs = (
            (self.qkv_hbm, self.w_qkv), (self.out_hbm, self.w_out), (self.up_hbm, self.w_up),
            (self.down_hbm, self.w_down), (self.proj_hbm, self.w_proj),
        )
        self.loads = load_weights(pairs, self.sems)

    def bands(self, step):
        pl.loop(0, self.tokens // self.band)(
            lambda i: step(pl.ds(pl.multiple_of(i * self.band, self.band), self.band))
        )

    def prepare(self):
        set_lengths(self.lengths, self.lens, self.key_bias)

        def first_norm(rows):
            norm = layer_norm(self.tok[rows, :].astype(f32), as_row(self.gain1), as_row(self.bias1))
            self.norm[rows, :] = norm.astype(bf16)

        self.bands(first_norm)

    def attention(self):
        width = self.width
        self.loads[0].wait()

        @wide_steps(3 * width)
        def _(columns):
            self.heads[:, columns] = dot_nn(self.norm[...], self.w_qkv[:, columns]).astype(bf16)

        first, second = lane_halves(128)
        factor = (width // HEADS) ** -0.5

        @pl.loop(0, self.tokens // self.band)
        def _(block):
            rows = pl.ds(pl.multiple_of(block * self.band, self.band), self.band)
            bias = text_bias(self.key_bias, block, self.band, self.length)
            for at in range(0, width, 128):
                query = stack_heads(self.heads[rows, at : at + 128], first, second)
                key = self.heads[rows, width + at : width + at + 128]
                weights, scale = soft_weights(query, key, bias, factor)
                value = self.heads[rows, 2 * width + at : 2 * width + at + 128]
                mixed = dot_nn(weights.astype(bf16), value) * scale
                self.mixed[rows, at : at + 128] = join_heads(mixed).astype(bf16)

    def middle(self):
        self.loads[1].wait()

        def second_norm(rows):
            mid = self.tok[rows, :].astype(f32) + dot_nn(self.mixed[rows, :], self.w_out[...])
            self.mid[rows, :] = mid
            self.norm[rows, :] = layer_norm(mid, as_row(self.gain2), as_row(self.bias2)).astype(bf16)

        self.bands(second_norm)

    def feed(self):
        self.loads[2].wait()
        self.chosen = member(self.lens, self.captions, self.tokens).astype(bf16)
        place = lax.broadcasted_iota(jnp.int32, (self.captions, self.length, 1), 1)
        valid = (place < self.lens[...].reshape(self.captions, 1, 1)).astype(f32).reshape(self.tokens, 1)

        @wide_steps(self.wide)
        def _(columns):
            value, slope = gelu_and_slope(dot_nn(self.norm[...], self.w_up[:, columns]))
            value = value.astype(bf16)
            self.inner[:, columns] = value
            self.slope[:, columns] = (slope * valid).astype(bf16)
            self.inner_sum[:, columns] = dot_nn(self.chosen, value).astype(bf16)

    def finish(self):
        self.loads[3].wait()
        inverse = 1.0 / self.lens[...].astype(f32)

        @wide_steps(self.width)
        def _(columns):
            state = self.mid[:, columns] + dot_nn(self.inner[...], self.w_down[:, columns])
            self.hidden[:, columns] = state.astype(bf16)
            high, low = split_low(state)
            pooled = (dot_nn(self.chosen, high) + dot_nn(self.chosen, low)) * inverse
            self.pooled[:, columns] = pooled.astype(bf16)

        self.loads[4].wait()
        projected = dot_nn(self.pooled[...], self.w_proj[...])
        self.projected[...] = projected
        scale = lax.rsqrt(jnp.sum(projected * projected, axis=-1, keepdims=True) + norm_eps)
        self.text_embed[...] = (projected * scale).astype(bf16)


text_ins = (
    "tok", "lengths", "gain1", "bias1", "gain2", "bias2", "qkv_hbm", "out_hbm", "up_hbm", "down_hbm", "proj_hbm",
)
text_names = ("hidden", "text_embed", "projected", "pooled", "inner_sum", "heads", "mixed", "mid", "slope")
text_scratch = ("w_qkv", "w_out", "w_up", "w_down", "w_proj", "norm", "inner", "lens", "key_bias", "sems")


def text_forward_kernel(*refs):
    t = TextForward(text_ins + text_names + text_scratch, refs)
    t.prepare()
    t.attention()
    t.middle()
    t.feed()
    t.finish()


def load_weights(pairs, sems):
    loads = [pltpu.make_async_copy(s, d, sems.at[i]) for i, (s, d) in enumerate(pairs)]
    for load in loads:
        load.start()
    return loads


def spans(count, size):
    return lambda i: pl.ds(pl.multiple_of(i * size, size), size)


def norm_backward(outer, unit, spread, gain):
    outer = outer * gain
    inner = outer - jnp.mean(outer, axis=-1, keepdims=True)
    return spread * (inner - unit * jnp.mean(outer * unit, axis=-1, keepdims=True))


class TextBackward:
    band = 128

    def __init__(self, names, refs):
        for name, ref in zip(names, refs, strict=True):
            setattr(self, name, ref)
        self.tokens, self.width = self.tok.shape
        self.captions = self.lens.shape[0]
        self.length = self.tokens // self.captions
        self.wide = self.w_up.shape[1]
        order = ("w_proj", "mid", "w_down", "slope", "w_up", "mixed", "w_out", "tok", "heads", "w_qkv")
        pairs = [(getattr(self, name + "_hbm"), getattr(self, name)) for name in order]
        self.loads = dict(zip(order, load_weights(pairs, self.sems)))
        self.pre_grad = self.slope

    def rows(self, i):
        return pl.ds(pl.multiple_of(i * self.band, self.band), self.band)

    def bands(self, step):
        pl.loop(0, self.tokens // self.band)(lambda i: step(self.rows(i)))

    def valid(self):
        place = lax.broadcasted_iota(jnp.int32, (self.captions, self.length, 1), 1)
        valid = place < self.lens[...].reshape(self.captions, 1, 1)
        return valid.astype(f32).reshape(self.tokens, 1)

    def project(self):
        set_lengths(self.lengths, self.lens, self.key_bias)
        projected = self.projected[...]
        embed_grad = self.embed_grad[...]
        r = lax.rsqrt(jnp.sum(projected * projected, axis=-1, keepdims=True) + norm_eps)
        along = jnp.sum(projected * embed_grad, axis=-1, keepdims=True)
        proj_grad = (r * embed_grad - (r * r * r) * projected * along).astype(bf16)
        self.loads["w_proj"].wait()
        state_grad = dot_nt(proj_grad, self.w_proj[...]) * (1.0 / self.lens[...].astype(f32))
        self.branch[...] = state_grad.astype(bf16)
        self.mid_grad[...] = spread_rows(state_grad, self.length) * self.valid()
        return proj_grad, self.branch[...]

    def inner(self):
        self.loads["w_down"].wait()
        self.loads["slope"].wait()
        branch = self.branch[...]

        @wide_steps(self.wide)
        def _(columns):
            inner_grad = dot_nt(branch, self.w_down[columns, :])
            pre_grad = spread_rows(inner_grad, self.length) * self.slope[:, columns].astype(f32)
            self.pre_grad[:, columns] = pre_grad.astype(bf16)

        self.loads["mid"].wait()

        def second_norm(rows):
            self.norm[rows, :] = layer_norm(
                self.mid[rows, :], as_row(self.gain2), as_row(self.bias2)
            ).astype(bf16)

        self.bands(second_norm)
        self.turned[...] = self.norm[...].T

    def up_block(self, columns):
        return dot_nn(self.turned[...], self.pre_grad[:, columns]).astype(bf16)

    def to_middle(self):
        self.loads["w_up"].wait()

        @wide_steps(self.width)
        def _(columns):
            self.outer[:, columns] = dot_nt(self.pre_grad[...], self.w_up[columns, :])

    def middle(self):
        self.norm_grad[...] = jnp.zeros_like(self.norm_grad)

        def through_norm(rows):
            unit, spread = normed(self.mid[rows, :])
            outer = self.outer[rows, :]
            self.norm_grad[2:3, :] += jnp.sum(outer * unit, axis=0, keepdims=True)
            self.norm_grad[3:4, :] += jnp.sum(outer, axis=0, keepdims=True)
            mid_grad = self.mid_grad[rows, :] + norm_backward(outer, unit, spread, as_row(self.gain2))
            self.mid_grad[rows, :] = mid_grad
            self.low_grad[rows, :] = mid_grad.astype(bf16)

        self.bands(through_norm)

    def out_block(self, columns):
        return dot_tn(self.mixed[...], self.low_grad[:, columns]).astype(bf16)

    def to_heads(self):
        self.loads["w_out"].wait()
        self.loads["tok"].wait()

        def through_out(rows):
            self.mixed_grad[rows, :] = dot_nt(self.low_grad[rows, :], self.w_out[...]).astype(bf16)
            norm = layer_norm(self.tok[rows, :].astype(f32), as_row(self.gain1), as_row(self.bias1))
            self.norm[rows, :] = norm.astype(bf16)

        self.bands(through_out)

    def attention(self, after=lambda block: None):
        first, second = lane_halves(128)
        width = self.width
        factor = (width // HEADS) ** -0.5
        self.loads["heads"].wait()
        self.key_column[...] = (1.0 - self.valid()) * masked_score

        @pl.loop(0, self.tokens // self.band)
        def _(block):
            rows = self.rows(block)
            near = lax.broadcasted_iota(jnp.int32, (self.band, self.band), 0) // self.length
            far = lax.broadcasted_iota(jnp.int32, (self.band, self.band), 1) // self.length
            bias = jnp.where(near == far, self.key_column[rows, :], masked_score)
            bias = jnp.concatenate([bias, bias], axis=1)
            for at in range(0, width, 128):
                query = stack_heads(self.heads[rows, at : at + 128], first, second)
                key = self.heads[rows, width + at : width + at + 128]
                value = self.heads[rows, 2 * width + at : 2 * width + at + 128]
                grad = stack_heads(self.mixed_grad[rows, at : at + 128], first, second)
                scores = dot_nt(key, query) * (factor * log2e) + bias
                weights = jnp.exp2(scores - jnp.max(scores, axis=0, keepdims=True))
                probs = weights * (1.0 / jnp.sum(weights, axis=0, keepdims=True))
                prob_grad = dot_nt(value, grad)
                total = jnp.sum(prob_grad * probs, axis=0, keepdims=True)
                score_grad = (probs * (prob_grad - total)).astype(bf16)
                query_grad = join_heads(dot_tn(score_grad, key)) * factor
                self.heads_grad[rows, at : at + 128] = query_grad.astype(bf16)
                key_grad = dot_nn(score_grad, query) * factor
                self.heads_grad[rows, width + at : width + at + 128] = key_grad.astype(bf16)
                value_grad = dot_nn(probs.astype(bf16), grad)
                self.heads_grad[rows, 2 * width + at : 2 * width + at + 128] = value_grad.astype(bf16)
            after(block)

    def qkv_block(self, columns):
        return dot_tn(self.norm[...], self.heads_grad[:, columns]).astype(bf16)

    def input(self):
        self.loads["w_qkv"].wait()

        @wide_steps(self.width)
        def _(columns):
            self.outer[:, columns] = dot_nt(self.heads_grad[...], self.w_qkv[columns, :])

        def through_norm(rows):
            unit, spread = normed(self.tok[rows, :].astype(f32))
            outer = self.outer[rows, :]
            self.norm_grad[0:1, :] += jnp.sum(outer * unit, axis=0, keepdims=True)
            self.norm_grad[1:2, :] += jnp.sum(outer, axis=0, keepdims=True)
            inner = norm_backward(outer, unit, spread, as_row(self.gain1))
            self.input_grad[rows, :] = (self.mid_grad[rows, :] + inner).astype(bf16)

        self.bands(through_norm)


backward_ins = (
    "lengths", "gain1", "bias1", "gain2", "bias2", "embed_grad", "projected", "tok_hbm", "heads_hbm", "mixed_hbm",
    "mid_hbm", "slope_hbm", "w_qkv_hbm", "w_out_hbm", "w_up_hbm", "w_down_hbm", "w_proj_hbm",
)
backward_scratch = (
    "tok", "heads", "mixed", "mid", "slope", "w_qkv", "w_out", "w_up", "w_down", "w_proj", "norm", "turned",
    "outer", "mid_grad", "low_grad", "mixed_grad", "heads_grad", "lens", "key_bias", "key_column",
    "sems",
)


def text_backward_kernel(*refs):
    outs = ("proj_grad", "branch", "up_grad", "out_grad", "qkv_grad", "input_grad", "norm_grad")
    t = TextBackward(backward_ins + outs + backward_scratch, refs)
    parts = t.up_grad.shape[0]

    def blocks(target, block):
        step = target.shape[2]
        for part in range(parts):
            target[part] = block(slice(part * step, (part + 1) * step))

    t.proj_grad[...] = t.project()[0]
    t.inner()
    blocks(t.up_grad, t.up_block)
    t.to_middle()
    t.middle()
    t.loads["mixed"].wait()
    blocks(t.out_grad, t.out_block)
    t.to_heads()
    t.attention()
    blocks(t.qkv_grad, t.qkv_block)
    t.input()


class Place:
    def __init__(self, z_count=4, y_count=2, x_count=2, k_count=2):
        self.row, self.col = lax.axis_index("row"), lax.axis_index("col")
        self.z, self.y = self.row // y_count, self.row % y_count
        self.x, self.k = self.col // k_count, self.col % k_count
        self.rows, self.cols = z_count * y_count, x_count * k_count
        self.count = self.rows * self.cols
        self.me = self.row * self.cols + self.col
        self.slot = self.col * self.rows + self.row

    def at(self, **moved):
        z, y, x, k = (moved.get(name, getattr(self, name)) for name in "zyxk")
        return z * 2 + y, x * 2 + k

    def peer(self, distance):
        other = (self.me + distance) % self.count
        return other // self.cols, other % self.cols

    def greet(self):
        barrier = pltpu.get_barrier_semaphore()

        @pl.loop(1, self.count)
        def _(distance):
            pl.semaphore_signal(barrier, inc=1, device_id=self.peer(distance), device_id_type=MESH)

    def meet(self):
        pl.semaphore_wait(pltpu.get_barrier_semaphore(), self.count - 1)


def remote(src, dst, send, recv, to):
    return pltpu.make_async_remote_copy(
        src_ref=src, dst_ref=dst, send_sem=send, recv_sem=recv, device_id=to, device_id_type=MESH
    )


class Gather:
    def __init__(self, place, shard, whole, local, sends, recvs):
        depth = shard.shape[0]
        half = depth // 2
        y = place.y
        mate, next_x, next_y = place.at(k=1 - place.k), place.at(x=1 - place.x), place.at(y=1 - y)

        def block(col, part):
            return whole.at[pl.ds(pl.multiple_of(col * depth + part * half, 16), half)]

        own = whole.at[pl.ds(pl.multiple_of(place.col * depth, 16), depth)]
        across = next_x[1]
        shard_half = shard.at[pl.ds(pl.multiple_of(y * half, 16), half)]
        self.local = pltpu.make_async_copy(shard, own, local)
        self.near = remote(shard, own, sends.at[0], recvs.at[0], mate)
        self.far = remote(shard_half, block(place.col, y), sends.at[1], recvs.at[1], next_x)
        self.along = remote(block(across, y), block(across, y), sends.at[2], recvs.at[2], next_y)
        self.first = remote(block(across, y), block(across, y), sends.at[3], recvs.at[3], mate)
        self.second = remote(block(across, 1 - y), block(across, 1 - y), sends.at[4], recvs.at[4], mate)

    def start(self):
        self.far.start()
        self.near.start()
        self.local.start()

    def share(self):
        self.far.wait()
        self.along.start()
        self.first.start()

    def relay(self):
        self.along.wait()
        self.second.start()

    def finish(self):
        self.local.wait()
        self.near.wait()
        self.first.wait()
        self.second.wait()


class RowFactors:
    def __init__(self, place, own, held, local, sends, recvs):
        self.place, self.own, self.held, self.sends, self.recvs = place, own, held, sends, recvs
        self.local = pltpu.make_async_copy(own.at[place.row], held.at[place.col, place.row], local)
        mine, across = held.at[place.col], held.at[place.at(x=1 - place.x)[1]]
        mate, next_x = place.at(k=1 - place.k), place.at(x=1 - place.x)
        n = place.rows - 1
        self.far = remote(mine, mine, sends.at[n], recvs.at[n], next_x)
        self.near = remote(mine, mine, sends.at[n + 1], recvs.at[n + 1], mate)
        self.passed = remote(across, across, sends.at[n + 2], recvs.at[n + 2], mate)

    def copy(self, distance):
        p = self.place
        row = (p.row + distance) % p.rows
        sems = self.sends.at[distance - 1], self.recvs.at[distance - 1]
        return remote(self.own.at[row], self.held.at[p.col, p.row], *sems, (row, p.col))

    def start(self):
        self.local.start()
        pl.loop(1, self.place.rows)(lambda distance: self.copy(distance).start())

    def share(self):
        self.local.wait()
        pl.loop(1, self.place.rows)(lambda distance: self.copy(distance).wait())
        self.far.start()
        self.near.start()

    def relay(self):
        self.far.wait()
        self.passed.start()

    def finish(self):
        self.near.wait()
        self.passed.wait()


class Exchange:
    def __init__(self, place, source, slots, sends, recvs):
        self.place, self.source, self.slots, self.sends, self.recvs = place, source, slots, sends, recvs

    def copy(self, distance):
        to = self.place.peer(distance)
        sems = self.sends.at[distance - 1], self.recvs.at[distance - 1]
        return remote(self.source(to), self.slots.at[self.place.slot], *sems, to)

    def start(self):
        pl.loop(1, self.place.count)(lambda distance: self.copy(distance).start())

    def finish(self):
        pl.loop(1, self.place.count)(lambda distance: self.copy(distance).wait())


class GradientScatter:
    chunks = 3

    def __init__(self, place, held, near, x1, y1, x2, y2, far, sends, recvs):
        self.place, self.held, self.near, self.far = place, held, near, far
        self.x1, self.y1, self.x2, self.y2 = x1, y1, x2, y2
        self.sends, self.recvs = sends, recvs
        self.step = held.shape[5] // self.chunks

    def lanes(self, chunk):
        step, half = self.step, self.step // 2
        at = chunk * step
        return pl.ds(at, step), pl.ds(at, half), pl.ds(at + half, half), pl.ds(chunk * half, half)

    def copies(self, chunk, stage):
        p, held = self.place, self.held
        x, y, z, k = p.x, p.y, p.z, p.k
        whole, one, two, part = self.lanes(chunk)

        def copy(n, src, dst, **moved):
            return remote(src, dst, self.sends.at[chunk, n], self.recvs.at[chunk, n], p.at(**moved))

        if stage == 0:
            return [copy(0, held.at[:, 1 - k, :, :, :, whole], self.near.at[:, :, :, :, whole], k=1 - k)]
        if stage == 1:
            return [
                copy(1, held.at[1 - x, k, :, :, :, one], self.x1.at[:, :, :, part], x=1 - x),
                copy(2, held.at[:, k, :, 1 - y, :, two], self.y1.at[:, :, :, part], y=1 - y),
            ]
        if stage == 2:
            return [
                copy(3, held.at[x, k, :, 1 - y, :, one], self.y2.at[:, :, part], y=1 - y),
                copy(4, held.at[1 - x, k, :, y, :, two], self.x2.at[:, :, part], x=1 - x),
            ]
        copies = []
        for distance in range(1, held.shape[2]):
            other = (z + distance) % held.shape[2]
            copies.append(
                copy(4 + distance, held.at[x, k, other, y, :, whole], self.far.at[distance - 1, :, whole], z=other)
            )
        return copies

    def start(self, chunk, stage):
        for copy in self.copies(chunk, stage):
            copy.start()

    def finish(self, chunk, stage):
        for copy in self.copies(chunk, stage):
            copy.wait()
        p, held = self.place, self.held
        x, y, k = p.x, p.y, p.k
        z_count = held.shape[2]
        whole, one, two, part = self.lanes(chunk)

        def add(target, source):
            target[...] = (target[...].astype(f32) + source[...].astype(f32)).astype(bf16)

        if stage == 0:

            @pl.loop(0, z_count)
            def _(z):
                for i in range(2):
                    for j in range(2):
                        add(held.at[i, k, z, j, :, whole], self.near.at[i, z, j, :, whole])

        if stage == 1:

            @pl.loop(0, z_count)
            def _(z):
                for i in range(2):
                    add(held.at[x, k, z, i, :, one], self.x1.at[z, i, :, part])
                    add(held.at[i, k, z, y, :, two], self.y1.at[i, z, :, part])

        if stage == 2:

            @pl.loop(0, z_count)
            def _(z):
                add(held.at[x, k, z, y, :, one], self.y2.at[z, :, part])
                add(held.at[x, k, z, y, :, two], self.x2.at[z, :, part])

    def step_on(self, chunk, stage):
        self.finish(chunk, stage - 1)
        self.start(chunk, stage)

    def total(self):
        p = self.place
        total = self.held[p.x, p.k, p.z, p.y].astype(f32)
        for i in range(self.far.shape[0]):
            total = total + self.far[i].astype(f32)
        return total


def scatter_scratch(rows, columns):
    shapes = [
        (2, 2, 4, 2, rows, columns), (2, 4, 2, rows, columns), (4, 2, rows, columns // 2), (2, 4, rows, columns // 2),
        (4, rows, columns // 2), (4, rows, columns // 2), (3, rows, columns),
    ]
    return [pltpu.VMEM(shape, bf16) for shape in shapes] + [pltpu.SemaphoreType.DMA((GradientScatter.chunks, 8))] * 2


scatter_names = ("held", "near", "x1", "y1", "x2", "y2", "far", "sends", "recvs")
exchange_names = ("own", "all", "sends", "recvs")


def text_backward_joined_kernel(*refs):
    ins = backward_ins + ("factors", "loss")
    outs = ("up_out", "out_out", "qkv_out", "down_out", "proj_out", "input_grad", "norm_out")
    sets = tuple(name + tag for tag in ("_a", "_b") for name in scatter_names)
    swaps = tuple(name + tag for tag in ("_factors", "_late", "_last") for name in exchange_names)
    names = ins + outs + backward_scratch + sets + ("branch", "norm_grad") + swaps
    t = TextBackward(names, refs)
    place = Place()
    place.greet()
    width = t.width
    a, b = (GradientScatter(place, *(getattr(t, name + tag) for name in scatter_names)) for tag in ("_a", "_b"))
    factors = Exchange(
        place, lambda to: t.own_factors.at[to[1]], t.all_factors, t.sends_factors, t.recvs_factors
    )
    late = Exchange(place, lambda to: t.own_late, t.all_late, t.sends_late, t.recvs_late)
    last = Exchange(place, lambda to: t.own_last, t.all_last, t.sends_last, t.recvs_last)
    cols = place.cols
    up_step, qkv_step, out_step = t.wide // cols, 3 * width // cols, width // cols

    def blocked(value):
        return value.reshape(4, 2, value.shape[0] // 8, value.shape[1])

    proj_grad, branch = t.project()
    for part in range(cols):
        columns = slice(part * out_step, (part + 1) * out_step)
        t.own_factors[part] = jnp.concatenate([branch[:, columns], proj_grad[:, columns]], axis=1)
    t.all_factors[place.slot] = t.own_factors[place.col]
    place.meet()
    factors.start()
    t.inner()
    for chunk in range(a.chunks):
        for part in range(cols):
            at = part * up_step + chunk * a.step
            t.held_a[part // 2, part % 2, :, :, :, chunk * a.step : (chunk + 1) * a.step] = blocked(
                t.up_block(slice(at, at + a.step))
            )
        a.start(chunk, 0)
        if chunk > 0:
            a.step_on(chunk - 1, 1)
    t.to_middle()
    a.step_on(2, 1)
    t.middle()
    t.own_late[...] = jnp.concatenate([t.norm_grad[2:3, :], t.norm_grad[3:4, :], t.loss[...]], axis=1)
    t.all_late[place.slot] = t.own_late[...]
    late.start()
    a.step_on(0, 2)
    t.loads["mixed"].wait()
    for part in range(cols):
        t.held_b[part // 2, part % 2, :, :, :, qkv_step:] = blocked(
            t.out_block(slice(part * out_step, (part + 1) * out_step))
        )
    t.to_heads()

    def after(block):
        @pl.when(block == 0)
        def _():
            a.step_on(1, 2)
            a.step_on(0, 3)

        @pl.when(block == 1)
        def _():
            a.step_on(2, 2)

        @pl.when(block == 2)
        def _():
            a.step_on(1, 3)

    t.attention(after)
    for part in range(cols):
        t.held_b[part // 2, part % 2, :, :, :, :qkv_step] = blocked(
            t.qkv_block(slice(part * qkv_step, (part + 1) * qkv_step))
        )
    for chunk in range(b.chunks):
        b.start(chunk, 0)
    a.step_on(2, 3)
    for chunk in range(b.chunks):
        b.step_on(chunk, 1)
    t.input()
    t.own_last[...] = jnp.concatenate([t.norm_grad[0:1, :], t.norm_grad[1:2, :]], axis=1)
    t.all_last[place.slot] = t.own_last[...]
    last.start()
    b.step_on(0, 2)
    for chunk in range(a.chunks):
        a.finish(chunk, 3)
    t.up_out[...] = a.total()
    factors.finish()
    b.step_on(1, 2)
    b.step_on(0, 3)
    grown = dot_tn(
        t.factors[...].reshape(-1, t.factors.shape[3]), t.all_factors[...].reshape(-1, t.all_factors.shape[2])
    )
    inner_step = t.wide // place.rows
    t.down_out[...] = grown[:inner_step, :out_step]
    t.proj_out[...] = grown[inner_step : inner_step + width // place.rows, out_step:]
    b.step_on(2, 2)
    b.step_on(1, 3)
    late.finish()
    last.finish()
    t.norm_out[:, : 2 * width] = jnp.sum(t.all_last[...], axis=0)
    t.norm_out[:, 2 * width :] = jnp.sum(t.all_late[...], axis=0)
    b.step_on(2, 3)
    for chunk in range(b.chunks):
        b.finish(chunk, 3)
    total = b.total()
    t.qkv_out[...] = total[:, :qkv_step]
    t.out_out[...] = total[:, qkv_step:]


def group_mean(images, rows):
    token = lax.broadcasted_iota(jnp.int32, (images, rows), 1)
    image = lax.broadcasted_iota(jnp.int32, (images, rows), 0)
    inside = (token >= image * IMG_TOK) & (token < (image + 1) * IMG_TOK)
    return inside.astype(f32).astype(bf16)


def load_parts(parts, target, sems, col, col_count):
    depth = target.shape[0] // col_count
    copies = []
    for k, part in enumerate(parts):
        place = pl.multiple_of((col ^ k) * depth, depth)
        copies.append(pltpu.make_async_copy(part, target.at[pl.ds(place, depth)], sems.at[k]))
    return copies


def image_mix(tokens, gain_ref, bias_ref, w_qkv, w_out, norm_ref, heads_ref, mixed_ref):
    rows, width = tokens.shape
    images = rows // IMG_TOK
    norm_ref[...] = layer_norm(tokens.astype(f32), gain_ref[0:1, :], bias_ref[0:1, :]).astype(bf16)

    @wide_steps(3 * width)
    def _(columns):
        heads_ref[:, columns] = dot_nn(norm_ref[...], w_qkv[:, columns]).astype(bf16)

    first, second = lane_halves(128)
    factor = (width // HEADS) ** -0.5
    window = 112

    @pl.loop(0, images // 2)
    def _(pair):
        start = pair * (2 * IMG_TOK)
        low = pl.multiple_of(start // 16 * 16, 16)
        near = lax.broadcasted_iota(jnp.int32, (window, window), 0) + low
        far = lax.broadcasted_iota(jnp.int32, (window, window), 1) + low
        same = (near >= start) & (near < start + 2 * IMG_TOK) & (far >= start) & (far < start + 2 * IMG_TOK)
        same = same & ((near >= start + IMG_TOK) == (far >= start + IMG_TOK))
        bias = jnp.where(same, 0.0, masked_score)
        bias = jnp.concatenate([bias, bias], axis=0)
        keep = lax.broadcasted_iota(jnp.int32, (16, 128), 0) + low < start
        span, head, tail = pl.ds(low, window), pl.ds(low, 16), pl.ds(low + 16, window - 16)
        for at in range(0, width, 128):
            query = stack_heads(heads_ref[span, at : at + 128], first, second)
            key = heads_ref[span, width + at : width + at + 128]
            weights, scale = soft_weights(query, key, bias, factor)
            value = heads_ref[span, 2 * width + at : 2 * width + at + 128]
            mixed = join_heads(dot_nn(weights.astype(bf16), value) * scale)
            former = mixed_ref[head, at : at + 128].astype(f32)
            mixed_ref[head, at : at + 128] = jnp.where(keep, former, mixed[:16]).astype(bf16)
            mixed_ref[tail, at : at + 128] = mixed[16:].astype(bf16)

    mid = tokens.astype(f32) + dot_nn(mixed_ref[...], w_out[...])
    high, low = split_low(mid)
    select = group_mean(images, rows)
    mean = (dot_nn(select, high) + dot_nn(select, low)) * (1.0 / IMG_TOK)
    return layer_norm(mid, gain_ref[1:2, :], bias_ref[1:2, :]).astype(bf16), mean


def image_mix_kernel(col_count, tok_ref, gain_ref, bias_ref, *refs):
    qkv_parts, out_parts = refs[:col_count], refs[col_count : 2 * col_count]
    normed_ref, mean_ref, w_qkv, w_out, *buffers, sems = refs[2 * col_count :]
    col = lax.axis_index("col")

    @pl.when(pl.program_id(0) == 0)
    def _():
        copies = load_parts(qkv_parts, w_qkv, sems.at[0], col, col_count)
        copies += load_parts(out_parts, w_out, sems.at[1], col, col_count)
        for copy in copies:
            copy.start()
        for copy in copies:
            copy.wait()

    normed_ref[...], mean_ref[...] = image_mix(tok_ref[...], gain_ref, bias_ref, w_qkv, w_out, *buffers)


def image_embed_kernel(col_count, normed_ref, mean_ref, *refs):
    up_parts, down_parts = refs[:col_count], refs[col_count : 2 * col_count]
    embed_ref, w_up, w_down, sum_ref, sems = refs[2 * col_count :]
    rows, width = normed_ref.shape
    images = rows // IMG_TOK
    wide = w_up.shape[1]
    step = pl.program_id(0)
    col = lax.axis_index("col")
    downs = load_parts(down_parts, w_down, sems.at[1], col, col_count)

    @pl.when(step == 0)
    def _():
        ups = load_parts(up_parts, w_up, sems.at[0], col, col_count)
        for copy in ups + downs:
            copy.start()
        for copy in ups:
            copy.wait()

    select = group_mean(images, rows)

    @wide_steps(wide)
    def _(columns):
        inner = gelu(dot_nn(normed_ref[...], w_up[:, columns])).astype(bf16)
        sum_ref[pl.ds(pl.multiple_of(step * images, images), images), columns] = dot_nn(select, inner)

    @pl.when(step == pl.num_programs(0) - 1)
    def _():
        for copy in downs:
            copy.wait()
        high, low = split_low(sum_ref[...] * (1.0 / IMG_TOK))
        pooled = mean_ref[...] + dot_nn(high, w_down[...]) + dot_nn(low, w_down[...])
        embed_ref[...] = (
            pooled * lax.rsqrt(jnp.sum(pooled * pooled, axis=-1, keepdims=True) + norm_eps)
        ).astype(bf16)


image_ins = (
    "image_hbm", "image_gain", "image_bias", "image_qkv_hbm", "image_out_hbm", "image_up_hbm", "image_down_hbm",
)
saved_names = ("hidden", "projected", "heads", "mixed", "mid", "slope", "held_factors")
image_scratch = (
    "image_tok", "iw_qkv", "iw_out", "iw_up", "iw_down", "image_norm", "image_heads", "image_mixed", "image_normed",
    "image_mean", "sums", "own", "images", "own_factors", "held_factors", "own_sums", "all_sums", "save_sems",
    "tok_sem", "local", "sends", "recvs", "factor_local", "factor_sends", "factor_recvs", "image_sends",
    "image_recvs", "pass_sends", "pass_recvs", "sum_sends", "sum_recvs",
)


def forward_joined_kernel(*refs):
    saves = tuple(name + "_out" for name in saved_names)
    names = text_ins + image_ins + saves + ("embed_grad", "loss") + text_names + text_scratch + image_scratch
    t = TextForward(names, refs)
    place = Place()
    place.greet()
    load_images = pltpu.make_async_copy(t.image_hbm, t.image_tok, t.tok_sem.at[0])
    load_images.start()
    save = {
        name: pltpu.make_async_copy(getattr(t, name), getattr(t, name + "_out"), t.save_sems.at[i])
        for i, name in enumerate(saved_names)
    }
    shards = (
        (t.image_qkv_hbm, t.iw_qkv), (t.image_out_hbm, t.iw_out), (t.image_up_hbm, t.iw_up),
        (t.image_down_hbm, t.iw_down),
    )
    qkv, out, up, down = (
        Gather(place, *pair, t.local.at[i], t.sends.at[i], t.recvs.at[i]) for i, pair in enumerate(shards)
    )
    factors = RowFactors(
        place, t.own_factors, t.held_factors, t.factor_local.at[0], t.factor_sends, t.factor_recvs
    )
    t.prepare()
    place.meet()
    qkv.start()
    out.start()
    t.attention()
    save["heads"].start()
    save["mixed"].start()
    qkv.share()
    out.share()
    up.start()
    t.middle()
    save["mid"].start()
    t.feed()
    save["slope"].start()
    t.finish()
    save["hidden"].start()
    save["projected"].start()
    inner_step, width_step = t.wide // place.rows, t.width // place.rows
    pooled = t.pooled[...]
    for row in range(place.rows):
        block = pooled[:, row * width_step : (row + 1) * width_step]
        spare = t.own_factors.shape[2] - inner_step - width_step
        t.own_factors[row, :, :inner_step] = t.inner_sum[:, row * inner_step : (row + 1) * inner_step]
        t.own_factors[row, :, inner_step:] = jnp.concatenate([block, jnp.zeros((t.captions, spare), bf16)], axis=1)
    factors.start()
    qkv.relay()
    out.relay()
    qkv.finish()
    out.finish()
    load_images.wait()

    rows, width = t.image_tok.shape
    group_rows = t.image_norm.shape[0]
    groups = rows // group_rows
    group_images = group_rows // IMG_TOK

    @pl.loop(0, groups)
    def _(group):
        span = pl.ds(pl.multiple_of(group * group_rows, 16), group_rows)
        normed2, mean = image_mix(
            t.image_tok[span, :], t.image_gain, t.image_bias, t.iw_qkv, t.iw_out,
            t.image_norm, t.image_heads, t.image_mixed,
        )
        t.image_normed[span, :] = normed2
        t.image_mean[pl.ds(pl.multiple_of(group * group_images, 8), group_images), :] = mean

        @pl.when(group == 0)
        def _():
            up.share()
            down.start()

        @pl.when(group == 2)
        def _():
            up.relay()
            down.share()

    factors.share()
    up.finish()

    halves, _, chips, half_images, _ = t.images.shape
    half_rows = half_images * IMG_TOK
    chip = place.row * 2 + place.x

    def image_copy(half, distance):
        other = (chip + distance) % chips
        mine = t.images.at[half, place.k, chip]
        sems = t.image_sends.at[half, distance - 1], t.image_recvs.at[half, distance - 1]
        return remote(mine, mine, *sems, (other // 2, other % 2 * 2 + place.k))

    def pass_copy(half):
        held = t.images.at[half, place.k]
        return remote(held, held, t.pass_sends.at[half], t.pass_recvs.at[half], place.at(k=1 - place.k))

    select = group_mean(half_images, half_rows)
    for half in range(halves):

        @wide_steps(t.wide)
        def _(columns):
            total = 0.0
            for group in range(half_rows // group_rows):
                local = slice(group * group_rows, (group + 1) * group_rows)
                at = half * half_rows + group * group_rows
                inner = gelu(dot_nn(t.image_normed[at : at + group_rows, :], t.iw_up[:, columns])).astype(bf16)
                total = total + dot_nn(select[:, local], inner)
            t.sums[:, columns] = total

        if half == 0:
            down.relay()
            factors.relay()
            down.finish()
        else:
            pl.loop(1, chips)(lambda distance: image_copy(half - 1, distance).wait())
            pass_copy(half - 1).start()
        high, low = split_low(t.sums[...] * (1.0 / IMG_TOK))
        pooled = dot_nn(jnp.concatenate([high, low], axis=0), t.iw_down[...])
        part = slice(half * half_images, (half + 1) * half_images)
        pooled = t.image_mean[part, :] + pooled[:half_images] + pooled[half_images:]
        embed = pooled * lax.rsqrt(jnp.sum(pooled * pooled, axis=-1, keepdims=True) + norm_eps)
        t.own[part, :] = embed.astype(bf16)
        t.images[half, place.k, chip] = embed.astype(bf16)
        pl.loop(1, chips)(lambda distance: image_copy(half, distance).start())

    factors.finish()
    save["held_factors"].start()
    pl.loop(1, chips)(lambda distance: image_copy(halves - 1, distance).wait())
    pass_copy(halves - 1).start()
    for half in range(halves):
        pass_copy(half).wait()

    images = t.images[...].reshape(-1, width)
    own = t.own[...].astype(f32)
    lifted = jnp.exp2(dot_nt(t.text_embed[...], images) * (logit_scale * log2e))
    t.own_sums[...] = jnp.sum(lifted, axis=0, keepdims=True)
    t.all_sums[place.slot] = t.own_sums[...]
    sums = Exchange(place, lambda to: t.own_sums, t.all_sums, t.sum_sends, t.sum_recvs)
    sums.start()
    col_sums = jnp.sum(lifted, axis=1, keepdims=True)
    positives = logit_scale * jnp.sum(own * t.text_embed[...].astype(f32), axis=(0, 1), keepdims=True)
    sums.finish()
    row_sums = jnp.sum(t.all_sums[...], axis=0)
    sim_grad = (0.5 * (lifted * (1.0 / row_sums) + lifted * (1.0 / col_sums))).astype(bf16)
    t.embed_grad[...] = logit_scale * (dot_nn(sim_grad, images) - own)
    logs = jnp.sum(jnp.log(col_sums), axis=(0, 1), keepdims=True)
    logs = logs + jnp.sum(jnp.log(row_sums), axis=(0, 1), keepdims=True) * (1.0 / place.count)
    t.loss[...] = jnp.broadcast_to(0.5 * logs - positives, t.loss.shape)
    for copy in save.values():
        copy.wait()


def whole(shape):
    return pl.BlockSpec(shape, lambda *_: (0,) * len(shape))


in_vmem = pl.BlockSpec(memory_space=pltpu.VMEM)
in_smem = pl.BlockSpec(memory_space=pltpu.SMEM)
anywhere = pl.BlockSpec(memory_space=pl.ANY)


def plain(kernel, outs, ins, scratch, name, out_specs=None, **settings):
    return pl.pallas_call(
        kernel,
        out_shape=outs,
        in_specs=ins,
        out_specs=out_specs or [in_vmem] * len(outs),
        scratch_shapes=scratch,
        compiler_params=pltpu.CompilerParams(vmem_limit_bytes=VMEM_LIMIT, **settings),
        name=name,
    )


def array(shape, dtype):
    return jax.ShapeDtypeStruct(shape, dtype)


def partners(x, col_count):
    order = [(i, i ^ 2) for i in range(col_count)]
    near = [(i, i ^ 1) for i in range(col_count)]
    far = lax.ppermute(x, "col", order)
    return [x, lax.ppermute(x, "col", near), far, lax.ppermute(far, "col", near)]


def body(
    image_tokens, image_norm_gain, image_norm_bias, image_qkv, image_out, image_up, image_down,
    text_tokens, text_lengths, norm1_gain, norm1_bias, norm2_gain, norm2_bias,
    text_qkv, text_out, text_up, text_down, text_proj,
):
    tokens, width = text_tokens.shape
    captions = text_lengths.shape[0]
    length = tokens // captions
    wide = text_up.shape[1]
    row_count, col_count = lax.axis_size("row"), lax.axis_size("col")
    row, col = lax.axis_index("row"), lax.axis_index("col")
    pair_total = captions * row_count * col_count
    image_rows, images = image_tokens.shape[0], image_tokens.shape[0] // IMG_TOK

    count = row_count * col_count
    joined = (row_count, col_count) == (8, 4)
    vectors = (norm1_gain, norm1_bias, norm2_gain, norm2_bias)
    weights = (text_qkv, text_out, text_up, text_down, text_proj)
    weight_scratch = [pltpu.VMEM(w.shape, bf16) for w in weights]

    text_shapes = (
        array((tokens, width), bf16),
        array((captions, width), bf16),
        array((captions, width), f32),
        array((captions, width), bf16),
        array((captions, wide), bf16),
        array((tokens, 3 * width), bf16),
        array((tokens, width), bf16),
        array((tokens, width), f32),
        array((tokens, wide), bf16),
    )
    text_specs = [in_vmem, in_smem] + [in_vmem] * 4 + [anywhere] * 5
    text_buffers = weight_scratch + [
        pltpu.VMEM((tokens, width), bf16),
        pltpu.VMEM((tokens, wide), bf16),
        pltpu.VMEM((captions, 1), jnp.int32),
        pltpu.VMEM((1, tokens), f32),
        pltpu.SemaphoreType.DMA((5,)),
    ]
    text_in = (text_tokens, text_lengths, *vectors, *weights)
    groups = 4
    group_rows, group_images = image_rows // groups, images // groups
    mix_buffers = [
        pltpu.VMEM((group_rows, width), bf16),
        pltpu.VMEM((group_rows, 3 * width), bf16),
        pltpu.VMEM((group_rows, width), bf16),
    ]
    mix_weights = [pltpu.VMEM((width, 3 * width), bf16), pltpu.VMEM((width, width), bf16)]
    embed_weights = [pltpu.VMEM((width, wide), bf16), pltpu.VMEM((wide, width), bf16)]
    both = ("row", "col")

    if joined:
        chips, halves = count // 2, 2
        packed = -(-(wide // row_count + width // row_count) // 128) * 128
        shapes = dict(zip(text_names, text_shapes))
        shapes["held_factors"] = array((col_count, row_count, captions, packed), bf16)
        dma = pltpu.SemaphoreType.DMA
        hidden, projected, heads, mixed, mid, slope, factors, embed_grad, loss_part = plain(
            forward_joined_kernel,
            tuple(shapes[name] for name in saved_names) + (array((captions, width), f32), array((1, 128), f32)),
            text_specs + [anywhere, in_vmem, in_vmem] + [anywhere] * 4,
            [pltpu.VMEM(shape.shape, shape.dtype) for shape in text_shapes]
            + text_buffers
            + [pltpu.VMEM((image_rows, width), bf16)]
            + mix_weights
            + embed_weights
            + mix_buffers
            + [
                pltpu.VMEM((image_rows, width), bf16),
                pltpu.VMEM((images, width), f32),
                pltpu.VMEM((images // halves, wide), f32),
                pltpu.VMEM((images, width), bf16),
                pltpu.VMEM((halves, 2, chips, images // halves, width), bf16),
                pltpu.VMEM((row_count, captions, packed), bf16),
                pltpu.VMEM((col_count, row_count, captions, packed), bf16),
                pltpu.VMEM((1, pair_total), f32),
                pltpu.VMEM((count, 1, pair_total), f32),
                dma((len(saved_names),)),
                dma((1,)),
                dma((4,)),
                dma((4, 5)),
                dma((4, 5)),
                dma((1,)),
                dma((row_count + 2,)),
                dma((row_count + 2,)),
                dma((halves, chips - 1)),
                dma((halves, chips - 1)),
                dma((halves,)),
                dma((halves,)),
                dma((count - 1,)),
                dma((count - 1,)),
            ],
            "forward_joined",
            out_specs=[anywhere] * len(saved_names) + [in_vmem] * 2,
            collective_id=1,
            has_side_effects=True,
        )(*text_in, image_tokens, image_norm_gain, image_norm_bias, image_qkv, image_out, image_up, image_down)
    else:
        (hidden, text_embed, projected, pooled, inner_sum, heads, mixed, mid, slope) = plain(
            text_forward_kernel, text_shapes, text_specs, text_buffers, "text_forward"
        )(*text_in)
        qkv_parts = partners(image_qkv, col_count)
        out_parts = partners(image_out, col_count)
        up_parts = partners(image_up, col_count)
        down_parts = partners(image_down, col_count)
        parts = [anywhere] * (2 * col_count)
        image_normed, image_mean = pl.pallas_call(
            functools.partial(image_mix_kernel, col_count),
            grid=(groups,),
            out_shape=(array((image_rows, width), bf16), array((images, width), f32)),
            in_specs=[
                pl.BlockSpec((group_rows, width), lambda i: (i, 0)),
                whole(image_norm_gain.shape),
                whole(image_norm_bias.shape),
            ]
            + parts,
            out_specs=(
                pl.BlockSpec((group_rows, width), lambda i: (i, 0)),
                pl.BlockSpec((group_images, width), lambda i: (i, 0)),
            ),
            scratch_shapes=mix_weights + mix_buffers + [pltpu.SemaphoreType.DMA((2, col_count))],
            compiler_params=pltpu.CompilerParams(vmem_limit_bytes=VMEM_LIMIT),
            name="image_mix",
        )(image_tokens, image_norm_gain, image_norm_bias, *qkv_parts, *out_parts)
        image_embed = pl.pallas_call(
            functools.partial(image_embed_kernel, col_count),
            grid=(groups,),
            out_shape=array((images, width), bf16),
            in_specs=[pl.BlockSpec((group_rows, width), lambda i: (i, 0)), whole((images, width))] + parts,
            out_specs=whole((images, width)),
            scratch_shapes=embed_weights
            + [pltpu.VMEM((images, wide), f32), pltpu.SemaphoreType.DMA((2, col_count))],
            compiler_params=pltpu.CompilerParams(vmem_limit_bytes=VMEM_LIMIT),
            name="image_embed",
        )(image_normed, image_mean, *up_parts, *down_parts)

        image_all = lax.all_gather(image_embed, both, axis=0, tiled=True)
        lifted = jnp.exp(logit_scale * dot_nt(image_all, text_embed))
        row_sums = lax.psum(jnp.sum(lifted, axis=1), both)
        col_sums = jnp.sum(lifted, axis=0)
        sim_grad = (0.5 * (lifted / row_sums[:, None] + lifted / col_sums[None, :])).astype(bf16)
        image_own = image_embed.astype(f32)
        embed_grad = logit_scale * (dot_tn(sim_grad, image_all) - image_own)
        positives = logit_scale * jnp.sum(image_own * text_embed.astype(f32), axis=1)
        loss_part = 0.5 * jnp.sum(jnp.log(col_sums) - 2.0 * positives)
        loss_part = loss_part + 0.5 * jnp.sum(jnp.log(row_sums)) / count

    backward_in = (text_lengths, *vectors, embed_grad, projected, text_tokens, heads, mixed, mid, slope, *weights)
    backward_specs = [in_smem] + [in_vmem] * 6 + [anywhere] * 10
    backward_buffers = (
        [
            pltpu.VMEM((tokens, width), bf16),
            pltpu.VMEM((tokens, 3 * width), bf16),
            pltpu.VMEM((tokens, width), bf16),
            pltpu.VMEM((tokens, width), f32),
            pltpu.VMEM((tokens, wide), bf16),
        ]
        + weight_scratch
        + [
            pltpu.VMEM((tokens, width), bf16),
            pltpu.VMEM((width, tokens), bf16),
            pltpu.VMEM((tokens, width), f32),
            pltpu.VMEM((tokens, width), f32),
            pltpu.VMEM((tokens, width), bf16),
            pltpu.VMEM((tokens, width), bf16),
            pltpu.VMEM((tokens, 3 * width), bf16),
            pltpu.VMEM((captions, 1), jnp.int32),
            pltpu.VMEM((1, tokens), f32),
            pltpu.VMEM((tokens, 1), f32),
            pltpu.SemaphoreType.DMA((10,)),
        ]
    )

    def by_row(x):
        x = lax.all_to_all(x, "row", split_axis=1, concat_axis=0, tiled=True)
        return lax.all_gather(x, "col", axis=0, tiled=True)

    def by_col(x):
        x = lax.all_gather(x, "row", axis=0, tiled=True)
        return lax.all_to_all(x, "col", split_axis=1, concat_axis=0, tiled=True)

    if joined:
        out_step, inner_step = width // col_count, wide // row_count
        rows = width // row_count
        up_grad, out_grad, qkv_grad, grad_down, grad_proj, input_grad, norm_total = plain(
            text_backward_joined_kernel,
            (
                array((rows, wide // col_count), f32),
                array((rows, out_step), f32),
                array((rows, 3 * out_step), f32),
                array((inner_step, out_step), f32),
                array((rows, out_step), f32),
                array((tokens, width), bf16),
                array((1, 4 * width + 128), f32),
            ),
            backward_specs + [in_vmem] * 2,
            backward_buffers
            + scatter_scratch(rows, wide // col_count)
            + scatter_scratch(rows, 4 * out_step)
            + [
                pltpu.VMEM((captions, width), bf16),
                pltpu.VMEM((8, width), f32),
                pltpu.VMEM((col_count, captions, 2 * out_step), bf16),
                pltpu.VMEM((count, captions, 2 * out_step), bf16),
                pltpu.SemaphoreType.DMA((count - 1,)),
                pltpu.SemaphoreType.DMA((count - 1,)),
                pltpu.VMEM((1, 2 * width + 128), f32),
                pltpu.VMEM((count, 1, 2 * width + 128), f32),
                pltpu.SemaphoreType.DMA((count - 1,)),
                pltpu.SemaphoreType.DMA((count - 1,)),
                pltpu.VMEM((1, 2 * width), f32),
                pltpu.VMEM((count, 1, 2 * width), f32),
                pltpu.SemaphoreType.DMA((count - 1,)),
                pltpu.SemaphoreType.DMA((count - 1,)),
            ],
            "text_backward_joined",
            collective_id=3,
            has_side_effects=True,
        )(*backward_in, factors, loss_part)
        norm_total = norm_total[0]
        norms = [norm_total[i * width : (i + 1) * width] for i in range(4)]
        loss_total = norm_total[4 * width]
    else:
        (proj_grad, branch, up_grad, out_grad, qkv_grad, input_grad, norm_grads) = plain(
            text_backward_kernel,
            (
                array((captions, width), bf16),
                array((captions, width), bf16),
                array((col_count, width, wide // col_count), bf16),
                array((col_count, width, width // col_count), bf16),
                array((col_count, width, 3 * width // col_count), bf16),
                array((tokens, width), bf16),
                array((8, width), f32),
            ),
            backward_specs,
            backward_buffers,
            "text_backward",
        )(*backward_in)

        def scattered(matrix):
            blocks = matrix.reshape(count, width // row_count, matrix.shape[2])
            return lax.psum_scatter(blocks, ("col", "row"), scatter_dimension=0, tiled=True)[0].astype(f32)

        up_grad, out_grad, qkv_grad = scattered(up_grad), scattered(out_grad), scattered(qkv_grad)
        grad_down = dot_tn(by_row(inner_sum), by_col(branch))
        grad_proj = dot_tn(by_row(pooled), by_col(proj_grad))
        loss_total, norm_total = lax.psum((loss_part, norm_grads), both)
        norms = [norm_total[i] for i in range(4)]
    mean_loss = loss_total / pair_total
    return (
        mean_loss, hidden, input_grad, *norms, qkv_grad, out_grad, up_grad, grad_down, grad_proj,
    )


def solution(mesh):
    split = P(("row", "col"), None)
    grid = P("row", "col")
    in_specs = (
        split, P(), P(), P("col", None), P("col", None), P("col", None), P("col", None), split, P(("row", "col")),
    ) + (P(),) * 9
    out_specs = (P(), split, split, P(), P(), P(), P(), grid, grid, grid, grid, grid)
    return jax.shard_map(body, mesh=mesh, in_specs=in_specs, out_specs=out_specs, check_vma=False)
```

```python
import functools
import math
from types import SimpleNamespace

import jax
import jax.numpy as jnp
from jax import lax
from jax.experimental import pallas as pl
from jax.experimental.pallas import tpu as pltpu
from jax.sharding import PartitionSpec as P

HEADS = 12
IMG_TOK = 50
norm_eps = 1e-06
logit_scale = 50.0
masked_score = -1e30
log2e = math.log2(math.e)
f32 = jnp.float32
bf16 = jnp.bfloat16
VMEM_LIMIT = 60 * 2**20
MESH = pl.DeviceIdType.MESH


def dot_nn(a, b):
    return lax.dot_general(a, b, (((1,), (0,)), ((), ())), preferred_element_type=f32)


def dot_nt(a, b):
    return lax.dot_general(a, b, (((1,), (1,)), ((), ())), preferred_element_type=f32)


def dot_tn(a, b):
    return lax.dot_general(a, b, (((0,), (0,)), ((), ())), preferred_element_type=f32)


def split_low(x):
    high = x.astype(bf16)
    return high, (x - high.astype(f32)).astype(bf16)


def normed(x):
    centered = x - jnp.mean(x, axis=-1, keepdims=True)
    spread = lax.rsqrt(jnp.mean(centered * centered, axis=-1, keepdims=True) + norm_eps)
    return centered * spread, spread


def layer_norm(x, gain, bias):
    return normed(x)[0] * gain + bias


def gelu(x):
    return x * (0.5 + 0.5 * lax.erf(x * math.sqrt(0.5)))


def gelu_and_slope(x):
    below = 0.5 + 0.5 * lax.erf(x * math.sqrt(0.5))
    bell = jnp.exp2((-0.5 * log2e) * (x * x))
    return x * below, below + x * (bell * (1.0 / math.sqrt(2.0 * math.pi)))


def lane_halves(width):
    lane = lax.broadcasted_iota(jnp.int32, (1, width), 1)
    first = (lane < width // 2).astype(f32)
    return first.astype(bf16), (1.0 - first).astype(bf16)


def stack_heads(x, first, second):
    return jnp.concatenate([x * first, x * second], axis=0)


def join_heads(stacked):
    rows, width = stacked.shape[0] // 2, stacked.shape[1]
    lane = lax.broadcasted_iota(jnp.int32, (rows, width), 1)
    return jnp.where(lane < width // 2, stacked[:rows], stacked[rows:])


def soft_weights(query, key, bias, factor):
    scores = dot_nt(query, key) * (factor * log2e) + bias
    weights = jnp.exp2(scores - jnp.max(scores, axis=-1, keepdims=True))
    return weights, 1.0 / jnp.sum(weights, axis=-1, keepdims=True)


def set_lengths(lengths_ref, lens_ref, key_bias_ref):
    captions, tokens = lens_ref.shape[0], key_bias_ref.shape[1]
    length = tokens // captions
    caption = lax.broadcasted_iota(jnp.int32, (captions, 1), 0)
    token = lax.broadcasted_iota(jnp.int32, (1, tokens), 1)
    column, row = jnp.zeros((captions, 1), jnp.int32), jnp.zeros((1, tokens), jnp.int32)
    for n in range(captions):
        column = jnp.where(caption == n, lengths_ref[n], column)
        row = jnp.where(token // length == n, lengths_ref[n], row)
    lens_ref[...] = column
    key_bias_ref[...] = jnp.where(token % length < row, 0.0, masked_score)


def as_row(ref):
    return ref[...].reshape(1, ref.shape[0])


def text_bias(key_bias_ref, block, rows, length):
    near = lax.broadcasted_iota(jnp.int32, (rows, rows), 0) // length
    far = lax.broadcasted_iota(jnp.int32, (rows, rows), 1) // length
    columns = pl.ds(pl.multiple_of(block * rows, rows), rows)
    bias = jnp.where(near == far, key_bias_ref[:, columns], masked_score)
    return jnp.concatenate([bias, bias], axis=0)


def member(len_ref, captions, tokens):
    length = tokens // captions
    token = lax.broadcasted_iota(jnp.int32, (captions, tokens), 1)
    caption = lax.broadcasted_iota(jnp.int32, (captions, tokens), 0)
    return ((token // length == caption) & (token % length < len_ref[...])).astype(f32)


def spread_rows(x, length):
    rows, width = x.shape
    return jnp.broadcast_to(x[:, None, :], (rows, length, width)).reshape(rows * length, width)


def wide_steps(total, most=768, part=0, parts=1):
    step = math.gcd(total, most)
    count = total // step // parts

    def loop(body):
        @pl.loop(part * count, (part + 1) * count)
        def _(j):
            body(pl.ds(pl.multiple_of(j * step, 128), step))

    return loop


class TextForward:
    band = 128

    def __init__(self, names, refs):
        for name, ref in zip(names, refs, strict=True):
            setattr(self, name, ref)
        self.tokens, self.width = self.tok.shape
        self.captions = self.lens.shape[0]
        self.length = self.tokens // self.captions
        self.wide = self.w_up.shape[1]
        pairs = (
            (self.qkv_hbm, self.w_qkv), (self.out_hbm, self.w_out), (self.up_hbm, self.w_up),
            (self.down_hbm, self.w_down), (self.proj_hbm, self.w_proj),
        )
        self.loads = load_weights(pairs, self.sems)

    def bands(self, step):
        pl.loop(0, self.tokens // self.band)(
            lambda i: step(pl.ds(pl.multiple_of(i * self.band, self.band), self.band))
        )

    def prepare(self):
        set_lengths(self.lengths, self.lens, self.key_bias)

        def first_norm(rows):
            norm = layer_norm(self.tok[rows, :].astype(f32), as_row(self.gain1), as_row(self.bias1))
            self.norm[rows, :] = norm.astype(bf16)

        self.bands(first_norm)

    def attention(self):
        width = self.width
        self.loads[0].wait()

        @wide_steps(3 * width)
        def _(columns):
            self.heads[:, columns] = dot_nn(self.norm[...], self.w_qkv[:, columns]).astype(bf16)

        first, second = lane_halves(128)
        factor = (width // HEADS) ** -0.5

        @pl.loop(0, self.tokens // self.band)
        def _(block):
            rows = pl.ds(pl.multiple_of(block * self.band, self.band), self.band)
            bias = text_bias(self.key_bias, block, self.band, self.length)
            for at in range(0, width, 128):
                query = stack_heads(self.heads[rows, at : at + 128], first, second)
                key = self.heads[rows, width + at : width + at + 128]
                weights, scale = soft_weights(query, key, bias, factor)
                value = self.heads[rows, 2 * width + at : 2 * width + at + 128]
                mixed = dot_nn(weights.astype(bf16), value) * scale
                self.mixed[rows, at : at + 128] = join_heads(mixed).astype(bf16)

    def middle(self):
        self.loads[1].wait()

        def second_norm(rows):
            mid = self.tok[rows, :].astype(f32) + dot_nn(self.mixed[rows, :], self.w_out[...])
            self.mid[rows, :] = mid
            self.norm[rows, :] = layer_norm(mid, as_row(self.gain2), as_row(self.bias2)).astype(bf16)

        self.bands(second_norm)

    def feed(self, part=0, parts=1):
        if part == 0:
            self.loads[2].wait()
        self.chosen = member(self.lens, self.captions, self.tokens).astype(bf16)
        place = lax.broadcasted_iota(jnp.int32, (self.captions, self.length, 1), 1)
        valid = (place < self.lens[...].reshape(self.captions, 1, 1)).astype(f32).reshape(self.tokens, 1)

        @wide_steps(self.wide, part=part, parts=parts)
        def _(columns):
            value, slope = gelu_and_slope(dot_nn(self.norm[...], self.w_up[:, columns]))
            value = value.astype(bf16)
            self.inner[:, columns] = value
            self.slope[:, columns] = (slope * valid).astype(bf16)
            self.inner_sum[:, columns] = dot_nn(self.chosen, value).astype(bf16)

    def finish(self):
        self.loads[3].wait()
        self.turned[...] = self.norm[...].T
        inverse = 1.0 / self.lens[...].astype(f32)

        @wide_steps(self.width)
        def _(columns):
            state = self.mid[:, columns] + dot_nn(self.inner[...], self.w_down[:, columns])
            self.hidden[:, columns] = state.astype(bf16)
            high, low = split_low(state)
            pooled = (dot_nn(self.chosen, high) + dot_nn(self.chosen, low)) * inverse
            self.pooled[:, columns] = pooled.astype(bf16)

        self.loads[4].wait()
        projected = dot_nn(self.pooled[...], self.w_proj[...])
        self.projected[...] = projected
        scale = lax.rsqrt(jnp.sum(projected * projected, axis=-1, keepdims=True) + norm_eps)
        self.text_embed[...] = (projected * scale).astype(bf16)


text_ins = (
    "tok", "lengths", "gain1", "bias1", "gain2", "bias2", "qkv_hbm", "out_hbm", "up_hbm", "down_hbm", "proj_hbm",
)
text_names = (
    "hidden", "text_embed", "projected", "pooled", "inner_sum", "heads", "mixed", "mid", "slope", "turned",
)
text_scratch = ("w_qkv", "w_out", "w_up", "w_down", "w_proj", "norm", "inner", "lens", "key_bias", "sems")


def text_forward_kernel(*refs):
    t = TextForward(text_ins + text_names + text_scratch, refs)
    t.prepare()
    t.attention()
    t.middle()
    t.feed()
    t.finish()


def load_weights(pairs, sems):
    loads = [pltpu.make_async_copy(s, d, sems.at[i]) for i, (s, d) in enumerate(pairs)]
    for load in loads:
        load.start()
    return loads


def spans(count, size):
    return lambda i: pl.ds(pl.multiple_of(i * size, size), size)


def norm_backward(outer, unit, spread, gain):
    outer = outer * gain
    inner = outer - jnp.mean(outer, axis=-1, keepdims=True)
    return spread * (inner - unit * jnp.mean(outer * unit, axis=-1, keepdims=True))


class TextBackward:
    band = 128

    def __init__(self, names, refs):
        for name, ref in zip(names, refs, strict=True):
            setattr(self, name, ref)
        self.tokens, self.width = self.tok.shape
        self.captions = self.lens.shape[0]
        self.length = self.tokens // self.captions
        self.wide = self.w_up.shape[1]
        order = ("w_proj", "turned", "w_down", "slope", "w_up", "mid", "mixed", "w_out", "tok", "heads", "w_qkv")
        pairs = [(getattr(self, name + "_hbm"), getattr(self, name)) for name in order]
        self.loads = dict(zip(order, load_weights(pairs, self.sems)))
        self.pre_grad = self.slope

    def rows(self, i):
        return pl.ds(pl.multiple_of(i * self.band, self.band), self.band)

    def bands(self, step):
        pl.loop(0, self.tokens // self.band)(lambda i: step(self.rows(i)))

    def valid(self):
        place = lax.broadcasted_iota(jnp.int32, (self.captions, self.length, 1), 1)
        valid = place < self.lens[...].reshape(self.captions, 1, 1)
        return valid.astype(f32).reshape(self.tokens, 1)

    def project(self):
        set_lengths(self.lengths, self.lens, self.key_bias)
        projected = self.projected[...]
        embed_grad = self.embed_grad[...]
        r = lax.rsqrt(jnp.sum(projected * projected, axis=-1, keepdims=True) + norm_eps)
        along = jnp.sum(projected * embed_grad, axis=-1, keepdims=True)
        proj_grad = (r * embed_grad - (r * r * r) * projected * along).astype(bf16)
        self.loads["w_proj"].wait()
        state_grad = dot_nt(proj_grad, self.w_proj[...]) * (1.0 / self.lens[...].astype(f32))
        self.branch[...] = state_grad.astype(bf16)
        self.mid_grad[...] = spread_rows(state_grad, self.length) * self.valid()
        return proj_grad, self.branch[...]

    def wait_inner(self):
        self.loads["turned"].wait()
        self.loads["w_down"].wait()
        self.loads["slope"].wait()

    def inner(self, columns):
        inner_grad = dot_nt(self.branch[...], self.w_down[columns, :])
        pre_grad = spread_rows(inner_grad, self.length) * self.slope[:, columns].astype(f32)
        self.pre_grad[:, columns] = pre_grad.astype(bf16)

    def up_block(self, columns):
        return dot_nn(self.turned[...], self.pre_grad[:, columns]).astype(bf16)

    def to_middle(self):
        self.loads["w_up"].wait()

        @wide_steps(self.width)
        def _(columns):
            self.outer[:, columns] = dot_nt(self.pre_grad[...], self.w_up[columns, :])

    def middle(self):
        self.loads["mid"].wait()
        self.norm_grad[...] = jnp.zeros_like(self.norm_grad)

        def through_norm(rows):
            unit, spread = normed(self.mid[rows, :])
            outer = self.outer[rows, :]
            self.norm_grad[2:3, :] += jnp.sum(outer * unit, axis=0, keepdims=True)
            self.norm_grad[3:4, :] += jnp.sum(outer, axis=0, keepdims=True)
            mid_grad = self.mid_grad[rows, :] + norm_backward(outer, unit, spread, as_row(self.gain2))
            self.mid_grad[rows, :] = mid_grad
            self.low_grad[rows, :] = mid_grad.astype(bf16)

        self.bands(through_norm)

    def out_block(self, columns):
        return dot_tn(self.mixed[...], self.low_grad[:, columns]).astype(bf16)

    def to_heads(self):
        self.loads["w_out"].wait()
        self.loads["tok"].wait()

        def through_out(rows):
            self.mixed_grad[rows, :] = dot_nt(self.low_grad[rows, :], self.w_out[...]).astype(bf16)
            norm = layer_norm(self.tok[rows, :].astype(f32), as_row(self.gain1), as_row(self.bias1))
            self.norm[rows, :] = norm.astype(bf16)

        self.bands(through_out)

    def attention(self, after=lambda block: None):
        first, second = lane_halves(128)
        width = self.width
        factor = (width // HEADS) ** -0.5
        self.loads["heads"].wait()
        self.key_column[...] = (1.0 - self.valid()) * masked_score

        @pl.loop(0, self.tokens // self.band)
        def _(block):
            rows = self.rows(block)
            near = lax.broadcasted_iota(jnp.int32, (self.band, self.band), 0) // self.length
            far = lax.broadcasted_iota(jnp.int32, (self.band, self.band), 1) // self.length
            bias = jnp.where(near == far, self.key_column[rows, :], masked_score)
            bias = jnp.concatenate([bias, bias], axis=1)
            for at in range(0, width, 128):
                query = stack_heads(self.heads[rows, at : at + 128], first, second)
                key = self.heads[rows, width + at : width + at + 128]
                value = self.heads[rows, 2 * width + at : 2 * width + at + 128]
                grad = stack_heads(self.mixed_grad[rows, at : at + 128], first, second)
                scores = dot_nt(key, query) * (factor * log2e) + bias
                weights = jnp.exp2(scores - jnp.max(scores, axis=0, keepdims=True))
                probs = weights * (1.0 / jnp.sum(weights, axis=0, keepdims=True))
                prob_grad = dot_nt(value, grad)
                total = jnp.sum(prob_grad * probs, axis=0, keepdims=True)
                score_grad = (probs * (prob_grad - total)).astype(bf16)
                query_grad = join_heads(dot_tn(score_grad, key)) * factor
                self.heads_grad[rows, at : at + 128] = query_grad.astype(bf16)
                key_grad = dot_nn(score_grad, query) * factor
                self.heads_grad[rows, width + at : width + at + 128] = key_grad.astype(bf16)
                value_grad = dot_nn(probs.astype(bf16), grad)
                self.heads_grad[rows, 2 * width + at : 2 * width + at + 128] = value_grad.astype(bf16)
            after(block)

    def qkv_block(self, columns):
        return dot_tn(self.norm[...], self.heads_grad[:, columns]).astype(bf16)

    def input(self, between=lambda: None):
        self.loads["w_qkv"].wait()

        @wide_steps(self.width)
        def _(columns):
            self.outer[:, columns] = dot_nt(self.heads_grad[...], self.w_qkv[columns, :])

        between()

        def through_norm(rows):
            unit, spread = normed(self.tok[rows, :].astype(f32))
            outer = self.outer[rows, :]
            self.norm_grad[0:1, :] += jnp.sum(outer * unit, axis=0, keepdims=True)
            self.norm_grad[1:2, :] += jnp.sum(outer, axis=0, keepdims=True)
            inner = norm_backward(outer, unit, spread, as_row(self.gain1))
            self.input_grad[rows, :] = (self.mid_grad[rows, :] + inner).astype(bf16)

        self.bands(through_norm)


backward_ins = (
    "lengths", "gain1", "bias1", "gain2", "bias2", "embed_grad", "projected", "tok_hbm", "heads_hbm", "mixed_hbm",
    "mid_hbm", "slope_hbm", "turned_hbm", "w_qkv_hbm", "w_out_hbm", "w_up_hbm", "w_down_hbm", "w_proj_hbm",
)
backward_scratch = (
    "tok", "heads", "mixed", "mid", "slope", "w_qkv", "w_out", "w_up", "w_down", "w_proj", "norm", "turned",
    "outer", "mid_grad", "low_grad", "mixed_grad", "heads_grad", "lens", "key_bias", "key_column",
    "sems",
)


def text_backward_kernel(*refs):
    outs = ("proj_grad", "branch", "up_grad", "out_grad", "qkv_grad", "input_grad", "norm_grad")
    t = TextBackward(backward_ins + outs + backward_scratch, refs)
    parts = t.up_grad.shape[0]

    def blocks(target, block):
        step = target.shape[2]
        for part in range(parts):
            target[part] = block(slice(part * step, (part + 1) * step))

    t.proj_grad[...] = t.project()[0]
    t.wait_inner()
    wide_steps(t.wide)(t.inner)
    blocks(t.up_grad, t.up_block)
    t.to_middle()
    t.middle()
    t.loads["mixed"].wait()
    blocks(t.out_grad, t.out_block)
    t.to_heads()
    t.attention()
    blocks(t.qkv_grad, t.qkv_block)
    t.input()


class Place:
    def __init__(self, z_count=4, y_count=2, x_count=2, k_count=2):
        self.row, self.col = lax.axis_index("row"), lax.axis_index("col")
        self.z, self.y = self.row // y_count, self.row % y_count
        self.x, self.k = self.col // k_count, self.col % k_count
        self.rows, self.cols = z_count * y_count, x_count * k_count
        self.count = self.rows * self.cols
        self.me = self.row * self.cols + self.col
        self.slot = self.col * self.rows + self.row
        self.near_z, self.far_z = self.z + 1 - 2 * (self.z % 2), (self.z + 2) % 4

    def at(self, **moved):
        z, y, x, k = (moved.get(name, getattr(self, name)) for name in "zyxk")
        return z * 2 + y, x * 2 + k

    def peer(self, distance):
        other = (self.me + distance) % self.count
        return other // self.cols, other % self.cols

    def greet(self):
        barrier = pltpu.get_barrier_semaphore()

        @pl.loop(1, self.count)
        def _(distance):
            pl.semaphore_signal(barrier, inc=1, device_id=self.peer(distance), device_id_type=MESH)

    def meet(self):
        pl.semaphore_wait(pltpu.get_barrier_semaphore(), self.count - 1)


def remote(src, dst, send, recv, to):
    return pltpu.make_async_remote_copy(
        src_ref=src, dst_ref=dst, send_sem=send, recv_sem=recv, device_id=to, device_id_type=MESH
    )


class Gather:
    def __init__(self, place, axis, shard, whole, local, sends, recvs):
        depth = shard.shape[0]
        half = depth // 2
        part = place.y if axis == "y" else place.z % 2
        mate, next_x = place.at(k=1 - place.k), place.at(x=1 - place.x)
        partner = place.at(y=1 - place.y) if axis == "y" else place.at(z=place.near_z)

        def block(col, part):
            return whole.at[pl.ds(pl.multiple_of(col * depth + part * half, 16), half)]

        own = whole.at[pl.ds(pl.multiple_of(place.col * depth, 16), depth)]
        across = next_x[1]
        shard_half = shard.at[pl.ds(pl.multiple_of(part * half, 16), half)]
        mine, others = block(across, part), block(across, 1 - part)
        self.local = pltpu.make_async_copy(shard, own, local)
        self.near = remote(shard, own, sends.at[0], recvs.at[0], mate)
        self.far = remote(shard_half, block(place.col, part), sends.at[1], recvs.at[1], next_x)
        self.along = remote(mine, mine, sends.at[2], recvs.at[2], partner)
        self.first = remote(mine, mine, sends.at[3], recvs.at[3], mate)
        self.second = remote(others, others, sends.at[4], recvs.at[4], mate)

    def start(self):
        self.far.start()
        self.near.start()
        self.local.start()

    def share(self):
        self.far.wait()
        self.along.start()
        self.first.start()

    def relay(self):
        self.along.wait()
        self.second.start()

    def finish(self):
        self.local.wait()
        self.near.wait()
        self.first.wait()
        self.second.wait()


class RowFactors:
    def __init__(self, place, own, held, local, sends, recvs):
        self.place, self.own, self.held, self.sends, self.recvs = place, own, held, sends, recvs
        self.local = pltpu.make_async_copy(own.at[place.row], held.at[place.col, place.row], local)
        mine, across = held.at[place.col], held.at[place.at(x=1 - place.x)[1]]
        mate, next_x = place.at(k=1 - place.k), place.at(x=1 - place.x)
        n = place.rows - 1
        self.far = remote(mine, mine, sends.at[n], recvs.at[n], next_x)
        self.near = remote(mine, mine, sends.at[n + 1], recvs.at[n + 1], mate)
        self.passed = remote(across, across, sends.at[n + 2], recvs.at[n + 2], mate)

    def copy(self, distance):
        p = self.place
        row = (p.row + distance) % p.rows
        sems = self.sends.at[distance - 1], self.recvs.at[distance - 1]
        return remote(self.own.at[row], self.held.at[p.col, p.row], *sems, (row, p.col))

    def start(self):
        self.local.start()
        pl.loop(1, self.place.rows)(lambda distance: self.copy(distance).start())

    def share(self):
        self.local.wait()
        pl.loop(1, self.place.rows)(lambda distance: self.copy(distance).wait())
        self.far.start()
        self.near.start()

    def relay(self):
        self.far.wait()
        self.passed.start()

    def finish(self):
        self.near.wait()
        self.passed.wait()


class Exchange:
    def __init__(self, place, source, slots, sends, recvs):
        self.place, self.source, self.slots, self.sends, self.recvs = place, source, slots, sends, recvs

    def copy(self, distance):
        to = self.place.peer(distance)
        sems = self.sends.at[distance - 1], self.recvs.at[distance - 1]
        return remote(self.source(to), self.slots.at[self.place.slot], *sems, to)

    def start(self):
        pl.loop(1, self.place.count)(lambda distance: self.copy(distance).start())

    def finish(self):
        pl.loop(1, self.place.count)(lambda distance: self.copy(distance).wait())


class ChipSum:
    def __init__(self, place, total, got, slots, sends, recvs):
        self.place, self.total, self.got, self.slots = place, total, got, slots
        self.sends, self.recvs = sends, recvs
        self.chip, self.chips = place.row * 2 + place.x, place.rows * 2

    def near(self):
        p = self.place
        return remote(self.total, self.got, self.sends.at[0], self.recvs.at[0], p.at(k=1 - p.k))

    def copy(self, distance):
        other = (self.chip + distance) % self.chips
        to = other // 2, other % 2 * 2 + self.place.k
        sems = self.sends.at[distance], self.recvs.at[distance]
        return remote(self.total, self.slots.at[self.chip], *sems, to)

    def start(self):
        self.near().start()

    def spread(self):
        self.near().wait()
        self.total[...] = self.total[...] + self.got[...]
        self.slots[self.chip] = self.total[...]
        pl.loop(1, self.chips)(lambda distance: self.copy(distance).start())

    def finish(self):
        pl.loop(1, self.chips)(lambda distance: self.copy(distance).wait())
        return jnp.sum(self.slots[...], axis=0)


class GradientScatter:
    def __init__(self, place, straight, halves, held, near, x1, y1, x2, y2, far, sends, recvs):
        self.straight = straight
        self.place, self.held, self.near, self.far = place, held, near, far
        self.x1, self.y1, self.x2, self.y2 = x1, y1, x2, y2
        self.sends, self.recvs = sends, recvs
        self.halves = halves

    def lanes(self, chunk):
        ones, twos = zip(*self.halves[:chunk], (0, 0))
        at_one, at_two = sum(ones), sum(twos)
        at = at_one + at_two
        one, two = self.halves[chunk]
        return (
            pl.ds(at, one + two), pl.ds(at, one), pl.ds(at + one, two), pl.ds(at_one, one), pl.ds(at_two, two)
        )

    def copies(self, chunk, stage):
        p, held = self.place, self.held
        x, y, z, k = p.x, p.y, p.z, p.k
        whole, one, two, part_one, part_two = self.lanes(chunk)

        def copy(n, src, dst, **moved):
            return remote(src, dst, self.sends.at[chunk, n], self.recvs.at[chunk, n], p.at(**moved))

        if stage == 0:
            return [copy(0, held.at[:, 1 - k, :, :, :, whole], self.near.at[:, :, :, :, whole], k=1 - k)]
        if stage == 1:
            copies = []
            if one.size:
                copies.append(copy(1, held.at[1 - x, k, :, :, :, one], self.x1.at[:, :, :, part_one], x=1 - x))
            if two.size:
                copies.append(copy(2, held.at[:, k, :, 1 - y, :, two], self.y1.at[:, :, :, part_two], y=1 - y))
            return copies
        if stage == 2:
            copies = []
            if one.size:
                copies.append(copy(3, held.at[x, k, :, 1 - y, :, one], self.y2.at[:, :, part_one], y=1 - y))
            if two.size:
                copies.append(copy(4, held.at[1 - x, k, :, y, :, two], self.x2.at[:, :, part_two], x=1 - x))
            return copies
        if stage == 3 and self.straight:
            return [
                copy(4 + i, held.at[x, k, (z + i) % 4, y, :, whole], self.far.at[i - 1, :, whole], z=(z + i) % 4)
                for i in range(1, 4)
            ]
        if stage == 3:
            blocks = p.near_z, held.shape[2] - 1 - z
            return [
                copy(5 + i, held.at[x, k, block, y, :, whole], self.far.at[i, :, whole], z=p.near_z)
                for i, block in enumerate(blocks)
            ]
        return [copy(7, held.at[x, k, p.far_z, y, :, whole], self.far.at[2, :, whole], z=p.far_z)]

    def start(self, chunk, stage):
        for copy in self.copies(chunk, stage):
            copy.start()

    def finish(self, chunk, stage):
        for copy in self.copies(chunk, stage):
            copy.wait()
        p, held = self.place, self.held
        x, y, k = p.x, p.y, p.k
        z_count = held.shape[2]
        whole, one, two, part_one, part_two = self.lanes(chunk)

        def add(target, source):
            target[...] = (target[...].astype(f32) + source[...].astype(f32)).astype(bf16)

        if stage == 0:

            @pl.loop(0, z_count)
            def _(z):
                for i in range(2):
                    for j in range(2):
                        add(held.at[i, k, z, j, :, whole], self.near.at[i, z, j, :, whole])

        if stage == 1:

            @pl.loop(0, z_count)
            def _(z):
                for i in range(2):
                    if one.size:
                        add(held.at[x, k, z, i, :, one], self.x1.at[z, i, :, part_one])
                    if two.size:
                        add(held.at[i, k, z, y, :, two], self.y1.at[i, z, :, part_two])

        if stage == 2:

            @pl.loop(0, z_count)
            def _(z):
                if one.size:
                    add(held.at[x, k, z, y, :, one], self.y2.at[z, :, part_one])
                if two.size:
                    add(held.at[x, k, z, y, :, two], self.x2.at[z, :, part_two])

        if stage == 3 and not self.straight:
            add(held.at[x, k, p.far_z, y, :, whole], self.far.at[1, :, whole])

    def step_on(self, chunk, stage):
        self.finish(chunk, stage - 1)
        self.start(chunk, stage)

    def total(self):
        p = self.place
        total = self.held[p.x, p.k, p.z, p.y].astype(f32)
        for i in (0, 1, 2) if self.straight else (0, 2):
            total = total + self.far[i].astype(f32)
        return total


def chip_sum_scratch(size, chips):
    return [
        pltpu.VMEM((1, size), f32), pltpu.VMEM((1, size), f32), pltpu.VMEM((chips, 1, size), f32),
        pltpu.SemaphoreType.DMA((chips,)), pltpu.SemaphoreType.DMA((chips,)),
    ]


def scatter_scratch(rows, halves):
    one, two = (sum(widths) for widths in zip(*halves))
    spare = max(two, 128)
    shapes = [
        (2, 2, 4, 2, rows, one + two), (2, 4, 2, rows, one + two), (4, 2, rows, one), (2, 4, rows, spare),
        (4, rows, spare), (4, rows, one), (3, rows, one + two),
    ]
    return [pltpu.VMEM(shape, bf16) for shape in shapes] + [pltpu.SemaphoreType.DMA((len(halves), 8))] * 2


class ColFactors:
    def __init__(self, place, own, held, sends, recvs):
        self.place, self.own, self.held, self.sends, self.recvs = place, own, held, sends, recvs

    def copies(self, stage):
        p, held = self.place, self.held

        def copy(n, src, dst, **moved):
            return remote(src, dst, self.sends.at[n], self.recvs.at[n], p.at(**moved))

        if stage == 0:
            mine = held.at[p.col, p.row]
            moves = ({"x": 1 - p.x}, {"k": 1 - p.k}, {"x": 1 - p.x, "k": 1 - p.k})
            return [copy(i, self.own.at[p.at(**move)[1]], mine, **move) for i, move in enumerate(moves)]
        if stage == 1:
            mine = held.at[:, p.row]
            return [copy(3, mine, mine, y=1 - p.y)]
        mine, other = (held.at[:, pl.ds(z * 2, 2)] for z in (p.z, p.far_z))
        if stage == 2:
            return [copy(4, mine, mine, z=p.far_z)]
        return [copy(5, mine, mine, z=p.near_z), copy(6, other, other, z=p.near_z)]

    def start(self, stage):
        for copy in self.copies(stage):
            copy.start()

    def finish(self, stage):
        for copy in self.copies(stage):
            copy.wait()


def scatter_widths(wide, width, cols):
    ups = tuple((128, 128) for _ in range(wide // cols // 256))
    rest = 4 * width // cols - 128
    return ups, ((128, 0),), ((128, 128), (128, 128), (0, rest - 512))


scatter_names = ("held", "near", "x1", "y1", "x2", "y2", "far", "sends", "recvs")
exchange_names = ("own", "all", "sends", "recvs")
total_names = ("total", "got", "slots", "sends", "recvs")


def text_backward_joined_kernel(*refs):
    ins = backward_ins + ("factors", "loss")
    outs = ("up_out", "out_out", "qkv_out", "down_out", "proj_out", "input_grad", "norm_out")
    sets = tuple(name + tag for tag in ("_up", "_outs", "_qkv") for name in scatter_names)
    swaps = tuple(name + "_factors" for name in exchange_names)
    totals = tuple(name + tag for tag in ("_late", "_last") for name in total_names)
    names = ins + outs + backward_scratch + sets + ("branch", "norm_grad") + swaps + totals
    t = TextBackward(names, refs)
    place = Place()
    place.greet()
    width, cols = t.width, place.cols
    widths = scatter_widths(t.wide, width, cols)
    up, out, qkv = (
        GradientScatter(place, tag == "_qkv", halves, *(getattr(t, name + tag) for name in scatter_names))
        for halves, tag in zip(widths, ("_up", "_outs", "_qkv"))
    )
    factors = ColFactors(place, t.own_factors, t.all_factors, t.sends_factors, t.recvs_factors)
    late, last = (
        ChipSum(place, *(getattr(t, name + tag) for name in total_names)) for tag in ("_late", "_last")
    )

    def store(scatter, part, at, value):
        held = scatter.held
        size = value.shape[1]
        held[part // 2, part % 2, :, :, :, at : at + size] = value.reshape(*held.shape[2:5], size)

    def fill(scatter, chunk, total, block):
        at, size = scatter.lanes(chunk)[0].start, scatter.lanes(chunk)[0].size
        true = min(size, total // cols - at)
        for part in range(cols):
            start = part * (total // cols) + at
            store(scatter, part, at, block(slice(start, start + true)))

    def fill_up(chunk):
        at = up.lanes(chunk)[0].start
        size = up.lanes(chunk)[0].size
        for part in range(cols):
            start = part * up.held.shape[5] + at
            t.inner(pl.ds(start, size))
        fill(up, chunk, t.wide, t.up_block)
        up.start(chunk, 0)

    proj_grad, branch = t.project()
    out_step = width // cols
    for part in range(cols):
        columns = slice(part * out_step, (part + 1) * out_step)
        t.own_factors[part] = jnp.concatenate([branch[:, columns], proj_grad[:, columns]], axis=1)
    t.all_factors[place.col, place.row] = t.own_factors[place.col]
    t.wait_inner()
    place.meet()
    factors.start(0)
    fill_up(0)
    factors.finish(0)
    factors.start(1)
    fill_up(1)
    up.step_on(0, 1)
    fill_up(2)
    up.step_on(1, 1)
    factors.finish(1)
    factors.start(2)
    t.to_middle()
    up.step_on(2, 1)
    t.middle()
    t.loads["mixed"].wait()
    for part in range(cols):
        value = t.out_block(slice(part * out_step, (part + 1) * out_step))
        store(out, part, 0, value[:, :128])
        store(qkv, part, 3 * out_step, value[:, 128:])
    out.start(0, 0)
    up.step_on(0, 2)
    t.total_late[...] = jnp.concatenate([t.norm_grad[2:3, :], t.norm_grad[3:4, :], t.loss[...]], axis=1)
    late.start()
    t.to_heads()
    factors.finish(2)
    factors.start(3)
    out.step_on(0, 1)
    late.spread()

    def after(block):
        @pl.when(block == 0)
        def _():
            up.step_on(1, 2)

        @pl.when(block == 2)
        def _():
            up.step_on(0, 3)
            up.step_on(2, 2)

    t.attention(after)
    fill(qkv, 0, 3 * width, t.qkv_block)
    qkv.start(0, 0)
    fill(qkv, 1, 3 * width, t.qkv_block)
    qkv.start(1, 0)
    out.step_on(0, 2)
    qkv.step_on(0, 1)
    fill(qkv, 2, 3 * width, t.qkv_block)
    qkv.start(2, 0)
    up.step_on(1, 3)
    up.step_on(0, 4)
    up.step_on(2, 3)

    def between():
        qkv.step_on(0, 2)
        qkv.step_on(1, 1)

    t.input(between)
    t.total_last[...] = jnp.concatenate([t.norm_grad[0:1, :], t.norm_grad[1:2, :]], axis=1)
    last.start()
    up.step_on(1, 4)
    out.step_on(0, 3)
    up.step_on(2, 4)
    qkv.step_on(0, 3)
    qkv.step_on(2, 1)
    last.spread()
    factors.finish(3)
    grown = dot_tn(
        t.all_factors[...].reshape(-1, t.all_factors.shape[3]), t.factors[...].reshape(-1, t.factors.shape[3])
    )
    inner_step = t.wide // place.rows
    t.down_out[...] = grown[:out_step, :inner_step]
    t.proj_out[...] = grown[out_step:, inner_step:].T[: width // place.rows]
    qkv.step_on(1, 2)
    out.step_on(0, 4)
    t.norm_out[:, 2 * width :] = late.finish()
    qkv.step_on(2, 2)
    qkv.step_on(1, 3)
    qkv.step_on(2, 3)
    for chunk in range(len(up.halves)):
        up.finish(chunk, 4)
    t.up_out[...] = up.total()
    t.norm_out[:, : 2 * width] = last.finish()
    out.finish(0, 4)
    t.out_out[:, :128] = out.total()
    for chunk in range(len(qkv.halves)):
        qkv.finish(chunk, 3)
    total = qkv.total()
    t.qkv_out[...] = total[:, : 3 * out_step]
    t.out_out[:, 128:] = total[:, 3 * out_step : 4 * out_step - 128]


def hand_over_kernel(pair_total, norms, *refs):
    sources, (loss, *vectors), targets = refs[:7], refs[7:12], refs[12:]
    width = vectors[0].shape[0]
    loss[...] = norms[:, 4 * width : 4 * width + 1] * (1.0 / pair_total)
    for i, vector in enumerate(vectors):
        vector[...] = norms[:, i * width : (i + 1) * width].reshape(width)
    for source, target in zip(sources, targets, strict=True):
        target[...] = source[...]


def group_mean(images, rows):
    token = lax.broadcasted_iota(jnp.int32, (images, rows), 1)
    image = lax.broadcasted_iota(jnp.int32, (images, rows), 0)
    inside = (token >= image * IMG_TOK) & (token < (image + 1) * IMG_TOK)
    return inside.astype(f32).astype(bf16)


def load_parts(parts, target, sems, col, col_count):
    depth = target.shape[0] // col_count
    copies = []
    for k, part in enumerate(parts):
        place = pl.multiple_of((col ^ k) * depth, depth)
        copies.append(pltpu.make_async_copy(part, target.at[pl.ds(place, depth)], sems.at[k]))
    return copies


def image_mix(tokens, gain_ref, bias_ref, w_qkv, w_out, norm_ref, heads_ref, mixed_ref):
    rows, width = tokens.shape
    images = rows // IMG_TOK
    norm_ref[...] = layer_norm(tokens.astype(f32), gain_ref[0:1, :], bias_ref[0:1, :]).astype(bf16)

    @wide_steps(3 * width)
    def _(columns):
        heads_ref[:, columns] = dot_nn(norm_ref[...], w_qkv[:, columns]).astype(bf16)

    first, second = lane_halves(128)
    factor = (width // HEADS) ** -0.5
    window = 112

    @pl.loop(0, images // 2)
    def _(pair):
        start = pair * (2 * IMG_TOK)
        low = pl.multiple_of(start // 16 * 16, 16)
        near = lax.broadcasted_iota(jnp.int32, (window, window), 0) + low
        far = lax.broadcasted_iota(jnp.int32, (window, window), 1) + low
        same = (near >= start) & (near < start + 2 * IMG_TOK) & (far >= start) & (far < start + 2 * IMG_TOK)
        same = same & ((near >= start + IMG_TOK) == (far >= start + IMG_TOK))
        bias = jnp.where(same, 0.0, masked_score)
        bias = jnp.concatenate([bias, bias], axis=0)
        keep = lax.broadcasted_iota(jnp.int32, (16, 128), 0) + low < start
        span, head, tail = pl.ds(low, window), pl.ds(low, 16), pl.ds(low + 16, window - 16)
        for at in range(0, width, 128):
            query = stack_heads(heads_ref[span, at : at + 128], first, second)
            key = heads_ref[span, width + at : width + at + 128]
            weights, scale = soft_weights(query, key, bias, factor)
            value = heads_ref[span, 2 * width + at : 2 * width + at + 128]
            mixed = join_heads(dot_nn(weights.astype(bf16), value) * scale)
            former = mixed_ref[head, at : at + 128].astype(f32)
            mixed_ref[head, at : at + 128] = jnp.where(keep, former, mixed[:16]).astype(bf16)
            mixed_ref[tail, at : at + 128] = mixed[16:].astype(bf16)

    mid = tokens.astype(f32) + dot_nn(mixed_ref[...], w_out[...])
    high, low = split_low(mid)
    select = group_mean(images, rows)
    mean = (dot_nn(select, high) + dot_nn(select, low)) * (1.0 / IMG_TOK)
    return layer_norm(mid, gain_ref[1:2, :], bias_ref[1:2, :]).astype(bf16), mean


def image_mix_kernel(col_count, tok_ref, gain_ref, bias_ref, *refs):
    qkv_parts, out_parts = refs[:col_count], refs[col_count : 2 * col_count]
    normed_ref, mean_ref, w_qkv, w_out, *buffers, sems = refs[2 * col_count :]
    col = lax.axis_index("col")

    @pl.when(pl.program_id(0) == 0)
    def _():
        copies = load_parts(qkv_parts, w_qkv, sems.at[0], col, col_count)
        copies += load_parts(out_parts, w_out, sems.at[1], col, col_count)
        for copy in copies:
            copy.start()
        for copy in copies:
            copy.wait()

    normed_ref[...], mean_ref[...] = image_mix(tok_ref[...], gain_ref, bias_ref, w_qkv, w_out, *buffers)


def image_embed_kernel(col_count, normed_ref, mean_ref, *refs):
    up_parts, down_parts = refs[:col_count], refs[col_count : 2 * col_count]
    embed_ref, w_up, w_down, sum_ref, sems = refs[2 * col_count :]
    rows, width = normed_ref.shape
    images = rows // IMG_TOK
    wide = w_up.shape[1]
    step = pl.program_id(0)
    col = lax.axis_index("col")
    downs = load_parts(down_parts, w_down, sems.at[1], col, col_count)

    @pl.when(step == 0)
    def _():
        ups = load_parts(up_parts, w_up, sems.at[0], col, col_count)
        for copy in ups + downs:
            copy.start()
        for copy in ups:
            copy.wait()

    select = group_mean(images, rows)

    @wide_steps(wide)
    def _(columns):
        inner = gelu(dot_nn(normed_ref[...], w_up[:, columns])).astype(bf16)
        sum_ref[pl.ds(pl.multiple_of(step * images, images), images), columns] = dot_nn(select, inner)

    @pl.when(step == pl.num_programs(0) - 1)
    def _():
        for copy in downs:
            copy.wait()
        high, low = split_low(sum_ref[...] * (1.0 / IMG_TOK))
        pooled = mean_ref[...] + dot_nn(high, w_down[...]) + dot_nn(low, w_down[...])
        embed_ref[...] = (
            pooled * lax.rsqrt(jnp.sum(pooled * pooled, axis=-1, keepdims=True) + norm_eps)
        ).astype(bf16)


image_ins = (
    "image_hbm", "image_gain", "image_bias", "image_qkv_hbm", "image_out_hbm", "image_up_hbm", "image_down_hbm",
)
saved_names = ("hidden", "projected", "heads", "mixed", "mid", "slope", "turned", "held_factors")
image_scratch = (
    "image_tok", "iw_qkv", "iw_out", "iw_up", "iw_down", "image_norm", "image_heads", "image_mixed", "image_normed",
    "image_mean", "sums", "own", "images", "own_factors", "held_factors", "own_sums", "all_sums", "save_sems",
    "tok_sem", "local", "sends", "recvs", "factor_local", "factor_sends", "factor_recvs", "image_sends",
    "image_recvs", "sum_sends", "sum_recvs",
)


def forward_joined_kernel(*refs):
    saves = tuple(name + "_out" for name in saved_names)
    names = text_ins + image_ins + saves + ("embed_grad", "loss") + text_names + text_scratch + image_scratch
    t = TextForward(names, refs)
    place = Place()
    place.greet()
    load_images = pltpu.make_async_copy(t.image_hbm, t.image_tok, t.tok_sem.at[0])
    load_images.start()
    save = {
        name: pltpu.make_async_copy(getattr(t, name), getattr(t, name + "_out"), t.save_sems.at[i])
        for i, name in enumerate(saved_names)
    }
    shards = (
        (t.image_qkv_hbm, t.iw_qkv), (t.image_out_hbm, t.iw_out), (t.image_up_hbm, t.iw_up),
        (t.image_down_hbm, t.iw_down),
    )
    pieces = [
        (shard, whole, i * whole.shape[1] // n, whole.shape[1] // n)
        for (shard, whole), n in zip(shards, (2, 1, 2, 2))
        for i in range(n)
    ]
    qkv_a, qkv_b, out, up_a, up_b, down_a, down_b = (
        Gather(
            place, axis, shard.at[:, pl.ds(at, size)], whole.at[:, pl.ds(at, size)],
            t.local.at[i], t.sends.at[i], t.recvs.at[i],
        )
        for i, (axis, (shard, whole, at, size)) in enumerate(zip("yyzyzyz", pieces))
    )
    factors = RowFactors(
        place, t.own_factors, t.held_factors, t.factor_local.at[0], t.factor_sends, t.factor_recvs
    )
    t.prepare()
    place.meet()
    qkv_a.start()
    qkv_b.start()
    out.start()
    t.attention()
    qkv_a.share()
    save["heads"].start()
    save["mixed"].start()
    t.middle()
    save["mid"].start()
    t.feed(0, 2)
    qkv_b.share()
    t.feed(2, 4)
    out.share()
    up_a.start()
    up_b.start()
    t.feed(3, 4)
    save["slope"].start()
    t.finish()
    save["hidden"].start()
    save["projected"].start()
    save["turned"].start()
    qkv_a.relay()
    qkv_b.relay()
    inner_step, width_step = t.wide // place.rows, t.width // place.rows
    pooled = t.pooled[...]
    for row in range(place.rows):
        block = pooled[:, row * width_step : (row + 1) * width_step]
        spare = t.own_factors.shape[2] - inner_step - width_step
        t.own_factors[row, :, :inner_step] = t.inner_sum[:, row * inner_step : (row + 1) * inner_step]
        t.own_factors[row, :, inner_step:] = jnp.concatenate([block, jnp.zeros((t.captions, spare), bf16)], axis=1)
    load_images.wait()
    out.relay()
    qkv_a.finish()
    qkv_b.finish()
    out.finish()
    factors.start()

    rows, width = t.image_tok.shape
    group_rows = t.image_norm.shape[0]
    groups = rows // group_rows
    group_images = group_rows // IMG_TOK

    @pl.loop(0, groups)
    def _(group):
        span = pl.ds(pl.multiple_of(group * group_rows, 16), group_rows)
        normed2, mean = image_mix(
            t.image_tok[span, :], t.image_gain, t.image_bias, t.iw_qkv, t.iw_out,
            t.image_norm, t.image_heads, t.image_mixed,
        )
        t.image_normed[span, :] = normed2
        t.image_mean[pl.ds(pl.multiple_of(group * group_images, 8), group_images), :] = mean

        @pl.when(group == 0)
        def _():
            up_a.share()
            up_b.share()
            down_a.start()
            down_b.start()

        @pl.when(group == 2)
        def _():
            up_a.relay()
            up_b.relay()
            down_a.share()
            down_b.share()

    down_a.relay()
    up_a.finish()

    halves, _, _, _, half_images, _ = t.images.shape
    half_rows = half_images * IMG_TOK
    corner = place.y * 2 + place.x

    def image_copies(half, stage):
        mine = t.images.at[half, place.k, corner]
        own = mine.at[place.z]

        def copy(n, block, **moved):
            return remote(block, block, t.image_sends.at[half, n], t.image_recvs.at[half, n], place.at(**moved))

        if stage == 0:
            return [copy(i - 1, own, z=(place.z + i) % 4) for i in range(1, 4)]
        if stage == 1:
            moves = ({"x": 1 - place.x}, {"y": 1 - place.y}, {"x": 1 - place.x, "y": 1 - place.y})
            return [copy(3 + i, mine, **move) for i, move in enumerate(moves)]
        return [copy(6, t.images.at[half, place.k], k=1 - place.k)]

    def image_start(half, stage):
        for copy in image_copies(half, stage):
            copy.start()

    def image_finish(half, stage):
        for copy in image_copies(half, stage):
            copy.wait()

    select = group_mean(half_images, half_rows)
    for half in range(halves):

        def feed(columns):
            total = 0.0
            for group in range(half_rows // group_rows):
                local = slice(group * group_rows, (group + 1) * group_rows)
                at = half * half_rows + group * group_rows
                inner = gelu(dot_nn(t.image_normed[at : at + group_rows, :], t.iw_up[:, columns])).astype(bf16)
                total = total + dot_nn(select[:, local], inner)
            t.sums[:, columns] = total

        wide_steps(t.wide, part=0, parts=2)(feed)
        if half == 0:
            up_b.finish()
            down_b.relay()
        else:
            image_finish(half - 1, 0)
            image_start(half - 1, 1)
        wide_steps(t.wide, part=1, parts=2)(feed)
        if half == 0:
            down_a.finish()
            down_b.finish()
            factors.share()
        high, low = split_low(t.sums[...] * (1.0 / IMG_TOK))
        pooled = dot_nn(jnp.concatenate([high, low], axis=0), t.iw_down[...])
        part = slice(half * half_images, (half + 1) * half_images)
        pooled = t.image_mean[part, :] + pooled[:half_images] + pooled[half_images:]
        embed = pooled * lax.rsqrt(jnp.sum(pooled * pooled, axis=-1, keepdims=True) + norm_eps)
        t.own[part, :] = embed.astype(bf16)
        t.images[half, place.k, corner, place.z] = embed.astype(bf16)
        image_start(half, 0)

    factors.relay()
    image_finish(halves - 1, 0)
    image_start(halves - 1, 1)
    image_finish(0, 1)
    image_start(0, 2)
    factors.finish()
    save["held_factors"].start()
    image_finish(halves - 1, 1)
    image_start(halves - 1, 2)
    for half in range(halves):
        image_finish(half, 2)

    images = t.images[...].reshape(-1, width)
    own = t.own[...].astype(f32)
    lifted = jnp.exp2(dot_nt(t.text_embed[...], images) * (logit_scale * log2e))
    t.own_sums[...] = jnp.sum(lifted, axis=0, keepdims=True)
    t.all_sums[place.slot] = t.own_sums[...]
    sums = Exchange(place, lambda to: t.own_sums, t.all_sums, t.sum_sends, t.sum_recvs)
    sums.start()
    col_sums = jnp.sum(lifted, axis=1, keepdims=True)
    positives = logit_scale * jnp.sum(own * t.text_embed[...].astype(f32), axis=(0, 1), keepdims=True)
    sums.finish()
    row_sums = jnp.sum(t.all_sums[...], axis=0)
    sim_grad = (0.5 * (lifted * (1.0 / row_sums) + lifted * (1.0 / col_sums))).astype(bf16)
    t.embed_grad[...] = logit_scale * (dot_nn(sim_grad, images) - own)
    logs = jnp.sum(jnp.log(col_sums), axis=(0, 1), keepdims=True)
    logs = logs + jnp.sum(jnp.log(row_sums), axis=(0, 1), keepdims=True) * (1.0 / place.count)
    t.loss[...] = jnp.broadcast_to(0.5 * logs - positives, t.loss.shape)
    for copy in save.values():
        copy.wait()


def whole(shape):
    return pl.BlockSpec(shape, lambda *_: (0,) * len(shape))


in_vmem = pl.BlockSpec(memory_space=pltpu.VMEM)
in_smem = pl.BlockSpec(memory_space=pltpu.SMEM)
anywhere = pl.BlockSpec(memory_space=pl.ANY)


def plain(kernel, outs, ins, scratch, name, out_specs=None, **settings):
    return pl.pallas_call(
        kernel,
        out_shape=outs,
        in_specs=ins,
        out_specs=out_specs or [in_vmem] * len(outs),
        scratch_shapes=scratch,
        compiler_params=pltpu.CompilerParams(vmem_limit_bytes=VMEM_LIMIT, **settings),
        name=name,
    )


def array(shape, dtype):
    return jax.ShapeDtypeStruct(shape, dtype)


def partners(x, col_count):
    order = [(i, i ^ 2) for i in range(col_count)]
    near = [(i, i ^ 1) for i in range(col_count)]
    far = lax.ppermute(x, "col", order)
    return [x, lax.ppermute(x, "col", near), far, lax.ppermute(far, "col", near)]


def body(
    image_tokens, image_norm_gain, image_norm_bias, image_qkv, image_out, image_up, image_down,
    text_tokens, text_lengths, norm1_gain, norm1_bias, norm2_gain, norm2_bias,
    text_qkv, text_out, text_up, text_down, text_proj,
):
    tokens, width = text_tokens.shape
    captions = text_lengths.shape[0]
    length = tokens // captions
    wide = text_up.shape[1]
    row_count, col_count = lax.axis_size("row"), lax.axis_size("col")
    row, col = lax.axis_index("row"), lax.axis_index("col")
    pair_total = captions * row_count * col_count
    image_rows, images = image_tokens.shape[0], image_tokens.shape[0] // IMG_TOK

    count = row_count * col_count
    joined = (row_count, col_count) == (8, 4)
    vectors = (norm1_gain, norm1_bias, norm2_gain, norm2_bias)
    weights = (text_qkv, text_out, text_up, text_down, text_proj)
    weight_scratch = [pltpu.VMEM(w.shape, bf16) for w in weights]

    text_shapes = (
        array((tokens, width), bf16),
        array((captions, width), bf16),
        array((captions, width), f32),
        array((captions, width), bf16),
        array((captions, wide), bf16),
        array((tokens, 3 * width), bf16),
        array((tokens, width), bf16),
        array((tokens, width), f32),
        array((tokens, wide), bf16),
        array((width, tokens), bf16),
    )
    text_specs = [in_vmem, in_smem] + [in_vmem] * 4 + [anywhere] * 5
    text_buffers = weight_scratch + [
        pltpu.VMEM((tokens, width), bf16),
        pltpu.VMEM((tokens, wide), bf16),
        pltpu.VMEM((captions, 1), jnp.int32),
        pltpu.VMEM((1, tokens), f32),
        pltpu.SemaphoreType.DMA((5,)),
    ]
    text_in = (text_tokens, text_lengths, *vectors, *weights)
    groups = 4
    group_rows, group_images = image_rows // groups, images // groups
    mix_buffers = [
        pltpu.VMEM((group_rows, width), bf16),
        pltpu.VMEM((group_rows, 3 * width), bf16),
        pltpu.VMEM((group_rows, width), bf16),
    ]
    mix_weights = [pltpu.VMEM((width, 3 * width), bf16), pltpu.VMEM((width, width), bf16)]
    embed_weights = [pltpu.VMEM((width, wide), bf16), pltpu.VMEM((wide, width), bf16)]
    both = ("row", "col")

    if joined:
        halves = 2
        packed = -(-(wide // row_count + width // row_count) // 128) * 128
        shapes = dict(zip(text_names, text_shapes))
        shapes["held_factors"] = array((col_count, row_count, captions, packed), bf16)
        dma = pltpu.SemaphoreType.DMA
        hidden, projected, heads, mixed, mid, slope, turned, factors, embed_grad, loss_part = plain(
            forward_joined_kernel,
            tuple(shapes[name] for name in saved_names) + (array((captions, width), f32), array((1, 128), f32)),
            text_specs + [anywhere, in_vmem, in_vmem] + [anywhere] * 4,
            [pltpu.VMEM(shape.shape, shape.dtype) for shape in text_shapes]
            + text_buffers
            + [pltpu.VMEM((image_rows, width), bf16)]
            + mix_weights
            + embed_weights
            + mix_buffers
            + [
                pltpu.VMEM((image_rows, width), bf16),
                pltpu.VMEM((images, width), f32),
                pltpu.VMEM((images // halves, wide), f32),
                pltpu.VMEM((images, width), bf16),
                pltpu.VMEM((halves, 2, 4, 4, images // halves, width), bf16),
                pltpu.VMEM((row_count, captions, packed), bf16),
                pltpu.VMEM((col_count, row_count, captions, packed), bf16),
                pltpu.VMEM((1, pair_total), f32),
                pltpu.VMEM((count, 1, pair_total), f32),
                dma((len(saved_names),)),
                dma((1,)),
                dma((7,)),
                dma((7, 5)),
                dma((7, 5)),
                dma((1,)),
                dma((row_count + 2,)),
                dma((row_count + 2,)),
                dma((halves, 7)),
                dma((halves, 7)),
                dma((count - 1,)),
                dma((count - 1,)),
            ],
            "forward_joined",
            out_specs=[anywhere] * len(saved_names) + [in_vmem] * 2,
            collective_id=1,
            has_side_effects=True,
        )(*text_in, image_tokens, image_norm_gain, image_norm_bias, image_qkv, image_out, image_up, image_down)
    else:
        (hidden, text_embed, projected, pooled, inner_sum, heads, mixed, mid, slope, turned) = plain(
            text_forward_kernel, text_shapes, text_specs, text_buffers, "text_forward"
        )(*text_in)
        qkv_parts = partners(image_qkv, col_count)
        out_parts = partners(image_out, col_count)
        up_parts = partners(image_up, col_count)
        down_parts = partners(image_down, col_count)
        parts = [anywhere] * (2 * col_count)
        image_normed, image_mean = pl.pallas_call(
            functools.partial(image_mix_kernel, col_count),
            grid=(groups,),
            out_shape=(array((image_rows, width), bf16), array((images, width), f32)),
            in_specs=[
                pl.BlockSpec((group_rows, width), lambda i: (i, 0)),
                whole(image_norm_gain.shape),
                whole(image_norm_bias.shape),
            ]
            + parts,
            out_specs=(
                pl.BlockSpec((group_rows, width), lambda i: (i, 0)),
                pl.BlockSpec((group_images, width), lambda i: (i, 0)),
            ),
            scratch_shapes=mix_weights + mix_buffers + [pltpu.SemaphoreType.DMA((2, col_count))],
            compiler_params=pltpu.CompilerParams(vmem_limit_bytes=VMEM_LIMIT),
            name="image_mix",
        )(image_tokens, image_norm_gain, image_norm_bias, *qkv_parts, *out_parts)
        image_embed = pl.pallas_call(
            functools.partial(image_embed_kernel, col_count),
            grid=(groups,),
            out_shape=array((images, width), bf16),
            in_specs=[pl.BlockSpec((group_rows, width), lambda i: (i, 0)), whole((images, width))] + parts,
            out_specs=whole((images, width)),
            scratch_shapes=embed_weights
            + [pltpu.VMEM((images, wide), f32), pltpu.SemaphoreType.DMA((2, col_count))],
            compiler_params=pltpu.CompilerParams(vmem_limit_bytes=VMEM_LIMIT),
            name="image_embed",
        )(image_normed, image_mean, *up_parts, *down_parts)

        image_all = lax.all_gather(image_embed, both, axis=0, tiled=True)
        lifted = jnp.exp(logit_scale * dot_nt(image_all, text_embed))
        row_sums = lax.psum(jnp.sum(lifted, axis=1), both)
        col_sums = jnp.sum(lifted, axis=0)
        sim_grad = (0.5 * (lifted / row_sums[:, None] + lifted / col_sums[None, :])).astype(bf16)
        image_own = image_embed.astype(f32)
        embed_grad = logit_scale * (dot_tn(sim_grad, image_all) - image_own)
        positives = logit_scale * jnp.sum(image_own * text_embed.astype(f32), axis=1)
        loss_part = 0.5 * jnp.sum(jnp.log(col_sums) - 2.0 * positives)
        loss_part = loss_part + 0.5 * jnp.sum(jnp.log(row_sums)) / count

    saved = (text_tokens, heads, mixed, mid, slope, turned)
    backward_in = (text_lengths, *vectors, embed_grad, projected, *saved, *weights)
    backward_specs = [in_smem] + [in_vmem] * 6 + [anywhere] * 11
    backward_buffers = (
        [
            pltpu.VMEM((tokens, width), bf16),
            pltpu.VMEM((tokens, 3 * width), bf16),
            pltpu.VMEM((tokens, width), bf16),
            pltpu.VMEM((tokens, width), f32),
            pltpu.VMEM((tokens, wide), bf16),
        ]
        + weight_scratch
        + [
            pltpu.VMEM((tokens, width), bf16),
            pltpu.VMEM((width, tokens), bf16),
            pltpu.VMEM((tokens, width), f32),
            pltpu.VMEM((tokens, width), f32),
            pltpu.VMEM((tokens, width), bf16),
            pltpu.VMEM((tokens, width), bf16),
            pltpu.VMEM((tokens, 3 * width), bf16),
            pltpu.VMEM((captions, 1), jnp.int32),
            pltpu.VMEM((1, tokens), f32),
            pltpu.VMEM((tokens, 1), f32),
            pltpu.SemaphoreType.DMA((11,)),
        ]
    )

    def by_row(x):
        x = lax.all_to_all(x, "row", split_axis=1, concat_axis=0, tiled=True)
        return lax.all_gather(x, "col", axis=0, tiled=True)

    def by_col(x):
        x = lax.all_gather(x, "row", axis=0, tiled=True)
        return lax.all_to_all(x, "col", split_axis=1, concat_axis=0, tiled=True)

    if joined:
        out_step, inner_step = width // col_count, wide // row_count
        rows = width // row_count
        up_grad, out_grad, qkv_grad, grad_down, grad_proj, input_grad, norm_total = plain(
            text_backward_joined_kernel,
            (
                array((rows, wide // col_count), f32),
                array((rows, out_step), f32),
                array((rows, 3 * out_step), f32),
                array((out_step, inner_step), f32),
                array((rows, out_step), f32),
                array((tokens, width), bf16),
                array((1, 4 * width + 128), f32),
            ),
            backward_specs + [in_vmem] * 2,
            backward_buffers
            + [buffer for halves in scatter_widths(wide, width, col_count) for buffer in scatter_scratch(rows, halves)]
            + [
                pltpu.VMEM((captions, width), bf16),
                pltpu.VMEM((8, width), f32),
                pltpu.VMEM((col_count, captions, 2 * out_step), bf16),
                pltpu.VMEM((col_count, row_count, captions, 2 * out_step), bf16),
                pltpu.SemaphoreType.DMA((7,)),
                pltpu.SemaphoreType.DMA((7,)),
            ]
            + chip_sum_scratch(2 * width + 128, count // 2)
            + chip_sum_scratch(2 * width, count // 2),
            "text_backward_joined",
            collective_id=3,
            has_side_effects=True,
        )(*backward_in, factors, loss_part)
        large = (hidden, input_grad, qkv_grad, out_grad, up_grad, grad_down, grad_proj)
        results = (array((1, 1), f32), *[array((width,), f32)] * 4, *(array(g.shape, g.dtype) for g in large))
        loss, *rest = plain(
            functools.partial(hand_over_kernel, pair_total), results, [in_vmem] * 8, [], "hand_over"
        )(norm_total, *large)
        norms, (hidden, input_grad, qkv_grad, out_grad, up_grad, grad_down, grad_proj) = rest[:4], rest[4:]
        return (
            loss.reshape(()), hidden, input_grad, *norms, qkv_grad, out_grad, up_grad, grad_down.T, grad_proj,
        )
    else:
        (proj_grad, branch, up_grad, out_grad, qkv_grad, input_grad, norm_grads) = plain(
            text_backward_kernel,
            (
                array((captions, width), bf16),
                array((captions, width), bf16),
                array((col_count, width, wide // col_count), bf16),
                array((col_count, width, width // col_count), bf16),
                array((col_count, width, 3 * width // col_count), bf16),
                array((tokens, width), bf16),
                array((8, width), f32),
            ),
            backward_specs,
            backward_buffers,
            "text_backward",
        )(*backward_in)

        def scattered(matrix):
            blocks = matrix.reshape(count, width // row_count, matrix.shape[2])
            return lax.psum_scatter(blocks, ("col", "row"), scatter_dimension=0, tiled=True)[0].astype(f32)

        up_grad, out_grad, qkv_grad = scattered(up_grad), scattered(out_grad), scattered(qkv_grad)
        grad_down = dot_tn(by_row(inner_sum), by_col(branch))
        grad_proj = dot_tn(by_row(pooled), by_col(proj_grad))
        loss_total, norm_total = lax.psum((loss_part, norm_grads), both)
        norms = [norm_total[i] for i in range(4)]
    mean_loss = loss_total / pair_total
    return (
        mean_loss, hidden, input_grad, *norms, qkv_grad, out_grad, up_grad, grad_down, grad_proj,
    )


def solution(mesh):
    split = P(("row", "col"), None)
    grid = P("row", "col")
    in_specs = (
        split, P(), P(), P("col", None), P("col", None), P("col", None), P("col", None), split, P(("row", "col")),
    ) + (P(),) * 9
    out_specs = (P(), split, split, P(), P(), P(), P(), grid, grid, grid, grid, grid)
    return jax.shard_map(body, mesh=mesh, in_specs=in_specs, out_specs=out_specs, check_vma=False)
```

```python
import functools
import math
from types import SimpleNamespace

import jax
import jax.numpy as jnp
from jax import lax
from jax.experimental import pallas as pl
from jax.experimental.pallas import tpu as pltpu
from jax.sharding import PartitionSpec as P

HEADS = 12
IMG_TOK = 50
norm_eps = 1e-06
logit_scale = 50.0
masked_score = -1e30
log2e = math.log2(math.e)
f32 = jnp.float32
bf16 = jnp.bfloat16
VMEM_LIMIT = 62 * 2**20
MESH = pl.DeviceIdType.MESH


def dot_nn(a, b):
    return lax.dot_general(a, b, (((1,), (0,)), ((), ())), preferred_element_type=f32)


def dot_nt(a, b):
    return lax.dot_general(a, b, (((1,), (1,)), ((), ())), preferred_element_type=f32)


def dot_tn(a, b):
    return lax.dot_general(a, b, (((0,), (0,)), ((), ())), preferred_element_type=f32)


def split_low(x):
    high = x.astype(bf16)
    return high, (x - high.astype(f32)).astype(bf16)


def normed(x):
    centered = x - jnp.mean(x, axis=-1, keepdims=True)
    spread = lax.rsqrt(jnp.mean(centered * centered, axis=-1, keepdims=True) + norm_eps)
    return centered * spread, spread


def layer_norm(x, gain, bias):
    return normed(x)[0] * gain + bias


def gelu(x):
    return x * (0.5 + 0.5 * lax.erf(x * math.sqrt(0.5)))


def gelu_and_slope(x):
    below = 0.5 + 0.5 * lax.erf(x * math.sqrt(0.5))
    bell = jnp.exp2((-0.5 * log2e) * (x * x))
    return x * below, below + x * (bell * (1.0 / math.sqrt(2.0 * math.pi)))


def lane_halves(width):
    lane = lax.broadcasted_iota(jnp.int32, (1, width), 1)
    first = (lane < width // 2).astype(f32)
    return first.astype(bf16), (1.0 - first).astype(bf16)


def stack_heads(x, first, second):
    return jnp.concatenate([x * first, x * second], axis=0)


def join_heads(stacked):
    rows, width = stacked.shape[0] // 2, stacked.shape[1]
    lane = lax.broadcasted_iota(jnp.int32, (rows, width), 1)
    return jnp.where(lane < width // 2, stacked[:rows], stacked[rows:])


def soft_weights(query, key, bias, factor):
    scores = dot_nt(query, key) * (factor * log2e) + bias
    weights = jnp.exp2(scores - jnp.max(scores, axis=-1, keepdims=True))
    return weights, 1.0 / jnp.sum(weights, axis=-1, keepdims=True)


def set_lengths(lengths_ref, lens_ref, key_bias_ref):
    captions, tokens = lens_ref.shape[0], key_bias_ref.shape[1]
    length = tokens // captions
    caption = lax.broadcasted_iota(jnp.int32, (captions, 1), 0)
    token = lax.broadcasted_iota(jnp.int32, (1, tokens), 1)
    column, row = jnp.zeros((captions, 1), jnp.int32), jnp.zeros((1, tokens), jnp.int32)
    for n in range(captions):
        column = jnp.where(caption == n, lengths_ref[n], column)
        row = jnp.where(token // length == n, lengths_ref[n], row)
    lens_ref[...] = column
    key_bias_ref[...] = jnp.where(token % length < row, 0.0, masked_score)


def as_row(ref):
    return ref[...].reshape(1, ref.shape[0])


def text_bias(key_bias_ref, block, rows, length):
    near = lax.broadcasted_iota(jnp.int32, (rows, rows), 0) // length
    far = lax.broadcasted_iota(jnp.int32, (rows, rows), 1) // length
    columns = pl.ds(pl.multiple_of(block * rows, rows), rows)
    bias = jnp.where(near == far, key_bias_ref[:, columns], masked_score)
    return jnp.concatenate([bias, bias], axis=0)


def member(len_ref, captions, tokens):
    length = tokens // captions
    token = lax.broadcasted_iota(jnp.int32, (captions, tokens), 1)
    caption = lax.broadcasted_iota(jnp.int32, (captions, tokens), 0)
    return ((token // length == caption) & (token % length < len_ref[...])).astype(f32)


def spread_rows(x, length):
    rows, width = x.shape
    return jnp.broadcast_to(x[:, None, :], (rows, length, width)).reshape(rows * length, width)


def wide_steps(total, most=768, part=0, parts=1):
    step = math.gcd(total, most)
    count = total // step // parts

    def loop(body):
        @pl.loop(part * count, (part + 1) * count)
        def _(j):
            body(pl.ds(pl.multiple_of(j * step, 128), step))

    return loop


class TextForward:
    band = 128

    def __init__(self, refs):
        for name, ref in refs.items():
            setattr(self, name, ref)
        self.tokens, self.width = self.tok.shape
        self.captions = self.lens.shape[0]
        self.length = self.tokens // self.captions
        self.wide = self.w_up.shape[1]
        pairs = (
            (self.qkv_hbm, self.w_qkv), (self.out_hbm, self.w_out), (self.up_hbm, self.w_up),
            (self.down_hbm, self.w_down),
        )
        self.loads = load_weights(pairs, self.sems)
        self.load_proj = pltpu.make_async_copy(self.proj_hbm, self.w_proj, self.sems.at[4])

    def bands(self, step):
        pl.loop(0, self.tokens // self.band)(
            lambda i: step(pl.ds(pl.multiple_of(i * self.band, self.band), self.band))
        )

    def prepare(self):
        set_lengths(self.lengths, self.lens, self.key_bias)

        def first_norm(rows):
            norm = layer_norm(self.tok[rows, :].astype(f32), as_row(self.gain1), as_row(self.bias1))
            self.norm[rows, :] = norm.astype(bf16)

        self.bands(first_norm)

    def attention(self):
        width = self.width
        self.loads[0].wait()

        @wide_steps(3 * width)
        def _(columns):
            self.heads[:, columns] = dot_nn(self.norm[...], self.w_qkv[:, columns]).astype(bf16)

        first, second = lane_halves(128)
        factor = (width // HEADS) ** -0.5

        @pl.loop(0, self.tokens // self.band)
        def _(block):
            rows = pl.ds(pl.multiple_of(block * self.band, self.band), self.band)
            bias = text_bias(self.key_bias, block, self.band, self.length)
            for at in range(0, width, 128):
                query = stack_heads(self.heads[rows, at : at + 128], first, second)
                key = self.heads[rows, width + at : width + at + 128]
                weights, scale = soft_weights(query, key, bias, factor)
                value = self.heads[rows, 2 * width + at : 2 * width + at + 128]
                mixed = dot_nn(weights.astype(bf16), value) * scale
                self.mixed[rows, at : at + 128] = join_heads(mixed).astype(bf16)

    def middle(self):
        self.loads[1].wait()

        def second_norm(rows):
            mid = self.tok[rows, :].astype(f32) + dot_nn(self.mixed[rows, :], self.w_out[...])
            self.mid[rows, :] = mid
            self.norm[rows, :] = layer_norm(mid, as_row(self.gain2), as_row(self.bias2)).astype(bf16)

        self.bands(second_norm)

    def feed(self, part=0, parts=1):
        if part == 0:
            self.loads[2].wait()
        self.chosen = member(self.lens, self.captions, self.tokens).astype(bf16)
        place = lax.broadcasted_iota(jnp.int32, (self.captions, self.length, 1), 1)
        valid = (place < self.lens[...].reshape(self.captions, 1, 1)).astype(f32).reshape(self.tokens, 1)

        @wide_steps(self.wide, part=part, parts=parts)
        def _(columns):
            value, slope = gelu_and_slope(dot_nn(self.norm[...], self.w_up[:, columns]))
            value = value.astype(bf16)
            self.inner[:, columns] = value
            self.slope[:, columns] = (slope * valid).astype(bf16)
            self.inner_sum[:, columns] = dot_nn(self.chosen, value).astype(bf16)

    def finish(self):
        self.loads[3].wait()
        self.turned[...] = self.norm[...].T
        inverse = 1.0 / self.lens[...].astype(f32)

        @wide_steps(self.width)
        def _(columns):
            state = self.mid[:, columns] + dot_nn(self.inner[...], self.w_down[:, columns])
            self.hidden[:, columns] = state.astype(bf16)
            high, low = split_low(state)
            pooled = (dot_nn(self.chosen, high) + dot_nn(self.chosen, low)) * inverse
            self.pooled[:, columns] = pooled.astype(bf16)

    def embed(self):
        self.load_proj.wait()
        projected = dot_nn(self.pooled[...], self.w_proj[...])
        self.projected[...] = projected
        scale = lax.rsqrt(jnp.sum(projected * projected, axis=-1, keepdims=True) + norm_eps)
        self.text_embed[...] = (projected * scale).astype(bf16)


text_ins = (
    "tok", "lengths", "gain1", "bias1", "gain2", "bias2", "qkv_hbm", "out_hbm", "up_hbm", "down_hbm", "proj_hbm",
)
text_names = (
    "hidden", "text_embed", "projected", "pooled", "inner_sum", "heads", "mixed", "mid", "slope", "turned",
)
text_scratch = ("w_qkv", "w_out", "w_up", "w_down", "w_proj", "norm", "inner", "lens", "key_bias", "sems")


def text_forward_kernel(*refs):
    t = TextForward(dict(zip(text_ins + text_names + text_scratch, refs, strict=True)))
    t.load_proj.start()
    t.prepare()
    t.attention()
    t.middle()
    t.feed()
    t.finish()
    t.embed()


def load_weights(pairs, sems):
    loads = [pltpu.make_async_copy(s, d, sems.at[i]) for i, (s, d) in enumerate(pairs)]
    for load in loads:
        load.start()
    return loads


def spans(count, size):
    return lambda i: pl.ds(pl.multiple_of(i * size, size), size)


def norm_backward(outer, unit, spread, gain):
    outer = outer * gain
    inner = outer - jnp.mean(outer, axis=-1, keepdims=True)
    return spread * (inner - unit * jnp.mean(outer * unit, axis=-1, keepdims=True))


class TextBackward:
    band = 128

    def __init__(self, refs, loads):
        for name, ref in refs.items():
            setattr(self, name, ref)
        self.loads = loads
        self.tokens, self.width = self.tok.shape
        self.captions = self.lens.shape[0]
        self.length = self.tokens // self.captions
        self.wide = self.w_up.shape[1]
        self.pre_grad = self.slope

    def wait(self, name):
        if name in self.loads:
            self.loads[name].wait()

    def rows(self, i):
        return pl.ds(pl.multiple_of(i * self.band, self.band), self.band)

    def bands(self, step):
        pl.loop(0, self.tokens // self.band)(lambda i: step(self.rows(i)))

    def valid(self):
        place = lax.broadcasted_iota(jnp.int32, (self.captions, self.length, 1), 1)
        valid = place < self.lens[...].reshape(self.captions, 1, 1)
        return valid.astype(f32).reshape(self.tokens, 1)

    def project(self):
        projected = self.projected[...]
        embed_grad = self.embed_grad[...]
        r = lax.rsqrt(jnp.sum(projected * projected, axis=-1, keepdims=True) + norm_eps)
        along = jnp.sum(projected * embed_grad, axis=-1, keepdims=True)
        proj_grad = (r * embed_grad - (r * r * r) * projected * along).astype(bf16)
        self.wait("w_proj")
        state_grad = dot_nt(proj_grad, self.w_proj[...]) * (1.0 / self.lens[...].astype(f32))
        self.branch[...] = state_grad.astype(bf16)
        self.mid_grad[...] = spread_rows(state_grad, self.length) * self.valid()
        return proj_grad, self.branch[...]

    def wait_inner(self):
        self.wait("turned")
        self.wait("w_down")
        self.wait("slope")

    def inner_grad(self, columns):
        grad = dot_nt(self.branch[...], self.w_down[columns, :])
        pre_grad = spread_rows(grad, self.length) * self.slope[:, columns].astype(f32)
        self.pre_grad[:, columns] = pre_grad.astype(bf16)

    def up_block(self, columns):
        return dot_nn(self.turned[...], self.pre_grad[:, columns]).astype(bf16)

    def to_middle(self):
        self.wait("w_up")

        @wide_steps(self.width)
        def _(columns):
            self.outer[:, columns] = dot_nt(self.pre_grad[...], self.w_up[columns, :])

    def middle(self):
        self.wait("mid")
        self.norm_grad[...] = jnp.zeros_like(self.norm_grad)

        def through_norm(rows):
            unit, spread = normed(self.mid[rows, :])
            outer = self.outer[rows, :]
            self.norm_grad[2:3, :] += jnp.sum(outer * unit, axis=0, keepdims=True)
            self.norm_grad[3:4, :] += jnp.sum(outer, axis=0, keepdims=True)
            mid_grad = self.mid_grad[rows, :] + norm_backward(outer, unit, spread, as_row(self.gain2))
            self.mid_grad[rows, :] = mid_grad
            self.low_grad[rows, :] = mid_grad.astype(bf16)

        self.bands(through_norm)

    def out_block(self, columns):
        return dot_tn(self.mixed[...], self.low_grad[:, columns]).astype(bf16)

    def to_heads(self):
        self.wait("w_out")
        self.wait("tok")

        def through_out(rows):
            self.mixed_grad[rows, :] = dot_nt(self.low_grad[rows, :], self.w_out[...]).astype(bf16)
            norm = layer_norm(self.tok[rows, :].astype(f32), as_row(self.gain1), as_row(self.bias1))
            self.norm[rows, :] = norm.astype(bf16)

        self.bands(through_out)

    def attention(self, after=lambda block: None):
        first, second = lane_halves(128)
        width = self.width
        factor = (width // HEADS) ** -0.5
        self.wait("heads")
        self.key_column[...] = jnp.broadcast_to((1.0 - self.valid()) * masked_score, self.key_column.shape)

        @pl.loop(0, self.tokens // self.band)
        def _(block):
            rows = self.rows(block)
            near = lax.broadcasted_iota(jnp.int32, (self.band, self.band), 0) // self.length
            far = lax.broadcasted_iota(jnp.int32, (self.band, self.band), 1) // self.length
            bias = jnp.where(near == far, self.key_column[rows, :], masked_score)
            bias = jnp.concatenate([bias, bias], axis=1)
            for at in range(0, width, 128):
                query = stack_heads(self.heads[rows, at : at + 128], first, second)
                key = self.heads[rows, width + at : width + at + 128]
                value = self.heads[rows, 2 * width + at : 2 * width + at + 128]
                grad = stack_heads(self.mixed_grad[rows, at : at + 128], first, second)
                scores = dot_nt(key, query) * (factor * log2e) + bias
                weights = jnp.exp2(scores - jnp.max(scores, axis=0, keepdims=True))
                probs = weights * (1.0 / jnp.sum(weights, axis=0, keepdims=True))
                prob_grad = dot_nt(value, grad)
                total = jnp.sum(prob_grad * probs, axis=0, keepdims=True)
                score_grad = (probs * (prob_grad - total)).astype(bf16)
                query_grad = join_heads(dot_tn(score_grad, key)) * factor
                self.heads_grad[rows, at : at + 128] = query_grad.astype(bf16)
                key_grad = dot_nn(score_grad, query) * factor
                self.heads_grad[rows, width + at : width + at + 128] = key_grad.astype(bf16)
                value_grad = dot_nn(probs.astype(bf16), grad)
                self.heads_grad[rows, 2 * width + at : 2 * width + at + 128] = value_grad.astype(bf16)
            after(block)

    def qkv_block(self, columns):
        return dot_tn(self.norm[...], self.heads_grad[:, columns]).astype(bf16)

    def input(self, between=lambda: None):
        self.wait("w_qkv")

        @wide_steps(self.width)
        def _(columns):
            self.outer[:, columns] = dot_nt(self.heads_grad[...], self.w_qkv[columns, :])

        between()

        def through_norm(rows):
            unit, spread = normed(self.tok[rows, :].astype(f32))
            outer = self.outer[rows, :]
            self.norm_grad[0:1, :] += jnp.sum(outer * unit, axis=0, keepdims=True)
            self.norm_grad[1:2, :] += jnp.sum(outer, axis=0, keepdims=True)
            inner = norm_backward(outer, unit, spread, as_row(self.gain1))
            self.tok[rows, :] = (self.mid_grad[rows, :] + inner).astype(bf16)

        self.bands(through_norm)


backward_ins = (
    "lengths", "gain1", "bias1", "gain2", "bias2", "embed_grad", "projected", "tok_hbm", "heads_hbm", "mixed_hbm",
    "mid_hbm", "slope_hbm", "turned_hbm", "w_qkv_hbm", "w_out_hbm", "w_up_hbm", "w_down_hbm", "w_proj_hbm",
)
backward_outs = ("proj_grad", "branch", "up_grad", "out_grad", "qkv_grad", "input_grad", "norm_grad")
backward_scratch = (
    "tok", "heads", "mixed", "mid", "slope", "w_qkv", "w_out", "w_up", "w_down", "w_proj", "norm", "turned",
    "outer", "mid_grad", "low_grad", "mixed_grad", "heads_grad", "lens", "key_bias", "key_column", "sems",
)


def text_backward_kernel(*refs):
    refs = dict(zip(backward_ins + backward_outs + backward_scratch, refs, strict=True))
    order = ("w_proj", "turned", "w_down", "slope", "w_up", "mid", "mixed", "w_out", "tok", "heads", "w_qkv")
    loads = load_weights([(refs[name + "_hbm"], refs[name]) for name in order], refs["sems"])
    t = TextBackward(refs, dict(zip(order, loads)))
    set_lengths(t.lengths, t.lens, t.key_bias)
    parts = t.up_grad.shape[0]

    def blocks(target, block):
        step = target.shape[2]
        for part in range(parts):
            target[part] = block(slice(part * step, (part + 1) * step))

    t.proj_grad[...] = t.project()[0]
    t.wait_inner()
    wide_steps(t.wide)(t.inner_grad)
    blocks(t.up_grad, t.up_block)
    t.to_middle()
    t.middle()
    t.wait("mixed")
    blocks(t.out_grad, t.out_block)
    t.to_heads()
    t.attention()
    blocks(t.qkv_grad, t.qkv_block)
    t.input()
    t.input_grad[...] = t.tok[...]


class Place:
    def __init__(self, z_count=4, y_count=2, x_count=2, k_count=2):
        self.row, self.col = lax.axis_index("row"), lax.axis_index("col")
        self.z, self.y = self.row // y_count, self.row % y_count
        self.x, self.k = self.col // k_count, self.col % k_count
        self.rows, self.cols = z_count * y_count, x_count * k_count
        self.count = self.rows * self.cols
        self.me = self.row * self.cols + self.col
        self.slot = self.col * self.rows + self.row
        self.near_z, self.far_z = self.z + 1 - 2 * (self.z % 2), (self.z + 2) % 4

    def at(self, **moved):
        z, y, x, k = (moved.get(name, getattr(self, name)) for name in "zyxk")
        return z * 2 + y, x * 2 + k

    def peer(self, distance):
        other = (self.me + distance) % self.count
        return other // self.cols, other % self.cols

    def greet(self):
        barrier = pltpu.get_barrier_semaphore()

        @pl.loop(1, self.count)
        def _(distance):
            pl.semaphore_signal(barrier, inc=1, device_id=self.peer(distance), device_id_type=MESH)

    def meet(self):
        pl.semaphore_wait(pltpu.get_barrier_semaphore(), self.count - 1)


def remote(src, dst, send, recv, to):
    return pltpu.make_async_remote_copy(
        src_ref=src, dst_ref=dst, send_sem=send, recv_sem=recv, device_id=to, device_id_type=MESH
    )


class Gather:
    def __init__(self, place, axis, own, half, block, part, local, sends, recvs):
        here = place.y if axis == "y" else place.z % 2
        mate, next_x = place.at(k=1 - place.k), place.at(x=1 - place.x)
        partner = place.at(y=1 - place.y) if axis == "y" else place.at(z=place.near_z)
        across = next_x[1]
        mine, others = part(across, here), part(across, 1 - here)
        self.local = pltpu.make_async_copy(own, block(place.col), local)
        self.near = remote(own, block(place.col), sends.at[0], recvs.at[0], mate)
        self.far = remote(half(here), part(place.col, here), sends.at[1], recvs.at[1], next_x)
        self.along = remote(mine, mine, sends.at[2], recvs.at[2], partner)
        self.first = remote(mine, mine, sends.at[3], recvs.at[3], mate)
        self.second = remote(others, others, sends.at[4], recvs.at[4], mate)

    def start(self):
        self.far.start()
        self.near.start()
        self.local.start()

    def share(self):
        self.far.wait()
        self.along.start()
        self.first.start()

    def relay(self):
        self.along.wait()
        self.second.start()

    def finish(self):
        self.local.wait()
        self.near.wait()
        self.first.wait()
        self.second.wait()


def wait_all(blocks, send, recv, to):
    remote(blocks, blocks, send, recv, to).wait()


class RowFactors:
    def __init__(self, place, own, held, local, sends, recvs):
        self.place, self.own, self.held, self.sends, self.recvs = place, own, held, sends, recvs
        self.local = pltpu.make_async_copy(own.at[place.row], held.at[place.col, place.row], local)
        mine, across = held.at[place.col], held.at[place.at(x=1 - place.x)[1]]
        mate, next_x = place.at(k=1 - place.k), place.at(x=1 - place.x)
        self.far = remote(mine, mine, sends.at[1], recvs.at[1], next_x)
        self.near = remote(mine, mine, sends.at[2], recvs.at[2], mate)
        self.passed = remote(across, across, sends.at[3], recvs.at[3], mate)

    def start(self):
        self.local.start()
        p = self.place

        @pl.loop(1, p.rows)
        def _(distance):
            row = (p.row + distance) % p.rows
            remote(
                self.own.at[row], self.held.at[p.col, p.row], self.sends.at[0], self.recvs.at[0], (row, p.col)
            ).start()

    def share(self):
        self.local.wait()
        p = self.place
        to = p.at(k=1 - p.k)
        wait_all(self.held.at[p.col, pl.ds(0, p.rows - 1)], self.sends.at[0], self.recvs.at[0], to)
        self.far.start()
        self.near.start()

    def relay(self):
        self.far.wait()
        self.passed.start()

    def finish(self):
        self.near.wait()
        self.passed.wait()


class Exchange:
    def __init__(self, place, source, slots, sends, recvs):
        self.place, self.source, self.slots = place, source, slots
        self.sems = sends.at[0], recvs.at[0]

    def start(self):
        p = self.place

        @pl.loop(1, p.count)
        def _(distance):
            remote(self.source, self.slots.at[p.slot], *self.sems, p.peer(distance)).start()

    def finish(self):
        p = self.place
        wait_all(self.slots.at[pl.ds(0, p.count - 1)], *self.sems, p.at(k=1 - p.k))


class ChipSum:
    def __init__(self, place, total, got, slots, sends, recvs):
        self.place, self.total, self.got, self.slots = place, total, got, slots
        self.sends, self.recvs = sends, recvs
        self.chip, self.chips = place.row * 2 + place.x, place.rows * 2
        self.mate = place.at(k=1 - place.k)

    def near(self):
        return remote(self.total, self.got, self.sends.at[0], self.recvs.at[0], self.mate)

    def start(self):
        self.near().start()

    def spread(self):
        self.near().wait()
        self.total[...] = self.total[...] + self.got[...]
        self.slots[self.chip] = self.total[...]

        @pl.loop(1, self.chips)
        def _(distance):
            other = (self.chip + distance) % self.chips
            to = other // 2, other % 2 * 2 + self.place.k
            remote(self.total, self.slots.at[self.chip], self.sends.at[1], self.recvs.at[1], to).start()

    def finish(self):
        wait_all(self.slots.at[pl.ds(0, self.chips - 1)], self.sends.at[1], self.recvs.at[1], self.mate)
        return jnp.sum(self.slots[...], axis=0)


class GradientScatter:
    def __init__(self, place, straight, halves, held, near, x1, y1, x2, y2, far, sends, recvs):
        self.straight = straight
        self.place, self.held, self.near, self.far = place, held, near, far
        self.x1, self.y1, self.x2, self.y2 = x1, y1, x2, y2
        self.sends, self.recvs = sends, recvs
        self.halves = halves

    def lanes(self, chunk):
        ones, twos = zip(*self.halves[:chunk], (0, 0))
        at_one, at_two = sum(ones), sum(twos)
        at = at_one + at_two
        one, two = self.halves[chunk]
        return (
            pl.ds(at, one + two), pl.ds(at, one), pl.ds(at + one, two), pl.ds(at_one, one), pl.ds(at_two, two)
        )

    def copies(self, chunk, stage):
        p, held = self.place, self.held
        x, y, z, k = p.x, p.y, p.z, p.k
        whole, one, two, part_one, part_two = self.lanes(chunk)

        def copy(n, src, dst, **moved):
            return remote(src, dst, self.sends.at[chunk, n], self.recvs.at[chunk, n], p.at(**moved))

        if stage == 0:
            return [copy(0, held.at[:, 1 - k, :, :, :, whole], self.near.at[:, :, :, :, whole], k=1 - k)]
        if stage == 1:
            copies = []
            if one.size:
                copies.append(copy(1, held.at[1 - x, k, :, :, :, one], self.x1.at[:, :, :, part_one], x=1 - x))
            if two.size:
                copies.append(copy(2, held.at[:, k, :, 1 - y, :, two], self.y1.at[:, :, :, part_two], y=1 - y))
            return copies
        if stage == 2:
            copies = []
            if one.size:
                copies.append(copy(3, held.at[x, k, :, 1 - y, :, one], self.y2.at[:, :, part_one], y=1 - y))
            if two.size:
                copies.append(copy(4, held.at[1 - x, k, :, y, :, two], self.x2.at[:, :, part_two], x=1 - x))
            return copies
        if stage == 3 and self.straight:
            return [
                copy(4 + i, held.at[x, k, (z + i) % 4, y, :, whole], self.far.at[i - 1, :, whole], z=(z + i) % 4)
                for i in range(1, 4)
            ]
        if stage == 3:
            blocks = p.near_z, held.shape[2] - 1 - z
            return [
                copy(5 + i, held.at[x, k, block, y, :, whole], self.far.at[i, :, whole], z=p.near_z)
                for i, block in enumerate(blocks)
            ]
        return [copy(7, held.at[x, k, p.far_z, y, :, whole], self.far.at[2, :, whole], z=p.far_z)]

    def start(self, chunk, stage):
        for copy in self.copies(chunk, stage):
            copy.start()

    def finish(self, chunk, stage):
        for copy in self.copies(chunk, stage):
            copy.wait()
        p, held = self.place, self.held
        x, y, k = p.x, p.y, p.k
        z_count = held.shape[2]
        whole, one, two, part_one, part_two = self.lanes(chunk)

        def add(target, source):
            target[...] = (target[...].astype(f32) + source[...].astype(f32)).astype(bf16)

        if stage == 0:

            @pl.loop(0, z_count)
            def _(z):
                for i in range(2):
                    for j in range(2):
                        add(held.at[i, k, z, j, :, whole], self.near.at[i, z, j, :, whole])

        if stage == 1:

            @pl.loop(0, z_count)
            def _(z):
                for i in range(2):
                    if one.size:
                        add(held.at[x, k, z, i, :, one], self.x1.at[z, i, :, part_one])
                    if two.size:
                        add(held.at[i, k, z, y, :, two], self.y1.at[i, z, :, part_two])

        if stage == 2:

            @pl.loop(0, z_count)
            def _(z):
                if one.size:
                    add(held.at[x, k, z, y, :, one], self.y2.at[z, :, part_one])
                if two.size:
                    add(held.at[x, k, z, y, :, two], self.x2.at[z, :, part_two])

        if stage == 3 and not self.straight:
            add(held.at[x, k, p.far_z, y, :, whole], self.far.at[1, :, whole])

    def step_on(self, chunk, stage):
        self.finish(chunk, stage - 1)
        self.start(chunk, stage)

    def total(self):
        p = self.place
        total = self.held[p.x, p.k, p.z, p.y, :, : self.far.shape[2]].astype(f32)
        for i in (0, 1, 2) if self.straight else (0, 2):
            total = total + self.far[i].astype(f32)
        return total


def chip_sum_scratch(size, chips):
    return [
        pltpu.VMEM((1, size), f32), pltpu.VMEM((1, size), f32), pltpu.VMEM((chips, 1, size), f32),
        pltpu.SemaphoreType.DMA((2,)), pltpu.SemaphoreType.DMA((2,)),
    ]


def scatter_scratch(rows, halves):
    one, two = (sum(widths) for widths in zip(*halves))
    spare = max(two, 128)
    shapes = [
        (2, 2, 4, 2, rows, one + two), (2, 4, 2, rows, one + two), (4, 2, rows, one), (2, 4, rows, spare),
        (4, rows, spare), (4, rows, one), (3, rows, one + two),
    ]
    return [pltpu.VMEM(shape, bf16) for shape in shapes] + [pltpu.SemaphoreType.DMA((len(halves), 8))] * 2


class ColFactors:
    def __init__(self, place, own, held, sends, recvs):
        self.place, self.own, self.held, self.sends, self.recvs = place, own, held, sends, recvs

    def copies(self, stage):
        p, held = self.place, self.held

        def copy(n, src, dst, **moved):
            return remote(src, dst, self.sends.at[n], self.recvs.at[n], p.at(**moved))

        if stage == 0:
            mine = held.at[p.col, p.row]
            moves = ({"x": 1 - p.x}, {"k": 1 - p.k}, {"x": 1 - p.x, "k": 1 - p.k})
            return [copy(i, self.own.at[p.at(**move)[1]], mine, **move) for i, move in enumerate(moves)]
        if stage == 1:
            mine = held.at[:, p.row]
            return [copy(3, mine, mine, y=1 - p.y)]
        mine, other = (held.at[:, pl.ds(z * 2, 2)] for z in (p.z, p.far_z))
        if stage == 2:
            return [copy(4, mine, mine, z=p.far_z)]
        return [copy(5, mine, mine, z=p.near_z), copy(6, other, other, z=p.near_z)]

    def start(self, stage):
        for copy in self.copies(stage):
            copy.start()

    def finish(self, stage):
        for copy in self.copies(stage):
            copy.wait()


def scatter_widths(wide, width, cols):
    ups = tuple((128, 128) for _ in range(wide // cols // 256))
    rest = 4 * width // cols - 128
    return ups, ((128, 0),), ((128, 128), (128, 128), (rest - 512, 0))


scatter_names = ("x2", "y2", "far", "sends", "recvs")
total_names = ("total", "got", "slots", "sends", "recvs")


def hand_over_kernel(pair_total, norms, *refs):
    sources, (loss, *vectors), targets = refs[:7], refs[7:12], refs[12:]
    width = vectors[0].shape[0]
    loss[...] = norms[:, 4 * width : 4 * width + 1] * (1.0 / pair_total)
    for i, vector in enumerate(vectors):
        vector[...] = norms[:, i * width : (i + 1) * width].reshape(width)
    for source, target in zip(sources, targets, strict=True):
        target[...] = source[...]


def group_mean(images, rows):
    token = lax.broadcasted_iota(jnp.int32, (images, rows), 1)
    image = lax.broadcasted_iota(jnp.int32, (images, rows), 0)
    inside = (token >= image * IMG_TOK) & (token < (image + 1) * IMG_TOK)
    return inside.astype(f32).astype(bf16)


def load_parts(parts, target, sems, col, col_count):
    depth = target.shape[0] // col_count
    copies = []
    for k, part in enumerate(parts):
        place = pl.multiple_of((col ^ k) * depth, depth)
        copies.append(pltpu.make_async_copy(part, target.at[pl.ds(place, depth)], sems.at[k]))
    return copies


def image_mix(tokens, gain_ref, bias_ref, qkv_block, between, out_weight, norm_ref, heads_ref, mixed_ref):
    rows, width = tokens.shape
    images = rows // IMG_TOK
    norm_ref[...] = layer_norm(tokens.astype(f32), gain_ref[0:1, :], bias_ref[0:1, :]).astype(bf16)

    @pl.loop(0, 3)
    def _(j):
        columns = pl.ds(pl.multiple_of(j * width, width), width)
        heads_ref[:, columns] = dot_nn(norm_ref[...], qkv_block(j)).astype(bf16)

    between()
    first, second = lane_halves(128)
    factor = (width // HEADS) ** -0.5
    window = 112

    @pl.loop(0, images // 2)
    def _(pair):
        start = pair * (2 * IMG_TOK)
        low = pl.multiple_of(start // 16 * 16, 16)
        near = lax.broadcasted_iota(jnp.int32, (window, window), 0) + low
        far = lax.broadcasted_iota(jnp.int32, (window, window), 1) + low
        same = (near >= start) & (near < start + 2 * IMG_TOK) & (far >= start) & (far < start + 2 * IMG_TOK)
        same = same & ((near >= start + IMG_TOK) == (far >= start + IMG_TOK))
        bias = jnp.where(same, 0.0, masked_score)
        bias = jnp.concatenate([bias, bias], axis=0)
        keep = lax.broadcasted_iota(jnp.int32, (16, 128), 0) + low < start
        span, head, tail = pl.ds(low, window), pl.ds(low, 16), pl.ds(low + 16, window - 16)
        for at in range(0, width, 128):
            query = stack_heads(heads_ref[span, at : at + 128], first, second)
            key = heads_ref[span, width + at : width + at + 128]
            weights, scale = soft_weights(query, key, bias, factor)
            value = heads_ref[span, 2 * width + at : 2 * width + at + 128]
            mixed = join_heads(dot_nn(weights.astype(bf16), value) * scale)
            former = mixed_ref[head, at : at + 128].astype(f32)
            mixed_ref[head, at : at + 128] = jnp.where(keep, former, mixed[:16]).astype(bf16)
            mixed_ref[tail, at : at + 128] = mixed[16:].astype(bf16)

    mid = tokens.astype(f32) + dot_nn(mixed_ref[...], out_weight())
    high, low = split_low(mid)
    select = group_mean(images, rows)
    mean = (dot_nn(select, high) + dot_nn(select, low)) * (1.0 / IMG_TOK)
    return layer_norm(mid, gain_ref[1:2, :], bias_ref[1:2, :]).astype(bf16), mean


def image_mix_kernel(col_count, tok_ref, gain_ref, bias_ref, *refs):
    qkv_parts, out_parts = refs[:col_count], refs[col_count : 2 * col_count]
    normed_ref, mean_ref, w_qkv, w_out, *buffers, sems = refs[2 * col_count :]
    col = lax.axis_index("col")

    @pl.when(pl.program_id(0) == 0)
    def _():
        copies = load_parts(qkv_parts, w_qkv, sems.at[0], col, col_count)
        copies += load_parts(out_parts, w_out, sems.at[1], col, col_count)
        for copy in copies:
            copy.start()
        for copy in copies:
            copy.wait()

    width = tok_ref.shape[1]

    def qkv_block(j):
        return w_qkv[:, pl.ds(pl.multiple_of(j * width, width), width)]

    normed_ref[...], mean_ref[...] = image_mix(
        tok_ref[...], gain_ref, bias_ref, qkv_block, lambda: None, lambda: w_out[...], *buffers
    )


def image_embed_kernel(col_count, normed_ref, mean_ref, *refs):
    up_parts, down_parts = refs[:col_count], refs[col_count : 2 * col_count]
    embed_ref, w_up, w_down, sum_ref, sems = refs[2 * col_count :]
    rows, width = normed_ref.shape
    images = rows // IMG_TOK
    wide = w_up.shape[1]
    step = pl.program_id(0)
    col = lax.axis_index("col")
    downs = load_parts(down_parts, w_down, sems.at[1], col, col_count)

    @pl.when(step == 0)
    def _():
        ups = load_parts(up_parts, w_up, sems.at[0], col, col_count)
        for copy in ups + downs:
            copy.start()
        for copy in ups:
            copy.wait()

    select = group_mean(images, rows)

    @wide_steps(wide)
    def _(columns):
        inner = gelu(dot_nn(normed_ref[...], w_up[:, columns])).astype(bf16)
        sum_ref[pl.ds(pl.multiple_of(step * images, images), images), columns] = dot_nn(select, inner)

    @pl.when(step == pl.num_programs(0) - 1)
    def _():
        for copy in downs:
            copy.wait()
        high, low = split_low(sum_ref[...] * (1.0 / IMG_TOK))
        pooled = mean_ref[...] + dot_nn(high, w_down[...]) + dot_nn(low, w_down[...])
        embed_ref[...] = (
            pooled * lax.rsqrt(jnp.sum(pooled * pooled, axis=-1, keepdims=True) + norm_eps)
        ).astype(bf16)


joined_ins = (
    "lengths", "gain1", "bias1", "gain2", "bias2", "image_gain", "image_bias", "tok_hbm", "qkv_hbm", "out_hbm",
    "up_hbm", "down_hbm", "proj_hbm", "image_hbm", "image_qkv_hbm", "image_out_hbm", "image_up_hbm",
    "image_down_hbm",
)
joined_outs = (
    "up_out", "out_out", "qkv_out", "down_out", "proj_out", "norm_out", "hidden_out", "input_out", "slope_out",
)


def joined_kernel(names, *refs):
    refs = dict(zip(joined_ins + joined_outs + names, refs, strict=True))
    tok_load = pltpu.make_async_copy(refs["tok_hbm"], refs["tok"], refs["tok_sems"].at[2])
    tok_load.start()
    t = TextForward(refs)
    place = Place()
    place.greet()
    groups, group_rows = t.image_hbm.shape[0] // t.image_tok.shape[1], t.image_tok.shape[1]
    group_images = group_rows // IMG_TOK
    width, cols = t.width, place.cols

    def load_group(group):
        span = pl.ds(pl.multiple_of(group * group_rows, 16), group_rows)
        slot = group % 2
        return pltpu.make_async_copy(t.image_hbm.at[span], t.image_tok.at[slot], t.tok_sems.at[slot])

    load_group(0).start()
    piece_count = iter(range(t.local.shape[0]))

    def gather(axis, own, half, block, part):
        i = next(piece_count)
        return Gather(place, axis, own, half, block, part, t.local.at[i], t.sends.at[i], t.recvs.at[i])

    def gather_columns(axis, shard, at, target):
        lanes = pl.ds(at, target.shape[-1])
        return gather(
            axis, shard.at[:, :, lanes], lambda half: shard.at[half, :, lanes],
            lambda col: target.at[col], lambda col, half: target.at[col, half],
        )

    qkv_pieces = [gather_columns("y", t.image_qkv_hbm, j * width, t.iw_qkv.at[j]) for j in range(3)]
    out_piece = gather(
        "z", t.image_out_hbm, lambda half: t.image_out_hbm.at[half],
        lambda col: t.iw_out.at[col // 2, pl.ds(col % 2 * 2, 2)],
        lambda col, half: t.iw_out.at[col // 2, col % 2 * 2 + half],
    )
    up_pieces = [
        gather_columns("yzyz"[j], t.image_up_hbm, j * width, t.iw_up.at[j // 2, j % 2]) for j in range(4)
    ]

    def gather_down(axis, lanes):
        return gather(
            axis, t.image_down_hbm.at[:, :, :, lanes],
            lambda half: t.image_down_hbm.at[pl.ds(half * 2, 2), :, :, lanes],
            lambda col: t.iw_down.at[col // 2, col % 2, :, :, :, lanes],
            lambda col, half: t.iw_down.at[col // 2, col % 2, pl.ds(half * 2, 2), :, :, lanes],
        )

    down_pieces = [gather_down("yz"[j], pl.ds(j * width // 2, width // 2)) for j in range(2)]

    def each(pieces, step):
        for piece in pieces:
            getattr(piece, step)()

    factors, pooled_factors = (
        RowFactors(
            place, getattr(t, "own" + tag), getattr(t, "held" + tag), t.factor_local.at[i], t.factor_sends.at[i],
            t.factor_recvs.at[i],
        )
        for i, tag in enumerate(("_inner", "_pooled"))
    )
    saves = {
        name: pltpu.make_async_copy(refs[name], refs[name + "_out"], t.save_sems.at[i])
        for i, name in enumerate(("hidden", "slope"))
    }
    tok_load.wait()
    t.prepare()
    place.meet()
    each(qkv_pieces, "start")
    out_piece.start()
    t.attention()
    qkv_pieces[0].share()
    t.middle()
    t.feed(0, 4)
    qkv_pieces[1].share()
    t.feed(1, 4)
    qkv_pieces[2].share()
    t.feed(2, 4)
    out_piece.share()
    each(up_pieces, "start")
    t.feed(3, 4)
    saves["slope"].start()
    inner_step = t.wide // place.rows
    for row in range(place.rows):
        t.own_inner[row] = t.inner_sum[:, row * inner_step : (row + 1) * inner_step]
    each(qkv_pieces, "relay")
    each(qkv_pieces, "finish")
    saves["slope"].wait()

    image_norm, image_mixed = t.w_out.at[pl.ds(0, group_rows)], t.w_proj.at[pl.ds(0, group_rows)]
    image_heads = t.w_qkv.at[pl.ds(0, group_rows)]

    def normed_group(group):
        return t.slope.at[pl.ds(0, group_rows), pl.ds(pl.multiple_of(group * width, 128), width)]

    @pl.loop(0, groups)
    def _(group):
        @pl.when(group + 1 < groups)
        def _():
            load_group(group + 1).start()

        load_group(group).wait()

        def between():
            pl.when(group == 0)(out_piece.relay)
            pl.when(group == groups - 1)(lambda: each(down_pieces, "share"))

        def out_weight():
            @pl.when(group == 0)
            def _():
                out_piece.finish()
                factors.start()

            return t.iw_out[...].reshape(width, width)

        normed2, mean = image_mix(
            t.image_tok[group % 2], t.image_gain, t.image_bias, lambda j: t.iw_qkv[j].reshape(width, width), between,
            out_weight, image_norm, image_heads, image_mixed,
        )
        normed_group(group)[...] = normed2
        t.image_mean[pl.ds(pl.multiple_of(group * group_images, 8), group_images), :] = mean

        @pl.when(group == 0)
        def _():
            each(down_pieces, "start")

        @pl.when(group == 1)
        def _():
            each(up_pieces, "share")

        @pl.when(group == 2)
        def _():
            each(up_pieces, "relay")

    again = (("w_out", t.out_hbm), ("w_qkv", t.qkv_hbm), ("slope", t.slope_out))
    again = {
        name: pltpu.make_async_copy(source, refs[name], t.again_sems.at[i]) for i, (name, source) in enumerate(again)
    }
    t.load_proj.start()
    again["w_out"].start()
    again["w_qkv"].start()
    each(up_pieces, "finish")

    halves, half_images = 2, t.own.shape[0] // 2
    half_groups = half_images // group_images
    corner = place.y * 2 + place.x

    def image_copies(half, stage):
        mine = t.near_qkv.at[half, corner, place.k, pl.ds(0, 4 * half_images)]
        own = mine.at[pl.ds(pl.multiple_of(place.z * half_images, 16), half_images)]

        def copy(n, block, **moved):
            return remote(block, block, t.image_sends.at[half, n], t.image_recvs.at[half, n], place.at(**moved))

        if stage == 0:
            return [copy(i - 1, own, z=(place.z + i) % 4) for i in range(1, 4)]
        if stage == 1:
            moves = ({"x": 1 - place.x}, {"y": 1 - place.y}, {"x": 1 - place.x, "y": 1 - place.y})
            return [copy(3 + i, mine, **move) for i, move in enumerate(moves)]
        held = t.near_qkv.at[half, :, place.k, pl.ds(0, 4 * half_images)]
        return [copy(6, held, k=1 - place.k)]

    def image_start(half, stage):
        for copy in image_copies(half, stage):
            copy.start()

    def image_finish(half, stage):
        for copy in image_copies(half, stage):
            copy.wait()

    select = group_mean(half_images, half_images * IMG_TOK)

    def image_feed(half, part):
        @pl.loop(part * 2, part * 2 + 2)
        def _(j):
            weight = t.iw_up[j // 2, j % 2].reshape(width, width)
            total = 0.0
            for group in range(half_groups):
                at = (half * half_groups + group) * width
                inner = gelu(dot_nn(t.slope[:group_rows, at : at + width], weight)).astype(bf16)
                total = total + dot_nn(select[:, group * group_rows : (group + 1) * group_rows], inner)
            t.sums[:, pl.ds(pl.multiple_of(j * width, 128), width)] = total

    for half in range(halves):
        image_feed(half, 0)
        if half == 0:
            each(down_pieces, "relay")
        else:
            image_finish(half - 1, 0)
            image_start(half - 1, 1)
        image_feed(half, 1)
        if half == 0:
            each(down_pieces, "finish")
            factors.share()
        else:
            again["slope"].start()
        high, low = split_low(t.sums[...] * (1.0 / IMG_TOK))
        pooled = dot_nn(jnp.concatenate([high, low], axis=0), t.iw_down[...].reshape(t.wide, width))
        part = slice(half * half_images, (half + 1) * half_images)
        pooled = t.image_mean[part, :] + pooled[:half_images] + pooled[half_images:]
        embed = pooled * lax.rsqrt(jnp.sum(pooled * pooled, axis=-1, keepdims=True) + norm_eps)
        t.own[part, :] = embed.astype(bf16)
        span = pl.ds(pl.multiple_of(place.z * half_images, 16), half_images)
        t.near_qkv[half, corner, place.k, span] = embed.astype(bf16)
        image_start(half, 0)

    factors.relay()
    t.finish()
    saves["hidden"].start()
    image_finish(halves - 1, 0)
    image_start(halves - 1, 1)
    image_finish(0, 1)
    image_start(0, 2)
    t.embed()
    width_step = width // place.rows
    pooled = t.pooled[...]
    spare = jnp.zeros((t.captions, t.own_pooled.shape[2] - width_step), bf16)
    for row in range(place.rows):
        block = pooled[:, row * width_step : (row + 1) * width_step]
        t.own_pooled[row] = jnp.concatenate([block, spare], axis=1)
    factors.finish()
    image_finish(halves - 1, 1)
    image_start(halves - 1, 2)
    for half in range(halves):
        image_finish(half, 2)

    images = t.near_qkv[:, :, :, : 4 * half_images].reshape(-1, width)
    own = t.own[...].astype(f32)
    lifted = jnp.exp2(dot_nt(t.text_embed[...], images) * (logit_scale * log2e))
    t.own_sums[...] = jnp.sum(lifted, axis=0, keepdims=True)
    t.all_sums[place.slot] = t.own_sums[...]
    sums = Exchange(place, t.own_sums, t.all_sums, t.sum_sends, t.sum_recvs)
    sums.start()
    col_sums = jnp.sum(lifted, axis=1, keepdims=True)
    positives = logit_scale * jnp.sum(own * t.text_embed[...].astype(f32), axis=(0, 1), keepdims=True)
    logs = jnp.sum(jnp.log(col_sums), axis=(0, 1), keepdims=True)
    saves["hidden"].wait()
    pooled_factors.start()
    sums.finish()
    row_sums = jnp.sum(t.all_sums[...], axis=0)
    sim_grad = (0.5 * (lifted * (1.0 / row_sums) + lifted * (1.0 / col_sums))).astype(bf16)
    t.embed_grad[...] = logit_scale * (dot_nn(sim_grad, images) - own)
    logs = logs + jnp.sum(jnp.log(row_sums), axis=(0, 1), keepdims=True) * (1.0 / place.count)
    t.loss[...] = jnp.broadcast_to(0.5 * logs - positives, t.loss.shape)

    shared = {
        "low_grad": t.inner.at[:, pl.ds(3 * width, width)], "heads_grad": t.inner.at[:, pl.ds(0, 3 * width)],
        "mixed_grad": t.hidden, "key_column": t.outer.at[:, pl.ds(0, 128)],
    }
    backward(place, TextBackward(refs | shared, again), pooled_factors)


def backward(place, t, pooled_factors):
    width, cols = t.width, place.cols
    widths = scatter_widths(t.wide, width, cols)
    shared = {
        "_up": (
            t.iw_up, t.iw_qkv.at[pl.ds(0, 2)], t.iw_qkv.at[2, :, :, :, pl.ds(0, 384)], t.iw_out.at[:, :, :, pl.ds(0, 384)]
        ),
        "_qkv": (
            t.iw_down, t.near_qkv, t.iw_qkv.at[2, :, :, :, pl.ds(384, 384)], t.iw_out.at[:, :, :, pl.ds(384, 384)]
        ),
        "_outs": (
            t.iw_down.at[:, :, :, :, :, pl.ds(640, 128)], t.near_qkv.at[:, :, :, :, pl.ds(640, 128)],
            t.x1_outs, t.y1_outs,
        ),
    }
    up, out, qkv = (
        GradientScatter(
            place, tag == "_qkv", halves, *shared[tag], *(getattr(t, name + tag) for name in scatter_names)
        )
        for halves, tag in zip(widths, ("_up", "_outs", "_qkv"))
    )
    factors = ColFactors(place, t.own_cols, t.held_cols, t.col_sends, t.col_recvs)
    late, last = (
        ChipSum(place, *(getattr(t, name + tag) for name in total_names)) for tag in ("_late", "_last")
    )

    left = []

    def leave(name, ref):
        left.append(pltpu.make_async_copy(ref, getattr(t, name + "_out"), t.leave_sems.at[len(left)]))
        left[-1].start()

    def store(scatter, part, at, value):
        held = scatter.held
        size = value.shape[1]
        held[part // 2, part % 2, :, :, :, at : at + size] = value.reshape(*held.shape[2:5], size)

    def fill(scatter, chunk, total, block):
        at, size = scatter.lanes(chunk)[0].start, scatter.lanes(chunk)[0].size
        true = min(size, total // cols - at)
        for part in range(cols):
            start = part * (total // cols) + at
            store(scatter, part, at, block(slice(start, start + true)))

    def fill_up(chunk, between=lambda: None):
        at = up.lanes(chunk)[0].start
        size = up.lanes(chunk)[0].size
        for part in range(cols):
            start = part * up.held.shape[5] + at
            t.inner_grad(pl.ds(start, size))
        between()
        fill(up, chunk, t.wide, t.up_block)
        up.start(chunk, 0)

    proj_grad, branch = t.project()
    out_step = width // cols
    for part in range(cols):
        columns = slice(part * out_step, (part + 1) * out_step)
        t.own_cols[part] = jnp.concatenate([branch[:, columns], proj_grad[:, columns]], axis=1)
    t.held_cols[place.col, place.row] = t.own_cols[place.col]
    factors.start(0)
    pooled_factors.share()
    t.wait("slope")
    fill_up(0)
    fill_up(1)
    up.step_on(0, 1)
    fill_up(2)
    up.step_on(1, 1)
    factors.finish(0)
    factors.start(1)
    t.to_middle()
    up.step_on(2, 1)
    up.step_on(0, 2)
    t.middle()
    factors.finish(1)
    factors.start(2)
    pooled_factors.relay()
    for part in range(cols):
        value = t.out_block(slice(part * out_step, (part + 1) * out_step))
        store(out, part, 0, value[:, :128])
        store(qkv, part, 3 * out_step, value[:, 128:])
    out.start(0, 0)
    t.total_late[...] = jnp.concatenate([t.norm_grad[2:3, :], t.norm_grad[3:4, :], t.loss[...]], axis=1)
    late.start()
    t.to_heads()
    up.step_on(1, 2)
    out.step_on(0, 1)
    late.spread()

    def after(block):
        @pl.when(block == 0)
        def _():
            up.step_on(2, 2)

        @pl.when(block == 1)
        def _():
            up.step_on(0, 3)

        @pl.when(block == 2)
        def _():
            factors.finish(2)
            factors.start(3)
            up.step_on(1, 3)

    t.attention(after)
    fill(qkv, 0, 3 * width, t.qkv_block)
    qkv.start(0, 0)
    fill(qkv, 1, 3 * width, t.qkv_block)
    qkv.start(1, 0)
    qkv.step_on(0, 1)
    out.step_on(0, 2)
    fill(qkv, 2, 3 * width, t.qkv_block)
    qkv.start(2, 0)
    qkv.step_on(1, 1)
    up.step_on(2, 3)
    up.step_on(0, 4)

    def between():
        qkv.step_on(2, 1)
        up.step_on(1, 4)

    t.input(between)
    leave("input", t.tok)
    t.total_last[...] = jnp.concatenate([t.norm_grad[0:1, :], t.norm_grad[1:2, :]], axis=1)
    last.start()
    qkv.step_on(0, 2)
    out.step_on(0, 3)
    up.step_on(2, 4)
    last.spread()
    factors.finish(3)
    pooled_factors.finish()
    col_factors = t.held_cols[...].reshape(-1, t.held_cols.shape[3])
    grown = dot_tn(col_factors, t.held_inner[...].reshape(-1, t.held_inner.shape[3]))
    t.down[...] = grown[:out_step]
    leave("down", t.down)
    grown = dot_tn(col_factors, t.held_pooled[...].reshape(-1, t.held_pooled.shape[3]))
    t.proj[...] = grown[out_step:].T[: width // place.rows]
    leave("proj", t.proj)
    qkv.step_on(1, 2)
    out.step_on(0, 4)
    qkv.step_on(0, 3)
    qkv.step_on(2, 2)
    t.norms[:, 2 * width :] = late.finish()
    qkv.step_on(1, 3)
    qkv.step_on(2, 3)
    for chunk in range(len(up.halves)):
        up.finish(chunk, 4)
    t.up[...] = up.total()
    leave("up", t.up)
    t.norms[:, : 2 * width] = last.finish()
    leave("norm", t.norms)
    out.finish(0, 4)
    t.out[:, :128] = out.total()
    for chunk in range(len(qkv.halves)):
        qkv.finish(chunk, 3)
    total = qkv.total()
    t.qkv[...] = total[:, : 3 * out_step]
    leave("qkv", t.qkv)
    t.out[:, 128:] = total[:, 3 * out_step : 4 * out_step - 128]
    leave("out", t.out)
    for copy in left:
        copy.wait()


def whole(shape):
    return pl.BlockSpec(shape, lambda *_: (0,) * len(shape))


in_vmem = pl.BlockSpec(memory_space=pltpu.VMEM)
in_smem = pl.BlockSpec(memory_space=pltpu.SMEM)
anywhere = pl.BlockSpec(memory_space=pl.ANY)


def plain(kernel, outs, ins, scratch, name, out_specs=None, **settings):
    return pl.pallas_call(
        kernel,
        out_shape=outs,
        in_specs=ins,
        out_specs=out_specs or [in_vmem] * len(outs),
        scratch_shapes=scratch,
        compiler_params=pltpu.CompilerParams(vmem_limit_bytes=VMEM_LIMIT, **settings),
        name=name,
    )


def array(shape, dtype):
    return jax.ShapeDtypeStruct(shape, dtype)


def partners(x, col_count):
    order = [(i, i ^ 2) for i in range(col_count)]
    near = [(i, i ^ 1) for i in range(col_count)]
    far = lax.ppermute(x, "col", order)
    return [x, lax.ppermute(x, "col", near), far, lax.ppermute(far, "col", near)]


def body(
    image_tokens, image_norm_gain, image_norm_bias, image_qkv, image_out, image_up, image_down,
    text_tokens, text_lengths, norm1_gain, norm1_bias, norm2_gain, norm2_bias,
    text_qkv, text_out, text_up, text_down, text_proj,
):
    tokens, width = text_tokens.shape
    captions = text_lengths.shape[0]
    length = tokens // captions
    wide = text_up.shape[1]
    row_count, col_count = lax.axis_size("row"), lax.axis_size("col")
    row, col = lax.axis_index("row"), lax.axis_index("col")
    pair_total = captions * row_count * col_count
    image_rows, images = image_tokens.shape[0], image_tokens.shape[0] // IMG_TOK

    count = row_count * col_count
    joined = (row_count, col_count) == (8, 4)
    vectors = (norm1_gain, norm1_bias, norm2_gain, norm2_bias)
    weights = (text_qkv, text_out, text_up, text_down, text_proj)
    weight_scratch = [pltpu.VMEM(w.shape, bf16) for w in weights]

    text_shapes = (
        array((tokens, width), bf16),
        array((captions, width), bf16),
        array((captions, width), f32),
        array((captions, width), bf16),
        array((captions, wide), bf16),
        array((tokens, 3 * width), bf16),
        array((tokens, width), bf16),
        array((tokens, width), f32),
        array((tokens, wide), bf16),
        array((width, tokens), bf16),
    )
    text_specs = [in_vmem, in_smem] + [in_vmem] * 4 + [anywhere] * 5
    text_buffers = weight_scratch + [
        pltpu.VMEM((tokens, width), bf16),
        pltpu.VMEM((tokens, wide), bf16),
        pltpu.VMEM((captions, 1), jnp.int32),
        pltpu.VMEM((1, tokens), f32),
        pltpu.SemaphoreType.DMA((5,)),
    ]
    text_in = (text_tokens, text_lengths, *vectors, *weights)
    groups = 4
    group_rows, group_images = image_rows // groups, images // groups
    mix_buffers = [
        pltpu.VMEM((group_rows, width), bf16),
        pltpu.VMEM((group_rows, 3 * width), bf16),
        pltpu.VMEM((group_rows, width), bf16),
    ]
    mix_weights = [pltpu.VMEM((width, 3 * width), bf16), pltpu.VMEM((width, width), bf16)]
    embed_weights = [pltpu.VMEM((width, wide), bf16), pltpu.VMEM((wide, width), bf16)]
    both = ("row", "col")

    if joined:
        halves, rows = 2, width // row_count
        out_step, inner_step = width // col_count, wide // row_count
        packed = -(-rows // 128) * 128
        dma = pltpu.SemaphoreType.DMA
        widths = scatter_widths(wide, width, col_count)
        sets = {tag: scatter_scratch(rows, each) for each, tag in zip(widths, ("_up", "_outs", "_qkv"))}
        scratch = dict(zip(text_names, (pltpu.VMEM(shape.shape, shape.dtype) for shape in text_shapes)))
        scratch |= dict(zip(text_scratch, text_buffers))
        scratch |= {
            "tok": pltpu.VMEM((tokens, width), bf16),
            "iw_qkv": pltpu.VMEM((3, 4, 2, rows, width), bf16),
            "iw_out": pltpu.VMEM((2, 4, rows, width), bf16),
            "iw_up": pltpu.VMEM((2, 2, 4, 2, rows, width), bf16),
            "iw_down": pltpu.VMEM((2, 2, 4, 2, rows, width), bf16),
            "image_tok": pltpu.VMEM((2, group_rows, width), bf16),
            "image_mean": pltpu.VMEM((images, width), f32),
            "sums": pltpu.VMEM((images // halves, wide), f32),
            "own": pltpu.VMEM((images, width), bf16),
            "own_inner": pltpu.VMEM((row_count, captions, inner_step), bf16),
            "held_inner": pltpu.VMEM((col_count, row_count, captions, inner_step), bf16),
            "own_pooled": pltpu.VMEM((row_count, captions, packed), bf16),
            "held_pooled": pltpu.VMEM((col_count, row_count, captions, packed), bf16),
            "up": pltpu.VMEM((rows, wide // col_count), f32),
            "out": pltpu.VMEM((rows, out_step), f32),
            "qkv": pltpu.VMEM((rows, 3 * out_step), f32),
            "down": pltpu.VMEM((out_step, inner_step), f32),
            "proj": pltpu.VMEM((rows, out_step), f32),
            "norms": pltpu.VMEM((1, 4 * width + 128), f32),
            "leave_sems": dma((7,)),
            "own_sums": pltpu.VMEM((1, pair_total), f32),
            "all_sums": pltpu.VMEM((count, 1, pair_total), f32),
            "tok_sems": dma((3,)),
            "again_sems": dma((3,)),
            "save_sems": dma((2,)),
            "local": dma((10,)),
            "sends": dma((10, 5)),
            "recvs": dma((10, 5)),
            "factor_local": dma((2,)),
            "factor_sends": dma((2, 4)),
            "factor_recvs": dma((2, 4)),
            "image_sends": dma((halves, 7)),
            "image_recvs": dma((halves, 7)),
            "sum_sends": dma((1,)),
            "sum_recvs": dma((1,)),
            "embed_grad": pltpu.VMEM((captions, width), f32),
            "loss": pltpu.VMEM((1, 128), f32),
            "branch": pltpu.VMEM((captions, width), bf16),
            "norm_grad": pltpu.VMEM((8, width), f32),
            "outer": pltpu.VMEM((tokens, width), f32),
            "mid_grad": pltpu.VMEM((tokens, width), f32),
            "near_qkv": pltpu.VMEM((2, 4, 2, rows, width), bf16),
            "own_cols": pltpu.VMEM((col_count, captions, 2 * out_step), bf16),
            "held_cols": pltpu.VMEM((col_count, row_count, captions, 2 * out_step), bf16),
            "col_sends": dma((7,)),
            "col_recvs": dma((7,)),
        }
        scratch |= dict(zip(("x1_outs", "y1_outs"), sets["_outs"][2:]))
        for tag, buffers in sets.items():
            scratch |= {name + tag: buffer for name, buffer in zip(scatter_names, buffers[4:])}
        for tag, size in (("_late", 2 * width + 128), ("_last", 2 * width)):
            scratch |= {name + tag: buffer for name, buffer in zip(total_names, chip_sum_scratch(size, count // 2))}
        up_grad, out_grad, qkv_grad, grad_down, grad_proj, norm_total, hidden, input_grad, _ = plain(
            functools.partial(joined_kernel, tuple(scratch)),
            (
                array((rows, wide // col_count), f32),
                array((rows, out_step), f32),
                array((rows, 3 * out_step), f32),
                array((out_step, inner_step), f32),
                array((rows, out_step), f32),
                array((1, 4 * width + 128), f32),
                array((tokens, width), bf16),
                array((tokens, width), bf16),
                array((tokens, wide), bf16),
            ),
            [in_smem] + [in_vmem] * 6 + [anywhere] * 11,
            list(scratch.values()),
            "joined",
            out_specs=[anywhere] * 9,
            collective_id=1,
            has_side_effects=True,
        )(
            text_lengths, *vectors, image_norm_gain, image_norm_bias, text_tokens, *weights, image_tokens,
            image_qkv.reshape(2, rows, -1), image_out.reshape(2, rows, -1), image_up.reshape(2, rows, -1),
            image_down.reshape(4, 2, rows, -1),
        )
        large = (hidden, input_grad, qkv_grad, out_grad, up_grad, grad_down, grad_proj)
        results = (array((1, 1), f32), *[array((width,), f32)] * 4, *(array(g.shape, g.dtype) for g in large))
        loss, *rest = plain(
            functools.partial(hand_over_kernel, pair_total), results, [in_vmem] * 8, [], "hand_over"
        )(norm_total, *large)
        norms, (hidden, input_grad, qkv_grad, out_grad, up_grad, grad_down, grad_proj) = rest[:4], rest[4:]
        return (
            loss.reshape(()), hidden, input_grad, *norms, qkv_grad, out_grad, up_grad, grad_down.T, grad_proj,
        )

    (hidden, text_embed, projected, pooled, inner_sum, heads, mixed, mid, slope, turned) = plain(
        text_forward_kernel, text_shapes, text_specs, text_buffers, "text_forward"
    )(*text_in)
    qkv_parts = partners(image_qkv, col_count)
    out_parts = partners(image_out, col_count)
    up_parts = partners(image_up, col_count)
    down_parts = partners(image_down, col_count)
    parts = [anywhere] * (2 * col_count)
    image_normed, image_mean = pl.pallas_call(
        functools.partial(image_mix_kernel, col_count),
        grid=(groups,),
        out_shape=(array((image_rows, width), bf16), array((images, width), f32)),
        in_specs=[
            pl.BlockSpec((group_rows, width), lambda i: (i, 0)),
            whole(image_norm_gain.shape),
            whole(image_norm_bias.shape),
        ]
        + parts,
        out_specs=(
            pl.BlockSpec((group_rows, width), lambda i: (i, 0)),
            pl.BlockSpec((group_images, width), lambda i: (i, 0)),
        ),
        scratch_shapes=mix_weights + mix_buffers + [pltpu.SemaphoreType.DMA((2, col_count))],
        compiler_params=pltpu.CompilerParams(vmem_limit_bytes=VMEM_LIMIT),
        name="image_mix",
    )(image_tokens, image_norm_gain, image_norm_bias, *qkv_parts, *out_parts)
    image_embed = pl.pallas_call(
        functools.partial(image_embed_kernel, col_count),
        grid=(groups,),
        out_shape=array((images, width), bf16),
        in_specs=[pl.BlockSpec((group_rows, width), lambda i: (i, 0)), whole((images, width))] + parts,
        out_specs=whole((images, width)),
        scratch_shapes=embed_weights
        + [pltpu.VMEM((images, wide), f32), pltpu.SemaphoreType.DMA((2, col_count))],
        compiler_params=pltpu.CompilerParams(vmem_limit_bytes=VMEM_LIMIT),
        name="image_embed",
    )(image_normed, image_mean, *up_parts, *down_parts)

    image_all = lax.all_gather(image_embed, both, axis=0, tiled=True)
    lifted = jnp.exp(logit_scale * dot_nt(image_all, text_embed))
    row_sums = lax.psum(jnp.sum(lifted, axis=1), both)
    col_sums = jnp.sum(lifted, axis=0)
    sim_grad = (0.5 * (lifted / row_sums[:, None] + lifted / col_sums[None, :])).astype(bf16)
    image_own = image_embed.astype(f32)
    embed_grad = logit_scale * (dot_tn(sim_grad, image_all) - image_own)
    positives = logit_scale * jnp.sum(image_own * text_embed.astype(f32), axis=1)
    loss_part = 0.5 * jnp.sum(jnp.log(col_sums) - 2.0 * positives)
    loss_part = loss_part + 0.5 * jnp.sum(jnp.log(row_sums)) / count

    saved = (text_tokens, heads, mixed, mid, slope, turned)
    backward_in = (text_lengths, *vectors, embed_grad, projected, *saved, *weights)
    backward_specs = [in_smem] + [in_vmem] * 6 + [anywhere] * 11
    backward_buffers = (
        [
            pltpu.VMEM((tokens, width), bf16),
            pltpu.VMEM((tokens, 3 * width), bf16),
            pltpu.VMEM((tokens, width), bf16),
            pltpu.VMEM((tokens, width), f32),
            pltpu.VMEM((tokens, wide), bf16),
        ]
        + weight_scratch
        + [
            pltpu.VMEM((tokens, width), bf16),
            pltpu.VMEM((width, tokens), bf16),
            pltpu.VMEM((tokens, width), f32),
            pltpu.VMEM((tokens, width), f32),
            pltpu.VMEM((tokens, width), bf16),
            pltpu.VMEM((tokens, width), bf16),
            pltpu.VMEM((tokens, 3 * width), bf16),
            pltpu.VMEM((captions, 1), jnp.int32),
            pltpu.VMEM((1, tokens), f32),
            pltpu.VMEM((tokens, 128), f32),
            pltpu.SemaphoreType.DMA((11,)),
        ]
    )

    def by_row(x):
        x = lax.all_to_all(x, "row", split_axis=1, concat_axis=0, tiled=True)
        return lax.all_gather(x, "col", axis=0, tiled=True)

    def by_col(x):
        x = lax.all_gather(x, "row", axis=0, tiled=True)
        return lax.all_to_all(x, "col", split_axis=1, concat_axis=0, tiled=True)

    (proj_grad, branch, up_grad, out_grad, qkv_grad, input_grad, norm_grads) = plain(
        text_backward_kernel,
        (
            array((captions, width), bf16),
            array((captions, width), bf16),
            array((col_count, width, wide // col_count), bf16),
            array((col_count, width, width // col_count), bf16),
            array((col_count, width, 3 * width // col_count), bf16),
            array((tokens, width), bf16),
            array((8, width), f32),
        ),
        backward_specs,
        backward_buffers,
        "text_backward",
    )(*backward_in)

    def scattered(matrix):
        blocks = matrix.reshape(count, width // row_count, matrix.shape[2])
        return lax.psum_scatter(blocks, ("col", "row"), scatter_dimension=0, tiled=True)[0].astype(f32)

    up_grad, out_grad, qkv_grad = scattered(up_grad), scattered(out_grad), scattered(qkv_grad)
    grad_down = dot_tn(by_row(inner_sum), by_col(branch))
    grad_proj = dot_tn(by_row(pooled), by_col(proj_grad))
    loss_total, norm_total = lax.psum((loss_part, norm_grads), both)
    norms = [norm_total[i] for i in range(4)]
    mean_loss = loss_total / pair_total
    return (
        mean_loss, hidden, input_grad, *norms, qkv_grad, out_grad, up_grad, grad_down, grad_proj,
    )


def solution(mesh):
    split = P(("row", "col"), None)
    grid = P("row", "col")
    in_specs = (
        split, P(), P(), P("col", None), P("col", None), P("col", None), P("col", None), split, P(("row", "col")),
    ) + (P(),) * 9
    out_specs = (P(), split, split, P(), P(), P(), P(), grid, grid, grid, grid, grid)
    return jax.shard_map(body, mesh=mesh, in_specs=in_specs, out_specs=out_specs, check_vma=False)
```

```python
import functools
import math
from types import SimpleNamespace

import jax
import jax.numpy as jnp
from jax import lax
from jax.experimental import pallas as pl
from jax.experimental.pallas import tpu as pltpu
from jax.sharding import PartitionSpec as P

HEADS = 12
IMG_TOK = 50
norm_eps = 1e-06
logit_scale = 50.0
masked_score = -1e30
log2e = math.log2(math.e)
f32 = jnp.float32
bf16 = jnp.bfloat16
VMEM_LIMIT = 62 * 2**20
MESH = pl.DeviceIdType.MESH


def dot_nn(a, b):
    return lax.dot_general(a, b, (((1,), (0,)), ((), ())), preferred_element_type=f32)


def dot_nt(a, b):
    return lax.dot_general(a, b, (((1,), (1,)), ((), ())), preferred_element_type=f32)


def dot_tn(a, b):
    return lax.dot_general(a, b, (((0,), (0,)), ((), ())), preferred_element_type=f32)


def split_low(x):
    high = x.astype(bf16)
    return high, (x - high.astype(f32)).astype(bf16)


def normed(x):
    centered = x - jnp.mean(x, axis=-1, keepdims=True)
    spread = lax.rsqrt(jnp.mean(centered * centered, axis=-1, keepdims=True) + norm_eps)
    return centered * spread, spread


def layer_norm(x, gain, bias):
    return normed(x)[0] * gain + bias


def gelu(x):
    return x * (0.5 + 0.5 * lax.erf(x * math.sqrt(0.5)))


def gelu_and_slope(x):
    below = 0.5 + 0.5 * lax.erf(x * math.sqrt(0.5))
    bell = jnp.exp2((-0.5 * log2e) * (x * x))
    return x * below, below + x * (bell * (1.0 / math.sqrt(2.0 * math.pi)))


def lane_halves(width):
    lane = lax.broadcasted_iota(jnp.int32, (1, width), 1)
    first = (lane < width // 2).astype(f32)
    return first.astype(bf16), (1.0 - first).astype(bf16)


def stack_heads(x, first, second):
    return jnp.concatenate([x * first, x * second], axis=0)


def join_heads(stacked):
    rows, width = stacked.shape[0] // 2, stacked.shape[1]
    lane = lax.broadcasted_iota(jnp.int32, (rows, width), 1)
    return jnp.where(lane < width // 2, stacked[:rows], stacked[rows:])


def soft_weights(query, key, bias, factor):
    scores = dot_nt(query, key) * (factor * log2e) + bias
    weights = jnp.exp2(scores - jnp.max(scores, axis=-1, keepdims=True))
    return weights, 1.0 / jnp.sum(weights, axis=-1, keepdims=True)


def set_lengths(lengths_ref, lens_ref, key_bias_ref):
    captions, tokens = lens_ref.shape[0], key_bias_ref.shape[1]
    length = tokens // captions
    caption = lax.broadcasted_iota(jnp.int32, (captions, 1), 0)
    token = lax.broadcasted_iota(jnp.int32, (1, tokens), 1)
    column, row = jnp.zeros((captions, 1), jnp.int32), jnp.zeros((1, tokens), jnp.int32)
    for n in range(captions):
        column = jnp.where(caption == n, lengths_ref[n], column)
        row = jnp.where(token // length == n, lengths_ref[n], row)
    lens_ref[...] = column
    key_bias_ref[...] = jnp.where(token % length < row, 0.0, masked_score)


def as_row(ref):
    return ref[...].reshape(1, ref.shape[0])


def text_bias(key_bias_ref, block, rows, length):
    near = lax.broadcasted_iota(jnp.int32, (rows, rows), 0) // length
    far = lax.broadcasted_iota(jnp.int32, (rows, rows), 1) // length
    columns = pl.ds(pl.multiple_of(block * rows, rows), rows)
    bias = jnp.where(near == far, key_bias_ref[:, columns], masked_score)
    return jnp.concatenate([bias, bias], axis=0)


def member(len_ref, captions, tokens):
    length = tokens // captions
    token = lax.broadcasted_iota(jnp.int32, (captions, tokens), 1)
    caption = lax.broadcasted_iota(jnp.int32, (captions, tokens), 0)
    return ((token // length == caption) & (token % length < len_ref[...])).astype(f32)


def spread_rows(x, length):
    rows, width = x.shape
    return jnp.broadcast_to(x[:, None, :], (rows, length, width)).reshape(rows * length, width)


def wide_steps(total, most=768):
    step = math.gcd(total, most)

    def loop(body):
        @pl.loop(0, total // step)
        def _(j):
            body(pl.ds(pl.multiple_of(j * step, 128), step))

    return loop


class TextForward:
    band = 128

    def __init__(self, refs):
        for name, ref in refs.items():
            setattr(self, name, ref)
        self.tokens, self.width = self.tok.shape
        self.captions = self.lens.shape[0]
        self.length = self.tokens // self.captions
        self.wide = self.w_up.shape[1]
        pairs = (
            (self.qkv_hbm, self.w_qkv), (self.out_hbm, self.w_out), (self.up_hbm, self.w_up),
            (self.down_hbm, self.w_down),
        )
        self.loads = load_weights(pairs, self.sems)
        self.load_proj = pltpu.make_async_copy(self.proj_hbm, self.w_proj, self.sems.at[4])

    def bands(self, step):
        pl.loop(0, self.tokens // self.band)(
            lambda i: step(pl.ds(pl.multiple_of(i * self.band, self.band), self.band))
        )

    def prepare(self):
        set_lengths(self.lengths, self.lens, self.key_bias)

        def first_norm(rows):
            norm = layer_norm(self.tok[rows, :].astype(f32), as_row(self.gain1), as_row(self.bias1))
            self.norm[rows, :] = norm.astype(bf16)

        self.bands(first_norm)

    def attention(self):
        width = self.width
        self.loads[0].wait()

        @wide_steps(3 * width)
        def _(columns):
            self.heads[:, columns] = dot_nn(self.norm[...], self.w_qkv[:, columns]).astype(bf16)

        first, second = lane_halves(128)
        factor = (width // HEADS) ** -0.5

        @pl.loop(0, self.tokens // self.band)
        def _(block):
            rows = pl.ds(pl.multiple_of(block * self.band, self.band), self.band)
            bias = text_bias(self.key_bias, block, self.band, self.length)
            for at in range(0, width, 128):
                query = stack_heads(self.heads[rows, at : at + 128], first, second)
                key = self.heads[rows, width + at : width + at + 128]
                weights, scale = soft_weights(query, key, bias, factor)
                value = self.heads[rows, 2 * width + at : 2 * width + at + 128]
                mixed = dot_nn(weights.astype(bf16), value) * scale
                self.mixed[rows, at : at + 128] = join_heads(mixed).astype(bf16)

    def middle(self):
        self.loads[1].wait()

        def second_norm(rows):
            mid = self.tok[rows, :].astype(f32) + dot_nn(self.mixed[rows, :], self.w_out[...])
            self.mid[rows, :] = mid
            self.norm[rows, :] = layer_norm(mid, as_row(self.gain2), as_row(self.bias2)).astype(bf16)

        self.bands(second_norm)

    def feed(self, after=lambda j: None):
        self.loads[2].wait()
        self.chosen = member(self.lens, self.captions, self.tokens).astype(bf16)
        place = lax.broadcasted_iota(jnp.int32, (self.captions, self.length, 1), 1)
        valid = (place < self.lens[...].reshape(self.captions, 1, 1)).astype(f32).reshape(self.tokens, 1)

        @pl.loop(0, self.wide // self.width)
        def _(j):
            columns = pl.ds(pl.multiple_of(j * self.width, 128), self.width)
            value, slope = gelu_and_slope(dot_nn(self.norm[...], self.w_up[:, columns]))
            value = value.astype(bf16)
            self.inner[:, columns] = value
            self.slope[:, columns] = (slope * valid).astype(bf16)
            self.inner_sum[:, columns] = dot_nn(self.chosen, value).astype(bf16)
            after(j)

    def finish(self):
        self.loads[3].wait()
        self.turned[...] = self.norm[...].T
        inverse = 1.0 / self.lens[...].astype(f32)

        @wide_steps(self.width)
        def _(columns):
            state = self.mid[:, columns] + dot_nn(self.inner[...], self.w_down[:, columns])
            self.hidden[:, columns] = state.astype(bf16)
            high, low = split_low(state)
            pooled = (dot_nn(self.chosen, high) + dot_nn(self.chosen, low)) * inverse
            self.pooled[:, columns] = pooled.astype(bf16)

    def embed(self):
        self.load_proj.wait()
        projected = dot_nn(self.pooled[...], self.w_proj[...])
        self.projected[...] = projected
        scale = lax.rsqrt(jnp.sum(projected * projected, axis=-1, keepdims=True) + norm_eps)
        self.text_embed[...] = (projected * scale).astype(bf16)


text_ins = (
    "tok", "lengths", "gain1", "bias1", "gain2", "bias2", "qkv_hbm", "out_hbm", "up_hbm", "down_hbm", "proj_hbm",
)
text_names = (
    "hidden", "text_embed", "projected", "pooled", "inner_sum", "heads", "mixed", "mid", "slope", "turned",
)
text_scratch = ("w_qkv", "w_out", "w_up", "w_down", "w_proj", "norm", "inner", "lens", "key_bias", "sems")


def text_forward_kernel(*refs):
    t = TextForward(dict(zip(text_ins + text_names + text_scratch, refs, strict=True)))
    t.load_proj.start()
    t.prepare()
    t.attention()
    t.middle()
    t.feed()
    t.finish()
    t.embed()


def load_weights(pairs, sems):
    loads = [pltpu.make_async_copy(s, d, sems.at[i]) for i, (s, d) in enumerate(pairs)]
    for load in loads:
        load.start()
    return loads


def spans(count, size):
    return lambda i: pl.ds(pl.multiple_of(i * size, size), size)


def norm_backward(outer, unit, spread, gain):
    outer = outer * gain
    inner = outer - jnp.mean(outer, axis=-1, keepdims=True)
    return spread * (inner - unit * jnp.mean(outer * unit, axis=-1, keepdims=True))


class TextBackward:
    band = 128

    def __init__(self, refs, loads):
        for name, ref in refs.items():
            setattr(self, name, ref)
        self.loads = loads
        self.tokens, self.width = self.tok.shape
        self.captions = self.lens.shape[0]
        self.length = self.tokens // self.captions
        self.wide = self.w_up.shape[1]
        self.pre_grad = self.slope

    def wait(self, name):
        if name in self.loads:
            self.loads[name].wait()

    def rows(self, i):
        return pl.ds(pl.multiple_of(i * self.band, self.band), self.band)

    def bands(self, step):
        pl.loop(0, self.tokens // self.band)(lambda i: step(self.rows(i)))

    def valid(self):
        place = lax.broadcasted_iota(jnp.int32, (self.captions, self.length, 1), 1)
        valid = place < self.lens[...].reshape(self.captions, 1, 1)
        return valid.astype(f32).reshape(self.tokens, 1)

    def project(self):
        projected = self.projected[...]
        embed_grad = self.embed_grad[...]
        r = lax.rsqrt(jnp.sum(projected * projected, axis=-1, keepdims=True) + norm_eps)
        along = jnp.sum(projected * embed_grad, axis=-1, keepdims=True)
        proj_grad = (r * embed_grad - (r * r * r) * projected * along).astype(bf16)
        self.wait("w_proj")
        state_grad = dot_nt(proj_grad, self.w_proj[...]) * (1.0 / self.lens[...].astype(f32))
        self.branch[...] = state_grad.astype(bf16)
        self.mid_grad[...] = spread_rows(state_grad, self.length) * self.valid()
        return proj_grad, self.branch[...]

    def wait_inner(self):
        self.wait("turned")
        self.wait("w_down")
        self.wait("slope")

    def inner_grad(self, columns):
        grad = dot_nt(self.branch[...], self.w_down[columns, :])
        pre_grad = spread_rows(grad, self.length) * self.slope[:, columns].astype(f32)
        self.pre_grad[:, columns] = pre_grad.astype(bf16)

    def up_block(self, columns):
        return dot_nn(self.turned[...], self.pre_grad[:, columns]).astype(bf16)

    def to_middle(self):
        self.wait("w_up")

        @wide_steps(self.width)
        def _(columns):
            self.outer[:, columns] = dot_nt(self.pre_grad[...], self.w_up[columns, :])

    def middle(self):
        self.wait("mid")
        self.norm_grad[...] = jnp.zeros_like(self.norm_grad)

        def through_norm(rows):
            unit, spread = normed(self.mid[rows, :])
            outer = self.outer[rows, :]
            self.norm_grad[2:3, :] += jnp.sum(outer * unit, axis=0, keepdims=True)
            self.norm_grad[3:4, :] += jnp.sum(outer, axis=0, keepdims=True)
            mid_grad = self.mid_grad[rows, :] + norm_backward(outer, unit, spread, as_row(self.gain2))
            self.mid_grad[rows, :] = mid_grad
            self.low_grad[rows, :] = mid_grad.astype(bf16)

        self.bands(through_norm)
        self.wait("mixed")
        self.turned[...] = self.mixed[...].T

    def out_block(self, columns):
        return dot_nn(self.turned[...], self.low_grad[:, columns]).astype(bf16)

    def to_heads(self):
        self.wait("w_out")
        self.wait("tok")

        def through_out(rows):
            self.mixed_grad[rows, :] = dot_nt(self.low_grad[rows, :], self.w_out[...]).astype(bf16)
            norm = layer_norm(self.tok[rows, :].astype(f32), as_row(self.gain1), as_row(self.bias1))
            self.norm[rows, :] = norm.astype(bf16)

        self.bands(through_out)
        self.turned[...] = self.norm[...].T

    def attention(self, after=lambda block: None):
        first, second = lane_halves(128)
        width = self.width
        factor = (width // HEADS) ** -0.5
        self.wait("heads")
        self.key_column[...] = jnp.broadcast_to((1.0 - self.valid()) * masked_score, self.key_column.shape)

        @pl.loop(0, self.tokens // self.band)
        def _(block):
            rows = self.rows(block)
            near = lax.broadcasted_iota(jnp.int32, (self.band, self.band), 0) // self.length
            far = lax.broadcasted_iota(jnp.int32, (self.band, self.band), 1) // self.length
            bias = jnp.where(near == far, self.key_column[rows, :], masked_score)
            bias = jnp.concatenate([bias, bias], axis=1)
            for at in range(0, width, 128):
                query = stack_heads(self.heads[rows, at : at + 128], first, second)
                key = self.heads[rows, width + at : width + at + 128]
                value = self.heads[rows, 2 * width + at : 2 * width + at + 128]
                grad = stack_heads(self.mixed_grad[rows, at : at + 128], first, second)
                scores = dot_nt(key, query) * (factor * log2e) + bias
                weights = jnp.exp2(scores - jnp.max(scores, axis=0, keepdims=True))
                probs = weights * (1.0 / jnp.sum(weights, axis=0, keepdims=True))
                prob_grad = dot_nt(value, grad)
                total = jnp.sum(prob_grad * probs, axis=0, keepdims=True)
                score_grad = (probs * (prob_grad - total)).astype(bf16)
                query_grad = join_heads(dot_tn(score_grad, key)) * factor
                self.heads_grad[rows, at : at + 128] = query_grad.astype(bf16)
                key_grad = dot_nn(score_grad, query) * factor
                self.heads_grad[rows, width + at : width + at + 128] = key_grad.astype(bf16)
                value_grad = dot_nn(probs.astype(bf16), grad)
                self.heads_grad[rows, 2 * width + at : 2 * width + at + 128] = value_grad.astype(bf16)
            after(block)

    def qkv_block(self, columns):
        return dot_nn(self.turned[...], self.heads_grad[:, columns]).astype(bf16)

    def input(self, between=lambda: None):
        self.wait("w_qkv")

        @wide_steps(self.width)
        def _(columns):
            self.outer[:, columns] = dot_nt(self.heads_grad[...], self.w_qkv[columns, :])

        between()

        def through_norm(rows):
            unit, spread = normed(self.tok[rows, :].astype(f32))
            outer = self.outer[rows, :]
            self.norm_grad[0:1, :] += jnp.sum(outer * unit, axis=0, keepdims=True)
            self.norm_grad[1:2, :] += jnp.sum(outer, axis=0, keepdims=True)
            inner = norm_backward(outer, unit, spread, as_row(self.gain1))
            self.tok[rows, :] = (self.mid_grad[rows, :] + inner).astype(bf16)

        self.bands(through_norm)


backward_ins = (
    "lengths", "gain1", "bias1", "gain2", "bias2", "embed_grad", "projected", "tok_hbm", "heads_hbm", "mixed_hbm",
    "mid_hbm", "slope_hbm", "turned_hbm", "w_qkv_hbm", "w_out_hbm", "w_up_hbm", "w_down_hbm", "w_proj_hbm",
)
backward_outs = ("proj_grad", "branch", "up_grad", "out_grad", "qkv_grad", "input_grad", "norm_grad")
backward_scratch = (
    "tok", "heads", "mixed", "mid", "slope", "w_qkv", "w_out", "w_up", "w_down", "w_proj", "norm", "turned",
    "outer", "mid_grad", "low_grad", "mixed_grad", "heads_grad", "lens", "key_bias", "key_column", "sems",
)


def text_backward_kernel(*refs):
    refs = dict(zip(backward_ins + backward_outs + backward_scratch, refs, strict=True))
    order = ("w_proj", "turned", "w_down", "slope", "w_up", "mid", "mixed", "w_out", "tok", "heads", "w_qkv")
    loads = load_weights([(refs[name + "_hbm"], refs[name]) for name in order], refs["sems"])
    t = TextBackward(refs, dict(zip(order, loads)))
    set_lengths(t.lengths, t.lens, t.key_bias)
    parts = t.up_grad.shape[0]

    def blocks(target, block):
        step = target.shape[2]
        for part in range(parts):
            target[part] = block(slice(part * step, (part + 1) * step))

    t.proj_grad[...] = t.project()[0]
    t.wait_inner()
    wide_steps(t.wide)(t.inner_grad)
    blocks(t.up_grad, t.up_block)
    t.to_middle()
    t.middle()
    blocks(t.out_grad, t.out_block)
    t.to_heads()
    t.attention()
    blocks(t.qkv_grad, t.qkv_block)
    t.input()
    t.input_grad[...] = t.tok[...]


class Place:
    def __init__(self, z_count=4, y_count=2, x_count=2, k_count=2):
        self.row, self.col = lax.axis_index("row"), lax.axis_index("col")
        self.z, self.y = self.row // y_count, self.row % y_count
        self.x, self.k = self.col // k_count, self.col % k_count
        self.rows, self.cols = z_count * y_count, x_count * k_count
        self.count = self.rows * self.cols
        self.me = self.row * self.cols + self.col
        self.slot = self.col * self.rows + self.row
        self.near_z, self.far_z = self.z + 1 - 2 * (self.z % 2), (self.z + 2) % 4

    def at(self, **moved):
        z, y, x, k = (moved.get(name, getattr(self, name)) for name in "zyxk")
        return z * 2 + y, x * 2 + k

    def peer(self, distance):
        other = (self.me + distance) % self.count
        return other // self.cols, other % self.cols

    def greet(self):
        barrier = pltpu.get_barrier_semaphore()

        @pl.loop(1, self.count)
        def _(distance):
            pl.semaphore_signal(barrier, inc=1, device_id=self.peer(distance), device_id_type=MESH)

    def meet(self):
        pl.semaphore_wait(pltpu.get_barrier_semaphore(), self.count - 1)


def remote(src, dst, send, recv, to):
    return pltpu.make_async_remote_copy(
        src_ref=src, dst_ref=dst, send_sem=send, recv_sem=recv, device_id=to, device_id_type=MESH
    )


def wait_all(blocks, send, recv, to):
    remote(blocks, blocks, send, recv, to).wait()


class Gather:
    def __init__(self, place, pieces, spans, sends, recvs):
        mate, next_x = place.at(k=1 - place.k), place.at(x=1 - place.x)
        across = next_x[1]
        self.spans, self.sends, self.recvs, self.mate = spans, sends, recvs, mate
        self.locals, self.nears, self.fars, self.alongs, self.passes = [], [], [], [], []
        for axis, own, half, block, part in pieces:
            here = place.y if axis == "y" else place.z % 2
            partner = place.at(y=1 - place.y) if axis == "y" else place.at(z=place.near_z)
            mine, theirs = part(across, here), block(across)
            self.locals.append(pltpu.make_async_copy(own, block(place.col), recvs.at[4]))
            self.nears.append(remote(own, block(place.col), sends.at[0], recvs.at[0], mate))
            self.fars.append(remote(half(here), part(place.col, here), sends.at[1], recvs.at[1], next_x))
            self.alongs.append(remote(mine, mine, sends.at[2], recvs.at[2], partner))
            self.passes.append(remote(theirs, theirs, sends.at[3], recvs.at[3], mate))

    def wait(self, i, span):
        wait_all(self.spans[span], self.sends.at[i], self.recvs.at[i], self.mate)

    def start(self):
        for copies in (self.fars, self.nears, self.locals):
            for copy in copies:
                copy.start()

    def share(self):
        self.wait(1, 1)
        for copy in self.alongs:
            copy.start()

    def relay(self):
        self.wait(2, 1)
        for copy in self.passes:
            copy.start()

    def finish(self):
        pltpu.make_async_copy(self.spans[0], self.spans[0], self.recvs.at[4]).wait()
        self.wait(0, 0)
        self.wait(3, 0)


class RowFactors:
    def __init__(self, place, own, held, local, sends, recvs):
        self.place, self.own, self.held, self.sends, self.recvs = place, own, held, sends, recvs
        self.local = pltpu.make_async_copy(own.at[place.row], held.at[place.col, place.row], local)
        mine, across = held.at[place.col], held.at[place.at(x=1 - place.x)[1]]
        mate, next_x = place.at(k=1 - place.k), place.at(x=1 - place.x)
        self.far = remote(mine, mine, sends.at[1], recvs.at[1], next_x)
        self.near = remote(mine, mine, sends.at[2], recvs.at[2], mate)
        self.passed = remote(across, across, sends.at[3], recvs.at[3], mate)

    def start(self):
        self.local.start()
        p = self.place

        @pl.loop(1, p.rows)
        def _(distance):
            row = (p.row + distance) % p.rows
            remote(
                self.own.at[row], self.held.at[p.col, p.row], self.sends.at[0], self.recvs.at[0], (row, p.col)
            ).start()

    def share(self):
        self.local.wait()
        p = self.place
        to = p.at(k=1 - p.k)
        wait_all(self.held.at[p.col, pl.ds(0, p.rows - 1)], self.sends.at[0], self.recvs.at[0], to)
        self.far.start()
        self.near.start()

    def relay(self):
        self.far.wait()
        self.passed.start()

    def finish(self):
        self.near.wait()
        self.passed.wait()


class Exchange:
    def __init__(self, place, source, slots, sends, recvs):
        self.place, self.source, self.slots = place, source, slots
        self.sems = sends.at[0], recvs.at[0]

    def start(self):
        p = self.place

        @pl.loop(1, p.count)
        def _(distance):
            remote(self.source, self.slots.at[p.slot], *self.sems, p.peer(distance)).start()

    def finish(self):
        p = self.place
        wait_all(self.slots.at[pl.ds(0, p.count - 1)], *self.sems, p.at(k=1 - p.k))


class ChipSum:
    def __init__(self, place, total, got, slots, sends, recvs):
        self.place, self.total, self.got, self.slots = place, total, got, slots
        self.sends, self.recvs = sends, recvs
        self.chip, self.chips = place.row * 2 + place.x, place.rows * 2
        self.mate = place.at(k=1 - place.k)

    def near(self):
        return remote(self.total, self.got, self.sends.at[0], self.recvs.at[0], self.mate)

    def start(self):
        self.near().start()

    def spread(self):
        self.near().wait()
        self.total[...] = self.total[...] + self.got[...]
        self.slots[self.chip] = self.total[...]

        @pl.loop(1, self.chips)
        def _(distance):
            other = (self.chip + distance) % self.chips
            to = other // 2, other % 2 * 2 + self.place.k
            remote(self.total, self.slots.at[self.chip], self.sends.at[1], self.recvs.at[1], to).start()

    def finish(self):
        wait_all(self.slots.at[pl.ds(0, self.chips - 1)], self.sends.at[1], self.recvs.at[1], self.mate)
        return jnp.sum(self.slots[...], axis=0)


class GradientScatter:
    def __init__(self, place, straight, halves, held, near, x1, y1, x2, y2, far, sends, recvs):
        self.straight = straight
        self.place, self.held, self.near, self.far = place, held, near, far
        self.x1, self.y1, self.x2, self.y2 = x1, y1, x2, y2
        self.sends, self.recvs = sends, recvs
        self.halves = halves

    def lanes(self, chunk):
        ones, twos = zip(*self.halves[:chunk], (0, 0))
        at_one, at_two = sum(ones), sum(twos)
        at = at_one + at_two
        one, two = self.halves[chunk]
        return (
            pl.ds(at, one + two), pl.ds(at, one), pl.ds(at + one, two), pl.ds(at_one, one), pl.ds(at_two, two)
        )

    def copies(self, chunk, stage):
        p, held = self.place, self.held
        x, y, z, k = p.x, p.y, p.z, p.k
        whole, one, two, part_one, part_two = self.lanes(chunk)

        def copy(n, src, dst, **moved):
            send = self.sends.at[chunk, (0, 0, 1, 0, 1, 0, 1, 2)[n]]
            return remote(src, dst, send, self.recvs.at[chunk, n], p.at(**moved))

        if stage == 0:
            return [copy(0, held.at[:, 1 - k, :, :, :, whole], self.near.at[:, :, :, :, whole], k=1 - k)]
        if stage == 1:
            copies = []
            if one.size:
                copies.append(copy(1, held.at[1 - x, k, :, :, :, one], self.x1.at[:, :, :, part_one], x=1 - x))
            if two.size:
                copies.append(copy(2, held.at[:, k, :, 1 - y, :, two], self.y1.at[:, :, :, part_two], y=1 - y))
            return copies
        if stage == 2:
            copies = []
            if one.size:
                copies.append(copy(3, held.at[x, k, :, 1 - y, :, one], self.y2.at[:, :, part_one], y=1 - y))
            if two.size:
                copies.append(copy(4, held.at[1 - x, k, :, y, :, two], self.x2.at[:, :, part_two], x=1 - x))
            return copies
        if stage == 3 and self.straight:
            return [
                copy(4 + i, held.at[x, k, (z + i) % 4, y, :, whole], self.far.at[i - 1, :, whole], z=(z + i) % 4)
                for i in range(1, 4)
            ]
        if stage == 3:
            blocks = p.near_z, held.shape[2] - 1 - z
            return [
                copy(5 + i, held.at[x, k, block, y, :, whole], self.far.at[i, :, whole], z=p.near_z)
                for i, block in enumerate(blocks)
            ]
        return [copy(7, held.at[x, k, p.far_z, y, :, whole], self.far.at[2, :, whole], z=p.far_z)]

    def start(self, chunk, stage):
        for copy in self.copies(chunk, stage):
            copy.start()

    def finish(self, chunk, stage):
        for copy in self.copies(chunk, stage):
            copy.wait()
        p, held = self.place, self.held
        x, y, k = p.x, p.y, p.k
        z_count = held.shape[2]
        whole, one, two, part_one, part_two = self.lanes(chunk)

        def add(target, source):
            target[...] = (target[...].astype(f32) + source[...].astype(f32)).astype(bf16)

        if stage == 0:

            @pl.loop(0, z_count)
            def _(z):
                for i in range(2):
                    for j in range(2):
                        add(held.at[i, k, z, j, :, whole], self.near.at[i, z, j, :, whole])

        if stage == 1:

            @pl.loop(0, z_count)
            def _(z):
                for i in range(2):
                    if one.size:
                        add(held.at[x, k, z, i, :, one], self.x1.at[z, i, :, part_one])
                    if two.size:
                        add(held.at[i, k, z, y, :, two], self.y1.at[i, z, :, part_two])

        if stage == 2:

            @pl.loop(0, z_count)
            def _(z):
                if one.size:
                    add(held.at[x, k, z, y, :, one], self.y2.at[z, :, part_one])
                if two.size:
                    add(held.at[x, k, z, y, :, two], self.x2.at[z, :, part_two])

        if stage == 3 and not self.straight:
            add(held.at[x, k, p.far_z, y, :, whole], self.far.at[1, :, whole])

    def step_on(self, chunk, stage):
        self.finish(chunk, stage - 1)
        self.start(chunk, stage)

    def total(self):
        p = self.place
        total = self.held[p.x, p.k, p.z, p.y, :, : self.far.shape[2]].astype(f32)
        for i in (0, 1, 2) if self.straight else (0, 2):
            total = total + self.far[i].astype(f32)
        return total


def chip_sum_scratch(size, chips):
    return [
        pltpu.VMEM((1, size), f32), pltpu.VMEM((1, size), f32), pltpu.VMEM((chips, 1, size), f32),
        pltpu.SemaphoreType.DMA((2,)), pltpu.SemaphoreType.DMA((2,)),
    ]


def scatter_scratch(rows, halves):
    one, two = (sum(widths) for widths in zip(*halves))
    spare = max(two, 128)
    shapes = [
        (2, 2, 4, 2, rows, one + two), (2, 4, 2, rows, one + two), (4, 2, rows, one), (2, 4, rows, spare),
        (4, rows, spare), (4, rows, one), (3, rows, one + two),
    ]
    sems = [pltpu.SemaphoreType.DMA((len(halves), 3)), pltpu.SemaphoreType.DMA((len(halves), 8))]
    return [pltpu.VMEM(shape, bf16) for shape in shapes] + sems


class ColFactors:
    def __init__(self, place, own, held, sends, recvs):
        self.place, self.own, self.held, self.sends, self.recvs = place, own, held, sends, recvs

    def copies(self, stage):
        p, held = self.place, self.held

        def copy(n, src, dst, **moved):
            return remote(src, dst, self.sends.at[n], self.recvs.at[n], p.at(**moved))

        if stage == 0:
            mine = held.at[p.col, p.row]
            moves = ({"x": 1 - p.x}, {"k": 1 - p.k}, {"x": 1 - p.x, "k": 1 - p.k})
            return [copy(i, self.own.at[p.at(**move)[1]], mine, **move) for i, move in enumerate(moves)]
        if stage == 1:
            mine = held.at[:, p.row]
            return [copy(3, mine, mine, y=1 - p.y)]
        mine, other = (held.at[:, pl.ds(z * 2, 2)] for z in (p.z, p.far_z))
        if stage == 2:
            return [copy(4, mine, mine, z=p.far_z)]
        return [copy(5, mine, mine, z=p.near_z), copy(6, other, other, z=p.near_z)]

    def start(self, stage):
        for copy in self.copies(stage):
            copy.start()

    def finish(self, stage):
        for copy in self.copies(stage):
            copy.wait()


def scatter_widths(wide, width, cols):
    ups = tuple((128, 128) for _ in range(wide // cols // 256))
    rest = 4 * width // cols - 128
    return ups, ((128, 0),), ((128, 128), (128, 128), (rest - 512, 0))


scatter_names = ("x2", "y2", "far", "sends", "recvs")
total_names = ("total", "got", "slots", "sends", "recvs")


def hand_over_kernel(pair_total, norms, *refs):
    sources, (loss, *vectors), targets = refs[:7], refs[7:12], refs[12:]
    width = vectors[0].shape[0]
    loss[...] = norms[:, 4 * width : 4 * width + 1] * (1.0 / pair_total)
    for i, vector in enumerate(vectors):
        vector[...] = norms[:, i * width : (i + 1) * width].reshape(width)
    for source, target in zip(sources, targets, strict=True):
        target[...] = source[...]


def group_mean(images, rows):
    token = lax.broadcasted_iota(jnp.int32, (images, rows), 1)
    image = lax.broadcasted_iota(jnp.int32, (images, rows), 0)
    inside = (token >= image * IMG_TOK) & (token < (image + 1) * IMG_TOK)
    return inside.astype(f32).astype(bf16)


def load_parts(parts, target, sems, col, col_count):
    depth = target.shape[0] // col_count
    copies = []
    for k, part in enumerate(parts):
        place = pl.multiple_of((col ^ k) * depth, depth)
        copies.append(pltpu.make_async_copy(part, target.at[pl.ds(place, depth)], sems.at[k]))
    return copies


def image_mix(tokens, gain_ref, bias_ref, qkv_block, between, out_weight, norm_ref, heads_ref, mixed_ref):
    rows, width = tokens.shape
    images = rows // IMG_TOK
    norm_ref[...] = layer_norm(tokens.astype(f32), gain_ref[0:1, :], bias_ref[0:1, :]).astype(bf16)

    @pl.loop(0, 3)
    def _(j):
        columns = pl.ds(pl.multiple_of(j * width, width), width)
        heads_ref[:, columns] = dot_nn(norm_ref[...], qkv_block(j)).astype(bf16)

    between()
    first, second = lane_halves(128)
    factor = (width // HEADS) ** -0.5
    window = 112

    @pl.loop(0, images // 2)
    def _(pair):
        start = pair * (2 * IMG_TOK)
        low = pl.multiple_of(start // 16 * 16, 16)
        near = lax.broadcasted_iota(jnp.int32, (window, window), 0) + low
        far = lax.broadcasted_iota(jnp.int32, (window, window), 1) + low
        same = (near >= start) & (near < start + 2 * IMG_TOK) & (far >= start) & (far < start + 2 * IMG_TOK)
        same = same & ((near >= start + IMG_TOK) == (far >= start + IMG_TOK))
        bias = jnp.where(same, 0.0, masked_score)
        bias = jnp.concatenate([bias, bias], axis=0)
        keep = lax.broadcasted_iota(jnp.int32, (16, 128), 0) + low < start
        span, head, tail = pl.ds(low, window), pl.ds(low, 16), pl.ds(low + 16, window - 16)
        for at in range(0, width, 128):
            query = stack_heads(heads_ref[span, at : at + 128], first, second)
            key = heads_ref[span, width + at : width + at + 128]
            weights, scale = soft_weights(query, key, bias, factor)
            value = heads_ref[span, 2 * width + at : 2 * width + at + 128]
            mixed = join_heads(dot_nn(weights.astype(bf16), value) * scale)
            former = mixed_ref[head, at : at + 128].astype(f32)
            mixed_ref[head, at : at + 128] = jnp.where(keep, former, mixed[:16]).astype(bf16)
            mixed_ref[tail, at : at + 128] = mixed[16:].astype(bf16)

    mid = tokens.astype(f32) + dot_nn(mixed_ref[...], out_weight())
    high, low = split_low(mid)
    select = group_mean(images, rows)
    mean = (dot_nn(select, high) + dot_nn(select, low)) * (1.0 / IMG_TOK)
    return layer_norm(mid, gain_ref[1:2, :], bias_ref[1:2, :]).astype(bf16), mean


def image_mix_kernel(col_count, tok_ref, gain_ref, bias_ref, *refs):
    qkv_parts, out_parts = refs[:col_count], refs[col_count : 2 * col_count]
    normed_ref, mean_ref, w_qkv, w_out, *buffers, sems = refs[2 * col_count :]
    col = lax.axis_index("col")

    @pl.when(pl.program_id(0) == 0)
    def _():
        copies = load_parts(qkv_parts, w_qkv, sems.at[0], col, col_count)
        copies += load_parts(out_parts, w_out, sems.at[1], col, col_count)
        for copy in copies:
            copy.start()
        for copy in copies:
            copy.wait()

    width = tok_ref.shape[1]

    def qkv_block(j):
        return w_qkv[:, pl.ds(pl.multiple_of(j * width, width), width)]

    normed_ref[...], mean_ref[...] = image_mix(
        tok_ref[...], gain_ref, bias_ref, qkv_block, lambda: None, lambda: w_out[...], *buffers
    )


def image_embed_kernel(col_count, normed_ref, mean_ref, *refs):
    up_parts, down_parts = refs[:col_count], refs[col_count : 2 * col_count]
    embed_ref, w_up, w_down, sum_ref, sems = refs[2 * col_count :]
    rows, width = normed_ref.shape
    images = rows // IMG_TOK
    wide = w_up.shape[1]
    step = pl.program_id(0)
    col = lax.axis_index("col")
    downs = load_parts(down_parts, w_down, sems.at[1], col, col_count)

    @pl.when(step == 0)
    def _():
        ups = load_parts(up_parts, w_up, sems.at[0], col, col_count)
        for copy in ups + downs:
            copy.start()
        for copy in ups:
            copy.wait()

    select = group_mean(images, rows)

    @wide_steps(wide)
    def _(columns):
        inner = gelu(dot_nn(normed_ref[...], w_up[:, columns])).astype(bf16)
        sum_ref[pl.ds(pl.multiple_of(step * images, images), images), columns] = dot_nn(select, inner)

    @pl.when(step == pl.num_programs(0) - 1)
    def _():
        for copy in downs:
            copy.wait()
        high, low = split_low(sum_ref[...] * (1.0 / IMG_TOK))
        pooled = mean_ref[...] + dot_nn(high, w_down[...]) + dot_nn(low, w_down[...])
        embed_ref[...] = (
            pooled * lax.rsqrt(jnp.sum(pooled * pooled, axis=-1, keepdims=True) + norm_eps)
        ).astype(bf16)


joined_ins = (
    "lengths", "gain1", "bias1", "gain2", "bias2", "image_gain", "image_bias", "tok_hbm", "qkv_hbm", "out_hbm",
    "up_hbm", "down_hbm", "proj_hbm", "image_hbm", "image_qkv_hbm", "image_out_hbm", "image_up_hbm",
    "image_down_hbm",
)
joined_outs = (
    "up_out", "out_out", "qkv_out", "down_out", "proj_out", "norm_out", "hidden_out", "input_out", "slope_out",
)


def joined_kernel(names, *refs):
    refs = dict(zip(joined_ins + joined_outs + names, refs, strict=True))
    tok_load = pltpu.make_async_copy(refs["tok_hbm"], refs["tok"], refs["tok_sems"].at[2])
    tok_load.start()
    t = TextForward(refs)
    place = Place()
    place.greet()
    groups, group_rows = t.image_hbm.shape[0] // t.image_tok.shape[1], t.image_tok.shape[1]
    group_images = group_rows // IMG_TOK
    width, cols = t.width, place.cols

    def load_group(group):
        span = pl.ds(pl.multiple_of(group * group_rows, 16), group_rows)
        slot = group % 2
        return pltpu.make_async_copy(t.image_hbm.at[span], t.image_tok.at[slot], t.tok_sems.at[slot])

    load_group(0).start()
    gathers = iter(range(t.sends.shape[0]))

    def gather(pieces, *spans):
        i = next(gathers)
        return Gather(place, pieces, spans, t.sends.at[i], t.recvs.at[i])

    def piece_of_columns(axis, shard, at, target):
        lanes = pl.ds(at, target.shape[-1])
        return (
            axis, shard.at[:, :, lanes], lambda half: shard.at[half, :, lanes],
            lambda col: target.at[col], lambda col, half: target.at[col, half],
        )

    qkv_gathers = [
        gather(
            [piece_of_columns("y", t.image_qkv_hbm, j * width, t.iw_qkv.at[j])], t.iw_qkv.at[j, 0], t.iw_qkv.at[j, 0, 0]
        )
        for j in range(3)
    ]
    out_piece = (
        "z", t.image_out_hbm, lambda half: t.image_out_hbm.at[half],
        lambda col: t.iw_out.at[col // 2, pl.ds(col % 2 * 2, 2)],
        lambda col, half: t.iw_out.at[col // 2, col % 2 * 2 + half],
    )
    out_gather = gather([out_piece], t.iw_out.at[0, pl.ds(0, 2)], t.iw_out.at[0, 0])
    up_pieces = [
        piece_of_columns("yzyz"[j], t.image_up_hbm, j * width, t.iw_up.at[j // 2, j % 2]) for j in range(4)
    ]
    up_gather = gather(up_pieces, t.iw_up.at[0, 0], t.iw_up.at[0, 0, pl.ds(0, 2)])

    def piece_of_down(axis, lanes):
        return (
            axis, t.image_down_hbm.at[:, :, :, lanes],
            lambda half: t.image_down_hbm.at[pl.ds(half * 2, 2), :, :, lanes],
            lambda col: t.iw_down.at[col // 2, col % 2, :, :, :, lanes],
            lambda col, half: t.iw_down.at[col // 2, col % 2, pl.ds(half * 2, 2), :, :, lanes],
        )

    down_pieces = [piece_of_down("yz"[j], pl.ds(j * width // 2, width // 2)) for j in range(2)]
    down_gather = gather(down_pieces, t.iw_down.at[0, 0], t.iw_down.at[0, 0, pl.ds(0, 2)])

    def each(pieces, step):
        for piece in pieces:
            getattr(piece, step)()

    factors, pooled_factors = (
        RowFactors(
            place, getattr(t, "own" + tag), getattr(t, "held" + tag), t.factor_local.at[i], t.factor_sends.at[i],
            t.factor_recvs.at[i],
        )
        for i, tag in enumerate(("_inner", "_pooled"))
    )
    saves = {
        name: pltpu.make_async_copy(refs[name], refs[name + "_out"], t.save_sems.at[i])
        for i, name in enumerate(("hidden", "slope"))
    }
    tok_load.wait()
    t.prepare()
    place.meet()
    each(qkv_gathers, "start")
    out_gather.start()
    t.attention()
    qkv_gathers[0].share()
    t.middle()

    def after_feed(j):
        pl.when(j == 0)(qkv_gathers[1].share)
        pl.when(j == 1)(qkv_gathers[2].share)

        @pl.when(j == 2)
        def _():
            out_gather.share()
            up_gather.start()

    t.feed(after_feed)
    saves["slope"].start()
    inner_step = t.wide // place.rows
    for row in range(place.rows):
        t.own_inner[row] = t.inner_sum[:, row * inner_step : (row + 1) * inner_step]
    each(qkv_gathers, "relay")
    each(qkv_gathers, "finish")
    saves["slope"].wait()

    image_norm, image_mixed = t.w_out.at[pl.ds(0, group_rows)], t.w_proj.at[pl.ds(0, group_rows)]
    image_heads = t.w_qkv.at[pl.ds(0, group_rows)]

    def normed_group(group):
        return t.slope.at[pl.ds(0, group_rows), pl.ds(pl.multiple_of(group * width, 128), width)]

    @pl.loop(0, groups)
    def _(group):
        @pl.when(group + 1 < groups)
        def _():
            load_group(group + 1).start()

        load_group(group).wait()

        def between():
            pl.when(group == 0)(out_gather.relay)
            pl.when(group == groups - 1)(down_gather.share)

        def out_weight():
            @pl.when(group == 0)
            def _():
                out_gather.finish()
                factors.start()

            return t.iw_out[...].reshape(width, width)

        normed2, mean = image_mix(
            t.image_tok[group % 2], t.image_gain, t.image_bias, lambda j: t.iw_qkv[j].reshape(width, width), between,
            out_weight, image_norm, image_heads, image_mixed,
        )
        normed_group(group)[...] = normed2
        t.image_mean[pl.ds(pl.multiple_of(group * group_images, 8), group_images), :] = mean

        @pl.when(group == 0)
        def _():
            down_gather.start()

        @pl.when(group == 1)
        def _():
            up_gather.share()

        @pl.when(group == 2)
        def _():
            up_gather.relay()

    again = (("w_out", t.out_hbm), ("w_qkv", t.qkv_hbm), ("slope", t.slope_out))
    again = {
        name: pltpu.make_async_copy(source, refs[name], t.again_sems.at[i]) for i, (name, source) in enumerate(again)
    }
    t.load_proj.start()
    again["w_out"].start()
    again["w_qkv"].start()
    up_gather.finish()

    halves, half_images = 2, t.own.shape[0] // 2
    half_groups = half_images // group_images
    corner = place.y * 2 + place.x

    def image_copies(half, stage):
        mine = t.near_qkv.at[half, corner, place.k, pl.ds(0, 4 * half_images)]
        own = mine.at[pl.ds(pl.multiple_of(place.z * half_images, 16), half_images)]

        def copy(n, block, **moved):
            return remote(block, block, t.image_sends.at[half, n], t.image_recvs.at[half, n], place.at(**moved))

        if stage == 0:
            return [copy(i - 1, own, z=(place.z + i) % 4) for i in range(1, 4)]
        if stage == 1:
            moves = ({"x": 1 - place.x}, {"y": 1 - place.y}, {"x": 1 - place.x, "y": 1 - place.y})
            return [copy(3 + i, mine, **move) for i, move in enumerate(moves)]
        held = t.near_qkv.at[half, :, place.k, pl.ds(0, 4 * half_images)]
        return [copy(6, held, k=1 - place.k)]

    def image_start(half, stage):
        for copy in image_copies(half, stage):
            copy.start()

    def image_finish(half, stage):
        for copy in image_copies(half, stage):
            copy.wait()

    select = group_mean(half_images, half_images * IMG_TOK)

    @pl.loop(0, halves)
    def _(half):
        @pl.loop(0, t.wide // width)
        def _(j):
            weight = t.iw_up[j // 2, j % 2].reshape(width, width)
            total = 0.0
            for group in range(half_groups):
                at = pl.ds(pl.multiple_of((half * half_groups + group) * width, 128), width)
                inner = gelu(dot_nn(t.slope[:group_rows, at], weight)).astype(bf16)
                total = total + dot_nn(select[:, group * group_rows : (group + 1) * group_rows], inner)
            t.sums[:, pl.ds(pl.multiple_of(j * width, 128), width)] = total

            @pl.when((half == 0) & (j == 1))
            def _():
                down_gather.relay()

            @pl.when((half == 1) & (j == 1))
            def _():
                image_finish(0, 0)
                image_start(0, 1)

        @pl.when(half == 0)
        def _():
            down_gather.finish()
            factors.share()

        pl.when(half == 1)(again["slope"].start)
        high, low = split_low(t.sums[...] * (1.0 / IMG_TOK))
        pooled = dot_nn(jnp.concatenate([high, low], axis=0), t.iw_down[...].reshape(t.wide, width))
        part = pl.ds(pl.multiple_of(half * half_images, 16), half_images)
        pooled = t.image_mean[part, :] + pooled[:half_images] + pooled[half_images:]
        embed = pooled * lax.rsqrt(jnp.sum(pooled * pooled, axis=-1, keepdims=True) + norm_eps)
        t.own[part, :] = embed.astype(bf16)
        span = pl.ds(pl.multiple_of(place.z * half_images, 16), half_images)
        t.near_qkv[half, corner, place.k, span] = embed.astype(bf16)
        image_start(half, 0)

    factors.relay()
    t.finish()
    saves["hidden"].start()
    image_finish(halves - 1, 0)
    image_start(halves - 1, 1)
    image_finish(0, 1)
    image_start(0, 2)
    t.embed()
    width_step = width // place.rows
    pooled = t.pooled[...]
    spare = jnp.zeros((t.captions, t.own_pooled.shape[2] - width_step), bf16)
    for row in range(place.rows):
        block = pooled[:, row * width_step : (row + 1) * width_step]
        t.own_pooled[row] = jnp.concatenate([block, spare], axis=1)
    factors.finish()
    image_finish(halves - 1, 1)
    image_start(halves - 1, 2)
    for half in range(halves):
        image_finish(half, 2)

    images = t.near_qkv[:, :, :, : 4 * half_images].reshape(-1, width)
    own = t.own[...].astype(f32)
    lifted = jnp.exp2(dot_nt(t.text_embed[...], images) * (logit_scale * log2e))
    t.own_sums[...] = jnp.sum(lifted, axis=0, keepdims=True)
    t.all_sums[place.slot] = t.own_sums[...]
    sums = Exchange(place, t.own_sums, t.all_sums, t.sum_sends, t.sum_recvs)
    sums.start()
    col_sums = jnp.sum(lifted, axis=1, keepdims=True)
    positives = logit_scale * jnp.sum(own * t.text_embed[...].astype(f32), axis=(0, 1), keepdims=True)
    logs = jnp.sum(jnp.log(col_sums), axis=(0, 1), keepdims=True)
    saves["hidden"].wait()
    pooled_factors.start()
    sums.finish()
    row_sums = jnp.sum(t.all_sums[...], axis=0)
    sim_grad = (0.5 * (lifted * (1.0 / row_sums) + lifted * (1.0 / col_sums))).astype(bf16)
    t.embed_grad[...] = logit_scale * (dot_nn(sim_grad, images) - own)
    logs = logs + jnp.sum(jnp.log(row_sums), axis=(0, 1), keepdims=True) * (1.0 / place.count)
    t.loss[...] = jnp.broadcast_to(0.5 * logs - positives, t.loss.shape)

    shared = {
        "low_grad": t.inner.at[:, pl.ds(3 * width, width)], "heads_grad": t.inner.at[:, pl.ds(0, 3 * width)],
        "mixed_grad": t.hidden, "key_column": t.outer.at[:, pl.ds(0, 128)],
    }
    backward(place, TextBackward(refs | shared, again), pooled_factors)


def backward(place, t, pooled_factors):
    width, cols = t.width, place.cols
    widths = scatter_widths(t.wide, width, cols)
    shared = {
        "_up": (
            t.iw_up, t.iw_qkv.at[pl.ds(0, 2)], t.iw_qkv.at[2, :, :, :, pl.ds(0, 384)], t.iw_out.at[:, :, :, pl.ds(0, 384)]
        ),
        "_qkv": (
            t.iw_down, t.near_qkv, t.iw_qkv.at[2, :, :, :, pl.ds(384, 384)], t.iw_out.at[:, :, :, pl.ds(384, 384)]
        ),
        "_outs": (
            t.iw_down.at[:, :, :, :, :, pl.ds(640, 128)], t.near_qkv.at[:, :, :, :, pl.ds(640, 128)],
            t.x1_outs, t.y1_outs,
        ),
    }
    up, out, qkv = (
        GradientScatter(
            place, tag == "_qkv", halves, *shared[tag], *(getattr(t, name + tag) for name in scatter_names)
        )
        for halves, tag in zip(widths, ("_up", "_outs", "_qkv"))
    )
    factors = ColFactors(place, t.own_cols, t.held_cols, t.col_sends, t.col_recvs)
    late, last = (
        ChipSum(place, *(getattr(t, name + tag) for name in total_names)) for tag in ("_late", "_last")
    )

    left = []

    def leave(name, ref):
        left.append(pltpu.make_async_copy(ref, getattr(t, name + "_out"), t.leave_sems.at[len(left)]))
        left[-1].start()

    def store(scatter, part, at, value):
        held = scatter.held
        size = value.shape[1]
        held[part // 2, part % 2, :, :, :, at : at + size] = value.reshape(*held.shape[2:5], size)

    def fill(scatter, chunk, total, block):
        at, size = scatter.lanes(chunk)[0].start, scatter.lanes(chunk)[0].size
        true = min(size, total // cols - at)
        for part in range(cols):
            start = part * (total // cols) + at
            store(scatter, part, at, block(slice(start, start + true)))

    def fill_up(chunk, between=lambda: None):
        at = up.lanes(chunk)[0].start
        size = up.lanes(chunk)[0].size
        for part in range(cols):
            start = part * up.held.shape[5] + at
            t.inner_grad(pl.ds(start, size))
        between()
        fill(up, chunk, t.wide, t.up_block)
        up.start(chunk, 0)

    proj_grad, branch = t.project()
    out_step = width // cols
    for part in range(cols):
        columns = slice(part * out_step, (part + 1) * out_step)
        t.own_cols[part] = jnp.concatenate([branch[:, columns], proj_grad[:, columns]], axis=1)
    t.held_cols[place.col, place.row] = t.own_cols[place.col]
    factors.start(0)
    pooled_factors.share()
    t.wait("slope")
    fill_up(0)
    fill_up(1)
    factors.finish(0)
    factors.start(1)
    up.step_on(0, 1)
    fill_up(2)
    up.step_on(1, 1)
    t.to_middle()
    factors.finish(1)
    factors.start(2)
    up.step_on(2, 1)
    pooled_factors.relay()
    t.middle()
    up.step_on(0, 2)
    for part in range(cols):
        value = t.out_block(slice(part * out_step, (part + 1) * out_step))
        store(out, part, 0, value[:, :128])
        store(qkv, part, 3 * out_step, value[:, 128:])
    out.start(0, 0)
    t.total_late[...] = jnp.concatenate([t.norm_grad[2:3, :], t.norm_grad[3:4, :], t.loss[...]], axis=1)
    late.start()
    t.to_heads()
    up.step_on(1, 2)
    out.step_on(0, 1)
    late.spread()

    def after(block):
        @pl.when(block == 0)
        def _():
            factors.finish(2)
            factors.start(3)

        @pl.when(block == 1)
        def _():
            up.step_on(2, 2)
            up.step_on(0, 3)

        @pl.when(block == 2)
        def _():
            up.step_on(1, 3)

    t.attention(after)
    fill(qkv, 0, 3 * width, t.qkv_block)
    qkv.start(0, 0)
    out.step_on(0, 2)
    fill(qkv, 1, 3 * width, t.qkv_block)
    qkv.start(1, 0)
    qkv.step_on(0, 1)
    fill(qkv, 2, 3 * width, t.qkv_block)
    qkv.start(2, 0)
    up.step_on(2, 3)
    qkv.step_on(1, 1)

    def between():
        up.step_on(0, 4)
        up.step_on(1, 4)
        qkv.step_on(0, 2)

    t.input(between)
    leave("input", t.tok)
    qkv.step_on(2, 1)
    out.step_on(0, 3)
    up.step_on(2, 4)
    t.total_last[...] = jnp.concatenate([t.norm_grad[0:1, :], t.norm_grad[1:2, :]], axis=1)
    last.start()
    qkv.step_on(0, 3)
    last.spread()
    factors.finish(3)
    pooled_factors.finish()
    col_factors = t.held_cols[...].reshape(-1, t.held_cols.shape[3])
    grown = dot_tn(col_factors, t.held_inner[...].reshape(-1, t.held_inner.shape[3]))
    t.down[...] = grown[:out_step]
    leave("down", t.down)
    grown = dot_tn(col_factors, t.held_pooled[...].reshape(-1, t.held_pooled.shape[3]))
    t.proj[...] = grown[out_step:].T[: width // place.rows]
    leave("proj", t.proj)
    qkv.step_on(1, 2)
    out.step_on(0, 4)
    qkv.step_on(2, 2)
    qkv.step_on(1, 3)
    t.norms[:, 2 * width :] = late.finish()
    qkv.step_on(2, 3)
    for chunk in range(len(up.halves)):
        up.finish(chunk, 4)
    t.up[...] = up.total()
    leave("up", t.up)
    t.norms[:, : 2 * width] = last.finish()
    leave("norm", t.norms)
    out.finish(0, 4)
    t.out[:, :128] = out.total()
    for chunk in range(len(qkv.halves)):
        qkv.finish(chunk, 3)
    total = qkv.total()
    t.qkv[...] = total[:, : 3 * out_step]
    leave("qkv", t.qkv)
    t.out[:, 128:] = total[:, 3 * out_step : 4 * out_step - 128]
    leave("out", t.out)
    for copy in left:
        copy.wait()


def whole(shape):
    return pl.BlockSpec(shape, lambda *_: (0,) * len(shape))


in_vmem = pl.BlockSpec(memory_space=pltpu.VMEM)
in_smem = pl.BlockSpec(memory_space=pltpu.SMEM)
anywhere = pl.BlockSpec(memory_space=pl.ANY)


def plain(kernel, outs, ins, scratch, name, out_specs=None, **settings):
    return pl.pallas_call(
        kernel,
        out_shape=outs,
        in_specs=ins,
        out_specs=out_specs or [in_vmem] * len(outs),
        scratch_shapes=scratch,
        compiler_params=pltpu.CompilerParams(vmem_limit_bytes=VMEM_LIMIT, **settings),
        name=name,
    )


def array(shape, dtype):
    return jax.ShapeDtypeStruct(shape, dtype)


def partners(x, col_count):
    order = [(i, i ^ 2) for i in range(col_count)]
    near = [(i, i ^ 1) for i in range(col_count)]
    far = lax.ppermute(x, "col", order)
    return [x, lax.ppermute(x, "col", near), far, lax.ppermute(far, "col", near)]


def body(
    image_tokens, image_norm_gain, image_norm_bias, image_qkv, image_out, image_up, image_down,
    text_tokens, text_lengths, norm1_gain, norm1_bias, norm2_gain, norm2_bias,
    text_qkv, text_out, text_up, text_down, text_proj,
):
    tokens, width = text_tokens.shape
    captions = text_lengths.shape[0]
    length = tokens // captions
    wide = text_up.shape[1]
    row_count, col_count = lax.axis_size("row"), lax.axis_size("col")
    row, col = lax.axis_index("row"), lax.axis_index("col")
    pair_total = captions * row_count * col_count
    image_rows, images = image_tokens.shape[0], image_tokens.shape[0] // IMG_TOK

    count = row_count * col_count
    joined = (row_count, col_count) == (8, 4)
    vectors = (norm1_gain, norm1_bias, norm2_gain, norm2_bias)
    weights = (text_qkv, text_out, text_up, text_down, text_proj)
    weight_scratch = [pltpu.VMEM(w.shape, bf16) for w in weights]

    text_shapes = (
        array((tokens, width), bf16),
        array((captions, width), bf16),
        array((captions, width), f32),
        array((captions, width), bf16),
        array((captions, wide), bf16),
        array((tokens, 3 * width), bf16),
        array((tokens, width), bf16),
        array((tokens, width), f32),
        array((tokens, wide), bf16),
        array((width, tokens), bf16),
    )
    text_specs = [in_vmem, in_smem] + [in_vmem] * 4 + [anywhere] * 5
    text_buffers = weight_scratch + [
        pltpu.VMEM((tokens, width), bf16),
        pltpu.VMEM((tokens, wide), bf16),
        pltpu.VMEM((captions, 1), jnp.int32),
        pltpu.VMEM((1, tokens), f32),
        pltpu.SemaphoreType.DMA((5,)),
    ]
    text_in = (text_tokens, text_lengths, *vectors, *weights)
    groups = 4
    group_rows, group_images = image_rows // groups, images // groups
    mix_buffers = [
        pltpu.VMEM((group_rows, width), bf16),
        pltpu.VMEM((group_rows, 3 * width), bf16),
        pltpu.VMEM((group_rows, width), bf16),
    ]
    mix_weights = [pltpu.VMEM((width, 3 * width), bf16), pltpu.VMEM((width, width), bf16)]
    embed_weights = [pltpu.VMEM((width, wide), bf16), pltpu.VMEM((wide, width), bf16)]
    both = ("row", "col")

    if joined:
        halves, rows = 2, width // row_count
        out_step, inner_step = width // col_count, wide // row_count
        packed = -(-rows // 128) * 128
        dma = pltpu.SemaphoreType.DMA
        widths = scatter_widths(wide, width, col_count)
        sets = {tag: scatter_scratch(rows, each) for each, tag in zip(widths, ("_up", "_outs", "_qkv"))}
        scratch = dict(zip(text_names, (pltpu.VMEM(shape.shape, shape.dtype) for shape in text_shapes)))
        scratch |= dict(zip(text_scratch, text_buffers))
        scratch |= {
            "tok": pltpu.VMEM((tokens, width), bf16),
            "iw_qkv": pltpu.VMEM((3, 4, 2, rows, width), bf16),
            "iw_out": pltpu.VMEM((2, 4, rows, width), bf16),
            "iw_up": pltpu.VMEM((2, 2, 4, 2, rows, width), bf16),
            "iw_down": pltpu.VMEM((2, 2, 4, 2, rows, width), bf16),
            "image_tok": pltpu.VMEM((2, group_rows, width), bf16),
            "image_mean": pltpu.VMEM((images, width), f32),
            "sums": pltpu.VMEM((images // halves, wide), f32),
            "own": pltpu.VMEM((images, width), bf16),
            "own_inner": pltpu.VMEM((row_count, captions, inner_step), bf16),
            "held_inner": pltpu.VMEM((col_count, row_count, captions, inner_step), bf16),
            "own_pooled": pltpu.VMEM((row_count, captions, packed), bf16),
            "held_pooled": pltpu.VMEM((col_count, row_count, captions, packed), bf16),
            "up": pltpu.VMEM((rows, wide // col_count), f32),
            "out": pltpu.VMEM((rows, out_step), f32),
            "qkv": pltpu.VMEM((rows, 3 * out_step), f32),
            "down": pltpu.VMEM((out_step, inner_step), f32),
            "proj": pltpu.VMEM((rows, out_step), f32),
            "norms": pltpu.VMEM((1, 4 * width + 128), f32),
            "leave_sems": dma((7,)),
            "own_sums": pltpu.VMEM((1, pair_total), f32),
            "all_sums": pltpu.VMEM((count, 1, pair_total), f32),
            "tok_sems": dma((3,)),
            "again_sems": dma((3,)),
            "save_sems": dma((2,)),
            "sends": dma((6, 4)),
            "recvs": dma((6, 5)),
            "factor_local": dma((2,)),
            "factor_sends": dma((2, 4)),
            "factor_recvs": dma((2, 4)),
            "image_sends": dma((halves, 7)),
            "image_recvs": dma((halves, 7)),
            "sum_sends": dma((1,)),
            "sum_recvs": dma((1,)),
            "embed_grad": pltpu.VMEM((captions, width), f32),
            "loss": pltpu.VMEM((1, 128), f32),
            "branch": pltpu.VMEM((captions, width), bf16),
            "norm_grad": pltpu.VMEM((8, width), f32),
            "outer": pltpu.VMEM((tokens, width), f32),
            "mid_grad": pltpu.VMEM((tokens, width), f32),
            "near_qkv": pltpu.VMEM((2, 4, 2, rows, width), bf16),
            "own_cols": pltpu.VMEM((col_count, captions, 2 * out_step), bf16),
            "held_cols": pltpu.VMEM((col_count, row_count, captions, 2 * out_step), bf16),
            "col_sends": dma((7,)),
            "col_recvs": dma((7,)),
        }
        scratch |= dict(zip(("x1_outs", "y1_outs"), sets["_outs"][2:]))
        for tag, buffers in sets.items():
            scratch |= {name + tag: buffer for name, buffer in zip(scatter_names, buffers[4:])}
        for tag, size in (("_late", 2 * width + 128), ("_last", 2 * width)):
            scratch |= {name + tag: buffer for name, buffer in zip(total_names, chip_sum_scratch(size, count // 2))}
        up_grad, out_grad, qkv_grad, grad_down, grad_proj, norm_total, hidden, input_grad, _ = plain(
            functools.partial(joined_kernel, tuple(scratch)),
            (
                array((rows, wide // col_count), f32),
                array((rows, out_step), f32),
                array((rows, 3 * out_step), f32),
                array((out_step, inner_step), f32),
                array((rows, out_step), f32),
                array((1, 4 * width + 128), f32),
                array((tokens, width), bf16),
                array((tokens, width), bf16),
                array((tokens, wide), bf16),
            ),
            [in_smem] + [in_vmem] * 6 + [anywhere] * 11,
            list(scratch.values()),
            "joined",
            out_specs=[anywhere] * 9,
            collective_id=1,
            has_side_effects=True,
        )(
            text_lengths, *vectors, image_norm_gain, image_norm_bias, text_tokens, *weights, image_tokens,
            image_qkv.reshape(2, rows, -1), image_out.reshape(2, rows, -1), image_up.reshape(2, rows, -1),
            image_down.reshape(4, 2, rows, -1),
        )
        large = (hidden, input_grad, qkv_grad, out_grad, up_grad, grad_down, grad_proj)
        results = (array((1, 1), f32), *[array((width,), f32)] * 4, *(array(g.shape, g.dtype) for g in large))
        loss, *rest = plain(
            functools.partial(hand_over_kernel, pair_total), results, [in_vmem] * 8, [], "hand_over"
        )(norm_total, *large)
        norms, (hidden, input_grad, qkv_grad, out_grad, up_grad, grad_down, grad_proj) = rest[:4], rest[4:]
        return (
            loss.reshape(()), hidden, input_grad, *norms, qkv_grad, out_grad, up_grad, grad_down.T, grad_proj,
        )

    (hidden, text_embed, projected, pooled, inner_sum, heads, mixed, mid, slope, turned) = plain(
        text_forward_kernel, text_shapes, text_specs, text_buffers, "text_forward"
    )(*text_in)
    qkv_parts = partners(image_qkv, col_count)
    out_parts = partners(image_out, col_count)
    up_parts = partners(image_up, col_count)
    down_parts = partners(image_down, col_count)
    parts = [anywhere] * (2 * col_count)
    image_normed, image_mean = pl.pallas_call(
        functools.partial(image_mix_kernel, col_count),
        grid=(groups,),
        out_shape=(array((image_rows, width), bf16), array((images, width), f32)),
        in_specs=[
            pl.BlockSpec((group_rows, width), lambda i: (i, 0)),
            whole(image_norm_gain.shape),
            whole(image_norm_bias.shape),
        ]
        + parts,
        out_specs=(
            pl.BlockSpec((group_rows, width), lambda i: (i, 0)),
            pl.BlockSpec((group_images, width), lambda i: (i, 0)),
        ),
        scratch_shapes=mix_weights + mix_buffers + [pltpu.SemaphoreType.DMA((2, col_count))],
        compiler_params=pltpu.CompilerParams(vmem_limit_bytes=VMEM_LIMIT),
        name="image_mix",
    )(image_tokens, image_norm_gain, image_norm_bias, *qkv_parts, *out_parts)
    image_embed = pl.pallas_call(
        functools.partial(image_embed_kernel, col_count),
        grid=(groups,),
        out_shape=array((images, width), bf16),
        in_specs=[pl.BlockSpec((group_rows, width), lambda i: (i, 0)), whole((images, width))] + parts,
        out_specs=whole((images, width)),
        scratch_shapes=embed_weights
        + [pltpu.VMEM((images, wide), f32), pltpu.SemaphoreType.DMA((2, col_count))],
        compiler_params=pltpu.CompilerParams(vmem_limit_bytes=VMEM_LIMIT),
        name="image_embed",
    )(image_normed, image_mean, *up_parts, *down_parts)

    image_all = lax.all_gather(image_embed, both, axis=0, tiled=True)
    lifted = jnp.exp(logit_scale * dot_nt(image_all, text_embed))
    row_sums = lax.psum(jnp.sum(lifted, axis=1), both)
    col_sums = jnp.sum(lifted, axis=0)
    sim_grad = (0.5 * (lifted / row_sums[:, None] + lifted / col_sums[None, :])).astype(bf16)
    image_own = image_embed.astype(f32)
    embed_grad = logit_scale * (dot_tn(sim_grad, image_all) - image_own)
    positives = logit_scale * jnp.sum(image_own * text_embed.astype(f32), axis=1)
    loss_part = 0.5 * jnp.sum(jnp.log(col_sums) - 2.0 * positives)
    loss_part = loss_part + 0.5 * jnp.sum(jnp.log(row_sums)) / count

    saved = (text_tokens, heads, mixed, mid, slope, turned)
    backward_in = (text_lengths, *vectors, embed_grad, projected, *saved, *weights)
    backward_specs = [in_smem] + [in_vmem] * 6 + [anywhere] * 11
    backward_buffers = (
        [
            pltpu.VMEM((tokens, width), bf16),
            pltpu.VMEM((tokens, 3 * width), bf16),
            pltpu.VMEM((tokens, width), bf16),
            pltpu.VMEM((tokens, width), f32),
            pltpu.VMEM((tokens, wide), bf16),
        ]
        + weight_scratch
        + [
            pltpu.VMEM((tokens, width), bf16),
            pltpu.VMEM((width, tokens), bf16),
            pltpu.VMEM((tokens, width), f32),
            pltpu.VMEM((tokens, width), f32),
            pltpu.VMEM((tokens, width), bf16),
            pltpu.VMEM((tokens, width), bf16),
            pltpu.VMEM((tokens, 3 * width), bf16),
            pltpu.VMEM((captions, 1), jnp.int32),
            pltpu.VMEM((1, tokens), f32),
            pltpu.VMEM((tokens, 128), f32),
            pltpu.SemaphoreType.DMA((11,)),
        ]
    )

    def by_row(x):
        x = lax.all_to_all(x, "row", split_axis=1, concat_axis=0, tiled=True)
        return lax.all_gather(x, "col", axis=0, tiled=True)

    def by_col(x):
        x = lax.all_gather(x, "row", axis=0, tiled=True)
        return lax.all_to_all(x, "col", split_axis=1, concat_axis=0, tiled=True)

    (proj_grad, branch, up_grad, out_grad, qkv_grad, input_grad, norm_grads) = plain(
        text_backward_kernel,
        (
            array((captions, width), bf16),
            array((captions, width), bf16),
            array((col_count, width, wide // col_count), bf16),
            array((col_count, width, width // col_count), bf16),
            array((col_count, width, 3 * width // col_count), bf16),
            array((tokens, width), bf16),
            array((8, width), f32),
        ),
        backward_specs,
        backward_buffers,
        "text_backward",
    )(*backward_in)

    def scattered(matrix):
        blocks = matrix.reshape(count, width // row_count, matrix.shape[2])
        return lax.psum_scatter(blocks, ("col", "row"), scatter_dimension=0, tiled=True)[0].astype(f32)

    up_grad, out_grad, qkv_grad = scattered(up_grad), scattered(out_grad), scattered(qkv_grad)
    grad_down = dot_tn(by_row(inner_sum), by_col(branch))
    grad_proj = dot_tn(by_row(pooled), by_col(proj_grad))
    loss_total, norm_total = lax.psum((loss_part, norm_grads), both)
    norms = [norm_total[i] for i in range(4)]
    mean_loss = loss_total / pair_total
    return (
        mean_loss, hidden, input_grad, *norms, qkv_grad, out_grad, up_grad, grad_down, grad_proj,
    )


def solution(mesh):
    split = P(("row", "col"), None)
    grid = P("row", "col")
    in_specs = (
        split, P(), P(), P("col", None), P("col", None), P("col", None), P("col", None), split, P(("row", "col")),
    ) + (P(),) * 9
    out_specs = (P(), split, split, P(), P(), P(), P(), grid, grid, grid, grid, grid)
    return jax.shard_map(body, mesh=mesh, in_specs=in_specs, out_specs=out_specs, check_vma=False)
```

```python
import functools
import math
from types import SimpleNamespace

import jax
import jax.numpy as jnp
from jax import lax
from jax.experimental import pallas as pl
from jax.experimental.pallas import tpu as pltpu
from jax.sharding import PartitionSpec as P

HEADS = 12
IMG_TOK = 50
norm_eps = 1e-06
logit_scale = 50.0
masked_score = -1e30
log2e = math.log2(math.e)
f32 = jnp.float32
bf16 = jnp.bfloat16
VMEM_LIMIT = 62 * 2**20
MESH = pl.DeviceIdType.MESH


def dot_nn(a, b):
    return lax.dot_general(a, b, (((1,), (0,)), ((), ())), preferred_element_type=f32)


def dot_nt(a, b):
    return lax.dot_general(a, b, (((1,), (1,)), ((), ())), preferred_element_type=f32)


def dot_tn(a, b):
    return lax.dot_general(a, b, (((0,), (0,)), ((), ())), preferred_element_type=f32)


def split_low(x):
    high = x.astype(bf16)
    return high, (x - high.astype(f32)).astype(bf16)


def normed(x):
    centered = x - jnp.mean(x, axis=-1, keepdims=True)
    spread = lax.rsqrt(jnp.mean(centered * centered, axis=-1, keepdims=True) + norm_eps)
    return centered * spread, spread


def layer_norm(x, gain, bias):
    return normed(x)[0] * gain + bias


def gelu(x):
    return x * (0.5 + 0.5 * lax.erf(x * math.sqrt(0.5)))


def gelu_and_slope(x):
    below = 0.5 + 0.5 * lax.erf(x * math.sqrt(0.5))
    bell = jnp.exp2((-0.5 * log2e) * (x * x))
    return x * below, below + x * (bell * (1.0 / math.sqrt(2.0 * math.pi)))


def lane_halves(width):
    lane = lax.broadcasted_iota(jnp.int32, (1, width), 1)
    first = (lane < width // 2).astype(f32)
    return first.astype(bf16), (1.0 - first).astype(bf16)


def stack_heads(x, first, second):
    return jnp.concatenate([x * first, x * second], axis=0)


def join_heads(stacked):
    rows, width = stacked.shape[0] // 2, stacked.shape[1]
    lane = lax.broadcasted_iota(jnp.int32, (rows, width), 1)
    return jnp.where(lane < width // 2, stacked[:rows], stacked[rows:])


def soft_weights(query, key, bias, factor):
    scores = dot_nt(query, key) * (factor * log2e) + bias
    weights = jnp.exp2(scores - jnp.max(scores, axis=-1, keepdims=True))
    return weights, 1.0 / jnp.sum(weights, axis=-1, keepdims=True)


def set_lengths(lengths_ref, lens_ref, key_bias_ref):
    captions, tokens = lens_ref.shape[0], key_bias_ref.shape[1]
    length = tokens // captions
    caption = lax.broadcasted_iota(jnp.int32, (captions, 1), 0)
    token = lax.broadcasted_iota(jnp.int32, (1, tokens), 1)
    column, row = jnp.zeros((captions, 1), jnp.int32), jnp.zeros((1, tokens), jnp.int32)
    for n in range(captions):
        column = jnp.where(caption == n, lengths_ref[n], column)
        row = jnp.where(token // length == n, lengths_ref[n], row)
    lens_ref[...] = column
    key_bias_ref[...] = jnp.where(token % length < row, 0.0, masked_score)


def as_row(ref):
    return ref[...].reshape(1, ref.shape[0])


def text_bias(key_bias_ref, block, rows, length):
    near = lax.broadcasted_iota(jnp.int32, (rows, rows), 0) // length
    far = lax.broadcasted_iota(jnp.int32, (rows, rows), 1) // length
    columns = pl.ds(pl.multiple_of(block * rows, rows), rows)
    bias = jnp.where(near == far, key_bias_ref[:, columns], masked_score)
    return jnp.concatenate([bias, bias], axis=0)


def member(len_ref, captions, tokens):
    length = tokens // captions
    token = lax.broadcasted_iota(jnp.int32, (captions, tokens), 1)
    caption = lax.broadcasted_iota(jnp.int32, (captions, tokens), 0)
    return ((token // length == caption) & (token % length < len_ref[...])).astype(f32)


def spread_rows(x, length):
    rows, width = x.shape
    return jnp.broadcast_to(x[:, None, :], (rows, length, width)).reshape(rows * length, width)


def wide_steps(total, most=768):
    step = math.gcd(total, most)

    def loop(body):
        @pl.loop(0, total // step)
        def _(j):
            body(pl.ds(pl.multiple_of(j * step, 128), step))

    return loop


class TextForward:
    band = 128

    def __init__(self, refs):
        for name, ref in refs.items():
            setattr(self, name, ref)
        self.tokens, self.width = self.tok.shape
        self.captions = self.lens.shape[0]
        self.length = self.tokens // self.captions
        self.wide = self.w_up.shape[1]
        pairs = (
            (self.qkv_hbm, self.w_qkv), (self.out_hbm, self.w_out), (self.up_hbm, self.w_up),
            (self.down_hbm, self.w_down),
        )
        self.loads = load_weights(pairs, self.sems)
        self.load_proj = pltpu.make_async_copy(self.proj_hbm, self.w_proj, self.sems.at[4])

    def bands(self, step):
        pl.loop(0, self.tokens // self.band)(
            lambda i: step(pl.ds(pl.multiple_of(i * self.band, self.band), self.band))
        )

    def prepare(self):
        set_lengths(self.lengths, self.lens, self.key_bias)

        def first_norm(rows):
            norm = layer_norm(self.tok[rows, :].astype(f32), as_row(self.gain1), as_row(self.bias1))
            self.norm[rows, :] = norm.astype(bf16)

        self.bands(first_norm)

    def attention(self):
        width = self.width
        self.loads[0].wait()

        @wide_steps(3 * width)
        def _(columns):
            self.heads[:, columns] = dot_nn(self.norm[...], self.w_qkv[:, columns]).astype(bf16)

        first, second = lane_halves(128)
        factor = (width // HEADS) ** -0.5

        @pl.loop(0, self.tokens // self.band)
        def _(block):
            rows = pl.ds(pl.multiple_of(block * self.band, self.band), self.band)
            bias = text_bias(self.key_bias, block, self.band, self.length)
            for at in range(0, width, 128):
                query = stack_heads(self.heads[rows, at : at + 128], first, second)
                key = self.heads[rows, width + at : width + at + 128]
                weights, scale = soft_weights(query, key, bias, factor)
                value = self.heads[rows, 2 * width + at : 2 * width + at + 128]
                mixed = dot_nn(weights.astype(bf16), value) * scale
                self.mixed[rows, at : at + 128] = join_heads(mixed).astype(bf16)

    def middle(self):
        self.loads[1].wait()

        def second_norm(rows):
            mid = self.tok[rows, :].astype(f32) + dot_nn(self.mixed[rows, :], self.w_out[...])
            self.mid[rows, :] = mid
            self.norm[rows, :] = layer_norm(mid, as_row(self.gain2), as_row(self.bias2)).astype(bf16)

        self.bands(second_norm)

    def feed(self, after=lambda j: None):
        self.loads[2].wait()
        self.chosen = member(self.lens, self.captions, self.tokens).astype(bf16)
        place = lax.broadcasted_iota(jnp.int32, (self.captions, self.length, 1), 1)
        valid = (place < self.lens[...].reshape(self.captions, 1, 1)).astype(f32).reshape(self.tokens, 1)

        @pl.loop(0, self.wide // self.width)
        def _(j):
            columns = pl.ds(pl.multiple_of(j * self.width, 128), self.width)
            value, slope = gelu_and_slope(dot_nn(self.norm[...], self.w_up[:, columns]))
            value = value.astype(bf16)
            self.inner[:, columns] = value
            self.slope[:, columns] = (slope * valid).astype(bf16)
            self.inner_sum[:, columns] = dot_nn(self.chosen, value).astype(bf16)
            after(j)

    def finish(self):
        self.loads[3].wait()
        self.turned[...] = self.norm[...].T
        inverse = 1.0 / self.lens[...].astype(f32)

        @wide_steps(self.width)
        def _(columns):
            state = self.mid[:, columns] + dot_nn(self.inner[...], self.w_down[:, columns])
            self.hidden[:, columns] = state.astype(bf16)
            high, low = split_low(state)
            pooled = (dot_nn(self.chosen, high) + dot_nn(self.chosen, low)) * inverse
            self.pooled[:, columns] = pooled.astype(bf16)

    def embed(self):
        self.load_proj.wait()
        projected = dot_nn(self.pooled[...], self.w_proj[...])
        self.projected[...] = projected
        scale = lax.rsqrt(jnp.sum(projected * projected, axis=-1, keepdims=True) + norm_eps)
        self.text_embed[...] = (projected * scale).astype(bf16)


text_ins = (
    "tok", "lengths", "gain1", "bias1", "gain2", "bias2", "qkv_hbm", "out_hbm", "up_hbm", "down_hbm", "proj_hbm",
)
text_names = (
    "hidden", "text_embed", "projected", "pooled", "inner_sum", "heads", "mixed", "mid", "slope", "turned",
)
text_scratch = ("w_qkv", "w_out", "w_up", "w_down", "w_proj", "norm", "inner", "lens", "key_bias", "sems")


def text_forward_kernel(*refs):
    t = TextForward(dict(zip(text_ins + text_names + text_scratch, refs, strict=True)))
    t.load_proj.start()
    t.prepare()
    t.attention()
    t.middle()
    t.feed()
    t.finish()
    t.embed()


def load_weights(pairs, sems):
    loads = [pltpu.make_async_copy(s, d, sems.at[i]) for i, (s, d) in enumerate(pairs)]
    for load in loads:
        load.start()
    return loads


def spans(count, size):
    return lambda i: pl.ds(pl.multiple_of(i * size, size), size)


def norm_backward(outer, unit, spread, gain):
    outer = outer * gain
    inner = outer - jnp.mean(outer, axis=-1, keepdims=True)
    return spread * (inner - unit * jnp.mean(outer * unit, axis=-1, keepdims=True))


class TextBackward:
    band = 128

    def __init__(self, refs, loads):
        for name, ref in refs.items():
            setattr(self, name, ref)
        self.loads = loads
        self.tokens, self.width = self.tok.shape
        self.captions = self.lens.shape[0]
        self.length = self.tokens // self.captions
        self.wide = self.w_up.shape[1]
        self.pre_grad = self.slope

    def wait(self, name):
        if name in self.loads:
            self.loads[name].wait()

    def rows(self, i):
        return pl.ds(pl.multiple_of(i * self.band, self.band), self.band)

    def bands(self, step):
        pl.loop(0, self.tokens // self.band)(lambda i: step(self.rows(i)))

    def valid(self):
        place = lax.broadcasted_iota(jnp.int32, (self.captions, self.length, 1), 1)
        valid = place < self.lens[...].reshape(self.captions, 1, 1)
        return valid.astype(f32).reshape(self.tokens, 1)

    def project(self):
        projected = self.projected[...]
        embed_grad = self.embed_grad[...]
        r = lax.rsqrt(jnp.sum(projected * projected, axis=-1, keepdims=True) + norm_eps)
        along = jnp.sum(projected * embed_grad, axis=-1, keepdims=True)
        proj_grad = (r * embed_grad - (r * r * r) * projected * along).astype(bf16)
        self.wait("w_proj")
        state_grad = dot_nt(proj_grad, self.w_proj[...]) * (1.0 / self.lens[...].astype(f32))
        self.branch[...] = state_grad.astype(bf16)
        self.mid_grad[...] = spread_rows(state_grad, self.length) * self.valid()
        return proj_grad, self.branch[...]

    def wait_inner(self):
        self.wait("turned")
        self.wait("w_down")
        self.wait("slope")

    def inner_grad(self, columns):
        grad = dot_nt(self.branch[...], self.w_down[columns, :])
        pre_grad = spread_rows(grad, self.length) * self.slope[:, columns].astype(f32)
        self.pre_grad[:, columns] = pre_grad.astype(bf16)

    def up_block(self, columns):
        return dot_nn(self.turned[...], self.pre_grad[:, columns]).astype(bf16)

    def to_middle(self):
        self.wait("w_up")

        @wide_steps(self.width)
        def _(columns):
            self.outer[:, columns] = dot_nt(self.pre_grad[...], self.w_up[columns, :])

    def middle(self):
        self.wait("mid")
        self.norm_grad[...] = jnp.zeros_like(self.norm_grad)

        def through_norm(rows):
            unit, spread = normed(self.mid[rows, :])
            outer = self.outer[rows, :]
            self.norm_grad[2:3, :] += jnp.sum(outer * unit, axis=0, keepdims=True)
            self.norm_grad[3:4, :] += jnp.sum(outer, axis=0, keepdims=True)
            mid_grad = self.mid_grad[rows, :] + norm_backward(outer, unit, spread, as_row(self.gain2))
            self.mid_grad[rows, :] = mid_grad
            self.low_grad[rows, :] = mid_grad.astype(bf16)

        self.bands(through_norm)
        self.wait("mixed")
        self.turned[...] = self.mixed[...].T

    def out_block(self, columns):
        return dot_nn(self.turned[...], self.low_grad[:, columns]).astype(bf16)

    def to_heads(self):
        self.wait("w_out")
        self.wait("tok")

        def through_out(rows):
            self.mixed_grad[rows, :] = dot_nt(self.low_grad[rows, :], self.w_out[...]).astype(bf16)
            norm = layer_norm(self.tok[rows, :].astype(f32), as_row(self.gain1), as_row(self.bias1))
            self.norm[rows, :] = norm.astype(bf16)

        self.bands(through_out)
        self.turned[...] = self.norm[...].T

    def attention(self, after=lambda block: None):
        first, second = lane_halves(128)
        width = self.width
        factor = (width // HEADS) ** -0.5
        self.wait("heads")
        self.key_column[...] = jnp.broadcast_to((1.0 - self.valid()) * masked_score, self.key_column.shape)

        @pl.loop(0, self.tokens // self.band)
        def _(block):
            rows = self.rows(block)
            near = lax.broadcasted_iota(jnp.int32, (self.band, self.band), 0) // self.length
            far = lax.broadcasted_iota(jnp.int32, (self.band, self.band), 1) // self.length
            bias = jnp.where(near == far, self.key_column[rows, :], masked_score)
            bias = jnp.concatenate([bias, bias], axis=1)
            for at in range(0, width, 128):
                query = stack_heads(self.heads[rows, at : at + 128], first, second)
                key = self.heads[rows, width + at : width + at + 128]
                value = self.heads[rows, 2 * width + at : 2 * width + at + 128]
                grad = stack_heads(self.mixed_grad[rows, at : at + 128], first, second)
                scores = dot_nt(key, query) * (factor * log2e) + bias
                weights = jnp.exp2(scores - jnp.max(scores, axis=0, keepdims=True))
                probs = weights * (1.0 / jnp.sum(weights, axis=0, keepdims=True))
                prob_grad = dot_nt(value, grad)
                total = jnp.sum(prob_grad * probs, axis=0, keepdims=True)
                score_grad = (probs * (prob_grad - total)).astype(bf16)
                query_grad = join_heads(dot_tn(score_grad, key)) * factor
                self.heads_grad[rows, at : at + 128] = query_grad.astype(bf16)
                key_grad = dot_nn(score_grad, query) * factor
                self.heads_grad[rows, width + at : width + at + 128] = key_grad.astype(bf16)
                value_grad = dot_nn(probs.astype(bf16), grad)
                self.heads_grad[rows, 2 * width + at : 2 * width + at + 128] = value_grad.astype(bf16)
            after(block)

    def qkv_block(self, columns):
        return dot_nn(self.turned[...], self.heads_grad[:, columns]).astype(bf16)

    def input(self, between=lambda: None):
        self.wait("w_qkv")

        @wide_steps(self.width)
        def _(columns):
            self.outer[:, columns] = dot_nt(self.heads_grad[...], self.w_qkv[columns, :])

        between()

        def through_norm(rows):
            unit, spread = normed(self.tok[rows, :].astype(f32))
            outer = self.outer[rows, :]
            self.norm_grad[0:1, :] += jnp.sum(outer * unit, axis=0, keepdims=True)
            self.norm_grad[1:2, :] += jnp.sum(outer, axis=0, keepdims=True)
            inner = norm_backward(outer, unit, spread, as_row(self.gain1))
            self.tok[rows, :] = (self.mid_grad[rows, :] + inner).astype(bf16)

        self.bands(through_norm)


backward_ins = (
    "lengths", "gain1", "bias1", "gain2", "bias2", "embed_grad", "projected", "tok_hbm", "heads_hbm", "mixed_hbm",
    "mid_hbm", "slope_hbm", "turned_hbm", "w_qkv_hbm", "w_out_hbm", "w_up_hbm", "w_down_hbm", "w_proj_hbm",
)
backward_outs = ("proj_grad", "branch", "up_grad", "out_grad", "qkv_grad", "input_grad", "norm_grad")
backward_scratch = (
    "tok", "heads", "mixed", "mid", "slope", "w_qkv", "w_out", "w_up", "w_down", "w_proj", "norm", "turned",
    "outer", "mid_grad", "low_grad", "mixed_grad", "heads_grad", "lens", "key_bias", "key_column", "sems",
)


def text_backward_kernel(*refs):
    refs = dict(zip(backward_ins + backward_outs + backward_scratch, refs, strict=True))
    order = ("w_proj", "turned", "w_down", "slope", "w_up", "mid", "mixed", "w_out", "tok", "heads", "w_qkv")
    loads = load_weights([(refs[name + "_hbm"], refs[name]) for name in order], refs["sems"])
    t = TextBackward(refs, dict(zip(order, loads)))
    set_lengths(t.lengths, t.lens, t.key_bias)
    parts = t.up_grad.shape[0]

    def blocks(target, block):
        step = target.shape[2]
        for part in range(parts):
            target[part] = block(slice(part * step, (part + 1) * step))

    t.proj_grad[...] = t.project()[0]
    t.wait_inner()
    wide_steps(t.wide)(t.inner_grad)
    blocks(t.up_grad, t.up_block)
    t.to_middle()
    t.middle()
    blocks(t.out_grad, t.out_block)
    t.to_heads()
    t.attention()
    blocks(t.qkv_grad, t.qkv_block)
    t.input()
    t.input_grad[...] = t.tok[...]


class Place:
    def __init__(self, z_count=4, y_count=2, x_count=2, k_count=2):
        self.row, self.col = lax.axis_index("row"), lax.axis_index("col")
        self.z, self.y = self.row // y_count, self.row % y_count
        self.x, self.k = self.col // k_count, self.col % k_count
        self.rows, self.cols = z_count * y_count, x_count * k_count
        self.count = self.rows * self.cols
        self.me = self.row * self.cols + self.col
        self.slot = self.col * self.rows + self.row
        self.near_z, self.far_z = self.z + 1 - 2 * (self.z % 2), (self.z + 2) % 4

    def at(self, **moved):
        z, y, x, k = (moved.get(name, getattr(self, name)) for name in "zyxk")
        return z * 2 + y, x * 2 + k

    def peer(self, distance):
        other = (self.me + distance) % self.count
        return other // self.cols, other % self.cols

    def greet(self):
        barrier = pltpu.get_barrier_semaphore()

        @pl.loop(1, self.count)
        def _(distance):
            pl.semaphore_signal(barrier, inc=1, device_id=self.peer(distance), device_id_type=MESH)

    def meet(self):
        pl.semaphore_wait(pltpu.get_barrier_semaphore(), self.count - 1)


def remote(src, dst, send, recv, to):
    return pltpu.make_async_remote_copy(
        src_ref=src, dst_ref=dst, send_sem=send, recv_sem=recv, device_id=to, device_id_type=MESH
    )


def wait_all(blocks, send, recv, to):
    remote(blocks, blocks, send, recv, to).wait()


class Gather:
    def __init__(self, place, pieces, spans, sends, recvs):
        mate, next_x = place.at(k=1 - place.k), place.at(x=1 - place.x)
        across = next_x[1]
        self.spans, self.sends, self.recvs, self.mate = spans, sends, recvs, mate
        self.locals, self.nears, self.fars, self.alongs, self.passes = [], [], [], [], []
        for axis, own, half, block, part in pieces:
            here = place.y if axis == "y" else place.z % 2
            partner = place.at(y=1 - place.y) if axis == "y" else place.at(z=place.near_z)
            mine, theirs = part(across, here), block(across)
            self.locals.append(pltpu.make_async_copy(own, block(place.col), recvs.at[4]))
            self.nears.append(remote(own, block(place.col), sends.at[0], recvs.at[0], mate))
            self.fars.append(remote(half(here), part(place.col, here), sends.at[1], recvs.at[1], next_x))
            self.alongs.append(remote(mine, mine, sends.at[2], recvs.at[2], partner))
            self.passes.append(remote(theirs, theirs, sends.at[3], recvs.at[3], mate))

    def wait(self, i, span):
        wait_all(self.spans[span], self.sends.at[i], self.recvs.at[i], self.mate)

    def start(self):
        for copies in (self.fars, self.nears, self.locals):
            for copy in copies:
                copy.start()

    def share(self):
        self.wait(1, 1)
        for copy in self.alongs:
            copy.start()

    def relay(self):
        self.wait(2, 1)
        for copy in self.passes:
            copy.start()

    def finish(self):
        pltpu.make_async_copy(self.spans[0], self.spans[0], self.recvs.at[4]).wait()
        self.wait(0, 0)
        self.wait(3, 0)


class RowFactors:
    def __init__(self, place, own, held, local, sends, recvs):
        self.place, self.own, self.held, self.sends, self.recvs = place, own, held, sends, recvs
        self.local = pltpu.make_async_copy(own.at[place.row], held.at[place.col, place.row], local)
        mine, across = held.at[place.col], held.at[place.at(x=1 - place.x)[1]]
        mate, next_x = place.at(k=1 - place.k), place.at(x=1 - place.x)
        self.far = remote(mine, mine, sends.at[1], recvs.at[1], next_x)
        self.near = remote(mine, mine, sends.at[2], recvs.at[2], mate)
        self.passed = remote(across, across, sends.at[3], recvs.at[3], mate)

    def start(self):
        self.local.start()
        p = self.place

        @pl.loop(1, p.rows)
        def _(distance):
            row = (p.row + distance) % p.rows
            remote(
                self.own.at[row], self.held.at[p.col, p.row], self.sends.at[0], self.recvs.at[0], (row, p.col)
            ).start()

    def share(self):
        self.local.wait()
        p = self.place
        to = p.at(k=1 - p.k)
        wait_all(self.held.at[p.col, pl.ds(0, p.rows - 1)], self.sends.at[0], self.recvs.at[0], to)
        self.far.start()
        self.near.start()

    def relay(self):
        self.far.wait()
        self.passed.start()

    def finish(self):
        self.near.wait()
        self.passed.wait()


class Exchange:
    def __init__(self, place, source, slots, sends, recvs):
        self.place, self.source, self.slots = place, source, slots
        self.sems = sends.at[0], recvs.at[0]

    def start(self):
        p = self.place

        @pl.loop(1, p.count)
        def _(distance):
            remote(self.source, self.slots.at[p.slot], *self.sems, p.peer(distance)).start()

    def finish(self):
        p = self.place
        wait_all(self.slots.at[pl.ds(0, p.count - 1)], *self.sems, p.at(k=1 - p.k))


class ChipSum:
    def __init__(self, place, total, got, slots, sends, recvs):
        self.place, self.total, self.got, self.slots = place, total, got, slots
        self.sends, self.recvs = sends, recvs
        self.chip, self.chips = place.row * 2 + place.x, place.rows * 2
        self.mate = place.at(k=1 - place.k)

    def near(self):
        return remote(self.total, self.got, self.sends.at[0], self.recvs.at[0], self.mate)

    def start(self):
        self.near().start()

    def spread(self):
        self.near().wait()
        self.total[...] = self.total[...] + self.got[...]
        self.slots[self.chip] = self.total[...]

        @pl.loop(1, self.chips)
        def _(distance):
            other = (self.chip + distance) % self.chips
            to = other // 2, other % 2 * 2 + self.place.k
            remote(self.total, self.slots.at[self.chip], self.sends.at[1], self.recvs.at[1], to).start()

    def finish(self):
        wait_all(self.slots.at[pl.ds(0, self.chips - 1)], self.sends.at[1], self.recvs.at[1], self.mate)
        return jnp.sum(self.slots[...], axis=0)


class GradientScatter:
    def __init__(self, place, straight, halves, held, near, x1, y1, x2, y2, far, sends, recvs):
        self.straight = straight
        self.place, self.held, self.near, self.far = place, held, near, far
        self.x1, self.y1, self.x2, self.y2 = x1, y1, x2, y2
        self.sends, self.recvs = sends, recvs
        self.halves = halves

    def lanes(self, chunk):
        ones, twos = zip(*self.halves[:chunk], (0, 0))
        at_one, at_two = sum(ones), sum(twos)
        at = at_one + at_two
        one, two = self.halves[chunk]
        return (
            pl.ds(at, one + two), pl.ds(at, one), pl.ds(at + one, two), pl.ds(at_one, one), pl.ds(at_two, two)
        )

    def copies(self, chunk, stage):
        p, held = self.place, self.held
        x, y, z, k = p.x, p.y, p.z, p.k
        whole, one, two, part_one, part_two = self.lanes(chunk)

        def copy(n, src, dst, **moved):
            send = self.sends.at[chunk, (0, 0, 1, 0, 1, 0, 1, 2)[n]]
            return remote(src, dst, send, self.recvs.at[chunk, n], p.at(**moved))

        if stage == 0:
            return [copy(0, held.at[:, 1 - k, :, :, :, whole], self.near.at[:, :, :, :, whole], k=1 - k)]
        if stage == 1:
            copies = []
            if one.size:
                copies.append(copy(1, held.at[1 - x, k, :, :, :, one], self.x1.at[:, :, :, part_one], x=1 - x))
            if two.size:
                copies.append(copy(2, held.at[:, k, :, 1 - y, :, two], self.y1.at[:, :, :, part_two], y=1 - y))
            return copies
        if stage == 2:
            copies = []
            if one.size:
                copies.append(copy(3, held.at[x, k, :, 1 - y, :, one], self.y2.at[:, :, part_one], y=1 - y))
            if two.size:
                copies.append(copy(4, held.at[1 - x, k, :, y, :, two], self.x2.at[:, :, part_two], x=1 - x))
            return copies
        if stage == 3 and self.straight:
            return [
                copy(4 + i, held.at[x, k, (z + i) % 4, y, :, whole], self.far.at[i - 1, :, whole], z=(z + i) % 4)
                for i in range(1, 4)
            ]
        if stage == 3:
            blocks = p.near_z, held.shape[2] - 1 - z
            return [
                copy(5 + i, held.at[x, k, block, y, :, whole], self.far.at[i, :, whole], z=p.near_z)
                for i, block in enumerate(blocks)
            ]
        return [copy(7, held.at[x, k, p.far_z, y, :, whole], self.far.at[2, :, whole], z=p.far_z)]

    def start(self, chunk, stage):
        for copy in self.copies(chunk, stage):
            copy.start()

    def finish(self, chunk, stage):
        for copy in self.copies(chunk, stage):
            copy.wait()
        p, held = self.place, self.held
        x, y, k = p.x, p.y, p.k
        z_count = held.shape[2]
        whole, one, two, part_one, part_two = self.lanes(chunk)

        def add(target, source):
            target[...] = (target[...].astype(f32) + source[...].astype(f32)).astype(bf16)

        if stage == 0:

            @pl.loop(0, z_count)
            def _(z):
                for i in range(2):
                    for j in range(2):
                        add(held.at[i, k, z, j, :, whole], self.near.at[i, z, j, :, whole])

        if stage == 1:

            @pl.loop(0, z_count)
            def _(z):
                for i in range(2):
                    if one.size:
                        add(held.at[x, k, z, i, :, one], self.x1.at[z, i, :, part_one])
                    if two.size:
                        add(held.at[i, k, z, y, :, two], self.y1.at[i, z, :, part_two])

        if stage == 2:

            @pl.loop(0, z_count)
            def _(z):
                if one.size:
                    add(held.at[x, k, z, y, :, one], self.y2.at[z, :, part_one])
                if two.size:
                    add(held.at[x, k, z, y, :, two], self.x2.at[z, :, part_two])

        if stage == 3 and not self.straight:
            add(held.at[x, k, p.far_z, y, :, whole], self.far.at[1, :, whole])

    def step_on(self, chunk, stage):
        self.finish(chunk, stage - 1)
        self.start(chunk, stage)

    def total(self):
        p = self.place
        total = self.held[p.x, p.k, p.z, p.y, :, : self.far.shape[2]].astype(f32)
        for i in (0, 1, 2) if self.straight else (0, 2):
            total = total + self.far[i].astype(f32)
        return total


def chip_sum_scratch(size, chips):
    return [
        pltpu.VMEM((1, size), f32), pltpu.VMEM((1, size), f32), pltpu.VMEM((chips, 1, size), f32),
        pltpu.SemaphoreType.DMA((2,)), pltpu.SemaphoreType.DMA((2,)),
    ]


def scatter_scratch(rows, halves):
    one, two = (sum(widths) for widths in zip(*halves))
    spare = max(two, 128)
    shapes = [
        (2, 2, 4, 2, rows, one + two), (2, 4, 2, rows, one + two), (4, 2, rows, one), (2, 4, rows, spare),
        (4, rows, spare), (4, rows, one), (3, rows, one + two),
    ]
    sems = [pltpu.SemaphoreType.DMA((len(halves), 3)), pltpu.SemaphoreType.DMA((len(halves), 8))]
    return [pltpu.VMEM(shape, bf16) for shape in shapes] + sems


class ColFactors:
    def __init__(self, place, own, held, sends, recvs):
        self.place, self.own, self.held, self.sends, self.recvs = place, own, held, sends, recvs

    def copies(self, stage):
        p, held = self.place, self.held

        def copy(n, src, dst, **moved):
            return remote(src, dst, self.sends.at[n], self.recvs.at[n], p.at(**moved))

        if stage == 0:
            mine = held.at[p.col, p.row]
            moves = ({"x": 1 - p.x}, {"k": 1 - p.k}, {"x": 1 - p.x, "k": 1 - p.k})
            return [copy(i, self.own.at[p.at(**move)[1]], mine, **move) for i, move in enumerate(moves)]
        if stage == 1:
            mine = held.at[:, p.row]
            return [copy(3, mine, mine, y=1 - p.y)]
        mine, other = (held.at[:, pl.ds(z * 2, 2)] for z in (p.z, p.far_z))
        if stage == 2:
            return [copy(4, mine, mine, z=p.far_z)]
        return [copy(5, mine, mine, z=p.near_z), copy(6, other, other, z=p.near_z)]

    def start(self, stage):
        for copy in self.copies(stage):
            copy.start()

    def finish(self, stage):
        for copy in self.copies(stage):
            copy.wait()


def scatter_widths(wide, width, cols):
    ups = tuple((128, 128) for _ in range(wide // cols // 256))
    rest = 4 * width // cols - 128
    return ups, ((128, 0),), ((128, 128), (128, 128), (rest - 512, 0))


scatter_names = ("x2", "y2", "far", "sends", "recvs")
total_names = ("total", "got", "slots", "sends", "recvs")


def hand_over_kernel(pair_total, norms, *refs):
    sources, (loss, *vectors), targets = refs[:7], refs[7:12], refs[12:]
    width = vectors[0].shape[0]
    loss[...] = norms[:, 4 * width : 4 * width + 1] * (1.0 / pair_total)
    for i, vector in enumerate(vectors):
        vector[...] = norms[:, i * width : (i + 1) * width].reshape(width)
    for source, target in zip(sources, targets, strict=True):
        target[...] = source[...]


def group_mean(images, rows):
    token = lax.broadcasted_iota(jnp.int32, (images, rows), 1)
    image = lax.broadcasted_iota(jnp.int32, (images, rows), 0)
    inside = (token >= image * IMG_TOK) & (token < (image + 1) * IMG_TOK)
    return inside.astype(f32).astype(bf16)


def load_parts(parts, target, sems, col, col_count):
    depth = target.shape[0] // col_count
    copies = []
    for k, part in enumerate(parts):
        place = pl.multiple_of((col ^ k) * depth, depth)
        copies.append(pltpu.make_async_copy(part, target.at[pl.ds(place, depth)], sems.at[k]))
    return copies


def image_mix(tokens, gain_ref, bias_ref, qkv_block, between, out_weight, norm_ref, heads_ref, mixed_ref):
    rows, width = tokens.shape
    images = rows // IMG_TOK
    norm_ref[...] = layer_norm(tokens.astype(f32), gain_ref[0:1, :], bias_ref[0:1, :]).astype(bf16)

    @pl.loop(0, 3)
    def _(j):
        columns = pl.ds(pl.multiple_of(j * width, width), width)
        heads_ref[:, columns] = dot_nn(norm_ref[...], qkv_block(j)).astype(bf16)

    between()
    first, second = lane_halves(128)
    factor = (width // HEADS) ** -0.5
    window = 112

    @pl.loop(0, images // 2)
    def _(pair):
        start = pair * (2 * IMG_TOK)
        low = pl.multiple_of(start // 16 * 16, 16)
        near = lax.broadcasted_iota(jnp.int32, (window, window), 0) + low
        far = lax.broadcasted_iota(jnp.int32, (window, window), 1) + low
        same = (near >= start) & (near < start + 2 * IMG_TOK) & (far >= start) & (far < start + 2 * IMG_TOK)
        same = same & ((near >= start + IMG_TOK) == (far >= start + IMG_TOK))
        bias = jnp.where(same, 0.0, masked_score)
        bias = jnp.concatenate([bias, bias], axis=0)
        keep = lax.broadcasted_iota(jnp.int32, (16, 128), 0) + low < start
        span, head, tail = pl.ds(low, window), pl.ds(low, 16), pl.ds(low + 16, window - 16)
        for at in range(0, width, 128):
            query = stack_heads(heads_ref[span, at : at + 128], first, second)
            key = heads_ref[span, width + at : width + at + 128]
            weights, scale = soft_weights(query, key, bias, factor)
            value = heads_ref[span, 2 * width + at : 2 * width + at + 128]
            mixed = join_heads(dot_nn(weights.astype(bf16), value) * scale)
            former = mixed_ref[head, at : at + 128].astype(f32)
            mixed_ref[head, at : at + 128] = jnp.where(keep, former, mixed[:16]).astype(bf16)
            mixed_ref[tail, at : at + 128] = mixed[16:].astype(bf16)

    mid = tokens.astype(f32) + dot_nn(mixed_ref[...], out_weight())
    high, low = split_low(mid)
    select = group_mean(images, rows)
    mean = (dot_nn(select, high) + dot_nn(select, low)) * (1.0 / IMG_TOK)
    return layer_norm(mid, gain_ref[1:2, :], bias_ref[1:2, :]).astype(bf16), mean


def image_mix_kernel(col_count, tok_ref, gain_ref, bias_ref, *refs):
    qkv_parts, out_parts = refs[:col_count], refs[col_count : 2 * col_count]
    normed_ref, mean_ref, w_qkv, w_out, *buffers, sems = refs[2 * col_count :]
    col = lax.axis_index("col")

    @pl.when(pl.program_id(0) == 0)
    def _():
        copies = load_parts(qkv_parts, w_qkv, sems.at[0], col, col_count)
        copies += load_parts(out_parts, w_out, sems.at[1], col, col_count)
        for copy in copies:
            copy.start()
        for copy in copies:
            copy.wait()

    width = tok_ref.shape[1]

    def qkv_block(j):
        return w_qkv[:, pl.ds(pl.multiple_of(j * width, width), width)]

    normed_ref[...], mean_ref[...] = image_mix(
        tok_ref[...], gain_ref, bias_ref, qkv_block, lambda: None, lambda: w_out[...], *buffers
    )


def image_embed_kernel(col_count, normed_ref, mean_ref, *refs):
    up_parts, down_parts = refs[:col_count], refs[col_count : 2 * col_count]
    embed_ref, w_up, w_down, sum_ref, sems = refs[2 * col_count :]
    rows, width = normed_ref.shape
    images = rows // IMG_TOK
    wide = w_up.shape[1]
    step = pl.program_id(0)
    col = lax.axis_index("col")
    downs = load_parts(down_parts, w_down, sems.at[1], col, col_count)

    @pl.when(step == 0)
    def _():
        ups = load_parts(up_parts, w_up, sems.at[0], col, col_count)
        for copy in ups + downs:
            copy.start()
        for copy in ups:
            copy.wait()

    select = group_mean(images, rows)

    @wide_steps(wide)
    def _(columns):
        inner = gelu(dot_nn(normed_ref[...], w_up[:, columns])).astype(bf16)
        sum_ref[pl.ds(pl.multiple_of(step * images, images), images), columns] = dot_nn(select, inner)

    @pl.when(step == pl.num_programs(0) - 1)
    def _():
        for copy in downs:
            copy.wait()
        high, low = split_low(sum_ref[...] * (1.0 / IMG_TOK))
        pooled = mean_ref[...] + dot_nn(high, w_down[...]) + dot_nn(low, w_down[...])
        embed_ref[...] = (
            pooled * lax.rsqrt(jnp.sum(pooled * pooled, axis=-1, keepdims=True) + norm_eps)
        ).astype(bf16)


joined_ins = (
    "lengths", "gain1", "bias1", "gain2", "bias2", "image_gain", "image_bias", "tok_hbm", "qkv_hbm", "out_hbm",
    "up_hbm", "down_hbm", "proj_hbm", "image_hbm", "image_qkv_hbm", "image_out_hbm", "image_up_hbm",
    "image_down_hbm",
)
joined_outs = (
    "up_out", "out_out", "qkv_out", "down_out", "proj_out", "norm_out", "hidden_out", "input_out", "slope_out",
)


def joined_kernel(names, *refs):
    refs = dict(zip(joined_ins + joined_outs + names, refs, strict=True))
    tok_load = pltpu.make_async_copy(refs["tok_hbm"], refs["tok"], refs["tok_sems"].at[2])
    tok_load.start()
    t = TextForward(refs)
    place = Place()
    place.greet()
    groups, group_rows = t.image_hbm.shape[0] // t.image_tok.shape[1], t.image_tok.shape[1]
    group_images = group_rows // IMG_TOK
    width, cols = t.width, place.cols

    def load_group(group):
        span = pl.ds(pl.multiple_of(group * group_rows, 16), group_rows)
        slot = group % 2
        return pltpu.make_async_copy(t.image_hbm.at[span], t.image_tok.at[slot], t.tok_sems.at[slot])

    load_group(0).start()
    gathers = iter(range(t.sends.shape[0]))

    def gather(pieces, *spans):
        i = next(gathers)
        return Gather(place, pieces, spans, t.sends.at[i], t.recvs.at[i])

    def piece_of_columns(axis, shard, at, target):
        lanes = pl.ds(at, target.shape[-1])
        return (
            axis, shard.at[:, :, lanes], lambda half: shard.at[half, :, lanes],
            lambda col: target.at[col], lambda col, half: target.at[col, half],
        )

    qkv_gathers = [
        gather(
            [piece_of_columns("y", t.image_qkv_hbm, j * width, t.iw_qkv.at[j])], t.iw_qkv.at[j, 0], t.iw_qkv.at[j, 0, 0]
        )
        for j in range(3)
    ]
    out_piece = (
        "z", t.image_out_hbm, lambda half: t.image_out_hbm.at[half],
        lambda col: t.iw_out.at[col // 2, pl.ds(col % 2 * 2, 2)],
        lambda col, half: t.iw_out.at[col // 2, col % 2 * 2 + half],
    )
    out_gather = gather([out_piece], t.iw_out.at[0, pl.ds(0, 2)], t.iw_out.at[0, 0])
    up_pieces = [
        piece_of_columns("yzyz"[j], t.image_up_hbm, j * width, t.iw_up.at[j // 2, j % 2]) for j in range(4)
    ]
    up_gather = gather(up_pieces, t.iw_up.at[0, 0], t.iw_up.at[0, 0, pl.ds(0, 2)])

    def piece_of_down(axis, lanes):
        return (
            axis, t.image_down_hbm.at[:, :, :, lanes],
            lambda half: t.image_down_hbm.at[pl.ds(half * 2, 2), :, :, lanes],
            lambda col: t.iw_down.at[col // 2, col % 2, :, :, :, lanes],
            lambda col, half: t.iw_down.at[col // 2, col % 2, pl.ds(half * 2, 2), :, :, lanes],
        )

    down_pieces = [piece_of_down("yz"[j], pl.ds(j * width // 2, width // 2)) for j in range(2)]
    down_gather = gather(down_pieces, t.iw_down.at[0, 0], t.iw_down.at[0, 0, pl.ds(0, 2)])

    def each(pieces, step):
        for piece in pieces:
            getattr(piece, step)()

    factors, pooled_factors = (
        RowFactors(
            place, getattr(t, "own" + tag), getattr(t, "held" + tag), t.factor_local.at[i], t.factor_sends.at[i],
            t.factor_recvs.at[i],
        )
        for i, tag in enumerate(("_inner", "_pooled"))
    )
    saves = {
        name: pltpu.make_async_copy(refs[name], refs[name + "_out"], t.save_sems.at[i])
        for i, name in enumerate(("hidden", "slope"))
    }
    tok_load.wait()
    t.prepare()
    place.meet()
    each(qkv_gathers, "start")
    out_gather.start()
    t.attention()
    qkv_gathers[0].share()
    t.middle()

    def after_feed(j):
        pl.when(j == 0)(qkv_gathers[1].share)
        pl.when(j == 1)(qkv_gathers[2].share)

        @pl.when(j == 2)
        def _():
            out_gather.share()
            up_gather.start()
            qkv_gathers[0].relay()

        pl.when(j == 3)(qkv_gathers[1].relay)

    t.feed(after_feed)
    saves["slope"].start()
    inner_step = t.wide // place.rows
    for row in range(place.rows):
        t.own_inner[row] = t.inner_sum[:, row * inner_step : (row + 1) * inner_step]
    saves["slope"].wait()

    image_norm, image_mixed = t.w_out.at[pl.ds(0, group_rows)], t.w_proj.at[pl.ds(0, group_rows)]
    image_heads = t.w_qkv.at[pl.ds(0, group_rows)]

    def normed_group(group):
        return t.slope.at[pl.ds(0, group_rows), pl.ds(pl.multiple_of(group * width, 128), width)]

    @pl.loop(0, groups)
    def _(group):
        @pl.when(group + 1 < groups)
        def _():
            load_group(group + 1).start()

        load_group(group).wait()

        def qkv_block(j):
            pl.when((group == 0) & (j == 0))(qkv_gathers[2].relay)
            for i, weight in enumerate(qkv_gathers):
                pl.when((group == 0) & (j == i))(weight.finish)
            return t.iw_qkv[j].reshape(width, width)

        def between():
            pl.when(group == 0)(out_gather.relay)

            @pl.when(group == groups - 1)
            def _():
                up_gather.relay()
                down_gather.share()

        def out_weight():
            @pl.when(group == 0)
            def _():
                out_gather.finish()
                factors.start()

            return t.iw_out[...].reshape(width, width)

        normed2, mean = image_mix(
            t.image_tok[group % 2], t.image_gain, t.image_bias, qkv_block, between,
            out_weight, image_norm, image_heads, image_mixed,
        )
        normed_group(group)[...] = normed2
        t.image_mean[pl.ds(pl.multiple_of(group * group_images, 8), group_images), :] = mean

        @pl.when(group == 0)
        def _():
            down_gather.start()

        @pl.when(group == 1)
        def _():
            up_gather.share()

    again = (("w_out", t.out_hbm), ("w_qkv", t.qkv_hbm), ("slope", t.slope_out))
    again = {
        name: pltpu.make_async_copy(source, refs[name], t.again_sems.at[i]) for i, (name, source) in enumerate(again)
    }
    t.load_proj.start()
    again["w_out"].start()
    again["w_qkv"].start()
    up_gather.finish()

    halves, half_images = 2, t.own.shape[0] // 2
    half_groups = half_images // group_images
    corner = place.y * 2 + place.x

    def image_block(half, z):
        span = pl.ds(pl.multiple_of(z * half_images, 16), half_images)
        return t.near_qkv.at[half, corner, place.k, span]

    in_plane = ({"x": 1 - place.x}, {"y": 1 - place.y}, {"x": 1 - place.x, "y": 1 - place.y})

    def image_start(half, stage):
        def start(i, block, **moved):
            sems = t.image_sends.at[half, i], t.image_recvs.at[half, i]
            remote(block, block, *sems, place.at(**moved)).start()

        if stage == 0:
            for i in range(1, 4):
                start(0, image_block(half, place.z), z=(place.z + i) % 4)
            for move in in_plane:
                start(1, image_block(half, place.z), **move)
        if stage == 1:
            for i in range(1, 4):
                for move in in_plane:
                    start(2, image_block(half, (place.z + i) % 4), **move)
        if stage == 2:
            start(3, t.near_qkv.at[half, :, place.k, pl.ds(0, 4 * half_images)], k=1 - place.k)

    def image_finish(half, stage):
        three, mate = pl.ds(0, 3 * half_images), place.at(k=1 - place.k)

        def wait(i, span):
            wait_all(span, t.image_sends.at[half, i], t.image_recvs.at[half, i], mate)

        if stage == 0:
            wait(0, t.near_qkv.at[half, 0, place.k, three])
        if stage == 1:
            wait(1, t.near_qkv.at[half, 0, place.k, three])
            wait(2, t.near_qkv.at[half, pl.ds(0, 3), place.k, three])
        if stage == 2:
            wait(3, t.near_qkv.at[half, :, place.k, pl.ds(0, 4 * half_images)])

    select = group_mean(half_images, half_images * IMG_TOK)

    @pl.loop(0, halves)
    def _(half):
        @pl.loop(0, t.wide // width)
        def _(j):
            weight = t.iw_up[j // 2, j % 2].reshape(width, width)
            total = 0.0
            for group in range(half_groups):
                at = pl.ds(pl.multiple_of((half * half_groups + group) * width, 128), width)
                inner = gelu(dot_nn(t.slope[:group_rows, at], weight)).astype(bf16)
                total = total + dot_nn(select[:, group * group_rows : (group + 1) * group_rows], inner)
            t.sums[:, pl.ds(pl.multiple_of(j * width, 128), width)] = total

            @pl.when((half == 0) & (j == 1))
            def _():
                down_gather.relay()

            @pl.when((half == 1) & (j == 1))
            def _():
                image_finish(0, 0)
                image_start(0, 1)

        @pl.when(half == 0)
        def _():
            down_gather.finish()
            factors.share()

        pl.when(half == 1)(again["slope"].start)
        high, low = split_low(t.sums[...] * (1.0 / IMG_TOK))
        pooled = dot_nn(jnp.concatenate([high, low], axis=0), t.iw_down[...].reshape(t.wide, width))
        part = pl.ds(pl.multiple_of(half * half_images, 16), half_images)
        pooled = t.image_mean[part, :] + pooled[:half_images] + pooled[half_images:]
        embed = pooled * lax.rsqrt(jnp.sum(pooled * pooled, axis=-1, keepdims=True) + norm_eps)
        t.own[part, :] = embed.astype(bf16)
        span = pl.ds(pl.multiple_of(place.z * half_images, 16), half_images)
        t.near_qkv[half, corner, place.k, span] = embed.astype(bf16)
        image_start(half, 0)

    factors.relay()
    t.finish()
    saves["hidden"].start()
    image_finish(halves - 1, 0)
    image_start(halves - 1, 1)
    image_finish(0, 1)
    image_start(0, 2)
    t.embed()
    width_step = width // place.rows
    pooled = t.pooled[...]
    spare = jnp.zeros((t.captions, t.own_pooled.shape[2] - width_step), bf16)
    for row in range(place.rows):
        block = pooled[:, row * width_step : (row + 1) * width_step]
        t.own_pooled[row] = jnp.concatenate([block, spare], axis=1)
    factors.finish()
    image_finish(halves - 1, 1)
    image_start(halves - 1, 2)
    for half in range(halves):
        image_finish(half, 2)

    images = t.near_qkv[:, :, :, : 4 * half_images].reshape(-1, width)
    own = t.own[...].astype(f32)
    lifted = jnp.exp2(dot_nt(t.text_embed[...], images) * (logit_scale * log2e))
    t.own_sums[...] = jnp.sum(lifted, axis=0, keepdims=True)
    t.all_sums[place.slot] = t.own_sums[...]
    sums = Exchange(place, t.own_sums, t.all_sums, t.sum_sends, t.sum_recvs)
    sums.start()
    col_sums = jnp.sum(lifted, axis=1, keepdims=True)
    positives = logit_scale * jnp.sum(own * t.text_embed[...].astype(f32), axis=(0, 1), keepdims=True)
    logs = jnp.sum(jnp.log(col_sums), axis=(0, 1), keepdims=True)
    saves["hidden"].wait()
    pooled_factors.start()
    sums.finish()
    row_sums = jnp.sum(t.all_sums[...], axis=0)
    sim_grad = (0.5 * (lifted * (1.0 / row_sums) + lifted * (1.0 / col_sums))).astype(bf16)
    t.embed_grad[...] = logit_scale * (dot_nn(sim_grad, images) - own)
    logs = logs + jnp.sum(jnp.log(row_sums), axis=(0, 1), keepdims=True) * (1.0 / place.count)
    t.loss[...] = jnp.broadcast_to(0.5 * logs - positives, t.loss.shape)

    shared = {
        "low_grad": t.inner.at[:, pl.ds(3 * width, width)], "heads_grad": t.inner.at[:, pl.ds(0, 3 * width)],
        "mixed_grad": t.hidden, "key_column": t.outer.at[:, pl.ds(0, 128)],
    }
    backward(place, TextBackward(refs | shared, again), pooled_factors)


def backward(place, t, pooled_factors):
    width, cols = t.width, place.cols
    widths = scatter_widths(t.wide, width, cols)
    shared = {
        "_up": (
            t.iw_up, t.iw_qkv.at[pl.ds(0, 2)], t.iw_qkv.at[2, :, :, :, pl.ds(0, 384)], t.iw_out.at[:, :, :, pl.ds(0, 384)]
        ),
        "_qkv": (
            t.iw_down, t.near_qkv, t.iw_qkv.at[2, :, :, :, pl.ds(384, 384)], t.iw_out.at[:, :, :, pl.ds(384, 384)]
        ),
        "_outs": (
            t.iw_down.at[:, :, :, :, :, pl.ds(640, 128)], t.near_qkv.at[:, :, :, :, pl.ds(640, 128)],
            t.x1_outs, t.y1_outs,
        ),
    }
    up, out, qkv = (
        GradientScatter(
            place, tag == "_qkv", halves, *shared[tag], *(getattr(t, name + tag) for name in scatter_names)
        )
        for halves, tag in zip(widths, ("_up", "_outs", "_qkv"))
    )
    factors = ColFactors(place, t.own_cols, t.held_cols, t.col_sends, t.col_recvs)
    late, last = (
        ChipSum(place, *(getattr(t, name + tag) for name in total_names)) for tag in ("_late", "_last")
    )

    left = []

    def leave(name, ref):
        left.append(pltpu.make_async_copy(ref, getattr(t, name + "_out"), t.leave_sems.at[len(left)]))
        left[-1].start()

    def store(scatter, part, at, value):
        held = scatter.held
        size = value.shape[1]
        held[part // 2, part % 2, :, :, :, at : at + size] = value.reshape(*held.shape[2:5], size)

    def fill(scatter, chunk, total, block):
        at, size = scatter.lanes(chunk)[0].start, scatter.lanes(chunk)[0].size
        true = min(size, total // cols - at)
        for part in range(cols):
            start = part * (total // cols) + at
            store(scatter, part, at, block(slice(start, start + true)))

    def fill_up(chunk, between=lambda: None):
        at = up.lanes(chunk)[0].start
        size = up.lanes(chunk)[0].size
        for part in range(cols):
            start = part * up.held.shape[5] + at
            t.inner_grad(pl.ds(start, size))
        between()
        fill(up, chunk, t.wide, t.up_block)
        up.start(chunk, 0)

    proj_grad, branch = t.project()
    out_step = width // cols
    for part in range(cols):
        columns = slice(part * out_step, (part + 1) * out_step)
        t.own_cols[part] = jnp.concatenate([branch[:, columns], proj_grad[:, columns]], axis=1)
    t.held_cols[place.col, place.row] = t.own_cols[place.col]
    factors.start(0)
    t.wait("slope")
    fill_up(0)
    pooled_factors.share()
    fill_up(1)
    factors.finish(0)
    factors.start(1)
    up.step_on(0, 1)
    fill_up(2)
    up.step_on(1, 1)
    t.to_middle()
    factors.finish(1)
    factors.start(2)
    up.step_on(2, 1)
    pooled_factors.relay()
    t.middle()
    up.step_on(0, 2)
    for part in range(cols):
        value = t.out_block(slice(part * out_step, (part + 1) * out_step))
        store(out, part, 0, value[:, :128])
        store(qkv, part, 3 * out_step, value[:, 128:])
    out.start(0, 0)
    t.total_late[...] = jnp.concatenate([t.norm_grad[2:3, :], t.norm_grad[3:4, :], t.loss[...]], axis=1)
    late.start()
    t.to_heads()
    up.step_on(1, 2)
    out.step_on(0, 1)
    late.spread()

    def after(block):
        @pl.when(block == 0)
        def _():
            factors.finish(2)
            factors.start(3)

        @pl.when(block == 1)
        def _():
            up.step_on(2, 2)
            up.step_on(0, 3)

        @pl.when(block == 2)
        def _():
            up.step_on(1, 3)

    t.attention(after)
    fill(qkv, 0, 3 * width, t.qkv_block)
    qkv.start(0, 0)
    out.step_on(0, 2)
    fill(qkv, 1, 3 * width, t.qkv_block)
    qkv.start(1, 0)
    qkv.step_on(0, 1)
    fill(qkv, 2, 3 * width, t.qkv_block)
    qkv.start(2, 0)
    up.step_on(2, 3)
    qkv.step_on(1, 1)

    def between():
        up.step_on(0, 4)
        up.step_on(1, 4)
        qkv.step_on(0, 2)

    t.input(between)
    leave("input", t.tok)
    qkv.step_on(2, 1)
    out.step_on(0, 3)
    up.step_on(2, 4)
    t.total_last[...] = jnp.concatenate([t.norm_grad[0:1, :], t.norm_grad[1:2, :]], axis=1)
    last.start()
    qkv.step_on(0, 3)
    last.spread()
    factors.finish(3)
    pooled_factors.finish()
    col_factors = t.held_cols[...].reshape(-1, t.held_cols.shape[3])
    grown = dot_tn(col_factors, t.held_inner[...].reshape(-1, t.held_inner.shape[3]))
    t.down[...] = grown[:out_step]
    leave("down", t.down)
    grown = dot_tn(col_factors, t.held_pooled[...].reshape(-1, t.held_pooled.shape[3]))
    t.proj[...] = grown[out_step:].T[: width // place.rows]
    leave("proj", t.proj)
    qkv.step_on(1, 2)
    out.step_on(0, 4)
    qkv.step_on(2, 2)
    qkv.step_on(1, 3)
    t.norms[:, 2 * width :] = late.finish()
    qkv.step_on(2, 3)
    for chunk in range(len(up.halves)):
        up.finish(chunk, 4)
    t.up[...] = up.total()
    leave("up", t.up)
    t.norms[:, : 2 * width] = last.finish()
    leave("norm", t.norms)
    out.finish(0, 4)
    t.out[:, :128] = out.total()
    for chunk in range(len(qkv.halves)):
        qkv.finish(chunk, 3)
    total = qkv.total()
    t.qkv[...] = total[:, : 3 * out_step]
    leave("qkv", t.qkv)
    t.out[:, 128:] = total[:, 3 * out_step : 4 * out_step - 128]
    leave("out", t.out)
    for copy in left:
        copy.wait()


def whole(shape):
    return pl.BlockSpec(shape, lambda *_: (0,) * len(shape))


in_vmem = pl.BlockSpec(memory_space=pltpu.VMEM)
in_smem = pl.BlockSpec(memory_space=pltpu.SMEM)
anywhere = pl.BlockSpec(memory_space=pl.ANY)


def plain(kernel, outs, ins, scratch, name, out_specs=None, **settings):
    return pl.pallas_call(
        kernel,
        out_shape=outs,
        in_specs=ins,
        out_specs=out_specs or [in_vmem] * len(outs),
        scratch_shapes=scratch,
        compiler_params=pltpu.CompilerParams(vmem_limit_bytes=VMEM_LIMIT, **settings),
        name=name,
    )


def array(shape, dtype):
    return jax.ShapeDtypeStruct(shape, dtype)


def partners(x, col_count):
    order = [(i, i ^ 2) for i in range(col_count)]
    near = [(i, i ^ 1) for i in range(col_count)]
    far = lax.ppermute(x, "col", order)
    return [x, lax.ppermute(x, "col", near), far, lax.ppermute(far, "col", near)]


def body(
    image_tokens, image_norm_gain, image_norm_bias, image_qkv, image_out, image_up, image_down,
    text_tokens, text_lengths, norm1_gain, norm1_bias, norm2_gain, norm2_bias,
    text_qkv, text_out, text_up, text_down, text_proj,
):
    tokens, width = text_tokens.shape
    captions = text_lengths.shape[0]
    length = tokens // captions
    wide = text_up.shape[1]
    row_count, col_count = lax.axis_size("row"), lax.axis_size("col")
    row, col = lax.axis_index("row"), lax.axis_index("col")
    pair_total = captions * row_count * col_count
    image_rows, images = image_tokens.shape[0], image_tokens.shape[0] // IMG_TOK

    count = row_count * col_count
    joined = (row_count, col_count) == (8, 4)
    vectors = (norm1_gain, norm1_bias, norm2_gain, norm2_bias)
    weights = (text_qkv, text_out, text_up, text_down, text_proj)
    weight_scratch = [pltpu.VMEM(w.shape, bf16) for w in weights]

    text_shapes = (
        array((tokens, width), bf16),
        array((captions, width), bf16),
        array((captions, width), f32),
        array((captions, width), bf16),
        array((captions, wide), bf16),
        array((tokens, 3 * width), bf16),
        array((tokens, width), bf16),
        array((tokens, width), f32),
        array((tokens, wide), bf16),
        array((width, tokens), bf16),
    )
    text_specs = [in_vmem, in_smem] + [in_vmem] * 4 + [anywhere] * 5
    text_buffers = weight_scratch + [
        pltpu.VMEM((tokens, width), bf16),
        pltpu.VMEM((tokens, wide), bf16),
        pltpu.VMEM((captions, 1), jnp.int32),
        pltpu.VMEM((1, tokens), f32),
        pltpu.SemaphoreType.DMA((5,)),
    ]
    text_in = (text_tokens, text_lengths, *vectors, *weights)
    groups = 4
    group_rows, group_images = image_rows // groups, images // groups
    mix_buffers = [
        pltpu.VMEM((group_rows, width), bf16),
        pltpu.VMEM((group_rows, 3 * width), bf16),
        pltpu.VMEM((group_rows, width), bf16),
    ]
    mix_weights = [pltpu.VMEM((width, 3 * width), bf16), pltpu.VMEM((width, width), bf16)]
    embed_weights = [pltpu.VMEM((width, wide), bf16), pltpu.VMEM((wide, width), bf16)]
    both = ("row", "col")

    if joined:
        halves, rows = 2, width // row_count
        out_step, inner_step = width // col_count, wide // row_count
        packed = -(-rows // 128) * 128
        dma = pltpu.SemaphoreType.DMA
        widths = scatter_widths(wide, width, col_count)
        sets = {tag: scatter_scratch(rows, each) for each, tag in zip(widths, ("_up", "_outs", "_qkv"))}
        scratch = dict(zip(text_names, (pltpu.VMEM(shape.shape, shape.dtype) for shape in text_shapes)))
        scratch |= dict(zip(text_scratch, text_buffers))
        scratch |= {
            "tok": pltpu.VMEM((tokens, width), bf16),
            "iw_qkv": pltpu.VMEM((3, 4, 2, rows, width), bf16),
            "iw_out": pltpu.VMEM((2, 4, rows, width), bf16),
            "iw_up": pltpu.VMEM((2, 2, 4, 2, rows, width), bf16),
            "iw_down": pltpu.VMEM((2, 2, 4, 2, rows, width), bf16),
            "image_tok": pltpu.VMEM((2, group_rows, width), bf16),
            "image_mean": pltpu.VMEM((images, width), f32),
            "sums": pltpu.VMEM((images // halves, wide), f32),
            "own": pltpu.VMEM((images, width), bf16),
            "own_inner": pltpu.VMEM((row_count, captions, inner_step), bf16),
            "held_inner": pltpu.VMEM((col_count, row_count, captions, inner_step), bf16),
            "own_pooled": pltpu.VMEM((row_count, captions, packed), bf16),
            "held_pooled": pltpu.VMEM((col_count, row_count, captions, packed), bf16),
            "up": pltpu.VMEM((rows, wide // col_count), f32),
            "out": pltpu.VMEM((rows, out_step), f32),
            "qkv": pltpu.VMEM((rows, 3 * out_step), f32),
            "down": pltpu.VMEM((out_step, inner_step), f32),
            "proj": pltpu.VMEM((rows, out_step), f32),
            "norms": pltpu.VMEM((1, 4 * width + 128), f32),
            "leave_sems": dma((7,)),
            "own_sums": pltpu.VMEM((1, pair_total), f32),
            "all_sums": pltpu.VMEM((count, 1, pair_total), f32),
            "tok_sems": dma((3,)),
            "again_sems": dma((3,)),
            "save_sems": dma((2,)),
            "sends": dma((6, 4)),
            "recvs": dma((6, 5)),
            "factor_local": dma((2,)),
            "factor_sends": dma((2, 4)),
            "factor_recvs": dma((2, 4)),
            "image_sends": dma((halves, 4)),
            "image_recvs": dma((halves, 4)),
            "sum_sends": dma((1,)),
            "sum_recvs": dma((1,)),
            "embed_grad": pltpu.VMEM((captions, width), f32),
            "loss": pltpu.VMEM((1, 128), f32),
            "branch": pltpu.VMEM((captions, width), bf16),
            "norm_grad": pltpu.VMEM((8, width), f32),
            "outer": pltpu.VMEM((tokens, width), f32),
            "mid_grad": pltpu.VMEM((tokens, width), f32),
            "near_qkv": pltpu.VMEM((2, 4, 2, rows, width), bf16),
            "own_cols": pltpu.VMEM((col_count, captions, 2 * out_step), bf16),
            "held_cols": pltpu.VMEM((col_count, row_count, captions, 2 * out_step), bf16),
            "col_sends": dma((7,)),
            "col_recvs": dma((7,)),
        }
        scratch |= dict(zip(("x1_outs", "y1_outs"), sets["_outs"][2:]))
        for tag, buffers in sets.items():
            scratch |= {name + tag: buffer for name, buffer in zip(scatter_names, buffers[4:])}
        for tag, size in (("_late", 2 * width + 128), ("_last", 2 * width)):
            scratch |= {name + tag: buffer for name, buffer in zip(total_names, chip_sum_scratch(size, count // 2))}
        up_grad, out_grad, qkv_grad, grad_down, grad_proj, norm_total, hidden, input_grad, _ = plain(
            functools.partial(joined_kernel, tuple(scratch)),
            (
                array((rows, wide // col_count), f32),
                array((rows, out_step), f32),
                array((rows, 3 * out_step), f32),
                array((out_step, inner_step), f32),
                array((rows, out_step), f32),
                array((1, 4 * width + 128), f32),
                array((tokens, width), bf16),
                array((tokens, width), bf16),
                array((tokens, wide), bf16),
            ),
            [in_smem] + [in_vmem] * 6 + [anywhere] * 11,
            list(scratch.values()),
            "joined",
            out_specs=[anywhere] * 9,
            collective_id=1,
            has_side_effects=True,
        )(
            text_lengths, *vectors, image_norm_gain, image_norm_bias, text_tokens, *weights, image_tokens,
            image_qkv.reshape(2, rows, -1), image_out.reshape(2, rows, -1), image_up.reshape(2, rows, -1),
            image_down.reshape(4, 2, rows, -1),
        )
        large = (hidden, input_grad, qkv_grad, out_grad, up_grad, grad_down, grad_proj)
        results = (array((1, 1), f32), *[array((width,), f32)] * 4, *(array(g.shape, g.dtype) for g in large))
        loss, *rest = plain(
            functools.partial(hand_over_kernel, pair_total), results, [in_vmem] * 8, [], "hand_over"
        )(norm_total, *large)
        norms, (hidden, input_grad, qkv_grad, out_grad, up_grad, grad_down, grad_proj) = rest[:4], rest[4:]
        return (
            loss.reshape(()), hidden, input_grad, *norms, qkv_grad, out_grad, up_grad, grad_down.T, grad_proj,
        )

    (hidden, text_embed, projected, pooled, inner_sum, heads, mixed, mid, slope, turned) = plain(
        text_forward_kernel, text_shapes, text_specs, text_buffers, "text_forward"
    )(*text_in)
    qkv_parts = partners(image_qkv, col_count)
    out_parts = partners(image_out, col_count)
    up_parts = partners(image_up, col_count)
    down_parts = partners(image_down, col_count)
    parts = [anywhere] * (2 * col_count)
    image_normed, image_mean = pl.pallas_call(
        functools.partial(image_mix_kernel, col_count),
        grid=(groups,),
        out_shape=(array((image_rows, width), bf16), array((images, width), f32)),
        in_specs=[
            pl.BlockSpec((group_rows, width), lambda i: (i, 0)),
            whole(image_norm_gain.shape),
            whole(image_norm_bias.shape),
        ]
        + parts,
        out_specs=(
            pl.BlockSpec((group_rows, width), lambda i: (i, 0)),
            pl.BlockSpec((group_images, width), lambda i: (i, 0)),
        ),
        scratch_shapes=mix_weights + mix_buffers + [pltpu.SemaphoreType.DMA((2, col_count))],
        compiler_params=pltpu.CompilerParams(vmem_limit_bytes=VMEM_LIMIT),
        name="image_mix",
    )(image_tokens, image_norm_gain, image_norm_bias, *qkv_parts, *out_parts)
    image_embed = pl.pallas_call(
        functools.partial(image_embed_kernel, col_count),
        grid=(groups,),
        out_shape=array((images, width), bf16),
        in_specs=[pl.BlockSpec((group_rows, width), lambda i: (i, 0)), whole((images, width))] + parts,
        out_specs=whole((images, width)),
        scratch_shapes=embed_weights
        + [pltpu.VMEM((images, wide), f32), pltpu.SemaphoreType.DMA((2, col_count))],
        compiler_params=pltpu.CompilerParams(vmem_limit_bytes=VMEM_LIMIT),
        name="image_embed",
    )(image_normed, image_mean, *up_parts, *down_parts)

    image_all = lax.all_gather(image_embed, both, axis=0, tiled=True)
    lifted = jnp.exp(logit_scale * dot_nt(image_all, text_embed))
    row_sums = lax.psum(jnp.sum(lifted, axis=1), both)
    col_sums = jnp.sum(lifted, axis=0)
    sim_grad = (0.5 * (lifted / row_sums[:, None] + lifted / col_sums[None, :])).astype(bf16)
    image_own = image_embed.astype(f32)
    embed_grad = logit_scale * (dot_tn(sim_grad, image_all) - image_own)
    positives = logit_scale * jnp.sum(image_own * text_embed.astype(f32), axis=1)
    loss_part = 0.5 * jnp.sum(jnp.log(col_sums) - 2.0 * positives)
    loss_part = loss_part + 0.5 * jnp.sum(jnp.log(row_sums)) / count

    saved = (text_tokens, heads, mixed, mid, slope, turned)
    backward_in = (text_lengths, *vectors, embed_grad, projected, *saved, *weights)
    backward_specs = [in_smem] + [in_vmem] * 6 + [anywhere] * 11
    backward_buffers = (
        [
            pltpu.VMEM((tokens, width), bf16),
            pltpu.VMEM((tokens, 3 * width), bf16),
            pltpu.VMEM((tokens, width), bf16),
            pltpu.VMEM((tokens, width), f32),
            pltpu.VMEM((tokens, wide), bf16),
        ]
        + weight_scratch
        + [
            pltpu.VMEM((tokens, width), bf16),
            pltpu.VMEM((width, tokens), bf16),
            pltpu.VMEM((tokens, width), f32),
            pltpu.VMEM((tokens, width), f32),
            pltpu.VMEM((tokens, width), bf16),
            pltpu.VMEM((tokens, width), bf16),
            pltpu.VMEM((tokens, 3 * width), bf16),
            pltpu.VMEM((captions, 1), jnp.int32),
            pltpu.VMEM((1, tokens), f32),
            pltpu.VMEM((tokens, 128), f32),
            pltpu.SemaphoreType.DMA((11,)),
        ]
    )

    def by_row(x):
        x = lax.all_to_all(x, "row", split_axis=1, concat_axis=0, tiled=True)
        return lax.all_gather(x, "col", axis=0, tiled=True)

    def by_col(x):
        x = lax.all_gather(x, "row", axis=0, tiled=True)
        return lax.all_to_all(x, "col", split_axis=1, concat_axis=0, tiled=True)

    (proj_grad, branch, up_grad, out_grad, qkv_grad, input_grad, norm_grads) = plain(
        text_backward_kernel,
        (
            array((captions, width), bf16),
            array((captions, width), bf16),
            array((col_count, width, wide // col_count), bf16),
            array((col_count, width, width // col_count), bf16),
            array((col_count, width, 3 * width // col_count), bf16),
            array((tokens, width), bf16),
            array((8, width), f32),
        ),
        backward_specs,
        backward_buffers,
        "text_backward",
    )(*backward_in)

    def scattered(matrix):
        blocks = matrix.reshape(count, width // row_count, matrix.shape[2])
        return lax.psum_scatter(blocks, ("col", "row"), scatter_dimension=0, tiled=True)[0].astype(f32)

    up_grad, out_grad, qkv_grad = scattered(up_grad), scattered(out_grad), scattered(qkv_grad)
    grad_down = dot_tn(by_row(inner_sum), by_col(branch))
    grad_proj = dot_tn(by_row(pooled), by_col(proj_grad))
    loss_total, norm_total = lax.psum((loss_part, norm_grads), both)
    norms = [norm_total[i] for i in range(4)]
    mean_loss = loss_total / pair_total
    return (
        mean_loss, hidden, input_grad, *norms, qkv_grad, out_grad, up_grad, grad_down, grad_proj,
    )


def solution(mesh):
    split = P(("row", "col"), None)
    grid = P("row", "col")
    in_specs = (
        split, P(), P(), P("col", None), P("col", None), P("col", None), P("col", None), split, P(("row", "col")),
    ) + (P(),) * 9
    out_specs = (P(), split, split, P(), P(), P(), P(), grid, grid, grid, grid, grid)
    return jax.shard_map(body, mesh=mesh, in_specs=in_specs, out_specs=out_specs, check_vma=False)
```

```python
import functools
import math
from types import SimpleNamespace

import jax
import jax.numpy as jnp
from jax import lax
from jax.experimental import pallas as pl
from jax.experimental.pallas import tpu as pltpu
from jax.sharding import PartitionSpec as P

HEADS = 12
IMG_TOK = 50
norm_eps = 1e-06
logit_scale = 50.0
masked_score = -1e30
log2e = math.log2(math.e)
f32 = jnp.float32
bf16 = jnp.bfloat16
VMEM_LIMIT = 62 * 2**20
MESH = pl.DeviceIdType.MESH


def dot_nn(a, b):
    return lax.dot_general(a, b, (((1,), (0,)), ((), ())), preferred_element_type=f32)


def dot_nt(a, b):
    return lax.dot_general(a, b, (((1,), (1,)), ((), ())), preferred_element_type=f32)


def dot_tn(a, b):
    return lax.dot_general(a, b, (((0,), (0,)), ((), ())), preferred_element_type=f32)


def split_low(x):
    high = x.astype(bf16)
    return high, (x - high.astype(f32)).astype(bf16)


def normed(x):
    centered = x - jnp.mean(x, axis=-1, keepdims=True)
    spread = lax.rsqrt(jnp.mean(centered * centered, axis=-1, keepdims=True) + norm_eps)
    return centered * spread, spread


def layer_norm(x, gain, bias):
    return normed(x)[0] * gain + bias


def gelu(x):
    return x * (0.5 + 0.5 * lax.erf(x * math.sqrt(0.5)))


def gelu_and_slope(x):
    below = 0.5 + 0.5 * lax.erf(x * math.sqrt(0.5))
    bell = jnp.exp2((-0.5 * log2e) * (x * x))
    return x * below, below + x * (bell * (1.0 / math.sqrt(2.0 * math.pi)))


def lane_halves(width):
    lane = lax.broadcasted_iota(jnp.int32, (1, width), 1)
    first = (lane < width // 2).astype(f32)
    return first.astype(bf16), (1.0 - first).astype(bf16)


def stack_heads(x, first, second):
    return jnp.concatenate([x * first, x * second], axis=0)


def join_heads(stacked):
    rows, width = stacked.shape[0] // 2, stacked.shape[1]
    lane = lax.broadcasted_iota(jnp.int32, (rows, width), 1)
    return jnp.where(lane < width // 2, stacked[:rows], stacked[rows:])


def soft_weights(query, key, bias, factor):
    scores = dot_nt(query, key) * (factor * log2e) + bias
    weights = jnp.exp2(scores - jnp.max(scores, axis=-1, keepdims=True))
    return weights, 1.0 / jnp.sum(weights, axis=-1, keepdims=True)


def set_lengths(lengths_ref, lens_ref, key_bias_ref):
    captions, tokens = lens_ref.shape[0], key_bias_ref.shape[1]
    length = tokens // captions
    caption = lax.broadcasted_iota(jnp.int32, (captions, 1), 0)
    token = lax.broadcasted_iota(jnp.int32, (1, tokens), 1)
    column, row = jnp.zeros((captions, 1), jnp.int32), jnp.zeros((1, tokens), jnp.int32)
    for n in range(captions):
        column = jnp.where(caption == n, lengths_ref[n], column)
        row = jnp.where(token // length == n, lengths_ref[n], row)
    lens_ref[...] = column
    key_bias_ref[...] = jnp.where(token % length < row, 0.0, masked_score)


def as_row(ref):
    return ref[...].reshape(1, ref.shape[0])


def text_bias(key_bias_ref, block, rows, length):
    near = lax.broadcasted_iota(jnp.int32, (rows, rows), 0) // length
    far = lax.broadcasted_iota(jnp.int32, (rows, rows), 1) // length
    columns = pl.ds(pl.multiple_of(block * rows, rows), rows)
    bias = jnp.where(near == far, key_bias_ref[:, columns], masked_score)
    return jnp.concatenate([bias, bias], axis=0)


def member(len_ref, captions, tokens):
    length = tokens // captions
    token = lax.broadcasted_iota(jnp.int32, (captions, tokens), 1)
    caption = lax.broadcasted_iota(jnp.int32, (captions, tokens), 0)
    return ((token // length == caption) & (token % length < len_ref[...])).astype(f32)


def spread_rows(x, length):
    rows, width = x.shape
    return jnp.broadcast_to(x[:, None, :], (rows, length, width)).reshape(rows * length, width)


def wide_steps(total, most=768):
    step = math.gcd(total, most)

    def loop(body):
        @pl.loop(0, total // step)
        def _(j):
            body(pl.ds(pl.multiple_of(j * step, 128), step))

    return loop


class TextForward:
    band = 128

    def __init__(self, refs):
        for name, ref in refs.items():
            setattr(self, name, ref)
        self.tokens, self.width = self.tok.shape
        self.captions = self.lens.shape[0]
        self.length = self.tokens // self.captions
        self.wide = self.w_up.shape[1]
        pairs = (
            (self.qkv_hbm, self.w_qkv), (self.out_hbm, self.w_out), (self.up_hbm, self.w_up),
            (self.down_hbm, self.w_down),
        )
        self.loads = load_weights(pairs, self.sems)
        self.load_proj = pltpu.make_async_copy(self.proj_hbm, self.w_proj, self.sems.at[4])

    def bands(self, step):
        pl.loop(0, self.tokens // self.band)(
            lambda i: step(pl.ds(pl.multiple_of(i * self.band, self.band), self.band))
        )

    def prepare(self):
        set_lengths(self.lengths, self.lens, self.key_bias)

        def first_norm(rows):
            norm = layer_norm(self.tok[rows, :].astype(f32), as_row(self.gain1), as_row(self.bias1))
            self.norm[rows, :] = norm.astype(bf16)

        self.bands(first_norm)

    def attention(self):
        width = self.width
        self.loads[0].wait()

        @wide_steps(3 * width)
        def _(columns):
            self.heads[:, columns] = dot_nn(self.norm[...], self.w_qkv[:, columns]).astype(bf16)

        first, second = lane_halves(128)
        factor = (width // HEADS) ** -0.5

        @pl.loop(0, self.tokens // self.band)
        def _(block):
            rows = pl.ds(pl.multiple_of(block * self.band, self.band), self.band)
            bias = text_bias(self.key_bias, block, self.band, self.length)
            for at in range(0, width, 128):
                query = stack_heads(self.heads[rows, at : at + 128], first, second)
                key = self.heads[rows, width + at : width + at + 128]
                weights, scale = soft_weights(query, key, bias, factor)
                value = self.heads[rows, 2 * width + at : 2 * width + at + 128]
                mixed = dot_nn(weights.astype(bf16), value) * scale
                self.mixed[rows, at : at + 128] = join_heads(mixed).astype(bf16)

    def middle(self):
        self.loads[1].wait()

        def second_norm(rows):
            mid = self.tok[rows, :].astype(f32) + dot_nn(self.mixed[rows, :], self.w_out[...])
            self.mid[rows, :] = mid
            self.norm[rows, :] = layer_norm(mid, as_row(self.gain2), as_row(self.bias2)).astype(bf16)

        self.bands(second_norm)

    def feed(self, after=lambda j: None):
        self.loads[2].wait()
        self.chosen = member(self.lens, self.captions, self.tokens).astype(bf16)
        place = lax.broadcasted_iota(jnp.int32, (self.captions, self.length, 1), 1)
        valid = (place < self.lens[...].reshape(self.captions, 1, 1)).astype(f32).reshape(self.tokens, 1)

        @pl.loop(0, self.wide // self.width)
        def _(j):
            columns = pl.ds(pl.multiple_of(j * self.width, 128), self.width)
            value, slope = gelu_and_slope(dot_nn(self.norm[...], self.w_up[:, columns]))
            value = value.astype(bf16)
            self.inner[:, columns] = value
            self.slope[:, columns] = (slope * valid).astype(bf16)
            self.inner_sum[:, columns] = dot_nn(self.chosen, value).astype(bf16)
            after(j)

    def finish(self):
        self.loads[3].wait()
        self.turned[...] = self.norm[...].T
        inverse = 1.0 / self.lens[...].astype(f32)

        @wide_steps(self.width)
        def _(columns):
            state = self.mid[:, columns] + dot_nn(self.inner[...], self.w_down[:, columns])
            self.hidden[:, columns] = state.astype(bf16)
            high, low = split_low(state)
            pooled = (dot_nn(self.chosen, high) + dot_nn(self.chosen, low)) * inverse
            self.pooled[:, columns] = pooled.astype(bf16)

    def embed(self):
        self.load_proj.wait()
        projected = dot_nn(self.pooled[...], self.w_proj[...])
        self.projected[...] = projected
        scale = lax.rsqrt(jnp.sum(projected * projected, axis=-1, keepdims=True) + norm_eps)
        self.text_embed[...] = (projected * scale).astype(bf16)


text_ins = (
    "tok", "lengths", "gain1", "bias1", "gain2", "bias2", "qkv_hbm", "out_hbm", "up_hbm", "down_hbm", "proj_hbm",
)
text_names = (
    "hidden", "text_embed", "projected", "pooled", "inner_sum", "heads", "mixed", "mid", "slope", "turned",
)
text_scratch = ("w_qkv", "w_out", "w_up", "w_down", "w_proj", "norm", "inner", "lens", "key_bias", "sems")


def text_forward_kernel(*refs):
    t = TextForward(dict(zip(text_ins + text_names + text_scratch, refs, strict=True)))
    t.load_proj.start()
    t.prepare()
    t.attention()
    t.middle()
    t.feed()
    t.finish()
    t.embed()


def load_weights(pairs, sems):
    loads = [pltpu.make_async_copy(s, d, sems.at[i]) for i, (s, d) in enumerate(pairs)]
    for load in loads:
        load.start()
    return loads


def spans(count, size):
    return lambda i: pl.ds(pl.multiple_of(i * size, size), size)


def norm_backward(outer, unit, spread, gain):
    outer = outer * gain
    inner = outer - jnp.mean(outer, axis=-1, keepdims=True)
    return spread * (inner - unit * jnp.mean(outer * unit, axis=-1, keepdims=True))


class TextBackward:
    band = 128

    def __init__(self, refs, loads):
        for name, ref in refs.items():
            setattr(self, name, ref)
        self.loads = loads
        self.tokens, self.width = self.tok.shape
        self.captions = self.lens.shape[0]
        self.length = self.tokens // self.captions
        self.wide = self.w_up.shape[1]
        self.pre_grad = self.slope

    def wait(self, name):
        if name in self.loads:
            self.loads[name].wait()

    def rows(self, i):
        return pl.ds(pl.multiple_of(i * self.band, self.band), self.band)

    def bands(self, step):
        pl.loop(0, self.tokens // self.band)(lambda i: step(self.rows(i)))

    def valid(self):
        place = lax.broadcasted_iota(jnp.int32, (self.captions, self.length, 1), 1)
        valid = place < self.lens[...].reshape(self.captions, 1, 1)
        return valid.astype(f32).reshape(self.tokens, 1)

    def project(self):
        projected = self.projected[...]
        embed_grad = self.embed_grad[...]
        r = lax.rsqrt(jnp.sum(projected * projected, axis=-1, keepdims=True) + norm_eps)
        along = jnp.sum(projected * embed_grad, axis=-1, keepdims=True)
        proj_grad = (r * embed_grad - (r * r * r) * projected * along).astype(bf16)
        self.wait("w_proj")
        state_grad = dot_nt(proj_grad, self.w_proj[...]) * (1.0 / self.lens[...].astype(f32))
        self.branch[...] = state_grad.astype(bf16)
        self.mid_grad[...] = spread_rows(state_grad, self.length) * self.valid()
        return proj_grad, self.branch[...]

    def wait_inner(self):
        self.wait("turned")
        self.wait("w_down")
        self.wait("slope")

    def inner_grad(self, columns):
        grad = dot_nt(self.branch[...], self.w_down[columns, :])
        pre_grad = spread_rows(grad, self.length) * self.slope[:, columns].astype(f32)
        self.pre_grad[:, columns] = pre_grad.astype(bf16)

    def up_block(self, columns):
        return dot_nn(self.turned[...], self.pre_grad[:, columns]).astype(bf16)

    def to_middle(self):
        self.wait("w_up")

        @wide_steps(self.width)
        def _(columns):
            self.outer[:, columns] = dot_nt(self.pre_grad[...], self.w_up[columns, :])

    def middle(self):
        self.wait("mid")
        self.norm_grad[...] = jnp.zeros_like(self.norm_grad)

        def through_norm(rows):
            unit, spread = normed(self.mid[rows, :])
            outer = self.outer[rows, :]
            self.norm_grad[2:3, :] += jnp.sum(outer * unit, axis=0, keepdims=True)
            self.norm_grad[3:4, :] += jnp.sum(outer, axis=0, keepdims=True)
            mid_grad = self.mid_grad[rows, :] + norm_backward(outer, unit, spread, as_row(self.gain2))
            self.mid_grad[rows, :] = mid_grad
            self.low_grad[rows, :] = mid_grad.astype(bf16)

        self.bands(through_norm)
        self.wait("mixed")
        self.turned[...] = self.mixed[...].T

    def out_block(self, columns):
        return dot_nn(self.turned[...], self.low_grad[:, columns]).astype(bf16)

    def to_heads(self):
        self.wait("w_out")
        self.wait("tok")

        def through_out(rows):
            self.mixed_grad[rows, :] = dot_nt(self.low_grad[rows, :], self.w_out[...]).astype(bf16)
            norm = layer_norm(self.tok[rows, :].astype(f32), as_row(self.gain1), as_row(self.bias1))
            self.norm[rows, :] = norm.astype(bf16)

        self.bands(through_out)
        self.turned[...] = self.norm[...].T

    def attention(self, after=lambda block: None):
        first, second = lane_halves(128)
        width = self.width
        factor = (width // HEADS) ** -0.5
        self.wait("heads")
        self.key_column[...] = jnp.broadcast_to((1.0 - self.valid()) * masked_score, self.key_column.shape)

        @pl.loop(0, self.tokens // self.band)
        def _(block):
            rows = self.rows(block)
            near = lax.broadcasted_iota(jnp.int32, (self.band, self.band), 0) // self.length
            far = lax.broadcasted_iota(jnp.int32, (self.band, self.band), 1) // self.length
            bias = jnp.where(near == far, self.key_column[rows, :], masked_score)
            bias = jnp.concatenate([bias, bias], axis=1)
            for at in range(0, width, 128):
                query = stack_heads(self.heads[rows, at : at + 128], first, second)
                key = self.heads[rows, width + at : width + at + 128]
                value = self.heads[rows, 2 * width + at : 2 * width + at + 128]
                grad = stack_heads(self.mixed_grad[rows, at : at + 128], first, second)
                scores = dot_nt(key, query) * (factor * log2e) + bias
                weights = jnp.exp2(scores - jnp.max(scores, axis=0, keepdims=True))
                probs = weights * (1.0 / jnp.sum(weights, axis=0, keepdims=True))
                prob_grad = dot_nt(value, grad)
                total = jnp.sum(prob_grad * probs, axis=0, keepdims=True)
                score_grad = (probs * (prob_grad - total)).astype(bf16)
                query_grad = join_heads(dot_tn(score_grad, key)) * factor
                self.heads_grad[rows, at : at + 128] = query_grad.astype(bf16)
                key_grad = dot_nn(score_grad, query) * factor
                self.heads_grad[rows, width + at : width + at + 128] = key_grad.astype(bf16)
                value_grad = dot_nn(probs.astype(bf16), grad)
                self.heads_grad[rows, 2 * width + at : 2 * width + at + 128] = value_grad.astype(bf16)
            after(block)

    def qkv_block(self, columns):
        return dot_nn(self.turned[...], self.heads_grad[:, columns]).astype(bf16)

    def input(self, between=lambda: None):
        self.wait("w_qkv")

        @wide_steps(self.width)
        def _(columns):
            self.outer[:, columns] = dot_nt(self.heads_grad[...], self.w_qkv[columns, :])

        between()

        def through_norm(rows):
            unit, spread = normed(self.tok[rows, :].astype(f32))
            outer = self.outer[rows, :]
            self.norm_grad[0:1, :] += jnp.sum(outer * unit, axis=0, keepdims=True)
            self.norm_grad[1:2, :] += jnp.sum(outer, axis=0, keepdims=True)
            inner = norm_backward(outer, unit, spread, as_row(self.gain1))
            self.tok[rows, :] = (self.mid_grad[rows, :] + inner).astype(bf16)

        self.bands(through_norm)


backward_ins = (
    "lengths", "gain1", "bias1", "gain2", "bias2", "embed_grad", "projected", "tok_hbm", "heads_hbm", "mixed_hbm",
    "mid_hbm", "slope_hbm", "turned_hbm", "w_qkv_hbm", "w_out_hbm", "w_up_hbm", "w_down_hbm", "w_proj_hbm",
)
backward_outs = ("proj_grad", "branch", "up_grad", "out_grad", "qkv_grad", "input_grad", "norm_grad")
backward_scratch = (
    "tok", "heads", "mixed", "mid", "slope", "w_qkv", "w_out", "w_up", "w_down", "w_proj", "norm", "turned",
    "outer", "mid_grad", "low_grad", "mixed_grad", "heads_grad", "lens", "key_bias", "key_column", "sems",
)


def text_backward_kernel(*refs):
    refs = dict(zip(backward_ins + backward_outs + backward_scratch, refs, strict=True))
    order = ("w_proj", "turned", "w_down", "slope", "w_up", "mid", "mixed", "w_out", "tok", "heads", "w_qkv")
    loads = load_weights([(refs[name + "_hbm"], refs[name]) for name in order], refs["sems"])
    t = TextBackward(refs, dict(zip(order, loads)))
    set_lengths(t.lengths, t.lens, t.key_bias)
    parts = t.up_grad.shape[0]

    def blocks(target, block):
        step = target.shape[2]
        for part in range(parts):
            target[part] = block(slice(part * step, (part + 1) * step))

    t.proj_grad[...] = t.project()[0]
    t.wait_inner()
    wide_steps(t.wide)(t.inner_grad)
    blocks(t.up_grad, t.up_block)
    t.to_middle()
    t.middle()
    blocks(t.out_grad, t.out_block)
    t.to_heads()
    t.attention()
    blocks(t.qkv_grad, t.qkv_block)
    t.input()
    t.input_grad[...] = t.tok[...]


class Place:
    def __init__(self, z_count=4, y_count=2, x_count=2, k_count=2):
        self.row, self.col = lax.axis_index("row"), lax.axis_index("col")
        self.z, self.y = self.row // y_count, self.row % y_count
        self.x, self.k = self.col // k_count, self.col % k_count
        self.rows, self.cols = z_count * y_count, x_count * k_count
        self.count = self.rows * self.cols
        self.me = self.row * self.cols + self.col
        self.slot = self.col * self.rows + self.row
        self.near_z, self.far_z = self.z + 1 - 2 * (self.z % 2), (self.z + 2) % 4

    def at(self, **moved):
        z, y, x, k = (moved.get(name, getattr(self, name)) for name in "zyxk")
        return z * 2 + y, x * 2 + k

    def peer(self, distance):
        other = (self.me + distance) % self.count
        return other // self.cols, other % self.cols

    def greet(self):
        barrier = pltpu.get_barrier_semaphore()

        @pl.loop(1, self.count)
        def _(distance):
            pl.semaphore_signal(barrier, inc=1, device_id=self.peer(distance), device_id_type=MESH)

    def meet(self):
        pl.semaphore_wait(pltpu.get_barrier_semaphore(), self.count - 1)


def remote(src, dst, send, recv, to):
    return pltpu.make_async_remote_copy(
        src_ref=src, dst_ref=dst, send_sem=send, recv_sem=recv, device_id=to, device_id_type=MESH
    )


def wait_all(blocks, send, recv, to):
    remote(blocks, blocks, send, recv, to).wait()


class Gather:
    def __init__(self, place, pieces, spans, sends, recvs):
        mate, next_x = place.at(k=1 - place.k), place.at(x=1 - place.x)
        across = next_x[1]
        self.spans, self.sends, self.recvs, self.mate = spans, sends, recvs, mate
        self.locals, self.nears, self.fars, self.alongs, self.passes = [], [], [], [], []
        for axis, own, half, block, part in pieces:
            here = place.y if axis == "y" else place.z % 2
            partner = place.at(y=1 - place.y) if axis == "y" else place.at(z=place.near_z)
            mine, theirs = part(across, here), block(across)
            self.locals.append(pltpu.make_async_copy(own, block(place.col), recvs.at[4]))
            self.nears.append(remote(own, block(place.col), sends.at[0], recvs.at[0], mate))
            self.fars.append(remote(half(here), part(place.col, here), sends.at[1], recvs.at[1], next_x))
            self.alongs.append(remote(mine, mine, sends.at[2], recvs.at[2], partner))
            self.passes.append(remote(theirs, theirs, sends.at[3], recvs.at[3], mate))

    def wait(self, i, span):
        wait_all(self.spans[span], self.sends.at[i], self.recvs.at[i], self.mate)

    def start(self):
        for copies in (self.fars, self.nears, self.locals):
            for copy in copies:
                copy.start()

    def share(self):
        self.wait(1, 1)
        for copy in self.alongs:
            copy.start()

    def relay(self):
        self.wait(2, 1)
        for copy in self.passes:
            copy.start()

    def finish(self):
        pltpu.make_async_copy(self.spans[0], self.spans[0], self.recvs.at[4]).wait()
        self.wait(0, 0)
        self.wait(3, 0)


class RowFactors:
    def __init__(self, place, own, held, local, sends, recvs):
        self.place, self.own, self.held, self.sends, self.recvs = place, own, held, sends, recvs
        self.local = pltpu.make_async_copy(own.at[place.row], held.at[place.col, place.row], local)
        mine, across = held.at[place.col], held.at[place.at(x=1 - place.x)[1]]
        mate, next_x = place.at(k=1 - place.k), place.at(x=1 - place.x)
        self.far = remote(mine, mine, sends.at[1], recvs.at[1], next_x)
        self.near = remote(mine, mine, sends.at[2], recvs.at[2], mate)
        self.passed = remote(across, across, sends.at[3], recvs.at[3], mate)

    def start(self):
        self.local.start()
        p = self.place

        @pl.loop(1, p.rows)
        def _(distance):
            row = (p.row + distance) % p.rows
            remote(
                self.own.at[row], self.held.at[p.col, p.row], self.sends.at[0], self.recvs.at[0], (row, p.col)
            ).start()

    def share(self):
        self.local.wait()
        p = self.place
        to = p.at(k=1 - p.k)
        wait_all(self.held.at[p.col, pl.ds(0, p.rows - 1)], self.sends.at[0], self.recvs.at[0], to)
        self.far.start()
        self.near.start()

    def relay(self):
        self.far.wait()
        self.passed.start()

    def finish(self):
        self.near.wait()
        self.passed.wait()


class Exchange:
    def __init__(self, place, source, slots, sends, recvs):
        self.place, self.source, self.slots = place, source, slots
        self.sems = sends.at[0], recvs.at[0]

    def start(self):
        p = self.place

        @pl.loop(1, p.count)
        def _(distance):
            remote(self.source, self.slots.at[p.slot], *self.sems, p.peer(distance)).start()

    def finish(self):
        p = self.place
        wait_all(self.slots.at[pl.ds(0, p.count - 1)], *self.sems, p.at(k=1 - p.k))


class ChipSum:
    def __init__(self, place, total, got, slots, both, sends, recvs):
        self.place, self.total, self.got, self.slots, self.both = place, total, got, slots, both
        self.half = slots.shape[2]
        self.sends, self.recvs = sends, recvs
        self.chip, self.chips = place.row * 2 + place.x, place.rows * 2
        self.mate = place.at(k=1 - place.k)

    def near(self):
        return remote(self.total, self.got, self.sends.at[0], self.recvs.at[0], self.mate)

    def start(self):
        self.near().start()

    def spread(self):
        self.near().wait()
        self.total[...] = self.total[...] + self.got[...]
        mine = pl.ds(pl.multiple_of(self.place.k * self.half, 128), self.half)
        self.slots[self.chip] = self.total[:, mine]

        @pl.loop(1, self.chips)
        def _(distance):
            other = (self.chip + distance) % self.chips
            to = other // 2, other % 2 * 2 + self.place.k
            src, dst = self.total.at[:, mine], self.slots.at[self.chip]
            remote(src, dst, self.sends.at[1], self.recvs.at[1], to).start()

    def passed(self):
        mine = self.both.at[self.place.k]
        return remote(mine, mine, self.sends.at[2], self.recvs.at[2], self.mate)

    def collect(self):
        wait_all(self.slots.at[pl.ds(0, self.chips - 1)], self.sends.at[1], self.recvs.at[1], self.mate)
        self.both[self.place.k] = jnp.sum(self.slots[...], axis=0)
        self.passed().start()

    def finish(self):
        self.passed().wait()
        return jnp.concatenate([self.both[0], self.both[1]], axis=1)


class GradientScatter:
    def __init__(self, place, straight, halves, held, near, x1, y1, x2, y2, far, sends, recvs):
        self.straight = straight
        self.place, self.held, self.near, self.far = place, held, near, far
        self.x1, self.y1, self.x2, self.y2 = x1, y1, x2, y2
        self.sends, self.recvs = sends, recvs
        self.halves = halves

    def lanes(self, chunk):
        ones, twos = zip(*self.halves[:chunk], (0, 0))
        at_one, at_two = sum(ones), sum(twos)
        at = at_one + at_two
        one, two = self.halves[chunk]
        return (
            pl.ds(at, one + two), pl.ds(at, one), pl.ds(at + one, two), pl.ds(at_one, one), pl.ds(at_two, two)
        )

    def copies(self, chunk, stage):
        p, held = self.place, self.held
        x, y, z, k = p.x, p.y, p.z, p.k
        whole, one, two, part_one, part_two = self.lanes(chunk)

        def copy(n, src, dst, **moved):
            send = self.sends.at[chunk, (0, 0, 1, 0, 1, 0, 1, 2)[n]]
            return remote(src, dst, send, self.recvs.at[chunk, n], p.at(**moved))

        if stage == 0:
            return [copy(0, held.at[:, 1 - k, :, :, :, whole], self.near.at[:, :, :, :, whole], k=1 - k)]
        if stage == 1:
            copies = []
            if one.size:
                copies.append(copy(1, held.at[1 - x, k, :, :, :, one], self.x1.at[:, :, :, part_one], x=1 - x))
            if two.size:
                copies.append(copy(2, held.at[:, k, :, 1 - y, :, two], self.y1.at[:, :, :, part_two], y=1 - y))
            return copies
        if stage == 2:
            copies = []
            if one.size:
                copies.append(copy(3, held.at[x, k, :, 1 - y, :, one], self.y2.at[:, :, part_one], y=1 - y))
            if two.size:
                copies.append(copy(4, held.at[1 - x, k, :, y, :, two], self.x2.at[:, :, part_two], x=1 - x))
            return copies
        if stage == 3 and self.straight:
            return [
                copy(4 + i, held.at[x, k, (z + i) % 4, y, :, whole], self.far.at[i - 1, :, whole], z=(z + i) % 4)
                for i in range(1, 4)
            ]
        if stage == 3:
            blocks = p.near_z, held.shape[2] - 1 - z
            return [
                copy(5 + i, held.at[x, k, block, y, :, whole], self.far.at[i, :, whole], z=p.near_z)
                for i, block in enumerate(blocks)
            ]
        return [copy(7, held.at[x, k, p.far_z, y, :, whole], self.far.at[2, :, whole], z=p.far_z)]

    def start(self, chunk, stage):
        for copy in self.copies(chunk, stage):
            copy.start()

    def finish(self, chunk, stage):
        for copy in self.copies(chunk, stage):
            copy.wait()
        p, held = self.place, self.held
        x, y, k = p.x, p.y, p.k
        z_count = held.shape[2]
        whole, one, two, part_one, part_two = self.lanes(chunk)

        def add(target, source):
            target[...] = (target[...].astype(f32) + source[...].astype(f32)).astype(bf16)

        if stage == 0:

            @pl.loop(0, z_count)
            def _(z):
                for i in range(2):
                    for j in range(2):
                        add(held.at[i, k, z, j, :, whole], self.near.at[i, z, j, :, whole])

        if stage == 1:

            @pl.loop(0, z_count)
            def _(z):
                for i in range(2):
                    if one.size:
                        add(held.at[x, k, z, i, :, one], self.x1.at[z, i, :, part_one])
                    if two.size:
                        add(held.at[i, k, z, y, :, two], self.y1.at[i, z, :, part_two])

        if stage == 2:

            @pl.loop(0, z_count)
            def _(z):
                if one.size:
                    add(held.at[x, k, z, y, :, one], self.y2.at[z, :, part_one])
                if two.size:
                    add(held.at[x, k, z, y, :, two], self.x2.at[z, :, part_two])

        if stage == 3 and not self.straight:
            add(held.at[x, k, p.far_z, y, :, whole], self.far.at[1, :, whole])

    def step_on(self, chunk, stage):
        self.finish(chunk, stage - 1)
        self.start(chunk, stage)

    def total(self):
        p = self.place
        total = self.held[p.x, p.k, p.z, p.y, :, : self.far.shape[2]].astype(f32)
        for i in (0, 1, 2) if self.straight else (0, 2):
            total = total + self.far[i].astype(f32)
        return total


def chip_sum_scratch(size, chips):
    return [
        pltpu.VMEM((1, size), f32), pltpu.VMEM((1, size), f32), pltpu.VMEM((chips, 1, size // 2), f32),
        pltpu.VMEM((2, 1, size // 2), f32), pltpu.SemaphoreType.DMA((3,)), pltpu.SemaphoreType.DMA((3,)),
    ]


def scatter_scratch(rows, halves):
    one, two = (sum(widths) for widths in zip(*halves))
    spare = max(two, 128)
    shapes = [
        (2, 2, 4, 2, rows, one + two), (2, 4, 2, rows, one + two), (4, 2, rows, one), (2, 4, rows, spare),
        (4, rows, spare), (4, rows, one), (3, rows, one + two),
    ]
    sems = [pltpu.SemaphoreType.DMA((len(halves), 3)), pltpu.SemaphoreType.DMA((len(halves), 8))]
    return [pltpu.VMEM(shape, bf16) for shape in shapes] + sems


class ColFactors:
    def __init__(self, place, own, held, sends, recvs):
        self.place, self.own, self.held, self.sends, self.recvs = place, own, held, sends, recvs

    def copies(self, stage):
        p, held = self.place, self.held

        def copy(n, src, dst, **moved):
            return remote(src, dst, self.sends.at[n], self.recvs.at[n], p.at(**moved))

        if stage == 0:
            mine = held.at[p.col, p.row]
            moves = ({"x": 1 - p.x}, {"k": 1 - p.k}, {"x": 1 - p.x, "k": 1 - p.k})
            return [copy(i, self.own.at[p.at(**move)[1]], mine, **move) for i, move in enumerate(moves)]
        if stage == 1:
            mine = held.at[:, p.row]
            return [copy(3, mine, mine, y=1 - p.y)]
        mine, other = (held.at[:, pl.ds(z * 2, 2)] for z in (p.z, p.far_z))
        if stage == 2:
            return [copy(4, mine, mine, z=p.far_z)]
        return [copy(5, mine, mine, z=p.near_z), copy(6, other, other, z=p.near_z)]

    def start(self, stage):
        for copy in self.copies(stage):
            copy.start()

    def finish(self, stage):
        for copy in self.copies(stage):
            copy.wait()


def scatter_widths(wide, width, cols):
    ups = tuple((128, 128) for _ in range(wide // cols // 256))
    rest = 4 * width // cols - 128
    return ups, ((128, 0),), ((128, 128), (128, 128), (rest - 512, 0))


scatter_names = ("x2", "y2", "far", "sends", "recvs")
total_names = ("total", "got", "slots", "both", "sends", "recvs")


def hand_over_kernel(pair_total, norms, *refs):
    sources, (loss, *vectors), targets = refs[:7], refs[7:12], refs[12:]
    width = vectors[0].shape[0]
    loss[...] = norms[:, 4 * width : 4 * width + 1] * (1.0 / pair_total)
    for i, vector in enumerate(vectors):
        vector[...] = norms[:, i * width : (i + 1) * width].reshape(width)
    for source, target in zip(sources, targets, strict=True):
        target[...] = source[...]


def group_mean(images, rows):
    token = lax.broadcasted_iota(jnp.int32, (images, rows), 1)
    image = lax.broadcasted_iota(jnp.int32, (images, rows), 0)
    inside = (token >= image * IMG_TOK) & (token < (image + 1) * IMG_TOK)
    return inside.astype(f32).astype(bf16)


def load_parts(parts, target, sems, col, col_count):
    depth = target.shape[0] // col_count
    copies = []
    for k, part in enumerate(parts):
        place = pl.multiple_of((col ^ k) * depth, depth)
        copies.append(pltpu.make_async_copy(part, target.at[pl.ds(place, depth)], sems.at[k]))
    return copies


def image_mix(tokens, gain_ref, bias_ref, qkv_block, between, out_weight, norm_ref, heads_ref, mixed_ref):
    rows, width = tokens.shape
    images = rows // IMG_TOK
    norm_ref[...] = layer_norm(tokens.astype(f32), gain_ref[0:1, :], bias_ref[0:1, :]).astype(bf16)

    @pl.loop(0, 3)
    def _(j):
        columns = pl.ds(pl.multiple_of(j * width, width), width)
        heads_ref[:, columns] = dot_nn(norm_ref[...], qkv_block(j)).astype(bf16)

    between()
    first, second = lane_halves(128)
    factor = (width // HEADS) ** -0.5
    window = 112

    @pl.loop(0, images // 2)
    def _(pair):
        start = pair * (2 * IMG_TOK)
        low = pl.multiple_of(start // 16 * 16, 16)
        near = lax.broadcasted_iota(jnp.int32, (window, window), 0) + low
        far = lax.broadcasted_iota(jnp.int32, (window, window), 1) + low
        same = (near >= start) & (near < start + 2 * IMG_TOK) & (far >= start) & (far < start + 2 * IMG_TOK)
        same = same & ((near >= start + IMG_TOK) == (far >= start + IMG_TOK))
        bias = jnp.where(same, 0.0, masked_score)
        bias = jnp.concatenate([bias, bias], axis=0)
        keep = lax.broadcasted_iota(jnp.int32, (16, 128), 0) + low < start
        span, head, tail = pl.ds(low, window), pl.ds(low, 16), pl.ds(low + 16, window - 16)
        for at in range(0, width, 128):
            query = stack_heads(heads_ref[span, at : at + 128], first, second)
            key = heads_ref[span, width + at : width + at + 128]
            weights, scale = soft_weights(query, key, bias, factor)
            value = heads_ref[span, 2 * width + at : 2 * width + at + 128]
            mixed = join_heads(dot_nn(weights.astype(bf16), value) * scale)
            former = mixed_ref[head, at : at + 128].astype(f32)
            mixed_ref[head, at : at + 128] = jnp.where(keep, former, mixed[:16]).astype(bf16)
            mixed_ref[tail, at : at + 128] = mixed[16:].astype(bf16)

    mid = tokens.astype(f32) + dot_nn(mixed_ref[...], out_weight())
    high, low = split_low(mid)
    select = group_mean(images, rows)
    mean = (dot_nn(select, high) + dot_nn(select, low)) * (1.0 / IMG_TOK)
    return layer_norm(mid, gain_ref[1:2, :], bias_ref[1:2, :]).astype(bf16), mean


def image_mix_kernel(col_count, tok_ref, gain_ref, bias_ref, *refs):
    qkv_parts, out_parts = refs[:col_count], refs[col_count : 2 * col_count]
    normed_ref, mean_ref, w_qkv, w_out, *buffers, sems = refs[2 * col_count :]
    col = lax.axis_index("col")

    @pl.when(pl.program_id(0) == 0)
    def _():
        copies = load_parts(qkv_parts, w_qkv, sems.at[0], col, col_count)
        copies += load_parts(out_parts, w_out, sems.at[1], col, col_count)
        for copy in copies:
            copy.start()
        for copy in copies:
            copy.wait()

    width = tok_ref.shape[1]

    def qkv_block(j):
        return w_qkv[:, pl.ds(pl.multiple_of(j * width, width), width)]

    normed_ref[...], mean_ref[...] = image_mix(
        tok_ref[...], gain_ref, bias_ref, qkv_block, lambda: None, lambda: w_out[...], *buffers
    )


def image_embed_kernel(col_count, normed_ref, mean_ref, *refs):
    up_parts, down_parts = refs[:col_count], refs[col_count : 2 * col_count]
    embed_ref, w_up, w_down, sum_ref, sems = refs[2 * col_count :]
    rows, width = normed_ref.shape
    images = rows // IMG_TOK
    wide = w_up.shape[1]
    step = pl.program_id(0)
    col = lax.axis_index("col")
    downs = load_parts(down_parts, w_down, sems.at[1], col, col_count)

    @pl.when(step == 0)
    def _():
        ups = load_parts(up_parts, w_up, sems.at[0], col, col_count)
        for copy in ups + downs:
            copy.start()
        for copy in ups:
            copy.wait()

    select = group_mean(images, rows)

    @wide_steps(wide)
    def _(columns):
        inner = gelu(dot_nn(normed_ref[...], w_up[:, columns])).astype(bf16)
        sum_ref[pl.ds(pl.multiple_of(step * images, images), images), columns] = dot_nn(select, inner)

    @pl.when(step == pl.num_programs(0) - 1)
    def _():
        for copy in downs:
            copy.wait()
        high, low = split_low(sum_ref[...] * (1.0 / IMG_TOK))
        pooled = mean_ref[...] + dot_nn(high, w_down[...]) + dot_nn(low, w_down[...])
        embed_ref[...] = (
            pooled * lax.rsqrt(jnp.sum(pooled * pooled, axis=-1, keepdims=True) + norm_eps)
        ).astype(bf16)


joined_ins = (
    "lengths", "gain1", "bias1", "gain2", "bias2", "image_gain", "image_bias", "tok_hbm", "qkv_hbm", "out_hbm",
    "up_hbm", "down_hbm", "proj_hbm", "image_hbm", "image_qkv_hbm", "image_out_hbm", "image_up_hbm",
    "image_down_hbm",
)
joined_outs = (
    "up_out", "out_out", "qkv_out", "down_out", "proj_out", "norm_out", "hidden_out", "input_out", "slope_out",
)


def joined_kernel(names, *refs):
    refs = dict(zip(joined_ins + joined_outs + names, refs, strict=True))
    tok_load = pltpu.make_async_copy(refs["tok_hbm"], refs["tok"], refs["tok_sems"].at[2])
    tok_load.start()
    t = TextForward(refs)
    place = Place()
    place.greet()
    groups, group_rows = t.image_hbm.shape[0] // t.image_tok.shape[1], t.image_tok.shape[1]
    group_images = group_rows // IMG_TOK
    width, cols = t.width, place.cols

    def load_group(group):
        span = pl.ds(pl.multiple_of(group * group_rows, 16), group_rows)
        slot = group % 2
        return pltpu.make_async_copy(t.image_hbm.at[span], t.image_tok.at[slot], t.tok_sems.at[slot])

    load_group(0).start()
    gathers = iter(range(t.sends.shape[0]))

    def gather(pieces, *spans):
        i = next(gathers)
        return Gather(place, pieces, spans, t.sends.at[i], t.recvs.at[i])

    def piece_of_columns(axis, shard, at, target):
        lanes = pl.ds(at, target.shape[-1])
        return (
            axis, shard.at[:, :, lanes], lambda half: shard.at[half, :, lanes],
            lambda col: target.at[col], lambda col, half: target.at[col, half],
        )

    qkv_gathers = [
        gather(
            [piece_of_columns("y", t.image_qkv_hbm, j * width, t.iw_qkv.at[j])], t.iw_qkv.at[j, 0], t.iw_qkv.at[j, 0, 0]
        )
        for j in range(3)
    ]
    out_piece = (
        "z", t.image_out_hbm, lambda half: t.image_out_hbm.at[half],
        lambda col: t.iw_out.at[col // 2, pl.ds(col % 2 * 2, 2)],
        lambda col, half: t.iw_out.at[col // 2, col % 2 * 2 + half],
    )
    out_gather = gather([out_piece], t.iw_out.at[0, pl.ds(0, 2)], t.iw_out.at[0, 0])
    up_pieces = [
        piece_of_columns("yzyz"[j], t.image_up_hbm, j * width, t.iw_up.at[j // 2, j % 2]) for j in range(4)
    ]
    up_gather = gather(up_pieces, t.iw_up.at[0, 0], t.iw_up.at[0, 0, pl.ds(0, 2)])

    def piece_of_down(axis, lanes):
        return (
            axis, t.image_down_hbm.at[:, :, :, lanes],
            lambda half: t.image_down_hbm.at[pl.ds(half * 2, 2), :, :, lanes],
            lambda col: t.iw_down.at[col // 2, col % 2, :, :, :, lanes],
            lambda col, half: t.iw_down.at[col // 2, col % 2, pl.ds(half * 2, 2), :, :, lanes],
        )

    down_pieces = [piece_of_down("yz"[j], pl.ds(j * width // 2, width // 2)) for j in range(2)]
    down_gather = gather(down_pieces, t.iw_down.at[0, 0], t.iw_down.at[0, 0, pl.ds(0, 2)])

    def each(pieces, step):
        for piece in pieces:
            getattr(piece, step)()

    factors, pooled_factors = (
        RowFactors(
            place, getattr(t, "own" + tag), getattr(t, "held" + tag), t.factor_local.at[i], t.factor_sends.at[i],
            t.factor_recvs.at[i],
        )
        for i, tag in enumerate(("_inner", "_pooled"))
    )
    saves = {
        name: pltpu.make_async_copy(refs[name], refs[name + "_out"], t.save_sems.at[i])
        for i, name in enumerate(("hidden", "slope"))
    }
    tok_load.wait()
    t.prepare()
    place.meet()
    each(qkv_gathers, "start")
    out_gather.start()
    t.attention()
    qkv_gathers[0].share()
    t.middle()

    def after_feed(j):
        pl.when(j == 0)(qkv_gathers[1].share)
        pl.when(j == 1)(qkv_gathers[2].share)

        @pl.when(j == 2)
        def _():
            out_gather.share()
            up_gather.start()
            qkv_gathers[0].relay()

        pl.when(j == 3)(qkv_gathers[1].relay)

    t.feed(after_feed)
    saves["slope"].start()
    inner_step = t.wide // place.rows
    for row in range(place.rows):
        t.own_inner[row] = t.inner_sum[:, row * inner_step : (row + 1) * inner_step]
    saves["slope"].wait()

    image_norm, image_mixed = t.w_out.at[pl.ds(0, group_rows)], t.w_proj.at[pl.ds(0, group_rows)]
    image_heads = t.w_qkv.at[pl.ds(0, group_rows)]

    def normed_group(group):
        return t.slope.at[pl.ds(0, group_rows), pl.ds(pl.multiple_of(group * width, 128), width)]

    @pl.loop(0, groups)
    def _(group):
        @pl.when(group + 1 < groups)
        def _():
            load_group(group + 1).start()

        load_group(group).wait()

        def qkv_block(j):
            pl.when((group == 0) & (j == 0))(qkv_gathers[2].relay)
            for i, weight in enumerate(qkv_gathers):
                pl.when((group == 0) & (j == i))(weight.finish)
            return t.iw_qkv[j].reshape(width, width)

        def between():
            pl.when(group == 0)(out_gather.relay)

            @pl.when(group == groups - 1)
            def _():
                up_gather.relay()
                down_gather.share()

        def out_weight():
            @pl.when(group == 0)
            def _():
                out_gather.finish()
                factors.start()

            return t.iw_out[...].reshape(width, width)

        normed2, mean = image_mix(
            t.image_tok[group % 2], t.image_gain, t.image_bias, qkv_block, between,
            out_weight, image_norm, image_heads, image_mixed,
        )
        normed_group(group)[...] = normed2
        t.image_mean[pl.ds(pl.multiple_of(group * group_images, 8), group_images), :] = mean

        @pl.when(group == 0)
        def _():
            down_gather.start()

        @pl.when(group == 1)
        def _():
            up_gather.share()

    again = (("w_out", t.out_hbm), ("w_qkv", t.qkv_hbm), ("slope", t.slope_out))
    again = {
        name: pltpu.make_async_copy(source, refs[name], t.again_sems.at[i]) for i, (name, source) in enumerate(again)
    }
    t.load_proj.start()
    again["w_out"].start()
    again["w_qkv"].start()
    up_gather.finish()

    halves, half_images = 2, t.own.shape[0] // 2
    half_groups = half_images // group_images
    corner = place.y * 2 + place.x

    def image_block(half, z):
        span = pl.ds(pl.multiple_of(z * half_images, 16), half_images)
        return t.near_qkv.at[half, corner, place.k, span]

    in_plane = ({"x": 1 - place.x}, {"y": 1 - place.y}, {"x": 1 - place.x, "y": 1 - place.y})

    def image_start(half, stage):
        def start(i, block, **moved):
            sems = t.image_sends.at[half, i], t.image_recvs.at[half, i]
            remote(block, block, *sems, place.at(**moved)).start()

        if stage == 0:
            for i in range(1, 4):
                start(0, image_block(half, place.z), z=(place.z + i) % 4)
            for move in in_plane:
                start(1, image_block(half, place.z), **move)
        if stage == 1:
            for i in range(1, 4):
                for move in in_plane:
                    start(2, image_block(half, (place.z + i) % 4), **move)
        if stage == 2:
            start(3, t.near_qkv.at[half, :, place.k, pl.ds(0, 4 * half_images)], k=1 - place.k)

    def image_finish(half, stage):
        three, mate = pl.ds(0, 3 * half_images), place.at(k=1 - place.k)

        def wait(i, span):
            wait_all(span, t.image_sends.at[half, i], t.image_recvs.at[half, i], mate)

        if stage == 0:
            wait(0, t.near_qkv.at[half, 0, place.k, three])
        if stage == 1:
            wait(1, t.near_qkv.at[half, 0, place.k, three])
            wait(2, t.near_qkv.at[half, pl.ds(0, 3), place.k, three])
        if stage == 2:
            wait(3, t.near_qkv.at[half, :, place.k, pl.ds(0, 4 * half_images)])

    select = group_mean(half_images, half_images * IMG_TOK)

    @pl.loop(0, halves)
    def _(half):
        @pl.loop(0, t.wide // width)
        def _(j):
            weight = t.iw_up[j // 2, j % 2].reshape(width, width)
            total = 0.0
            for group in range(half_groups):
                at = pl.ds(pl.multiple_of((half * half_groups + group) * width, 128), width)
                inner = gelu(dot_nn(t.slope[:group_rows, at], weight)).astype(bf16)
                total = total + dot_nn(select[:, group * group_rows : (group + 1) * group_rows], inner)
            t.sums[:, pl.ds(pl.multiple_of(j * width, 128), width)] = total

            @pl.when((half == 0) & (j == 1))
            def _():
                down_gather.relay()

            @pl.when((half == 1) & (j == 1))
            def _():
                image_finish(0, 0)
                image_start(0, 1)

        @pl.when(half == 0)
        def _():
            down_gather.finish()
            factors.share()

        pl.when(half == 1)(again["slope"].start)
        high, low = split_low(t.sums[...] * (1.0 / IMG_TOK))
        pooled = dot_nn(jnp.concatenate([high, low], axis=0), t.iw_down[...].reshape(t.wide, width))
        part = pl.ds(pl.multiple_of(half * half_images, 16), half_images)
        pooled = t.image_mean[part, :] + pooled[:half_images] + pooled[half_images:]
        embed = pooled * lax.rsqrt(jnp.sum(pooled * pooled, axis=-1, keepdims=True) + norm_eps)
        t.own[part, :] = embed.astype(bf16)
        span = pl.ds(pl.multiple_of(place.z * half_images, 16), half_images)
        t.near_qkv[half, corner, place.k, span] = embed.astype(bf16)
        image_start(half, 0)

    factors.relay()
    t.finish()
    saves["hidden"].start()
    image_finish(halves - 1, 0)
    image_start(halves - 1, 1)
    image_finish(0, 1)
    image_start(0, 2)
    t.embed()
    width_step = width // place.rows
    pooled = t.pooled[...]
    spare = jnp.zeros((t.captions, t.own_pooled.shape[2] - width_step), bf16)
    for row in range(place.rows):
        block = pooled[:, row * width_step : (row + 1) * width_step]
        t.own_pooled[row] = jnp.concatenate([block, spare], axis=1)
    factors.finish()
    image_finish(halves - 1, 1)
    image_start(halves - 1, 2)
    for half in range(halves):
        image_finish(half, 2)

    images = t.near_qkv[:, :, :, : 4 * half_images].reshape(-1, width)
    own = t.own[...].astype(f32)
    lifted = jnp.exp2(dot_nt(t.text_embed[...], images) * (logit_scale * log2e))
    t.own_sums[...] = jnp.sum(lifted, axis=0, keepdims=True)
    t.all_sums[place.slot] = t.own_sums[...]
    sums = Exchange(place, t.own_sums, t.all_sums, t.sum_sends, t.sum_recvs)
    sums.start()
    col_sums = jnp.sum(lifted, axis=1, keepdims=True)
    positives = logit_scale * jnp.sum(own * t.text_embed[...].astype(f32), axis=(0, 1), keepdims=True)
    logs = jnp.sum(jnp.log(col_sums), axis=(0, 1), keepdims=True)
    saves["hidden"].wait()
    pooled_factors.start()
    sums.finish()
    row_sums = jnp.sum(t.all_sums[...], axis=0)
    sim_grad = (0.5 * (lifted * (1.0 / row_sums) + lifted * (1.0 / col_sums))).astype(bf16)
    t.embed_grad[...] = logit_scale * (dot_nn(sim_grad, images) - own)
    logs = logs + jnp.sum(jnp.log(row_sums), axis=(0, 1), keepdims=True) * (1.0 / place.count)
    t.loss[...] = jnp.broadcast_to(0.5 * logs - positives, t.loss.shape)

    shared = {
        "low_grad": t.inner.at[:, pl.ds(3 * width, width)], "heads_grad": t.inner.at[:, pl.ds(0, 3 * width)],
        "mixed_grad": t.hidden, "key_column": t.outer.at[:, pl.ds(0, 128)],
    }
    backward(place, TextBackward(refs | shared, again), pooled_factors)


def backward(place, t, pooled_factors):
    width, cols = t.width, place.cols
    widths = scatter_widths(t.wide, width, cols)
    shared = {
        "_up": (
            t.iw_up, t.iw_qkv.at[pl.ds(0, 2)], t.iw_qkv.at[2, :, :, :, pl.ds(0, 384)], t.iw_out.at[:, :, :, pl.ds(0, 384)]
        ),
        "_qkv": (
            t.iw_down, t.near_qkv, t.iw_qkv.at[2, :, :, :, pl.ds(384, 384)], t.iw_out.at[:, :, :, pl.ds(384, 384)]
        ),
        "_outs": (
            t.iw_down.at[:, :, :, :, :, pl.ds(640, 128)], t.near_qkv.at[:, :, :, :, pl.ds(640, 128)],
            t.x1_outs, t.y1_outs,
        ),
    }
    up, out, qkv = (
        GradientScatter(
            place, tag == "_qkv", halves, *shared[tag], *(getattr(t, name + tag) for name in scatter_names)
        )
        for halves, tag in zip(widths, ("_up", "_outs", "_qkv"))
    )
    factors = ColFactors(place, t.own_cols, t.held_cols, t.col_sends, t.col_recvs)
    late, last = (
        ChipSum(place, *(getattr(t, name + tag) for name in total_names)) for tag in ("_late", "_last")
    )

    left = []

    def leave(name, ref):
        left.append(pltpu.make_async_copy(ref, getattr(t, name + "_out"), t.leave_sems.at[len(left)]))
        left[-1].start()

    def store(scatter, part, at, value):
        held = scatter.held
        size = value.shape[1]
        held[part // 2, part % 2, :, :, :, at : at + size] = value.reshape(*held.shape[2:5], size)

    def fill(scatter, chunk, total, block):
        at, size = scatter.lanes(chunk)[0].start, scatter.lanes(chunk)[0].size
        true = min(size, total // cols - at)
        for part in range(cols):
            start = part * (total // cols) + at
            store(scatter, part, at, block(slice(start, start + true)))

    def fill_up(chunk, between=lambda: None):
        at = up.lanes(chunk)[0].start
        size = up.lanes(chunk)[0].size
        for part in range(cols):
            start = part * up.held.shape[5] + at
            t.inner_grad(pl.ds(start, size))
        between()
        fill(up, chunk, t.wide, t.up_block)
        up.start(chunk, 0)

    proj_grad, branch = t.project()
    out_step = width // cols
    for part in range(cols):
        columns = slice(part * out_step, (part + 1) * out_step)
        t.own_cols[part] = jnp.concatenate([branch[:, columns], proj_grad[:, columns]], axis=1)
    t.held_cols[place.col, place.row] = t.own_cols[place.col]
    factors.start(0)
    t.wait("slope")
    fill_up(0)
    pooled_factors.share()
    fill_up(1)
    factors.finish(0)
    factors.start(1)
    up.step_on(0, 1)
    fill_up(2)
    up.step_on(1, 1)
    t.to_middle()
    factors.finish(1)
    factors.start(2)
    up.step_on(2, 1)
    pooled_factors.relay()
    t.middle()
    up.step_on(0, 2)
    for part in range(cols):
        value = t.out_block(slice(part * out_step, (part + 1) * out_step))
        store(out, part, 0, value[:, :128])
        store(qkv, part, 3 * out_step, value[:, 128:])
    out.start(0, 0)
    t.total_late[...] = jnp.concatenate([t.norm_grad[2:3, :], t.norm_grad[3:4, :], t.loss[...], t.loss[...]], axis=1)
    late.start()
    t.to_heads()
    up.step_on(1, 2)
    out.step_on(0, 1)
    late.spread()

    def after(block):
        @pl.when(block == 0)
        def _():
            factors.finish(2)
            factors.start(3)

        @pl.when(block == 1)
        def _():
            up.step_on(2, 2)
            up.step_on(0, 3)

        @pl.when(block == 2)
        def _():
            up.step_on(1, 3)

    t.attention(after)
    fill(qkv, 0, 3 * width, t.qkv_block)
    qkv.start(0, 0)
    out.step_on(0, 2)
    fill(qkv, 1, 3 * width, t.qkv_block)
    qkv.start(1, 0)
    qkv.step_on(0, 1)
    fill(qkv, 2, 3 * width, t.qkv_block)
    qkv.start(2, 0)
    up.step_on(2, 3)
    qkv.step_on(1, 1)

    def between():
        up.step_on(0, 4)
        up.step_on(1, 4)
        qkv.step_on(0, 2)

    t.input(between)
    leave("input", t.tok)
    late.collect()
    qkv.step_on(2, 1)
    out.step_on(0, 3)
    up.step_on(2, 4)
    t.total_last[...] = jnp.concatenate([t.norm_grad[0:1, :], t.norm_grad[1:2, :]], axis=1)
    last.start()
    qkv.step_on(0, 3)
    last.spread()
    factors.finish(3)
    pooled_factors.finish()
    col_factors = t.held_cols[...].reshape(-1, t.held_cols.shape[3])
    grown = dot_tn(col_factors, t.held_inner[...].reshape(-1, t.held_inner.shape[3]))
    t.down[...] = grown[:out_step]
    leave("down", t.down)
    grown = dot_tn(col_factors, t.held_pooled[...].reshape(-1, t.held_pooled.shape[3]))
    t.proj[...] = grown[out_step:].T[: width // place.rows]
    leave("proj", t.proj)
    qkv.step_on(1, 2)
    out.step_on(0, 4)
    qkv.step_on(2, 2)
    qkv.step_on(1, 3)
    t.norms[:, 2 * width :] = late.finish()[:, : 2 * width + 128]
    qkv.step_on(2, 3)
    last.collect()
    for chunk in range(len(up.halves)):
        up.finish(chunk, 4)
    t.up[...] = up.total()
    leave("up", t.up)
    t.norms[:, : 2 * width] = last.finish()
    leave("norm", t.norms)
    out.finish(0, 4)
    t.out[:, :128] = out.total()
    for chunk in range(len(qkv.halves)):
        qkv.finish(chunk, 3)
    total = qkv.total()
    t.qkv[...] = total[:, : 3 * out_step]
    leave("qkv", t.qkv)
    t.out[:, 128:] = total[:, 3 * out_step : 4 * out_step - 128]
    leave("out", t.out)
    for copy in left:
        copy.wait()


def whole(shape):
    return pl.BlockSpec(shape, lambda *_: (0,) * len(shape))


in_vmem = pl.BlockSpec(memory_space=pltpu.VMEM)
in_smem = pl.BlockSpec(memory_space=pltpu.SMEM)
anywhere = pl.BlockSpec(memory_space=pl.ANY)


def plain(kernel, outs, ins, scratch, name, out_specs=None, **settings):
    return pl.pallas_call(
        kernel,
        out_shape=outs,
        in_specs=ins,
        out_specs=out_specs or [in_vmem] * len(outs),
        scratch_shapes=scratch,
        compiler_params=pltpu.CompilerParams(vmem_limit_bytes=VMEM_LIMIT, **settings),
        name=name,
    )


def array(shape, dtype):
    return jax.ShapeDtypeStruct(shape, dtype)


def partners(x, col_count):
    order = [(i, i ^ 2) for i in range(col_count)]
    near = [(i, i ^ 1) for i in range(col_count)]
    far = lax.ppermute(x, "col", order)
    return [x, lax.ppermute(x, "col", near), far, lax.ppermute(far, "col", near)]


def body(
    image_tokens, image_norm_gain, image_norm_bias, image_qkv, image_out, image_up, image_down,
    text_tokens, text_lengths, norm1_gain, norm1_bias, norm2_gain, norm2_bias,
    text_qkv, text_out, text_up, text_down, text_proj,
):
    tokens, width = text_tokens.shape
    captions = text_lengths.shape[0]
    length = tokens // captions
    wide = text_up.shape[1]
    row_count, col_count = lax.axis_size("row"), lax.axis_size("col")
    row, col = lax.axis_index("row"), lax.axis_index("col")
    pair_total = captions * row_count * col_count
    image_rows, images = image_tokens.shape[0], image_tokens.shape[0] // IMG_TOK

    count = row_count * col_count
    joined = (row_count, col_count) == (8, 4)
    vectors = (norm1_gain, norm1_bias, norm2_gain, norm2_bias)
    weights = (text_qkv, text_out, text_up, text_down, text_proj)
    weight_scratch = [pltpu.VMEM(w.shape, bf16) for w in weights]

    text_shapes = (
        array((tokens, width), bf16),
        array((captions, width), bf16),
        array((captions, width), f32),
        array((captions, width), bf16),
        array((captions, wide), bf16),
        array((tokens, 3 * width), bf16),
        array((tokens, width), bf16),
        array((tokens, width), f32),
        array((tokens, wide), bf16),
        array((width, tokens), bf16),
    )
    text_specs = [in_vmem, in_smem] + [in_vmem] * 4 + [anywhere] * 5
    text_buffers = weight_scratch + [
        pltpu.VMEM((tokens, width), bf16),
        pltpu.VMEM((tokens, wide), bf16),
        pltpu.VMEM((captions, 1), jnp.int32),
        pltpu.VMEM((1, tokens), f32),
        pltpu.SemaphoreType.DMA((5,)),
    ]
    text_in = (text_tokens, text_lengths, *vectors, *weights)
    groups = 4
    group_rows, group_images = image_rows // groups, images // groups
    mix_buffers = [
        pltpu.VMEM((group_rows, width), bf16),
        pltpu.VMEM((group_rows, 3 * width), bf16),
        pltpu.VMEM((group_rows, width), bf16),
    ]
    mix_weights = [pltpu.VMEM((width, 3 * width), bf16), pltpu.VMEM((width, width), bf16)]
    embed_weights = [pltpu.VMEM((width, wide), bf16), pltpu.VMEM((wide, width), bf16)]
    both = ("row", "col")

    if joined:
        halves, rows = 2, width // row_count
        out_step, inner_step = width // col_count, wide // row_count
        packed = -(-rows // 128) * 128
        dma = pltpu.SemaphoreType.DMA
        widths = scatter_widths(wide, width, col_count)
        sets = {tag: scatter_scratch(rows, each) for each, tag in zip(widths, ("_up", "_outs", "_qkv"))}
        scratch = dict(zip(text_names, (pltpu.VMEM(shape.shape, shape.dtype) for shape in text_shapes)))
        scratch |= dict(zip(text_scratch, text_buffers))
        scratch |= {
            "tok": pltpu.VMEM((tokens, width), bf16),
            "iw_qkv": pltpu.VMEM((3, 4, 2, rows, width), bf16),
            "iw_out": pltpu.VMEM((2, 4, rows, width), bf16),
            "iw_up": pltpu.VMEM((2, 2, 4, 2, rows, width), bf16),
            "iw_down": pltpu.VMEM((2, 2, 4, 2, rows, width), bf16),
            "image_tok": pltpu.VMEM((2, group_rows, width), bf16),
            "image_mean": pltpu.VMEM((images, width), f32),
            "sums": pltpu.VMEM((images // halves, wide), f32),
            "own": pltpu.VMEM((images, width), bf16),
            "own_inner": pltpu.VMEM((row_count, captions, inner_step), bf16),
            "held_inner": pltpu.VMEM((col_count, row_count, captions, inner_step), bf16),
            "own_pooled": pltpu.VMEM((row_count, captions, packed), bf16),
            "held_pooled": pltpu.VMEM((col_count, row_count, captions, packed), bf16),
            "up": pltpu.VMEM((rows, wide // col_count), f32),
            "out": pltpu.VMEM((rows, out_step), f32),
            "qkv": pltpu.VMEM((rows, 3 * out_step), f32),
            "down": pltpu.VMEM((out_step, inner_step), f32),
            "proj": pltpu.VMEM((rows, out_step), f32),
            "norms": pltpu.VMEM((1, 4 * width + 128), f32),
            "leave_sems": dma((7,)),
            "own_sums": pltpu.VMEM((1, pair_total), f32),
            "all_sums": pltpu.VMEM((count, 1, pair_total), f32),
            "tok_sems": dma((3,)),
            "again_sems": dma((3,)),
            "save_sems": dma((2,)),
            "sends": dma((6, 4)),
            "recvs": dma((6, 5)),
            "factor_local": dma((2,)),
            "factor_sends": dma((2, 4)),
            "factor_recvs": dma((2, 4)),
            "image_sends": dma((halves, 4)),
            "image_recvs": dma((halves, 4)),
            "sum_sends": dma((1,)),
            "sum_recvs": dma((1,)),
            "embed_grad": pltpu.VMEM((captions, width), f32),
            "loss": pltpu.VMEM((1, 128), f32),
            "branch": pltpu.VMEM((captions, width), bf16),
            "norm_grad": pltpu.VMEM((8, width), f32),
            "outer": pltpu.VMEM((tokens, width), f32),
            "mid_grad": pltpu.VMEM((tokens, width), f32),
            "near_qkv": pltpu.VMEM((2, 4, 2, rows, width), bf16),
            "own_cols": pltpu.VMEM((col_count, captions, 2 * out_step), bf16),
            "held_cols": pltpu.VMEM((col_count, row_count, captions, 2 * out_step), bf16),
            "col_sends": dma((7,)),
            "col_recvs": dma((7,)),
        }
        scratch |= dict(zip(("x1_outs", "y1_outs"), sets["_outs"][2:]))
        for tag, buffers in sets.items():
            scratch |= {name + tag: buffer for name, buffer in zip(scatter_names, buffers[4:])}
        for tag, size in (("_late", 2 * width + 256), ("_last", 2 * width)):
            scratch |= {name + tag: buffer for name, buffer in zip(total_names, chip_sum_scratch(size, count // 2))}
        up_grad, out_grad, qkv_grad, grad_down, grad_proj, norm_total, hidden, input_grad, _ = plain(
            functools.partial(joined_kernel, tuple(scratch)),
            (
                array((rows, wide // col_count), f32),
                array((rows, out_step), f32),
                array((rows, 3 * out_step), f32),
                array((out_step, inner_step), f32),
                array((rows, out_step), f32),
                array((1, 4 * width + 128), f32),
                array((tokens, width), bf16),
                array((tokens, width), bf16),
                array((tokens, wide), bf16),
            ),
            [in_smem] + [in_vmem] * 6 + [anywhere] * 11,
            list(scratch.values()),
            "joined",
            out_specs=[anywhere] * 9,
            collective_id=1,
            has_side_effects=True,
        )(
            text_lengths, *vectors, image_norm_gain, image_norm_bias, text_tokens, *weights, image_tokens,
            image_qkv.reshape(2, rows, -1), image_out.reshape(2, rows, -1), image_up.reshape(2, rows, -1),
            image_down.reshape(4, 2, rows, -1),
        )
        large = (hidden, input_grad, qkv_grad, out_grad, up_grad, grad_down, grad_proj)
        results = (array((1, 1), f32), *[array((width,), f32)] * 4, *(array(g.shape, g.dtype) for g in large))
        loss, *rest = plain(
            functools.partial(hand_over_kernel, pair_total), results, [in_vmem] * 8, [], "hand_over"
        )(norm_total, *large)
        norms, (hidden, input_grad, qkv_grad, out_grad, up_grad, grad_down, grad_proj) = rest[:4], rest[4:]
        return (
            loss.reshape(()), hidden, input_grad, *norms, qkv_grad, out_grad, up_grad, grad_down.T, grad_proj,
        )

    (hidden, text_embed, projected, pooled, inner_sum, heads, mixed, mid, slope, turned) = plain(
        text_forward_kernel, text_shapes, text_specs, text_buffers, "text_forward"
    )(*text_in)
    qkv_parts = partners(image_qkv, col_count)
    out_parts = partners(image_out, col_count)
    up_parts = partners(image_up, col_count)
    down_parts = partners(image_down, col_count)
    parts = [anywhere] * (2 * col_count)
    image_normed, image_mean = pl.pallas_call(
        functools.partial(image_mix_kernel, col_count),
        grid=(groups,),
        out_shape=(array((image_rows, width), bf16), array((images, width), f32)),
        in_specs=[
            pl.BlockSpec((group_rows, width), lambda i: (i, 0)),
            whole(image_norm_gain.shape),
            whole(image_norm_bias.shape),
        ]
        + parts,
        out_specs=(
            pl.BlockSpec((group_rows, width), lambda i: (i, 0)),
            pl.BlockSpec((group_images, width), lambda i: (i, 0)),
        ),
        scratch_shapes=mix_weights + mix_buffers + [pltpu.SemaphoreType.DMA((2, col_count))],
        compiler_params=pltpu.CompilerParams(vmem_limit_bytes=VMEM_LIMIT),
        name="image_mix",
    )(image_tokens, image_norm_gain, image_norm_bias, *qkv_parts, *out_parts)
    image_embed = pl.pallas_call(
        functools.partial(image_embed_kernel, col_count),
        grid=(groups,),
        out_shape=array((images, width), bf16),
        in_specs=[pl.BlockSpec((group_rows, width), lambda i: (i, 0)), whole((images, width))] + parts,
        out_specs=whole((images, width)),
        scratch_shapes=embed_weights
        + [pltpu.VMEM((images, wide), f32), pltpu.SemaphoreType.DMA((2, col_count))],
        compiler_params=pltpu.CompilerParams(vmem_limit_bytes=VMEM_LIMIT),
        name="image_embed",
    )(image_normed, image_mean, *up_parts, *down_parts)

    image_all = lax.all_gather(image_embed, both, axis=0, tiled=True)
    lifted = jnp.exp(logit_scale * dot_nt(image_all, text_embed))
    row_sums = lax.psum(jnp.sum(lifted, axis=1), both)
    col_sums = jnp.sum(lifted, axis=0)
    sim_grad = (0.5 * (lifted / row_sums[:, None] + lifted / col_sums[None, :])).astype(bf16)
    image_own = image_embed.astype(f32)
    embed_grad = logit_scale * (dot_tn(sim_grad, image_all) - image_own)
    positives = logit_scale * jnp.sum(image_own * text_embed.astype(f32), axis=1)
    loss_part = 0.5 * jnp.sum(jnp.log(col_sums) - 2.0 * positives)
    loss_part = loss_part + 0.5 * jnp.sum(jnp.log(row_sums)) / count

    saved = (text_tokens, heads, mixed, mid, slope, turned)
    backward_in = (text_lengths, *vectors, embed_grad, projected, *saved, *weights)
    backward_specs = [in_smem] + [in_vmem] * 6 + [anywhere] * 11
    backward_buffers = (
        [
            pltpu.VMEM((tokens, width), bf16),
            pltpu.VMEM((tokens, 3 * width), bf16),
            pltpu.VMEM((tokens, width), bf16),
            pltpu.VMEM((tokens, width), f32),
            pltpu.VMEM((tokens, wide), bf16),
        ]
        + weight_scratch
        + [
            pltpu.VMEM((tokens, width), bf16),
            pltpu.VMEM((width, tokens), bf16),
            pltpu.VMEM((tokens, width), f32),
            pltpu.VMEM((tokens, width), f32),
            pltpu.VMEM((tokens, width), bf16),
            pltpu.VMEM((tokens, width), bf16),
            pltpu.VMEM((tokens, 3 * width), bf16),
            pltpu.VMEM((captions, 1), jnp.int32),
            pltpu.VMEM((1, tokens), f32),
            pltpu.VMEM((tokens, 128), f32),
            pltpu.SemaphoreType.DMA((11,)),
        ]
    )

    def by_row(x):
        x = lax.all_to_all(x, "row", split_axis=1, concat_axis=0, tiled=True)
        return lax.all_gather(x, "col", axis=0, tiled=True)

    def by_col(x):
        x = lax.all_gather(x, "row", axis=0, tiled=True)
        return lax.all_to_all(x, "col", split_axis=1, concat_axis=0, tiled=True)

    (proj_grad, branch, up_grad, out_grad, qkv_grad, input_grad, norm_grads) = plain(
        text_backward_kernel,
        (
            array((captions, width), bf16),
            array((captions, width), bf16),
            array((col_count, width, wide // col_count), bf16),
            array((col_count, width, width // col_count), bf16),
            array((col_count, width, 3 * width // col_count), bf16),
            array((tokens, width), bf16),
            array((8, width), f32),
        ),
        backward_specs,
        backward_buffers,
        "text_backward",
    )(*backward_in)

    def scattered(matrix):
        blocks = matrix.reshape(count, width // row_count, matrix.shape[2])
        return lax.psum_scatter(blocks, ("col", "row"), scatter_dimension=0, tiled=True)[0].astype(f32)

    up_grad, out_grad, qkv_grad = scattered(up_grad), scattered(out_grad), scattered(qkv_grad)
    grad_down = dot_tn(by_row(inner_sum), by_col(branch))
    grad_proj = dot_tn(by_row(pooled), by_col(proj_grad))
    loss_total, norm_total = lax.psum((loss_part, norm_grads), both)
    norms = [norm_total[i] for i in range(4)]
    mean_loss = loss_total / pair_total
    return (
        mean_loss, hidden, input_grad, *norms, qkv_grad, out_grad, up_grad, grad_down, grad_proj,
    )


def solution(mesh):
    split = P(("row", "col"), None)
    grid = P("row", "col")
    in_specs = (
        split, P(), P(), P("col", None), P("col", None), P("col", None), P("col", None), split, P(("row", "col")),
    ) + (P(),) * 9
    out_specs = (P(), split, split, P(), P(), P(), P(), grid, grid, grid, grid, grid)
    return jax.shard_map(body, mesh=mesh, in_specs=in_specs, out_specs=out_specs, check_vma=False)
```
